32 devices in a mesh: seq: 4 (over y, core), neur: 8 (over z, x).
Axes of the slice: x: 2, y: 2, z: 4, core: 2. Of those that a mesh axis runs over, the one named last changes fastest.
Arguments:
- inputs: bfloat16 [2048, 16384], P('neur', 'seq'), may hold values from -6 to 6
- weight_one: bfloat16 [2048, 2048], P('neur'), may hold values from -0.125 to 0.125
- weight_two: bfloat16 [2048, 2048], P('neur'), may hold values from -0.125 to 0.125
- gain_one: float32 [2048], P('neur'), may hold values from 0.5 to 1.5
- gain_two: float32 [2048], P('neur'), may hold values from 0.5 to 1.5
- bias_one: float32 [2048], P('neur'), may hold values from -3 to 3
- bias_two: float32 [2048], P('neur'), may hold values from -3 to 3
- decay_one: float32 [2048], P('neur'), may hold values from 0.95 to 0.9995
- decay_two: float32 [2048], P('neur'), may hold values from 0.95 to 0.9995
- lengths: int32 [4, 12], P('seq'), may hold values from 1 to 1024, 3584 in all within a row
- frame_mask: int32 [16384], P('seq'), may hold values 0 or 1
- out_grad: bfloat16 [2048, 16384], P('neur', 'seq'), may hold values from -6 to 6
Outputs:
- output: float32 [2048, 16384], P('neur', 'seq')
- input_grad: float32 [2048, 16384], P('neur', 'seq')
- weight_one_grad: float32 [2048, 2048], P('neur')
- gain_one_grad: float32 [2048], P('neur')
- bias_one_grad: float32 [2048], P('neur')
- decay_one_grad: float32 [2048], P('neur')
- weight_two_grad: float32 [2048, 2048], P('neur')
- gain_two_grad: float32 [2048], P('neur')
- bias_two_grad: float32 [2048], P('neur')
- decay_two_grad: float32 [2048], P('neur')
The draws below stay inside these ranges and needn't reach their ends.
Inputs may be any that keep to these rules, and one draw needn't show every extreme that they name: `lengths`: row b lists the 12 sequences packed from the first slot of block b; each row sums to 3584 and holds one sequence of exactly 1024 frames.
All inputs are finite; a program needn't handle non-finite values. No bound on the sum of `frame_mask` on one device may be relied on, other than what follows from the above.
Results may differ from the reference program's by a relative error of at most 0.0065.
Values may be sent and summed in bfloat16 or wider, within the bound.
A program may use at most 256 MiB of HBM per device.

```python
import math
from functools import partial
import jax
import jax.numpy as jnp
import numpy as np
from jax import lax

H = 2048
TOK_DEV = 4096
SEQS_DEV = 12
VALID_DEV = 3584
LONGEST = 1024
TOKENS = 16384
N_SEQ = 4


def plant(entries, key, least, largest):
    spot = [jax.random.randint(jax.random.fold_in(key, axis), (), 0, length) for axis, length in enumerate(entries.shape)]
    longest = entries.shape.index(max(entries.shape))
    next_to = spot[:longest] + [(spot[longest] + 1) % entries.shape[longest]] + spot[longest + 1:]
    return entries.at[tuple(spot)].set(least).at[tuple(next_to)].set(largest)


def steps_of(own_key, shape, split, least, largest):
    def one(axis_at, parts):
        heights = jax.random.uniform(jax.random.fold_in(jax.random.fold_in(own_key, 6), axis_at), (parts,), jnp.float32, least / len(split), largest / len(split))
        return jnp.repeat(jnp.exp(heights), shape[axis_at] // parts).reshape((-1,) + (1,) * (len(shape) - axis_at - 1))

    factor_of = one(*split[0])
    for cut in split[1:]:
        factor_of = factor_of * one(*cut)
    return factor_of


def length_profile(number_of, total, limit, lean):
    weights = [(1 << 20) // math.isqrt(rank ** lean) + 1 for rank in range(2, number_of + 1)]
    spare, given = total - limit - (number_of - 1), [1] * (number_of - 1)
    while spare > 0:
        candidates = [i for i in range(number_of - 1) if given[i] < limit]
        whole, left = sum([weights[i] for i in candidates]), spare
        for i in candidates:
            extra = min(limit - given[i], max(1, left * weights[i] // whole), spare)
            given[i] = given[i] + extra
            spare = spare - extra
    return np.array([limit] + given)


def ragged(stream_key, amount, total, bound, slope):
    if amount == 2:
        one = jax.random.randint(stream_key, (), max(1, total - bound), min(bound, total - 1) + 1)
        return jnp.stack([one, total - one])
    tallies = jnp.asarray(length_profile(amount, total, bound, slope), jnp.int32)
    twos = (amount - 1) // 2
    giver, taker = tallies[1:1 + 2 * twos:2], tallies[2:2 + 2 * twos:2]
    margin = jnp.minimum(giver - 1, bound - taker)
    shifted = jax.random.randint(jax.random.fold_in(stream_key, 1), (twos,), 0, 1 << 20) % (margin + 1)
    tallies = tallies.at[1:1 + 2 * twos:2].set(giver - shifted).at[2:2 + 2 * twos:2].set(taker + shifted)
    return tallies[jax.random.permutation(jax.random.fold_in(stream_key, 2), amount)]


def noise(own_key, dims, deviation, bound, shards=(), kind=jnp.bfloat16):
    values = deviation * jax.random.normal(own_key, dims, jnp.float32)
    if shards:
        values = values * steps_of(own_key, dims, shards, -0.22, 0.18)
    return jnp.clip(values, -bound, bound).astype(kind)


def setup_inputs(seed: int = 0) -> dict:
    keys = jax.random.split(jax.random.key(seed), 13)
    return {
        "inputs": noise(keys[0], (H, TOKENS), 1.0, 6.0, ((0, 8), (1, 4))),
        "weight_one": noise(keys[1], (H, H), H ** -0.5, 0.125, ((0, 8),)),
        "weight_two": noise(keys[2], (H, H), H ** -0.5, 0.125, ((0, 8),)),
        "gain_one": jnp.clip(1.0 + 0.1 * jax.random.normal(keys[3], (H,), jnp.float32), 0.5, 1.5),
        "gain_two": jnp.clip(1.0 + 0.1 * jax.random.normal(keys[4], (H,), jnp.float32), 0.5, 1.5),
        "bias_one": noise(keys[5], (H,), 0.5, 3.0, ((0, 8),), jnp.float32),
        "bias_two": noise(keys[6], (H,), 0.5, 3.0, ((0, 8),), jnp.float32),
        "decay_one": jnp.clip(0.95 + 0.04949999 * jax.random.uniform(keys[7], (H,), jnp.float32) ** steps_of(keys[7], (H,), ((0, 8),), -0.2, 0.2), 0.95, 0.9995),
        "decay_two": jnp.clip(0.95 + 0.04949999 * jax.random.uniform(keys[8], (H,), jnp.float32) ** steps_of(keys[8], (H,), ((0, 8),), -0.2, 0.2), 0.95, 0.9995),
        "lengths": jax.vmap(lambda own: ragged(own, SEQS_DEV, VALID_DEV, LONGEST, 2))(jax.random.split(keys[9], N_SEQ)).reshape((N_SEQ, SEQS_DEV)).astype(jnp.int32),
        "frame_mask": plant((jax.random.randint(keys[10], (TOKENS,), 0, 8) < 7).astype(jnp.int32), jax.random.fold_in(keys[10], 1), 0, 1),
        "out_grad": noise(keys[11], (H, TOKENS), 1.0, 6.0, ((0, 8), (1, 4))),
    }


epsilon = 1e-05

@jax.custom_vjp
def low(v):
    return lax.optimization_barrier(v.astype(jnp.bfloat16)).astype(jnp.float32)

@jax.custom_vjp
def low_back(v):
    return v

def low_keep(v):
    return (low(v), None)

def low_pass(kept, grad):
    return (grad,)

def back_keep(v):
    return (v, None)

def back_low(kept, grad):
    return (low(grad),)
low.defvjp(low_keep, low_pass)
low_back.defvjp(back_keep, back_low)

def frame_tables(lengths, frame_mask):
    positions = jnp.arange(TOK_DEV, dtype=jnp.int32)
    offsets = (jnp.cumsum(lengths, axis=1) - lengths).astype(jnp.int32)
    filled = lax.optimization_barrier(jnp.sum(lengths, axis=1)).astype(jnp.int32)
    begins = jnp.any(positions[None, :, None] == offsets[:, None, :], axis=2)
    inside = positions[None, :] < filled[:, None]
    continues = jnp.where(begins, 0.0, 1.0).astype(jnp.float32).reshape(TOKENS)
    counted = jnp.where(inside & (frame_mask.reshape(N_SEQ, TOK_DEV) > 0), 1.0, 0.0).astype(jnp.float32).reshape(TOKENS)
    return (continues, counted)

def neuron_block(projected, gain_row, bias_row, decay_rate, continues, counted):
    frames = jnp.sum(counted)
    average = lax.optimization_barrier(jnp.sum(counted[:, None] * projected, axis=0)) / frames
    second = lax.optimization_barrier(jnp.sum(counted[:, None] * projected * projected, axis=0)) / frames
    inv_std = lax.rsqrt(second - average * average + epsilon)
    normed = (projected - average) * inv_std
    driving = jnp.sqrt(1.0 - decay_rate * decay_rate) * gain_row * normed
    driving = driving.reshape(N_SEQ, TOK_DEV, -1).transpose(1, 0, 2)
    link_flags = continues.reshape(N_SEQ, TOK_DEV).T

    def advance(hidden_state, inputs_now):
        hidden_state = decay_rate * inputs_now[1][:, None] * hidden_state + inputs_now[0]
        return (hidden_state, hidden_state)
    initial = jnp.zeros((N_SEQ, projected.shape[1]), projected.dtype)
    _, states = lax.scan(advance, initial, (driving, link_flags))
    states = states.transpose(1, 0, 2).reshape(TOKENS, -1)
    return counted[:, None] * jax.nn.softplus(states + bias_row)

def recurrent_layer(layer_input, weight, gain_row, bias_row, decay_rate, continues, counted):
    rounded = low(low_back(layer_input))
    projected = low_back(low(jnp.dot(rounded, weight.T, precision=lax.Precision.HIGHEST, preferred_element_type=jnp.float32)))
    block_width = min(256, H)
    block_count = H // block_width
    stacked = projected.reshape(TOKENS, block_count, block_width).transpose(1, 0, 2)
    runner = jax.checkpoint(partial(neuron_block, continues=continues, counted=counted))

    def one_block(operands):
        return runner(operands[0], operands[1], operands[2], operands[3])
    result = lax.map(one_block, (stacked, gain_row.reshape(block_count, block_width), bias_row.reshape(block_count, block_width), decay_rate.reshape(block_count, block_width)))
    return result.transpose(1, 0, 2).reshape(TOKENS, H)

def reference(inputs, weight_one, weight_two, gain_one, gain_two, bias_one, bias_two, decay_one, decay_two, lengths, frame_mask, out_grad):
    continues, counted = frame_tables(lengths, frame_mask)

    def forward(layer_input, w_first, w_second, g_first, g_second, b_first, b_second, u_first, u_second):
        first_out = recurrent_layer(layer_input, w_first, g_first, b_first, u_first, continues, counted)
        second_out = recurrent_layer(first_out, w_second, g_second, b_second, u_second, continues, counted)
        return layer_input + second_out
    primals = (inputs.astype(jnp.float32).T, weight_one.astype(jnp.float32), weight_two.astype(jnp.float32), gain_one, gain_two, bias_one, bias_two, decay_one, decay_two)
    output, pullback = jax.vjp(forward, *primals)
    gradients = pullback(out_grad.astype(jnp.float32).T)
    return (output.T, gradients[0].T, gradients[1], gradients[3], gradients[5], gradients[7], gradients[2], gradients[4], gradients[6], gradients[8])
```

```python
import functools

import jax
import jax.numpy as jnp
from jax import lax
from jax.experimental import pallas as pl
from jax.experimental.pallas import tpu as pltpu
from jax.sharding import PartitionSpec as P

epsilon = 1e-05
block_span = 128
valid_frames = 3584
f32 = jnp.float32
bf16 = jnp.bfloat16
MESH = pl.DeviceIdType.MESH


def wide(tile, width):
    return jnp.concatenate([tile] * (width // 128), axis=1)


def at(index, size):
    if isinstance(index, int):
        return pl.ds(index * size, size)
    return pl.ds(pl.multiple_of(index * size, size), size)


def power(base, exponent):
    result = None
    while exponent:
        if exponent % 2:
            result = base if result is None else result * base
        exponent //= 2
        base = base * base
    return result


def log_of(rate):
    u = 1.0 - rate
    series = jnp.full_like(u, 1.0 / 8)
    for order in range(7, 0, -1):
        series = series * u + 1.0 / order
    return -u * series


GAIN, BIAS, DECAY = 0, 2, 4


class Sizes:
    def __init__(self, n, seqs, H, fb, tok_dev):
        self.n, self.seqs, self.H, self.fb, self.tok_dev = n, seqs, H, fb, tok_dev
        self.T = valid_frames // n
        self.steps = self.T // 8
        self.valid = valid_frames
        self.qc = H // seqs
        self.Z = n // 2
        self.odd = self.T % 128
        self.win = self.T + self.odd
        self.L = min(512, H)


def fits(n, seqs, H, fb, tok_dev):
    if valid_frames % n or n % 2 or n > 8 or seqs != 4 or fb * n != H or fb % 128 or H % 512:
        return False
    T = valid_frames // n
    return T % 64 == 0 and valid_frames % 128 == 0 and tok_dev >= valid_frames


class Gather:
    def __init__(self, env, source, full, sends, recvs, first, second):
        self.env, self.full, self.sends, self.recvs = env, full, sends, recvs
        self.first, self.second = first, second
        z = env.z
        Z = env.sz.Z
        self.source = source.at[:, at(env.s, env.sz.qc)]
        self.events = [(0, 0, 0)]
        for dz in range(1, Z):
            self.events += [(dz, 0, 0), (dz - 1, 1, 0)]
        self.events.append((Z - 1, 1, 0))
        self.events += [(dz, a, 1) for dz, a, _ in self.events]
        self.done = 0

    def block(self, dz, a, b, flip=0):
        env = self.env
        coords = {"x": env.x, "y": env.y}
        coords[self.first] = (coords[self.first] + a) % 2
        coords[self.second] = (coords[self.second] + b) % 2
        zz = (env.z + env.sz.Z - dz) % env.sz.Z
        cc = (env.c + flip) % 2
        return self.full.at[
            at(2 * zz + coords["x"], env.sz.fb), at(2 * coords["y"] + cc, env.sz.qc)
        ]

    def index(self, stage, dz, a, b):
        Z = self.env.sz.Z
        if stage == "z":
            return dz - 1
        if stage == "first":
            return Z - 1 + dz
        if stage == "second":
            return 2 * Z - 1 + 2 * dz + a
        return 4 * Z - 1 + 4 * dz + 2 * a + b

    def copy(self, stage, source, dest, dz, a, b, target):
        k = self.index(stage, dz, a, b)
        return pltpu.make_async_remote_copy(
            src_ref=source,
            dst_ref=dest,
            send_sem=self.sends.at[k],
            recv_sem=self.recvs.at[k],
            device_id=target,
            device_id_type=MESH,
        )

    def arrival(self, dz, a, b):
        stage = "second" if b else "first" if a else "z"
        block = self.block(dz, a, b)
        self.copy(stage, block, block, dz, a, b, self.env.across("x")).wait_recv()

    def start(self):
        env = self.env
        own = self.block(0, 0, 0)
        for dz in range(1, env.sz.Z):
            target = {"neur": 2 * ((env.z + dz) % env.sz.Z) + env.x}
            self.copy("z", self.source, own, dz, 0, 0, target).start()
        self.relay(self.source, 0, 0, 0)
        self.done = 1

    def relay(self, source, dz, a, b):
        env = self.env
        dest = self.block(dz, a, b)
        if not a and not b:
            self.copy("first", source, dest, dz, a, b, env.across(self.first)).start()
        if not b:
            self.copy("second", source, dest, dz, a, b, env.across(self.second)).start()
        self.copy("core", source, dest, dz, a, b, env.across("core")).start()

    def advance(self, count=None):
        last = len(self.events) if count is None else min(len(self.events), self.done + count)
        for dz, a, b in self.events[self.done : last]:
            self.arrival(dz, a, b)
            self.relay(self.block(dz, a, b), dz, a, b)
        self.done = last

    def finish(self):
        self.advance()
        for dz, a, b in self.events:
            block = self.block(dz, a, b, 1)
            self.copy("core", block, block, dz, a, b, self.env.across("core")).wait_recv()

    def drain(self):
        block = self.block(0, 0, 0)
        for k in range(8 * self.env.sz.Z - 1):
            pltpu.make_async_remote_copy(
                src_ref=block,
                dst_ref=block,
                send_sem=self.sends.at[k],
                recv_sem=self.recvs.at[k],
                device_id=self.env.across("x"),
                device_id_type=MESH,
            ).wait_send()


class Reduce:
    def __init__(self, env, grads, frames, land, stage, sends, recvs, first, second):
        self.env, self.grads, self.frames, self.land, self.stage = env, grads, frames, land, stage
        self.sends, self.recvs, self.first, self.second = sends, recvs, first, second

    def place(self, p):
        env, Z = self.env, self.env.sz.Z
        coords = {"x": env.x, "y": env.y}
        coords[self.first] = (coords[self.first] + 1 - p // (2 * Z)) % 2
        coords[self.second] = (coords[self.second] + 1 - (p // Z) % 2) % 2
        zz = (env.z + p % Z + 1) % Z
        return zz, coords["x"], coords["y"]

    def tile(self, p, cc):
        sz = self.env.sz
        zz, xx, yy = self.place(p)
        return jnp.dot(
            self.grads[at(2 * zz + xx, sz.fb), :],
            self.frames[:, at(2 * yy + cc, sz.qc)],
            preferred_element_type=f32,
        )

    def copy(self, k, target):
        return pltpu.make_async_remote_copy(
            src_ref=self.stage.at[k],
            dst_ref=self.land(k),
            send_sem=self.sends.at[k],
            recv_sem=self.recvs.at[k],
            device_id=target,
            device_id_type=MESH,
        )

    def landed(self, k):
        self.copy(k, self.env.across("x")).wait_recv()
        return self.land(k)[...].astype(f32)

    def send(self, k, tile, target):
        self.stage[k] = tile.astype(bf16)
        self.copy(k, target).start()

    def cores(self):
        env, Z = self.env, self.env.sz.Z

        def one(p, _):
            self.send(p, self.tile(p, (env.c + 1) % 2), env.across("core"))
            return 0

        lax.fori_loop(0, 4 * Z, one, 0)

    def firsts(self, low=0, high=None):
        env, Z = self.env, self.env.sz.Z

        def one(p, _):
            tile = self.tile(p, env.c) + self.landed(p)
            self.send(4 * Z + p, tile, env.across(self.first))
            return 0

        lax.fori_loop(low, 2 * Z if high is None else high, one, 0)

    def seconds(self):
        env, Z = self.env, self.env.sz.Z

        def one(p, _):
            tile = self.tile(p, env.c) + self.landed(p) + self.landed(p + 2 * Z)
            self.send(4 * Z + p, tile, env.across(self.second))
            return 0

        lax.fori_loop(2 * Z, 3 * Z, one, 0)

    def lines(self):
        env, Z = self.env, self.env.sz.Z

        def one(p, _):
            tile = self.tile(p, env.c) + self.landed(p) + self.landed(p + 2 * Z)
            tile = tile + self.landed(p + 3 * Z)
            target = {"neur": 2 * ((env.z + p % Z + 1) % Z) + env.x}
            self.send(4 * Z + p, tile, target)
            return 0

        lax.fori_loop(3 * Z, 4 * Z - 1, one, 0)

    def total(self):
        env, Z = self.env, self.env.sz.Z
        p = 4 * Z - 1
        tile = self.tile(p, env.c) + self.landed(p) + self.landed(p + 2 * Z)
        tile = tile + self.landed(p + 3 * Z)
        for k in range(7 * Z, 8 * Z - 1):
            tile = tile + self.landed(k)
        return tile

    def drain(self):
        for k in range(8 * self.env.sz.Z - 1):
            self.copy(k, self.env.across("x")).wait_send()


class Result:
    def __init__(self, env, whole, block, sends, recvs, local):
        self.env, self.whole, self.block = env, whole, block
        self.sends, self.recvs, self.local = sends, recvs, local

    def part(self, flip_y, flip_c):
        env = self.env
        s = 2 * ((env.y + flip_y) % 2) + (env.c + flip_c) % 2
        return self.whole.at[:, at(s, env.sz.qc)]

    def copy(self, k, source, dest, target):
        return pltpu.make_async_remote_copy(
            src_ref=source,
            dst_ref=dest,
            send_sem=self.sends.at[k],
            recv_sem=self.recvs.at[k],
            device_id=target,
            device_id_type=MESH,
        )

    def start(self):
        env, own = self.env, self.part(0, 0)
        self.copy(0, self.block, own, env.across("y")).start()
        self.copy(1, self.block, own, env.across("core")).start()
        pltpu.make_async_copy(self.block, own, self.local).start()

    def finish(self):
        env = self.env
        other = self.part(1, 0)
        self.copy(0, self.block, other, env.across("y")).wait_recv()
        forward = self.copy(2, other, other, env.across("core"))
        forward.start()
        own = self.part(0, 0)
        pltpu.make_async_copy(self.block, own, self.local).wait()
        self.copy(0, self.block, own, env.across("y")).wait_send()
        self.copy(1, self.block, self.part(0, 1), env.across("core")).wait()
        forward.wait_send()
        self.copy(2, other, self.part(1, 1), env.across("core")).wait_recv()


class Env:
    def across(self, axis):
        if axis == "x":
            return {"neur": 2 * self.z + 1 - self.x}
        if axis == "y":
            return {"seq": 2 * (1 - self.y) + self.c}
        return {"seq": 2 * self.y + 1 - self.c}


def network(
    sz,
    x_hbm,
    g_hbm,
    w_one,
    w_two,
    own_par,
    cont,
    counted,
    aux,
    out_land,
    dx_land,
    dw_one,
    dw_two,
    small,
    raw,
    perm,
    eye,
    xs,
    gs,
    xr,
    gr,
    p_one,
    p_two,
    x_two,
    dp,
    dpt,
    s_one,
    s_two,
    wf_one,
    wf_two,
    land,
    stage,
    fin,
    par,
    ends,
    work,
    pay,
    arrive,
    seqpay,
    seqland,
    back,
    backland,
    local_sems,
    par_sends,
    par_recvs,
    frame_sends,
    frame_recvs,
    gather_sends,
    gather_recvs,
    hop_sends,
    hop_recvs,
    seq_sends,
    seq_recvs,
    reduce_sends,
    reduce_recvs,
    final_sends,
    final_recvs,
):
    n, seqs, H, fb, T, steps, L = sz.n, sz.seqs, sz.H, sz.fb, sz.T, sz.steps, sz.L
    env = Env()
    env.sz = sz
    me = lax.axis_index("neur")
    mine = lax.axis_index("seq")
    env.j, env.s = me, mine
    env.z, env.x, env.y, env.c = me // 2, me % 2, mine // 2, mine % 2

    barrier = pltpu.get_barrier_semaphore()
    for o in range(1, n):
        pl.semaphore_signal(
            barrier, inc=1, device_id={"neur": (me + o) % n}, device_id_type=MESH
        )
    for o in range(1, seqs):
        pl.semaphore_signal(
            barrier, inc=1, device_id={"seq": (mine + o) % seqs}, device_id_type=MESH
        )
    load_x = pltpu.make_async_copy(x_hbm.at[:, pl.ds(0, sz.valid)], raw, local_sems.at[0])
    load_x.start()
    pl.semaphore_wait(barrier, n - 1 + seqs - 1)

    def neur_copy(source, dest, send, recv, i):
        return pltpu.make_async_remote_copy(
            src_ref=source,
            dst_ref=dest,
            send_sem=send,
            recv_sem=recv,
            device_id={"neur": i},
            device_id_type=MESH,
        )

    def seq_copy(source, dest, send, recv, i):
        return pltpu.make_async_remote_copy(
            src_ref=source,
            dst_ref=dest,
            send_sem=send,
            recv_sem=recv,
            device_id={"seq": i},
            device_id_type=MESH,
        )

    def others(body, count=n, own=me):
        def one(o, _):
            body((own + o) % count)
            return 0

        lax.fori_loop(1, count, one, 0)

    own_lanes = at(me, fb)

    def par_copy(i):
        return neur_copy(own_par, par.at[:, own_lanes], par_sends.at[i], par_recvs.at[me], i)

    def par_wait(i):
        neur_copy(own_par, par.at[:, at(i, fb)], par_sends.at[i], par_recvs.at[i], i).wait()

    others(lambda i: par_copy(i).start())
    par[:, own_lanes] = own_par[...]

    gather_one = Gather(env, w_one, wf_one, gather_sends.at[0], gather_recvs.at[0], "x", "y")
    gather_two = Gather(env, w_two, wf_two, gather_sends.at[1], gather_recvs.at[1], "y", "x")
    own_one = pltpu.make_async_copy(gather_one.source, gather_one.block(0, 0, 0), local_sems.at[2])
    own_two = pltpu.make_async_copy(gather_two.source, gather_two.block(0, 0, 0), local_sems.at[3])
    own_one.start()
    own_two.start()
    gather_one.start()

    row = lax.broadcasted_iota(jnp.int32, (T, sz.win), 0)
    column = lax.broadcasted_iota(jnp.int32, (T, sz.win), 1)
    frame = (row % 8) * steps + row // 8
    perm[0] = jnp.where(column == frame, 1.0, 0.0).astype(bf16)
    perm[1] = jnp.where(column == frame + sz.odd, 1.0, 0.0).astype(bf16)
    row = lax.broadcasted_iota(jnp.int32, (fb, fb), 0)
    column = lax.broadcasted_iota(jnp.int32, (fb, fb), 1)
    eye[...] = jnp.where(row == column, 1.0, 0.0).astype(bf16)

    def window(i):
        start = (i // 2) * (2 * T) + (i % 2) * (T - sz.odd)
        return pl.ds(pl.multiple_of(start, 128), sz.win)

    def turned(i):
        return lax.dot_general(
            perm[i % 2], raw[:, window(i)], (((1,), (1,)), ((), ())), preferred_element_type=f32
        ).astype(bf16)

    def frames_copy(a, source, dest, i):
        return neur_copy(source, dest, frame_sends.at[a, i], frame_recvs.at[a, me], i)

    def frames_wait(a, ref, i):
        part = ref.at[:, at(i, fb)]
        neur_copy(part, part, frame_sends.at[a, i], frame_recvs.at[a, i], i).wait_recv()

    def frames_sent(a, ref, i):
        part = ref.at[:, at(i, fb)]
        neur_copy(part, part, frame_sends.at[a, i], frame_recvs.at[a, i], i).wait_send()

    load_x.wait()

    def send_x(i):
        xs[:, at(i, fb)] = turned(i)
        frames_copy(0, xs.at[:, at(i, fb)], xr.at[:, own_lanes], i).start()

    others(send_x)
    xr[:, own_lanes] = turned(me)
    load_g = pltpu.make_async_copy(g_hbm.at[:, pl.ds(0, sz.valid)], raw, local_sems.at[1])
    load_g.start()
    gather_one.advance(2)
    load_g.wait()

    def turn_g(i):
        gs[:, at(i, fb)] = turned(i)

    others(turn_g)
    gr[:, own_lanes] = turned(me)
    gather_one.finish()
    gather_two.start()
    others(lambda i: frames_copy(1, gs.at[:, at(i, fb)], gr.at[:, own_lanes], i).start())
    own_one.wait()
    own_two.wait()
    others(lambda i: frames_wait(0, xr, i))
    others(par_wait)

    def blocks(body):
        def one(b, _):
            body(at(b, L))
            return 0

        lax.fori_loop(0, H // L, one, 0)

    def project(frames, weight, result):
        def one(b, _):
            result[:, at(b, fb)] = lax.dot_general(
                frames[...],
                weight[at(b, fb), :],
                (((1,), (1,)), ((), ())),
                preferred_element_type=f32,
            ).astype(bf16)
            return 0

        lax.fori_loop(0, n, one, 0)

    def flags(t):
        tile = pl.ds(pl.multiple_of(8 * t, 8), 8)
        return wide(cont[tile, :], L), wide(counted[tile, :], L)

    def spread8(ref, r, cols, width=L):
        return jnp.broadcast_to(ref[r : r + 1, cols], (8, width))

    zero = jnp.zeros((8, L), f32)

    def down(value):
        return jnp.sum(value, axis=0, keepdims=True)

    def exchange(e, gathered, totalled):
        def out_copy(i):
            return neur_copy(
                pay.at[e, :, at(i, fb)],
                arrive.at[e, me],
                hop_sends.at[2 * e, i],
                hop_recvs.at[2 * e, me],
                i,
            )

        others(lambda i: out_copy(i).start())
        arrive[e, me] = pay[e, :, own_lanes]

        def out_wait(i):
            neur_copy(
                pay.at[e, :, at(i, fb)],
                arrive.at[e, i],
                hop_sends.at[2 * e, i],
                hop_recvs.at[2 * e, i],
                i,
            ).wait()

        others(out_wait)
        gathered()

        def along_copy(i):
            return seq_copy(
                seqpay.at[e],
                seqland.at[e, mine],
                seq_sends.at[e, i],
                seq_recvs.at[e, mine],
                i,
            )

        def along_wait(i):
            seq_copy(
                seqpay.at[e], seqland.at[e, i], seq_sends.at[e, i], seq_recvs.at[e, i], i
            ).wait()

        others(lambda i: along_copy(i).start(), seqs, mine)
        seqland[e, mine] = seqpay[e]
        others(along_wait, seqs, mine)
        sums = seqland[e, 0]
        for i in range(1, seqs):
            sums = sums + seqland[e, i]
        totalled(sums)

        def back_copy(i):
            return neur_copy(
                back.at[e, i],
                backland.at[e, :, own_lanes],
                hop_sends.at[2 * e + 1, i],
                hop_recvs.at[2 * e + 1, me],
                i,
            )

        def back_wait(i):
            neur_copy(
                back.at[e, i],
                backland.at[e, :, at(i, fb)],
                hop_sends.at[2 * e + 1, i],
                hop_recvs.at[2 * e + 1, i],
                i,
            ).wait()

        others(lambda i: back_copy(i).start())
        backland[e, :, own_lanes] = back[e, me]
        others(back_wait)

    def layer_forward(layer, frames, weight, projected, states, store, meanwhile):
        e = layer
        decay_row, gain_row, bias_row = DECAY + layer, GAIN + layer, BIAS + layer
        project(frames, weight, projected)
        meanwhile(0)

        def local_ends(cols):
            decay = spread8(par, decay_row, cols)

            def step(i, carry):
                state, first, second = carry
                pair = projected[pl.ds(pl.multiple_of(16 * i, 16), 16), cols].astype(f32)
                for h in range(2):
                    value = pair[8 * h : 8 * h + 8, :]
                    goes, count = flags(2 * i + h)
                    state = (decay * goes) * state + value
                    held = count * value
                    first = first + held
                    second = second + held * value
                return state, first, second

            state, first, second = lax.fori_loop(0, T // 16, step, (zero, zero, zero))
            ends[:, cols] = state
            pay[e, 1:2, cols] = down(first)
            pay[e, 2:3, cols] = down(second)

        blocks(local_ends)
        run_power = power(par[decay_row : decay_row + 1, :], steps)
        total = jnp.zeros((1, H), f32)
        for k in range(8):
            total = run_power * wide(aux[16 + k : 17 + k, :], H) * total + ends[k : k + 1, :]
        pay[e, 0:1, :] = total
        pay[e, 3:8, :] = jnp.zeros((5, H), f32)
        meanwhile(1)

        own_decay = own_par[decay_row : decay_row + 1, :]

        def gathered():
            whole_power = power(own_decay, T)
            carried = jnp.zeros((1, fb), f32)
            sums = jnp.zeros((8, fb), f32)
            for i in range(n):
                rows = arrive[e, i]
                back[e, i, 0:1, :] = carried
                carried = whole_power * wide(aux[8 + i : 9 + i, :], fb) * carried + rows[0:1, :]
                sums = sums + rows
            seqpay[e] = sums
            seqpay[e, 0:1, :] = wide(aux[24:25, :], fb)

        def totalled(sums):
            frames_all = sums[0:1, :]
            average = sums[1:2, :] / frames_all
            inv_std = lax.rsqrt(sums[2:3, :] / frames_all - average * average + epsilon)
            for i in range(n):
                back[e, i, 1:2, :] = average
                back[e, i, 2:3, :] = inv_std
                back[e, i, 3:4, :] = frames_all
                back[e, i, 4:8, :] = jnp.zeros((4, fb), f32)

        exchange(e, gathered, totalled)
        meanwhile(2)

        total = backland[e, 0:1, :]
        for k in range(8):
            work[k : k + 1, :] = total
            total = run_power * wide(aux[16 + k : 17 + k, :], H) * total + ends[k : k + 1, :]

        def full_scan(cols):
            decay = spread8(par, decay_row, cols)
            average = spread8(backland.at[e], 1, cols)
            inv_std = spread8(backland.at[e], 2, cols)
            bias = spread8(par, bias_row, cols)
            scale = jnp.sqrt(1.0 - decay * decay) * spread8(par, gain_row, cols) * inv_std
            ones = (1.0 - jnp.exp(wide(aux[0:8, :], L) * log_of(decay))) / (1.0 - decay)
            state = scale * (work[0:8, cols] - average * ones)
            states[0:8, cols] = state

            def step(i, state):
                pair = projected[pl.ds(pl.multiple_of(16 * i, 16), 16), cols].astype(f32)
                outs = []
                for h in range(2):
                    goes, count = flags(2 * i + h)
                    state = (decay * goes) * state + scale * (pair[8 * h : 8 * h + 8, :] - average)
                    states[pl.ds(pl.multiple_of(16 * i + 8 * h + 8, 8), 8), cols] = state
                    v = state + bias
                    soft = jnp.maximum(v, 0.0) + jnp.log(1.0 + jnp.exp(-jnp.abs(v)))
                    outs.append(count * soft)
                store[pl.ds(pl.multiple_of(16 * i, 16), 16), cols] = jnp.concatenate(
                    outs, axis=0
                ).astype(bf16)
                return state

            lax.fori_loop(0, T // 16, step, state)

        blocks(full_scan)
        meanwhile(3)

    def layer_backward(layer, upstream, projected, states, meanwhile):
        e = 2 + (1 - layer)
        decay_row, gain_row, bias_row = DECAY + layer, GAIN + layer, BIAS + layer
        run_power = power(par[decay_row : decay_row + 1, :], steps)

        def local_ends(cols):
            decay = spread8(par, decay_row, cols)
            average = spread8(backland.at[layer], 1, cols)
            inv_std = spread8(backland.at[layer], 2, cols)
            bias = spread8(par, bias_row, cols)

            def step(o, carry):
                i = T // 16 - 1 - o
                rows = pl.ds(pl.multiple_of(16 * i, 16), 16)
                pair = projected[rows, cols].astype(f32)
                ups = upstream[rows, cols].astype(f32)
                for h in (1, 0):
                    run, reach, U, V, UN, VN, B, D, DA = carry
                    goes, count = flags(2 * i + h)
                    here = pl.ds(pl.multiple_of(16 * i + 8 * h + 8, 8), 8)
                    state = states[here, cols]
                    before = states[pl.ds(pl.multiple_of(16 * i + 8 * h, 8), 8), cols]
                    local = ups[8 * h : 8 * h + 8, :] * count / (1.0 + jnp.exp(-(state + bias)))
                    states[here, cols] = local
                    normed = (pair[8 * h : 8 * h + 8, :] - average) * inv_std
                    run = local + run
                    kept = goes * before
                    link = decay * goes
                    carry = (
                        link * run,
                        link * reach,
                        U + run,
                        V + reach,
                        UN + run * normed,
                        VN + reach * normed,
                        B + local,
                        D + run * kept,
                        DA + reach * kept,
                    )
                return carry

            one = jnp.ones((8, L), f32)
            run, _, U, V, UN, VN, B, D, DA = lax.fori_loop(
                0, T // 16, step, (zero, one, zero, zero, zero, zero, zero, zero, zero)
            )
            ends[:, cols] = run
            decay_run = power(par[decay_row : decay_row + 1, cols], steps)
            part, factor = jnp.zeros((1, L), f32), jnp.ones((1, L), f32)
            for k in range(7, -1, -1):
                work[k : k + 1, cols] = part
                work[8 + k : 9 + k, cols] = factor
                through = decay_run * wide(aux[16 + k : 17 + k, :], L)
                part = through * part + ends[k : k + 1, cols]
                factor = through * factor
            pay[e, 0:1, cols] = part
            entering, scaled = work[0:8, cols], work[8:16, cols]
            pay[e, 1:2, cols] = down(U + V * entering)
            pay[e, 2:3, cols] = down(V * scaled)
            pay[e, 3:4, cols] = down(UN + VN * entering)
            pay[e, 4:5, cols] = down(VN * scaled)
            pay[e, 5:6, cols] = down(B)
            pay[e, 6:7, cols] = down(D + DA * entering)
            pay[e, 7:8, cols] = down(DA * scaled)

        blocks(local_ends)
        meanwhile(0)
        own_decay = own_par[decay_row : decay_row + 1, :]
        own_gain = own_par[gain_row : gain_row + 1, :]

        def gathered():
            whole_power = power(own_decay, T)
            carried = jnp.zeros((1, fb), f32)
            sums = [jnp.zeros((1, fb), f32)] * 4
            for i in range(n - 1, -1, -1):
                rows = arrive[e, i]
                back[e, i, 0:1, :] = carried
                for a, (plain, times) in enumerate(((1, 2), (3, 4), (5, None), (6, 7))):
                    term = rows[plain : plain + 1, :]
                    if times is not None:
                        term = term + rows[times : times + 1, :] * carried
                    sums[a] = sums[a] + term
                carried = whole_power * wide(aux[8 + i : 9 + i, :], fb) * carried + rows[0:1, :]
            for a in range(4):
                seqpay[e, a : a + 1, :] = sums[a]
            seqpay[e, 4:8, :] = jnp.zeros((4, fb), f32)

        def totalled(sums):
            rec, rec_norm = sums[0:1, :], sums[1:2, :]
            for i in range(n):
                back[e, i, 1:2, :] = rec
                back[e, i, 2:3, :] = rec_norm
                back[e, i, 3:8, :] = jnp.zeros((5, fb), f32)
            spread = jnp.sqrt(1.0 - own_decay * own_decay)
            small[3 * layer : 3 * layer + 1, :] = spread * rec_norm
            small[3 * layer + 1 : 3 * layer + 2, :] = sums[2:3, :]
            small[3 * layer + 2 : 3 * layer + 3, :] = (
                sums[3:4, :] - own_decay / spread * own_gain * rec_norm
            )

        exchange(e, gathered, totalled)
        meanwhile(1)
        total = backland[e, 0:1, :]
        for k in range(7, -1, -1):
            work[k : k + 1, :] = total
            total = run_power * wide(aux[16 + k : 17 + k, :], H) * total + ends[k : k + 1, :]

        def full_scan(cols):
            decay = spread8(par, decay_row, cols)
            average = spread8(backland.at[layer], 1, cols)
            inv_std = spread8(backland.at[layer], 2, cols)
            frames_all = spread8(backland.at[layer], 3, cols)
            scale = jnp.sqrt(1.0 - decay * decay) * spread8(par, gain_row, cols) * inv_std
            rec = spread8(backland.at[e], 1, cols) / frames_all
            rec_norm = spread8(backland.at[e], 2, cols) / frames_all * inv_std

            def step(o, carry):
                i = T // 16 - 1 - o
                rows = pl.ds(pl.multiple_of(16 * i, 16), 16)
                pair = projected[rows, cols].astype(f32)
                outs = [None, None]
                for h in (1, 0):
                    goes, count = flags(2 * i + h)
                    here = pl.ds(pl.multiple_of(16 * i + 8 * h + 8, 8), 8)
                    run = states[here, cols] + carry
                    centred = pair[8 * h : 8 * h + 8, :] - average
                    outs[h] = scale * (run - count * (rec + rec_norm * centred))
                    carry = (decay * goes) * run
                dp[rows, cols] = jnp.concatenate(outs, axis=0).astype(bf16)
                return carry

            lax.fori_loop(0, T // 16, step, work[0:8, cols])

        blocks(full_scan)
        meanwhile(2)

        def turn(b, _):
            dpt[at(b, fb), :] = lax.dot_general(
                eye[...], dp[:, at(b, fb)], (((1,), (1,)), ((), ())), preferred_element_type=f32
            ).astype(bf16)
            return 0

        lax.fori_loop(0, n, turn, 0)

    def input_gradient(weight, result):
        def one(b, _):
            result[:, at(b, fb)] = jnp.dot(
                dp[...], weight[:, at(b, fb)], preferred_element_type=f32
            ).astype(bf16)
            return 0

        lax.fori_loop(0, n, one, 0)

    def relay_two(step):
        if step == 0:
            gather_two.advance(2)
        elif step < 3:
            gather_two.advance(3)

    layer_forward(0, xr, wf_one, p_one, s_one, x_two, relay_two)
    gather_two.finish()
    others(lambda i: frames_sent(0, xs, i))
    layer_forward(1, x_two, wf_two, p_two, s_two, xs, lambda step: None)

    def place_out(a, ref, dest, i):
        return neur_copy(
            ref.at[:, at(i, fb)], dest.at[me], frame_sends.at[a, i], frame_recvs.at[a, me], i
        )

    def out_arrived(a, ref, dest, i):
        neur_copy(
            ref.at[:, at(i, fb)], dest.at[i], frame_sends.at[a, i], frame_recvs.at[a, i], i
        ).wait()

    others(lambda i: place_out(2, xs, out_land, i).start())
    keep_out = pltpu.make_async_copy(xs.at[:, own_lanes], out_land.at[me], local_sems.at[4])
    keep_out.start()
    others(lambda i: frames_wait(1, gr, i))
    others(lambda i: frames_sent(1, gs, i))

    gather_two.drain()
    layer_backward(1, gr, p_two, s_two, lambda step: None)
    input_gradient(wf_two, gr)
    reduce_two = Reduce(
        env, dpt, x_two, lambda k: land.at[k], stage, reduce_sends.at[0], reduce_recvs.at[0], "y", "x"
    )
    reduce_one = Reduce(
        env,
        dpt,
        xr,
        lambda k: wf_two.at[at(k // 4, fb), at(k % 4, sz.qc)],
        stage,
        reduce_sends.at[1],
        reduce_recvs.at[1],
        "x",
        "y",
    )
    result_two = Result(
        env, dw_two, fin.at[0], final_sends.at[0], final_recvs.at[0], local_sems.at[6]
    )
    result_one = Result(
        env, dw_one, fin.at[1], final_sends.at[1], final_recvs.at[1], local_sems.at[7]
    )
    reduce_two.cores()

    def meanwhile(step):
        if step == 0:
            reduce_two.firsts()
        if step == 1:
            reduce_two.seconds()
            reduce_two.lines()
            fin[0] = reduce_two.total()
            result_two.start()

    layer_backward(0, gr, p_one, s_one, meanwhile)
    input_gradient(wf_one, gs)
    others(lambda i: place_out(3, gs, dx_land, i).start())
    keep_dx = pltpu.make_async_copy(gs.at[:, own_lanes], dx_land.at[me], local_sems.at[5])
    keep_dx.start()
    result_two.finish()
    reduce_two.drain()
    reduce_one.cores()
    reduce_one.firsts()
    reduce_one.seconds()
    reduce_one.lines()
    fin[1] = reduce_one.total()
    result_one.start()
    others(lambda i: out_arrived(2, xs, out_land, i))
    others(lambda i: out_arrived(3, gs, dx_land, i))
    keep_out.wait()
    keep_dx.wait()
    result_one.finish()
    reduce_one.drain()
    gather_one.drain()
    small[6:8, :] = jnp.zeros((2, fb), f32)


def turn_back(sz, x_ref, g_ref, out_ref, dx_ref, output, input_grad):
    step = pl.program_id(0)
    T, fb, win, odd = sz.T, sz.fb, sz.win, sz.odd
    output[...] = x_ref[...].astype(f32)
    input_grad[...] = g_ref[...].astype(f32)

    @pl.when(step < sz.n // 2)
    def _():
        row = lax.broadcasted_iota(jnp.int32, (T, win), 0)
        column = lax.broadcasted_iota(jnp.int32, (T, win), 1)
        frame = (row % 8) * sz.steps + row // 8
        row = lax.broadcasted_iota(jnp.int32, (fb, fb), 0)
        eye = jnp.where(row == lax.broadcasted_iota(jnp.int32, (fb, fb), 1), 1.0, 0.0).astype(bf16)
        for half in range(2):
            perm = jnp.where(column == frame + odd * half, 1.0, 0.0).astype(bf16)
            lanes = pl.ds((T - odd) * half, win)
            for source, result in ((out_ref, output), (dx_ref, input_grad)):
                turned = lax.dot_general(
                    eye, source[half], (((1,), (1,)), ((), ())), preferred_element_type=f32
                ).astype(bf16)
                result[:, lanes] += jnp.dot(turned, perm, preferred_element_type=f32)


def frame_rows(sz, lengths, frame_mask):
    T, steps = sz.T, sz.steps
    me = lax.axis_index("neur")
    starts = jnp.cumsum(lengths[0]) - lengths[0]
    row = jnp.arange(T, dtype=jnp.int32)
    slots = me * T + (row % 8) * steps + row // 8
    goes = jnp.where(jnp.any(slots[:, None] == starts[None, :], axis=1), 0.0, 1.0)
    part = lax.dynamic_slice(frame_mask, (me * T,), (T,)).reshape(8, steps).T.reshape(T)
    inside = slots < jnp.sum(lengths[0])
    count = jnp.where((part > 0) & inside, 1.0, 0.0)
    places = jnp.arange(frame_mask.shape[0], dtype=jnp.int32)
    block = jnp.sum(jnp.where((places < jnp.sum(lengths[0])) & (frame_mask > 0), 1.0, 0.0))
    run = jnp.arange(8, dtype=jnp.int32)
    first = me * T + run * steps
    behind = jnp.where(starts[None, :] < first[:, None], starts[None, :], 0)
    since = (first - jnp.max(behind, axis=1)).astype(f32)

    def unbroken(begin, length):
        inside = (starts[None, :] >= begin[:, None]) & (starts[None, :] < begin[:, None] + length)
        return jnp.where(jnp.any(inside, axis=1), 0.0, 1.0)

    whole = unbroken(run * T, T)
    own = unbroken(first, steps)
    aux = jnp.concatenate([since, whole, own, jnp.full((8,), 1.0) * block]).astype(f32)

    def lanes(values):
        return jnp.broadcast_to(values.astype(f32)[:, None], (values.shape[0], 128))

    return lanes(goes), lanes(count), lanes(aux)


def frames_apart(sz, inputs, weight_one, weight_two, params, lengths, frame_mask, out_grad):
    n, seqs, H, fb, T, Z, qc = sz.n, sz.seqs, sz.H, sz.fb, sz.T, sz.Z, sz.qc
    goes, count, aux = frame_rows(sz, lengths, frame_mask)
    own_par = jnp.concatenate([jnp.stack(params), jnp.zeros((2, fb), f32)], axis=0)
    whole = pl.BlockSpec(memory_space=pltpu.VMEM)
    anywhere = pl.BlockSpec(memory_space=pl.ANY)
    vmem, sem = pltpu.VMEM, pltpu.SemaphoreType.DMA
    frames_shape = (T, H)
    matmul = 2 * T * H * H
    out_land, dx_land, dw_one, dw_two, small = pl.pallas_call(
        functools.partial(network, sz),
        out_shape=(
            jax.ShapeDtypeStruct((n, T, fb), bf16),
            jax.ShapeDtypeStruct((n, T, fb), bf16),
            jax.ShapeDtypeStruct((fb, H), f32),
            jax.ShapeDtypeStruct((fb, H), f32),
            jax.ShapeDtypeStruct((8, fb), f32),
        ),
        in_specs=[anywhere] * 4 + [whole] * 4,
        out_specs=(anywhere, anywhere, anywhere, anywhere, whole),
        scratch_shapes=[
            vmem((fb, sz.valid), bf16),
            vmem((2, T, sz.win), bf16),
            vmem((fb, fb), bf16),
            vmem(frames_shape, bf16),
            vmem(frames_shape, bf16),
            vmem(frames_shape, bf16),
            vmem(frames_shape, bf16),
            vmem(frames_shape, bf16),
            vmem(frames_shape, bf16),
            vmem(frames_shape, bf16),
            vmem(frames_shape, bf16),
            vmem((H, T), bf16),
            vmem((T + 8, H), f32),
            vmem((T + 8, H), f32),
            vmem((H, H), bf16),
            vmem((H, H), bf16),
            vmem((8 * Z, fb, qc), bf16),
            vmem((8 * Z, fb, qc), bf16),
            vmem((2, fb, qc), f32),
            vmem((8, H), f32),
            vmem((8, H), f32),
            vmem((16, H), f32),
            vmem((4, 8, H), f32),
            vmem((4, n, 8, fb), f32),
            vmem((4, 8, fb), f32),
            vmem((4, seqs, 8, fb), f32),
            vmem((4, n, 8, fb), f32),
            vmem((4, 8, H), f32),
            sem((8,)),
            sem((n,)),
            sem((n,)),
            sem((4, n)),
            sem((4, n)),
            sem((2, 8 * Z)),
            sem((2, 8 * Z)),
            sem((8, n)),
            sem((8, n)),
            sem((4, seqs)),
            sem((4, seqs)),
            sem((2, 8 * Z)),
            sem((2, 8 * Z)),
            sem((2, 3)),
            sem((2, 3)),
        ],
        compiler_params=pltpu.CompilerParams(
            collective_id=0, has_side_effects=True, vmem_limit_bytes=63 * 1024 * 1024
        ),
        cost_estimate=pl.CostEstimate(
            flops=6 * matmul, bytes_accessed=16 * fb * H, transcendentals=6 * T * H
        ),
        name="network",
    )(inputs, out_grad, weight_one, weight_two, own_par, goes, count, aux)
    tok = inputs.shape[1]
    pairs = n // 2
    steps = pl.cdiv(tok, 2 * T)
    frames_spec = pl.BlockSpec((fb, 2 * T), lambda p: (0, p))
    land_spec = pl.BlockSpec((2, T, fb), lambda p: (jnp.minimum(p, pairs - 1), 0, 0))
    output, input_grad = pl.pallas_call(
        functools.partial(turn_back, sz),
        grid=(steps,),
        out_shape=(jax.ShapeDtypeStruct((fb, tok), f32),) * 2,
        in_specs=[frames_spec, frames_spec, land_spec, land_spec],
        out_specs=(frames_spec, frames_spec),
        compiler_params=pltpu.CompilerParams(vmem_limit_bytes=48 * 1024 * 1024),
        name="turn_back",
    )(inputs, out_grad, out_land, dx_land)
    return (
        output,
        input_grad,
        dw_one,
        small[0],
        small[1],
        small[2],
        dw_two,
        small[3],
        small[4],
        small[5],
    )


def frame_tables(lengths, frame_mask):
    positions = jnp.arange(frame_mask.shape[0], dtype=jnp.int32)
    offsets = jnp.cumsum(lengths[0]) - lengths[0]
    filled = jnp.sum(lengths[0])
    begins = jnp.any(positions[:, None] == offsets[None, :], axis=1)
    continues = jnp.where(begins, 0.0, 1.0).astype(jnp.float32)
    counted = jnp.where((positions < filled) & (frame_mask > 0), 1.0, 0.0).astype(jnp.float32)
    return (continues, counted)


def linear_scan(coef_rows, driving, backwards):
    row_count, length = driving.shape
    block_count = length // block_span
    factor = coef_rows.reshape(row_count, block_count, block_span)
    running = driving.reshape(row_count, block_count, block_span)
    places = jnp.arange(block_span, dtype=jnp.int32)
    step = 1
    while step < block_span:
        if backwards:
            mover = jnp.where(places[:, None] == places[None, :] + step, 1.0, 0.0).astype(
                jnp.float32
            )
            edge = jnp.where(places >= block_span - step, 1.0, 0.0).astype(jnp.float32)
        else:
            mover = jnp.where(places[:, None] == places[None, :] - step, 1.0, 0.0).astype(
                jnp.float32
            )
            edge = jnp.where(places < step, 1.0, 0.0).astype(jnp.float32)
        moved_factor = (
            jnp.dot(
                factor, mover, precision=lax.Precision.HIGHEST, preferred_element_type=jnp.float32
            )
            + edge
        )
        moved_running = jnp.dot(
            running, mover, precision=lax.Precision.HIGHEST, preferred_element_type=jnp.float32
        )
        running = factor * moved_running + running
        factor = factor * moved_factor
        step = step * 2
    end_place = 0 if backwards else block_span - 1
    total_factor = factor[:, :, end_place].T
    total_running = running[:, :, end_place].T

    def carry_step(carried, block_pair):
        return (block_pair[0] * carried + block_pair[1], carried)

    _, entering = lax.scan(
        carry_step,
        jnp.zeros((row_count,), jnp.float32),
        (total_factor, total_running),
        reverse=backwards,
    )
    result = running + factor * entering.T[:, :, None]
    return result.reshape(row_count, length)


def layer_forward(layer_input, weight, gain_row, bias_row, decay_rate, continues, counted):
    frames_in = lax.all_to_all(layer_input, "neur", split_axis=1, concat_axis=0, tiled=True)
    projected = jnp.dot(
        lax.all_gather(weight, "neur", axis=0, tiled=True),
        frames_in,
        preferred_element_type=jnp.float32,
    )
    neuron_proj = lax.all_to_all(
        projected.astype(jnp.bfloat16), "neur", split_axis=0, concat_axis=1, tiled=True
    ).astype(jnp.float32)
    sum_first = jnp.sum(counted[None, :] * neuron_proj, axis=1)
    sum_second = jnp.sum(counted[None, :] * neuron_proj * neuron_proj, axis=1)
    sum_first, sum_second, frames = lax.psum((sum_first, sum_second, jnp.sum(counted)), "seq")
    average = sum_first / frames
    inv_std = lax.rsqrt(sum_second / frames - average * average + epsilon)
    normed = (neuron_proj - average[:, None]) * inv_std[:, None]
    spread = jnp.sqrt(1.0 - decay_rate * decay_rate)
    states = linear_scan(
        decay_rate[:, None] * continues[None, :], (spread * gain_row)[:, None] * normed, False
    )
    layer_out = counted[None, :] * jax.nn.softplus(states + bias_row[:, None])
    return (layer_out, (frames_in, None, normed, inv_std, frames, states))


def layer_backward(
    upstream, weight, gain_row, bias_row, decay_rate, continues, counted, kept_state
):
    frames_in, full_weight, normed, inv_std, frames, states = kept_state
    local_grad = upstream * counted[None, :] * jax.nn.sigmoid(states + bias_row[:, None])
    following = jnp.concatenate([continues[1:], jnp.zeros((1,), jnp.float32)])
    coef_rows = decay_rate[:, None] * following[None, :]
    state_grad = linear_scan(coef_rows, local_grad, True)
    sum_rec, sum_rec_norm, sum_local = lax.psum(
        (
            jnp.sum(state_grad, axis=1),
            jnp.sum(state_grad * normed, axis=1),
            jnp.sum(local_grad, axis=1),
        ),
        "seq",
    )
    spread = jnp.sqrt(1.0 - decay_rate * decay_rate)
    gain_grad = spread * sum_rec_norm
    proj_grad = (spread * gain_row * inv_std)[:, None] * (
        state_grad - counted[None, :] * (sum_rec[:, None] + sum_rec_norm[:, None] * normed) / frames
    )
    driving = (spread * gain_row)[:, None] * normed
    decay_part = jnp.sum(state_grad * (states - driving), axis=1) / decay_rate
    grad_frames = lax.all_to_all(
        proj_grad.astype(jnp.bfloat16), "neur", split_axis=1, concat_axis=0, tiled=True
    )
    grad_rows = grad_frames
    input_frames = jnp.einsum(
        "ot,oi->it",
        grad_rows,
        lax.all_gather(weight, "neur", axis=0, tiled=True),
        preferred_element_type=jnp.float32,
    )
    input_grad = lax.all_to_all(
        input_frames.astype(jnp.bfloat16), "neur", split_axis=0, concat_axis=1, tiled=True
    ).astype(jnp.float32)
    grad_rows = grad_frames
    weight_rows = lax.psum_scatter(
        jnp.einsum("ot,it->oi", grad_rows, frames_in, preferred_element_type=jnp.float32),
        "neur",
        scatter_dimension=0,
        tiled=True,
    )
    weight_grad, decay_sum = lax.psum((weight_rows, decay_part), "seq")
    decay_grad = decay_sum - decay_rate / spread * gain_row * sum_rec_norm
    return (input_grad, weight_grad, gain_grad, sum_local, decay_grad)


def shards(
    inputs,
    weight_one,
    weight_two,
    gain_one,
    gain_two,
    bias_one,
    bias_two,
    decay_one,
    decay_two,
    lengths,
    frame_mask,
    out_grad,
):
    seqs, n = lax.axis_size("seq"), lax.axis_size("neur")
    H, (fb, tok) = weight_one.shape[1], inputs.shape
    if fits(n, seqs, H, fb, tok):
        params = (gain_one, gain_two, bias_one, bias_two, decay_one, decay_two)
        return frames_apart(
            Sizes(n, seqs, H, fb, tok),
            inputs,
            weight_one,
            weight_two,
            params,
            lengths,
            frame_mask,
            out_grad,
        )
    continues, counted = frame_tables(lengths, frame_mask)
    first_out, first_kept = layer_forward(
        inputs, weight_one, gain_one, bias_one, decay_one, continues, counted
    )
    second_out, second_kept = layer_forward(
        first_out.astype(jnp.bfloat16),
        weight_two,
        gain_two,
        bias_two,
        decay_two,
        continues,
        counted,
    )
    output = inputs.astype(jnp.float32) + second_out
    upstream = out_grad.astype(jnp.float32)
    middle_grad, weight_two_grad, gain_two_grad, bias_two_grad, decay_two_grad = layer_backward(
        upstream, weight_two, gain_two, bias_two, decay_two, continues, counted, second_kept
    )
    lower_grad, weight_one_grad, gain_one_grad, bias_one_grad, decay_one_grad = layer_backward(
        middle_grad, weight_one, gain_one, bias_one, decay_one, continues, counted, first_kept
    )
    return (
        output,
        upstream + lower_grad,
        weight_one_grad,
        gain_one_grad,
        bias_one_grad,
        decay_one_grad,
        weight_two_grad,
        gain_two_grad,
        bias_two_grad,
        decay_two_grad,
    )


def solution(mesh):
    placed = (
        P("neur", "seq"),
        P("neur", None),
        P("neur", None),
        P("neur"),
        P("neur"),
        P("neur"),
        P("neur"),
        P("neur"),
        P("neur"),
        P("seq", None),
        P("seq"),
        P("neur", "seq"),
    )
    return jax.shard_map(
        shards,
        mesh=mesh,
        in_specs=placed,
        out_specs=(
            P("neur", "seq"),
            P("neur", "seq"),
            P("neur", None),
            P("neur"),
            P("neur"),
            P("neur"),
            P("neur", None),
            P("neur"),
            P("neur"),
            P("neur"),
        ),
        check_vma=False,
    )
```

```python
import functools

import jax
import jax.numpy as jnp
from jax import lax
from jax.experimental import pallas as pl
from jax.experimental.pallas import tpu as pltpu
from jax.sharding import PartitionSpec as P

epsilon = 1e-05
block_span = 128
valid_frames = 3584
f32 = jnp.float32
bf16 = jnp.bfloat16
MESH = pl.DeviceIdType.MESH


def wide(tile, width):
    return jnp.concatenate([tile] * (width // 128), axis=1)


def at(index, size):
    if isinstance(index, int):
        return pl.ds(index * size, size)
    return pl.ds(pl.multiple_of(index * size, size), size)


def power(base, exponent):
    result = None
    while exponent:
        if exponent % 2:
            result = base if result is None else result * base
        exponent //= 2
        base = base * base
    return result


def log_of(rate):
    u = 1.0 - rate
    series = jnp.full_like(u, 1.0 / 8)
    for order in range(7, 0, -1):
        series = series * u + 1.0 / order
    return -u * series


GAIN, BIAS, DECAY = 0, 2, 4


class Sizes:
    def __init__(self, n, seqs, H, fb, tok_dev):
        self.n, self.seqs, self.H, self.fb, self.tok_dev = n, seqs, H, fb, tok_dev
        self.T = valid_frames // n
        self.steps = self.T // 8
        self.valid = valid_frames
        self.qc = H // seqs
        self.Z = n // 2
        self.odd = self.T % 128
        self.win = self.T + self.odd
        self.K = self.T + 16
        self.L = min(512, H)


def fits(n, seqs, H, fb, tok_dev):
    if valid_frames % n or n % 2 or n > 8 or seqs != 4 or fb * n != H or fb % 128 or H % 512:
        return False
    T = valid_frames // n
    return T % 64 == 0 and valid_frames % 128 == 0 and tok_dev >= valid_frames


class Line:
    def __init__(self, env, sends, recvs):
        self.env, self.sends, self.recvs = env, sends, recvs

    def copy(self, k, source, dest, target):
        return pltpu.make_async_remote_copy(
            src_ref=source,
            dst_ref=dest,
            send_sem=self.sends.at[k],
            recv_sem=self.recvs.at[k],
            device_id=target,
            device_id_type=MESH,
        )

    def arrived(self, k, ref):
        self.copy(k, ref, ref, self.env.across("x")).wait_recv()

    def sent(self, k, ref):
        self.copy(k, ref, ref, self.env.across("x")).wait_send()

    def along(self, dz):
        z, Z = self.env.z, self.env.sz.Z
        if dz == 0:
            return [(None, z, 0)]
        return [(z >= dz, z - dz, 1), (z + dz < Z, z + dz, -1)]


def if_so(condition, body):
    if condition is None:
        body()
    else:
        pl.when(condition)(body)


class Gather(Line):
    def __init__(self, env, source, full, sends, recvs):
        super().__init__(env, sends, recvs)
        self.full = full
        self.source = source.at[:, at(env.s, env.sz.qc)]
        Z = env.sz.Z
        self.steps = []
        for dz in range(1, Z):
            self.steps.append(functools.partial(self.line, dz))
            self.steps.append(functools.partial(self.sides, dz - 1))
        self.steps.append(functools.partial(self.sides, Z - 1))
        self.steps.append(self.diagonals)
        self.steps.append(self.cores)

    def block(self, zz, fx, fy, fc=0):
        env = self.env
        rows = at(2 * zz + (env.x + fx) % 2, env.sz.fb)
        return self.full.at[rows, at(2 * ((env.y + fy) % 2) + (env.c + fc) % 2, env.sz.qc)]

    def half(self, ref, h):
        return ref.at[pl.ds(h * (self.env.sz.fb // 2), self.env.sz.fb // 2), :]

    def spread(self, zz, source):
        env, Z = self.env, self.env.sz.Z
        dest = self.block(zz, 0, 0)
        self.copy(2 * Z + zz, source, dest, env.across("x")).start()
        self.copy(3 * Z + zz, source, dest, env.across("y")).start()
        self.copy(6 * Z + zz, source, dest, env.across("core")).start()

    def pass_on(self, zz, source, way):
        env, Z = self.env, self.env.sz.Z
        dest = self.block(zz, 0, 0)

        def go():
            pltpu.make_async_remote_copy(
                src_ref=source,
                dst_ref=dest,
                send_sem=self.sends.at[zz if way > 0 else Z + zz],
                recv_sem=self.recvs.at[zz],
                device_id={"neur": 2 * (env.z + way) + env.x},
                device_id_type=MESH,
            ).start()

        pl.when(env.z < Z - 1 if way > 0 else env.z > 0)(go)

    def start(self):
        z = self.env.z
        self.pass_on(z, self.source, 1)
        self.pass_on(z, self.source, -1)
        self.spread(z, self.source)

    def line(self, dz):
        for condition, zz, way in self.along(dz):

            def one(zz=zz, way=way):
                block = self.block(zz, 0, 0)
                self.arrived(zz, block)
                self.pass_on(zz, block, way)
                self.spread(zz, block)

            if_so(condition, one)

    def sides(self, dz):
        env, Z = self.env, self.env.sz.Z
        for condition, zz, _ in self.along(dz):

            def one(zz=zz):
                block = self.block(zz, 1, 0)
                self.arrived(2 * Z + zz, block)
                part = self.half(block, 1)
                self.copy(5 * Z + zz, part, part, env.across("y")).start()
                self.copy(7 * Z + zz, block, block, env.across("core")).start()
                block = self.block(zz, 0, 1)
                self.arrived(3 * Z + zz, block)
                part = self.half(block, 0)
                self.copy(4 * Z + zz, part, part, env.across("x")).start()
                self.copy(8 * Z + zz, block, block, env.across("core")).start()

            if_so(condition, one)

    def diagonals(self):
        env, Z = self.env, self.env.sz.Z
        for dz in range(Z):
            for condition, zz, _ in self.along(dz):

                def one(zz=zz):
                    block = self.block(zz, 1, 1)
                    self.arrived(4 * Z + zz, self.half(block, 0))
                    self.arrived(5 * Z + zz, self.half(block, 1))
                    self.copy(9 * Z + zz, block, block, env.across("core")).start()

                if_so(condition, one)

    def cores(self):
        Z = self.env.sz.Z
        for k, (fx, fy) in enumerate(((0, 0), (1, 0), (0, 1), (1, 1))):
            for zz in range(Z):
                self.arrived((6 + k) * Z + zz, self.block(zz, fx, fy, 1))

    def advance(self, count=None):
        for _ in range(len(self.steps) if count is None else min(count, len(self.steps))):
            self.steps.pop(0)()

    def drain(self):
        env, Z = self.env, self.env.sz.Z
        block = self.block(0, 0, 0)
        for zz in range(Z):
            pl.when((zz <= env.z) & (env.z < Z - 1))(lambda zz=zz: self.sent(zz, block))
            pl.when((zz >= env.z) & (env.z > 0))(lambda zz=zz: self.sent(Z + zz, block))
            for k in (2, 3, 6, 7, 8, 9):
                self.sent(k * Z + zz, block)
            for k in (4, 5):
                self.sent(k * Z + zz, self.half(block, 0))


class Reduce(Line):
    kinds = ((1, 1), (1, 0), (0, 1), (0, 0))

    def __init__(self, env, grads, frames, land, spare, stage, total, sends, recvs):
        super().__init__(env, sends, recvs)
        self.grads, self.frames, self.land, self.spare = grads, frames, land, spare
        self.stage, self.total = stage, total

    def product(self, kind, zz, fc=0):
        env, sz = self.env, self.env.sz
        fx, fy = self.kinds[kind]
        rows = at(2 * zz + (env.x + fx) % 2, sz.fb)
        columns = at(2 * ((env.y + fy) % 2) + (env.c + fc) % 2, sz.qc)
        return jnp.dot(
            self.grads[rows, :], self.frames[:, columns], preferred_element_type=f32
        )

    def half(self, ref, h):
        return ref.at[pl.ds(h * (self.env.sz.fb // 2), self.env.sz.fb // 2), :]

    def landed(self, k, slot):
        self.arrived(k, self.land(slot))
        return self.land(slot)[...].astype(f32)

    def cores(self, kind):
        env, Z = self.env, self.env.sz.Z

        def one(zz, _):
            k = kind * Z + zz
            held = (kind % 2) * Z + zz
            if kind >= 2:
                self.sent(k - 2 * Z, self.stage.at[held])
            self.stage[held] = self.product(kind, zz, 1).astype(bf16)
            self.copy(k, self.stage.at[held], self.land(k), env.across("core")).start()
            return 0

        lax.fori_loop(0, Z, one, 0)

    def diagonals(self):
        env, Z = self.env, self.env.sz.Z

        def one(zz, _):
            held = self.stage.at[2 * Z + zz]
            held[...] = (self.product(0, zz) + self.landed(zz, zz)).astype(bf16)
            slot = self.land(4 * Z + zz)
            for k, h, axis in ((4, 0, "x"), (5, 1, "y")):
                self.copy(
                    k * Z + zz, self.half(held, h), self.half(slot, h), env.across(axis)
                ).start()
            return 0

        lax.fori_loop(0, Z, one, 0)

    def sides(self, low=0, high=None):
        env, Z = self.env, self.env.sz.Z
        rows = env.sz.fb // 2

        def one(zz, _):
            slot = self.land(4 * Z + zz)
            for kind, h, wait, k, axis in ((1, 1, 5, 6, "x"), (2, 0, 4, 7, "y")):
                tile = self.product(kind, zz) + self.landed(kind * Z + zz, kind * Z + zz)
                part = self.half(slot, h)
                self.arrived(wait * Z + zz, part)
                held = self.stage.at[(2 + kind) * Z + zz]
                other = 1 - h
                own = slice(h * rows, (h + 1) * rows)
                rest = slice(other * rows, (other + 1) * rows)
                self.half(held, h)[...] = (tile[own, :] + part[...].astype(f32)).astype(bf16)
                self.half(held, other)[...] = tile[rest, :].astype(bf16)
                self.copy(
                    k * Z + zz, held, self.land((4 + kind) * Z + zz), env.across(axis)
                ).start()
            return 0

        lax.fori_loop(low, Z if high is None else high, one, 0)

    def joined(self, zz):
        Z = self.env.sz.Z
        tile = self.product(3, zz) + self.landed(3 * Z + zz, 3 * Z + zz)
        tile = tile + self.landed(6 * Z + zz, 5 * Z + zz)
        self.total[...] = tile + self.landed(7 * Z + zz, 6 * Z + zz)

    def lines(self):
        env, Z, z = self.env, self.env.sz.Z, self.env.z

        def onward(zz, way):
            k, slot = (8 if way > 0 else 9) * Z + zz, 7 * Z + zz
            self.joined(zz)

            @pl.when(z > 0 if way > 0 else z < Z - 1)
            def _():
                self.total[...] += self.landed(k, slot)

            held = self.stage.at[2 * Z + zz]
            self.sent(4 * Z + zz, self.half(held, 0))
            self.sent(5 * Z + zz, self.half(held, 0))
            held[...] = self.total[...].astype(bf16)
            target = {"neur": 2 * (z + way) + env.x}
            if way > 0:
                self.copy(k, held, self.land(slot), target).start()
            else:
                pl.when(zz == z - 1)(lambda: self.copy(k, held, self.spare, target).start())
                pl.when(zz != z - 1)(lambda: self.copy(k, held, self.land(slot), target).start())

        for i in range(Z - 1):
            pl.when(Z - 1 - i > z)(functools.partial(onward, Z - 1 - i, 1))
            pl.when(i < z)(functools.partial(onward, i, -1))

    def finish(self):
        Z, z = self.env.sz.Z, self.env.z
        self.joined(z)

        @pl.when(z > 0)
        def _():
            self.total[...] += self.landed(8 * Z + z, 7 * Z + z)

        @pl.when(z < Z - 1)
        def _():
            self.arrived(9 * Z + z, self.spare)
            self.total[...] += self.spare[...].astype(f32)

    def drain(self):
        Z, z = self.env.sz.Z, self.env.z
        held = self.stage.at[0]
        for zz in range(Z):
            for k in (2, 3, 6, 7):
                self.sent(k * Z + zz, held)
            for k in (4, 5):
                pl.when(zz == z)(lambda k=k, zz=zz: self.sent(k * Z + zz, self.half(held, 0)))
            pl.when(zz > z)(lambda zz=zz: self.sent(8 * Z + zz, held))
            pl.when(zz < z)(lambda zz=zz: self.sent(9 * Z + zz, held))


class Result:
    def __init__(self, env, whole, block, sends, recvs, local):
        self.env, self.whole, self.block = env, whole, block
        self.sends, self.recvs, self.local = sends, recvs, local

    def part(self, flip_y, flip_c):
        env = self.env
        s = 2 * ((env.y + flip_y) % 2) + (env.c + flip_c) % 2
        return self.whole.at[:, at(s, env.sz.qc)]

    def copy(self, k, source, dest, target):
        return pltpu.make_async_remote_copy(
            src_ref=source,
            dst_ref=dest,
            send_sem=self.sends.at[k],
            recv_sem=self.recvs.at[k],
            device_id=target,
            device_id_type=MESH,
        )

    def start(self):
        env, own = self.env, self.part(0, 0)
        self.copy(0, self.block, own, env.across("y")).start()
        self.copy(1, self.block, own, env.across("core")).start()
        pltpu.make_async_copy(self.block, own, self.local).start()

    def finish(self):
        env = self.env
        other = self.part(1, 0)
        self.copy(0, self.block, other, env.across("y")).wait_recv()
        forward = self.copy(2, other, other, env.across("core"))
        forward.start()
        own = self.part(0, 0)
        pltpu.make_async_copy(self.block, own, self.local).wait()
        self.copy(0, self.block, own, env.across("y")).wait_send()
        self.copy(1, self.block, self.part(0, 1), env.across("core")).wait()
        forward.wait_send()
        self.copy(2, other, self.part(1, 1), env.across("core")).wait_recv()


class Env:
    def across(self, axis):
        if axis == "x":
            return {"neur": 2 * self.z + 1 - self.x}
        if axis == "y":
            return {"seq": 2 * (1 - self.y) + self.c}
        return {"seq": 2 * self.y + 1 - self.c}


def network(
    sz,
    x_hbm,
    g_hbm,
    w_one,
    w_two,
    own_par,
    cont,
    counted,
    aux,
    out_land,
    dx_land,
    dw_one,
    dw_two,
    small,
    raw,
    perm,
    eye,
    xs,
    gs,
    xr,
    gr,
    p_one,
    p_two,
    x_two,
    dp,
    dpt_one,
    dpt_two,
    s_one,
    s_two,
    wf_one,
    wf_two,
    land,
    stage,
    spare,
    fin,
    par,
    ends,
    work,
    pay,
    arrive,
    seqpay,
    seqland,
    back,
    backland,
    sumpay,
    sumland,
    sumseq,
    sumseqland,
    local_sems,
    par_sends,
    par_recvs,
    frame_sends,
    frame_recvs,
    gather_sends,
    gather_recvs,
    hop_sends,
    hop_recvs,
    seq_sends,
    seq_recvs,
    reduce_sends,
    reduce_recvs,
    final_sends,
    final_recvs,
    sum_sends,
    sum_recvs,
):
    n, seqs, H, fb, T, steps, L = sz.n, sz.seqs, sz.H, sz.fb, sz.T, sz.steps, sz.L
    env = Env()
    env.sz = sz
    me = lax.axis_index("neur")
    mine = lax.axis_index("seq")
    env.j, env.s = me, mine
    env.z, env.x, env.y, env.c = me // 2, me % 2, mine // 2, mine % 2

    barrier = pltpu.get_barrier_semaphore()
    for o in range(1, n):
        pl.semaphore_signal(
            barrier, inc=1, device_id={"neur": (me + o) % n}, device_id_type=MESH
        )
    for o in range(1, seqs):
        pl.semaphore_signal(
            barrier, inc=1, device_id={"seq": (mine + o) % seqs}, device_id_type=MESH
        )
    load_x = pltpu.make_async_copy(x_hbm.at[:, pl.ds(0, sz.valid)], raw, local_sems.at[0])
    load_x.start()
    pl.semaphore_wait(barrier, n - 1 + seqs - 1)

    def neur_copy(source, dest, send, recv, i):
        return pltpu.make_async_remote_copy(
            src_ref=source,
            dst_ref=dest,
            send_sem=send,
            recv_sem=recv,
            device_id={"neur": i},
            device_id_type=MESH,
        )

    def seq_copy(source, dest, send, recv, i):
        return pltpu.make_async_remote_copy(
            src_ref=source,
            dst_ref=dest,
            send_sem=send,
            recv_sem=recv,
            device_id={"seq": i},
            device_id_type=MESH,
        )

    def others(body, count=n, own=me):
        def one(o, _):
            body((own + o) % count)
            return 0

        lax.fori_loop(1, count, one, 0)

    own_lanes = at(me, fb)

    def par_copy(i):
        return neur_copy(own_par, par.at[:, own_lanes], par_sends.at[i], par_recvs.at[me], i)

    def par_wait(i):
        neur_copy(own_par, par.at[:, at(i, fb)], par_sends.at[i], par_recvs.at[i], i).wait()

    others(lambda i: par_copy(i).start())
    par[:, own_lanes] = own_par[...]

    gather_one = Gather(env, w_one, wf_one, gather_sends.at[0], gather_recvs.at[0])
    gather_two = Gather(env, w_two, wf_two, gather_sends.at[1], gather_recvs.at[1])
    own_one = pltpu.make_async_copy(gather_one.source, gather_one.block(env.z, 0, 0), local_sems.at[2])
    own_two = pltpu.make_async_copy(gather_two.source, gather_two.block(env.z, 0, 0), local_sems.at[3])
    own_one.start()
    own_two.start()
    gather_one.start()

    row = lax.broadcasted_iota(jnp.int32, (T, sz.win), 0)
    column = lax.broadcasted_iota(jnp.int32, (T, sz.win), 1)
    frame = (row % 8) * steps + row // 8
    perm[0] = jnp.where(column == frame, 1.0, 0.0).astype(bf16)
    perm[1] = jnp.where(column == frame + sz.odd, 1.0, 0.0).astype(bf16)
    row = lax.broadcasted_iota(jnp.int32, (fb, fb), 0)
    column = lax.broadcasted_iota(jnp.int32, (fb, fb), 1)
    eye[...] = jnp.where(row == column, 1.0, 0.0).astype(bf16)

    def window(i):
        start = (i // 2) * (2 * T) + (i % 2) * (T - sz.odd)
        return pl.ds(pl.multiple_of(start, 128), sz.win)

    def turned(i):
        return lax.dot_general(
            perm[i % 2], raw[:, window(i)], (((1,), (1,)), ((), ())), preferred_element_type=f32
        ).astype(bf16)

    def frames_copy(a, source, dest, i):
        return neur_copy(source, dest, frame_sends.at[a, i], frame_recvs.at[a, me], i)

    def frames_wait(a, ref, i):
        part = ref.at[pl.ds(0, T), at(i, fb)]
        neur_copy(part, part, frame_sends.at[a, i], frame_recvs.at[a, i], i).wait_recv()

    def frames_sent(a, ref, i):
        part = ref.at[pl.ds(0, T), at(i, fb)]
        neur_copy(part, part, frame_sends.at[a, i], frame_recvs.at[a, i], i).wait_send()

    load_x.wait()

    def send_x(i):
        xs[:, at(i, fb)] = turned(i)
        frames_copy(0, xs.at[:, at(i, fb)], xr.at[pl.ds(0, T), own_lanes], i).start()

    others(send_x)
    xr[0:T, own_lanes] = turned(me)
    load_g = pltpu.make_async_copy(g_hbm.at[:, pl.ds(0, sz.valid)], raw, local_sems.at[1])
    load_g.start()
    gather_one.advance(2)
    load_g.wait()

    def turn_g(i):
        gs[:, at(i, fb)] = turned(i)

    others(turn_g)
    gr[:, own_lanes] = turned(me)
    gather_one.advance(len(gather_one.steps) - 1)
    gather_two.start()
    gather_one.advance()
    own_one.wait()
    own_two.wait()
    others(lambda i: frames_wait(0, xr, i))
    others(par_wait)

    def blocks(body):
        def one(b, _):
            body(at(b, L))
            return 0

        lax.fori_loop(0, H // L, one, 0)

    def project(frames, weight, result):
        def one(b, _):
            result[:, at(b, fb)] = lax.dot_general(
                frames[0:T, :],
                weight[at(b, fb), :],
                (((1,), (1,)), ((), ())),
                preferred_element_type=f32,
            ).astype(bf16)
            return 0

        lax.fori_loop(0, n, one, 0)

    def flags(t):
        tile = pl.ds(pl.multiple_of(8 * t, 8), 8)
        return wide(cont[tile, :], L), wide(counted[tile, :], L)

    def spread8(ref, r, cols, width=L):
        return jnp.broadcast_to(ref[r : r + 1, cols], (8, width))

    zero = jnp.zeros((8, L), f32)

    def down(value):
        return jnp.sum(value, axis=0, keepdims=True)

    def exchange(e, gathered, totalled, gap):
        def out_copy(i):
            return neur_copy(
                pay.at[e, :, at(i, fb)],
                arrive.at[e, me],
                hop_sends.at[2 * e, i],
                hop_recvs.at[2 * e, me],
                i,
            )

        others(lambda i: out_copy(i).start())
        arrive[e, me] = pay[e, :, own_lanes]
        gap()

        def out_wait(i):
            neur_copy(
                pay.at[e, :, at(i, fb)],
                arrive.at[e, i],
                hop_sends.at[2 * e, i],
                hop_recvs.at[2 * e, i],
                i,
            ).wait()

        others(out_wait)
        gathered()

        def along_copy(i):
            return seq_copy(
                seqpay.at[e],
                seqland.at[e, mine],
                seq_sends.at[e, i],
                seq_recvs.at[e, mine],
                i,
            )

        def along_wait(i):
            seq_copy(
                seqpay.at[e], seqland.at[e, i], seq_sends.at[e, i], seq_recvs.at[e, i], i
            ).wait()

        others(lambda i: along_copy(i).start(), seqs, mine)
        seqland[e, mine] = seqpay[e]
        gap()
        others(along_wait, seqs, mine)
        sums = seqland[e, 0]
        for i in range(1, seqs):
            sums = sums + seqland[e, i]
        totalled(sums)

        def back_copy(i):
            return neur_copy(
                back.at[e, i],
                backland.at[e, :, own_lanes],
                hop_sends.at[2 * e + 1, i],
                hop_recvs.at[2 * e + 1, me],
                i,
            )

        def back_wait(i):
            neur_copy(
                back.at[e, i],
                backland.at[e, :, at(i, fb)],
                hop_sends.at[2 * e + 1, i],
                hop_recvs.at[2 * e + 1, i],
                i,
            ).wait()

        others(lambda i: back_copy(i).start())
        backland[e, :, own_lanes] = back[e, me]
        gap()
        others(back_wait)

    def layer_forward(layer, frames, weight, projected, states, store, gap):
        e = layer
        decay_row, gain_row, bias_row = DECAY + layer, GAIN + layer, BIAS + layer
        project(frames, weight, projected)
        gap()

        def local_ends(cols):
            decay = spread8(par, decay_row, cols)

            def step(i, carry):
                state, first, second, inward = carry
                pair = projected[pl.ds(pl.multiple_of(16 * i, 16), 16), cols].astype(f32)
                for h in range(2):
                    value = pair[8 * h : 8 * h + 8, :]
                    goes, count = flags(2 * i + h)
                    state = (decay * goes) * state + value
                    held = count * value
                    first = first + held
                    second = second + held * value
                ins = frames[pl.ds(pl.multiple_of(16 * i, 16), 16), cols].astype(f32)
                return state, first, second, inward + ins[0:8, :] + ins[8:16, :]

            state, first, second, inward = lax.fori_loop(
                0, T // 16, step, (zero, zero, zero, zero)
            )
            ends[:, cols] = state
            pay[e, 1:2, cols] = down(first)
            pay[e, 2:3, cols] = down(second)
            pay[e, 3:4, cols] = down(inward)

        blocks(local_ends)
        run_power = power(par[decay_row : decay_row + 1, :], steps)
        total = jnp.zeros((1, H), f32)
        for k in range(8):
            total = run_power * wide(aux[16 + k : 17 + k, :], H) * total + ends[k : k + 1, :]
        pay[e, 0:1, :] = total
        pay[e, 4:8, :] = jnp.zeros((4, H), f32)
        gap()

        own_decay = own_par[decay_row : decay_row + 1, :]

        def gathered():
            whole_power = power(own_decay, T)
            carried = jnp.zeros((1, fb), f32)
            sums = jnp.zeros((8, fb), f32)
            for i in range(n):
                rows = arrive[e, i]
                back[e, i, 0:1, :] = carried
                carried = whole_power * wide(aux[8 + i : 9 + i, :], fb) * carried + rows[0:1, :]
                sums = sums + rows
            seqpay[e] = sums
            seqpay[e, 0:1, :] = wide(aux[24:25, :], fb)

        def totalled(sums):
            frames_all = sums[0:1, :]
            average = sums[1:2, :] / frames_all
            inv_std = lax.rsqrt(sums[2:3, :] / frames_all - average * average + epsilon)
            centre = sums[3:4, :] / (sz.valid * seqs)
            for i in range(n):
                back[e, i, 1:2, :] = average
                back[e, i, 2:3, :] = inv_std
                back[e, i, 3:4, :] = frames_all
                back[e, i, 4:5, :] = centre
                back[e, i, 5:8, :] = jnp.zeros((3, fb), f32)

        exchange(e, gathered, totalled, gap)
        centre = backland[e, 4:5, :]
        frames[T : T + 16, :] = jnp.concatenate(
            [-centre, -centre, -centre, jnp.zeros((13, H), f32)], axis=0
        ).astype(bf16)

        total = backland[e, 0:1, :]
        for k in range(8):
            work[k : k + 1, :] = total
            total = run_power * wide(aux[16 + k : 17 + k, :], H) * total + ends[k : k + 1, :]

        def full_scan(cols):
            decay = spread8(par, decay_row, cols)
            average = spread8(backland.at[e], 1, cols)
            inv_std = spread8(backland.at[e], 2, cols)
            bias = spread8(par, bias_row, cols)
            scale = jnp.sqrt(1.0 - decay * decay) * spread8(par, gain_row, cols) * inv_std
            ones = (1.0 - jnp.exp(wide(aux[0:8, :], L) * log_of(decay))) / (1.0 - decay)
            state = scale * (work[0:8, cols] - average * ones)
            states[0:8, cols] = state

            def step(i, state):
                pair = projected[pl.ds(pl.multiple_of(16 * i, 16), 16), cols].astype(f32)
                outs = []
                for h in range(2):
                    goes, count = flags(2 * i + h)
                    state = (decay * goes) * state + scale * (pair[8 * h : 8 * h + 8, :] - average)
                    states[pl.ds(pl.multiple_of(16 * i + 8 * h + 8, 8), 8), cols] = state
                    v = state + bias
                    soft = jnp.maximum(v, 0.0) + jnp.log(1.0 + jnp.exp(-jnp.abs(v)))
                    outs.append(count * soft)
                store[pl.ds(pl.multiple_of(16 * i, 16), 16), cols] = jnp.concatenate(
                    outs, axis=0
                ).astype(bf16)
                return state

            lax.fori_loop(0, T // 16, step, state)

        blocks(full_scan)
        gap()

    def layer_backward(layer, upstream, projected, states, turned_grads, gap):
        e = 2 + (1 - layer)
        decay_row, gain_row, bias_row = DECAY + layer, GAIN + layer, BIAS + layer
        run_power = power(par[decay_row : decay_row + 1, :], steps)

        def local_ends(cols):
            decay = spread8(par, decay_row, cols)
            average = spread8(backland.at[layer], 1, cols)
            inv_std = spread8(backland.at[layer], 2, cols)
            bias = spread8(par, bias_row, cols)

            def step(o, carry):
                i = T // 16 - 1 - o
                rows = pl.ds(pl.multiple_of(16 * i, 16), 16)
                pair = projected[rows, cols].astype(f32)
                ups = upstream[rows, cols].astype(f32)
                for h in (1, 0):
                    run, reach, U, V, UN, VN, B, D, DA = carry
                    goes, count = flags(2 * i + h)
                    here = pl.ds(pl.multiple_of(16 * i + 8 * h + 8, 8), 8)
                    state = states[here, cols]
                    before = states[pl.ds(pl.multiple_of(16 * i + 8 * h, 8), 8), cols]
                    local = ups[8 * h : 8 * h + 8, :] * count / (1.0 + jnp.exp(-(state + bias)))
                    states[here, cols] = local
                    normed = (pair[8 * h : 8 * h + 8, :] - average) * inv_std
                    run = local + run
                    kept = goes * before
                    link = decay * goes
                    carry = (
                        link * run,
                        link * reach,
                        U + run,
                        V + reach,
                        UN + run * normed,
                        VN + reach * normed,
                        B + local,
                        D + run * kept,
                        DA + reach * kept,
                    )
                return carry

            one = jnp.ones((8, L), f32)
            run, _, U, V, UN, VN, B, D, DA = lax.fori_loop(
                0, T // 16, step, (zero, one, zero, zero, zero, zero, zero, zero, zero)
            )
            ends[:, cols] = run
            decay_run = power(par[decay_row : decay_row + 1, cols], steps)
            part, factor = jnp.zeros((1, L), f32), jnp.ones((1, L), f32)
            for k in range(7, -1, -1):
                work[k : k + 1, cols] = part
                work[8 + k : 9 + k, cols] = factor
                through = decay_run * wide(aux[16 + k : 17 + k, :], L)
                part = through * part + ends[k : k + 1, cols]
                factor = through * factor
            pay[e, 0:1, cols] = part
            entering, scaled = work[0:8, cols], work[8:16, cols]
            pay[e, 1:2, cols] = down(U + V * entering)
            pay[e, 2:3, cols] = down(V * scaled)
            pay[e, 3:4, cols] = down(UN + VN * entering)
            pay[e, 4:5, cols] = down(VN * scaled)
            pay[e, 5:6, cols] = down(B)
            pay[e, 6:7, cols] = down(D + DA * entering)
            pay[e, 7:8, cols] = down(DA * scaled)

        blocks(local_ends)
        gap()
        own_decay = own_par[decay_row : decay_row + 1, :]
        own_gain = own_par[gain_row : gain_row + 1, :]

        def gathered():
            whole_power = power(own_decay, T)
            carried = jnp.zeros((1, fb), f32)
            sums = [jnp.zeros((1, fb), f32)] * 4
            for i in range(n - 1, -1, -1):
                rows = arrive[e, i]
                back[e, i, 0:1, :] = carried
                for a, (plain, times) in enumerate(((1, 2), (3, 4), (5, None), (6, 7))):
                    term = rows[plain : plain + 1, :]
                    if times is not None:
                        term = term + rows[times : times + 1, :] * carried
                    sums[a] = sums[a] + term
                carried = whole_power * wide(aux[8 + i : 9 + i, :], fb) * carried + rows[0:1, :]
            for a in range(4):
                seqpay[e, a : a + 1, :] = sums[a]
            seqpay[e, 4:8, :] = jnp.zeros((4, fb), f32)

        def totalled(sums):
            rec, rec_norm = sums[0:1, :], sums[1:2, :]
            for i in range(n):
                back[e, i, 1:2, :] = rec
                back[e, i, 2:3, :] = rec_norm
                back[e, i, 3:8, :] = jnp.zeros((5, fb), f32)
            spread = jnp.sqrt(1.0 - own_decay * own_decay)
            small[3 * layer : 3 * layer + 1, :] = spread * rec_norm
            small[3 * layer + 1 : 3 * layer + 2, :] = sums[2:3, :]
            small[3 * layer + 2 : 3 * layer + 3, :] = (
                sums[3:4, :] - own_decay / spread * own_gain * rec_norm
            )

        exchange(e, gathered, totalled, gap)
        total = backland[e, 0:1, :]
        for k in range(7, -1, -1):
            work[k : k + 1, :] = total
            total = run_power * wide(aux[16 + k : 17 + k, :], H) * total + ends[k : k + 1, :]

        def full_scan(cols):
            decay = spread8(par, decay_row, cols)
            average = spread8(backland.at[layer], 1, cols)
            inv_std = spread8(backland.at[layer], 2, cols)
            frames_all = spread8(backland.at[layer], 3, cols)
            scale = jnp.sqrt(1.0 - decay * decay) * spread8(par, gain_row, cols) * inv_std
            rec = spread8(backland.at[e], 1, cols) / frames_all
            rec_norm = spread8(backland.at[e], 2, cols) / frames_all * inv_std

            def step(o, carry):
                carry, added = carry
                i = T // 16 - 1 - o
                rows = pl.ds(pl.multiple_of(16 * i, 16), 16)
                pair = projected[rows, cols].astype(f32)
                outs = [None, None]
                for h in (1, 0):
                    goes, count = flags(2 * i + h)
                    here = pl.ds(pl.multiple_of(16 * i + 8 * h + 8, 8), 8)
                    run = states[here, cols] + carry
                    centred = pair[8 * h : 8 * h + 8, :] - average
                    outs[h] = scale * (run - count * (rec + rec_norm * centred))
                    carry = (decay * goes) * run
                rounded = jnp.concatenate(outs, axis=0).astype(bf16)
                dp[rows, cols] = rounded
                rounded = rounded.astype(f32)
                return carry, added + rounded[0:8, :] + rounded[8:16, :]

            _, added = lax.fori_loop(0, T // 16, step, (work[0:8, cols], zero))
            whole = down(added)
            sumpay[layer, 0:1, cols] = whole
            high = whole.astype(bf16).astype(f32)
            middle = (whole - high).astype(bf16).astype(f32)
            low = whole - high - middle
            dp[T : T + 16, cols] = jnp.concatenate(
                [high, middle, low, jnp.zeros((13, L), f32)], axis=0
            ).astype(bf16)

        blocks(full_scan)
        sumpay[layer, 1:8, :] = jnp.zeros((7, H), f32)
        gap()

        def turn(b, _):
            turned_grads[at(b, fb), :] = lax.dot_general(
                eye[...], dp[:, at(b, fb)], (((1,), (1,)), ((), ())), preferred_element_type=f32
            ).astype(bf16)
            return 0

        lax.fori_loop(0, n, turn, 0)

    def input_gradient(weight, result, i):
        result[:, at(i, fb)] = jnp.dot(
            dp[0:T, :], weight[:, at(i, fb)], preferred_element_type=f32
        ).astype(bf16)

    def sum_copy(layer, i):
        return neur_copy(
            sumpay.at[layer, :, at(i, fb)],
            sumland.at[layer, me],
            sum_sends.at[layer, i],
            sum_recvs.at[layer, me],
            i,
        )

    def sum_along(layer, i):
        return seq_copy(
            sumseq.at[layer],
            sumseqland.at[layer, mine],
            sum_sends.at[layer, n + i],
            sum_recvs.at[layer, n + mine],
            i,
        )

    def sum_start(layer):
        others(lambda i: sum_copy(layer, i).start())
        sumland[layer, me] = sumpay[layer, :, own_lanes]

    def sum_middle(layer):
        def wait(i):
            neur_copy(
                sumpay.at[layer, :, at(i, fb)],
                sumland.at[layer, i],
                sum_sends.at[layer, i],
                sum_recvs.at[layer, i],
                i,
            ).wait()

        others(wait)
        total = sumland[layer, 0]
        for i in range(1, n):
            total = total + sumland[layer, i]
        sumseq[layer] = total
        sumseqland[layer, mine] = total
        others(lambda i: sum_along(layer, i).start(), seqs, mine)

    def sum_finish(layer, frames, total):
        def wait(i):
            seq_copy(
                sumseq.at[layer],
                sumseqland.at[layer, i],
                sum_sends.at[layer, n + i],
                sum_recvs.at[layer, n + i],
                i,
            ).wait()

        others(wait, seqs, mine)
        whole = sumseqland[layer, 0]
        for i in range(1, seqs):
            whole = whole + sumseqland[layer, i]
        whole = whole[0:1, :]
        high = whole.astype(bf16).astype(f32)
        middle = (whole - high).astype(bf16).astype(f32)
        low = whole - high - middle
        rows = jnp.concatenate([high, middle, low, jnp.zeros((13, fb), f32)], axis=0).astype(bf16)
        columns = lax.dot_general(
            eye[...], rows, (((1,), (1,)), ((), ())), preferred_element_type=f32
        ).astype(bf16)
        total[...] -= jnp.dot(
            columns, frames[T : T + 16, at(mine, sz.qc)], preferred_element_type=f32
        )

    def place_out(a, ref, dest, i):
        return neur_copy(
            ref.at[:, at(i, fb)], dest.at[me], frame_sends.at[a, i], frame_recvs.at[a, me], i
        )

    def out_arrived(a, ref, dest, i):
        neur_copy(
            ref.at[:, at(i, fb)], dest.at[i], frame_sends.at[a, i], frame_recvs.at[a, i], i
        ).wait()

    def run_next(steps):
        if steps:
            steps.pop(0)()

    def send_g():
        others(lambda i: frames_copy(1, gs.at[:, at(i, fb)], gr.at[:, own_lanes], i).start())

    gather_two.steps.insert(2 * sz.Z - 3, send_g)
    layer_forward(0, xr, wf_one, p_one, s_one, x_two, lambda: gather_two.advance(1))
    gather_two.advance()
    others(lambda i: frames_sent(0, xs, i))
    layer_forward(1, x_two, wf_two, p_two, s_two, xs, lambda: None)

    others(lambda i: place_out(2, xs, out_land, i).start())
    keep_out = pltpu.make_async_copy(xs.at[:, own_lanes], out_land.at[me], local_sems.at[4])
    keep_out.start()
    others(lambda i: frames_wait(1, gr, i))
    others(lambda i: frames_sent(1, gs, i))
    gather_two.drain()

    layer_backward(1, gr, p_two, s_two, dpt_two, lambda: None)
    lax.fori_loop(0, n, lambda i, _: (input_gradient(wf_two, gr, i), 0)[1], 0)
    sum_start(1)
    reduce_two = Reduce(
        env,
        dpt_two,
        x_two,
        lambda k: land.at[k],
        spare.at[1],
        stage,
        fin.at[1],
        reduce_sends.at[1],
        reduce_recvs.at[1],
    )
    reduce_one = Reduce(
        env,
        dpt_one,
        xr,
        lambda k: wf_two.at[at(k // seqs, fb), at(k % seqs, sz.qc)],
        spare.at[0],
        stage,
        fin.at[0],
        reduce_sends.at[0],
        reduce_recvs.at[0],
    )
    result_two = Result(
        env, dw_two, fin.at[1], final_sends.at[1], final_recvs.at[1], local_sems.at[6]
    )
    result_one = Result(
        env, dw_one, fin.at[0], final_sends.at[0], final_recvs.at[0], local_sems.at[7]
    )
    for kind in range(4):
        reduce_two.cores(kind)

    half = sz.Z // 2
    layer_backward(
        0,
        gr,
        p_one,
        s_one,
        dpt_one,
        functools.partial(
            run_next,
            [
                reduce_two.diagonals,
                functools.partial(sum_middle, 1),
                functools.partial(reduce_two.sides, 0, half),
                functools.partial(reduce_two.sides, half, sz.Z),
            ],
        ),
    )
    sum_start(0)
    reduce_two.lines()
    reduce_two.finish()
    sum_finish(1, x_two, fin.at[1])
    result_two.start()
    reduce_two.drain()
    for kind in range(2):
        reduce_one.cores(kind)
    reduce_one.diagonals()

    def send_dx(i):
        input_gradient(wf_one, gs, i)
        place_out(3, gs, dx_land, i).start()

    others(send_dx)
    input_gradient(wf_one, gs, me)
    keep_dx = pltpu.make_async_copy(gs.at[:, own_lanes], dx_land.at[me], local_sems.at[5])
    keep_dx.start()
    for kind in range(2, 4):
        reduce_one.cores(kind)
    sum_middle(0)
    result_two.finish()
    reduce_one.sides()
    reduce_one.lines()
    reduce_one.finish()
    sum_finish(0, xr, fin.at[0])
    result_one.start()
    others(lambda i: out_arrived(2, xs, out_land, i))
    others(lambda i: out_arrived(3, gs, dx_land, i))
    keep_out.wait()
    keep_dx.wait()
    result_one.finish()
    reduce_one.drain()
    gather_one.drain()
    small[6:8, :] = jnp.zeros((2, fb), f32)


def turn_back(sz, x_ref, g_ref, out_ref, dx_ref, output, input_grad):
    step = pl.program_id(0)
    T, fb, win, odd = sz.T, sz.fb, sz.win, sz.odd
    output[...] = x_ref[...].astype(f32)
    input_grad[...] = g_ref[...].astype(f32)

    @pl.when(step < sz.n // 2)
    def _():
        row = lax.broadcasted_iota(jnp.int32, (T, win), 0)
        column = lax.broadcasted_iota(jnp.int32, (T, win), 1)
        frame = (row % 8) * sz.steps + row // 8
        row = lax.broadcasted_iota(jnp.int32, (fb, fb), 0)
        eye = jnp.where(row == lax.broadcasted_iota(jnp.int32, (fb, fb), 1), 1.0, 0.0).astype(bf16)
        for half in range(2):
            perm = jnp.where(column == frame + odd * half, 1.0, 0.0).astype(bf16)
            lanes = pl.ds((T - odd) * half, win)
            for source, result in ((out_ref, output), (dx_ref, input_grad)):
                turned = lax.dot_general(
                    eye, source[half], (((1,), (1,)), ((), ())), preferred_element_type=f32
                ).astype(bf16)
                result[:, lanes] += jnp.dot(turned, perm, preferred_element_type=f32)


def frame_rows(sz, lengths, frame_mask):
    T, steps = sz.T, sz.steps
    me = lax.axis_index("neur")
    starts = jnp.cumsum(lengths[0]) - lengths[0]
    row = jnp.arange(T, dtype=jnp.int32)
    slots = me * T + (row % 8) * steps + row // 8
    goes = jnp.where(jnp.any(slots[:, None] == starts[None, :], axis=1), 0.0, 1.0)
    part = lax.dynamic_slice(frame_mask, (me * T,), (T,)).reshape(8, steps).T.reshape(T)
    inside = slots < jnp.sum(lengths[0])
    count = jnp.where((part > 0) & inside, 1.0, 0.0)
    places = jnp.arange(frame_mask.shape[0], dtype=jnp.int32)
    block = jnp.sum(jnp.where((places < jnp.sum(lengths[0])) & (frame_mask > 0), 1.0, 0.0))
    run = jnp.arange(8, dtype=jnp.int32)
    first = me * T + run * steps
    behind = jnp.where(starts[None, :] < first[:, None], starts[None, :], 0)
    since = (first - jnp.max(behind, axis=1)).astype(f32)

    def unbroken(begin, length):
        inside = (starts[None, :] >= begin[:, None]) & (starts[None, :] < begin[:, None] + length)
        return jnp.where(jnp.any(inside, axis=1), 0.0, 1.0)

    whole = unbroken(run * T, T)
    own = unbroken(first, steps)
    aux = jnp.concatenate([since, whole, own, jnp.full((8,), 1.0) * block]).astype(f32)

    def lanes(values):
        return jnp.broadcast_to(values.astype(f32)[:, None], (values.shape[0], 128))

    return lanes(goes), lanes(count), lanes(aux)


def frames_apart(sz, inputs, weight_one, weight_two, params, lengths, frame_mask, out_grad):
    n, seqs, H, fb, T, Z, qc = sz.n, sz.seqs, sz.H, sz.fb, sz.T, sz.Z, sz.qc
    goes, count, aux = frame_rows(sz, lengths, frame_mask)
    own_par = jnp.concatenate([jnp.stack(params), jnp.zeros((2, fb), f32)], axis=0)
    whole = pl.BlockSpec(memory_space=pltpu.VMEM)
    anywhere = pl.BlockSpec(memory_space=pl.ANY)
    vmem, sem = pltpu.VMEM, pltpu.SemaphoreType.DMA
    frames_shape, longer_shape = (T, H), (sz.K, H)
    matmul = 2 * T * H * H
    out_land, dx_land, dw_one, dw_two, small = pl.pallas_call(
        functools.partial(network, sz),
        out_shape=(
            jax.ShapeDtypeStruct((n, T, fb), bf16),
            jax.ShapeDtypeStruct((n, T, fb), bf16),
            jax.ShapeDtypeStruct((fb, H), f32),
            jax.ShapeDtypeStruct((fb, H), f32),
            jax.ShapeDtypeStruct((8, fb), f32),
        ),
        in_specs=[anywhere] * 4 + [whole] * 4,
        out_specs=(anywhere, anywhere, anywhere, anywhere, whole),
        scratch_shapes=[
            vmem((fb, sz.valid), bf16),
            vmem((2, T, sz.win), bf16),
            vmem((fb, fb), bf16),
            vmem(frames_shape, bf16),
            vmem(frames_shape, bf16),
            vmem(longer_shape, bf16),
            vmem(frames_shape, bf16),
            vmem(frames_shape, bf16),
            vmem(frames_shape, bf16),
            vmem(longer_shape, bf16),
            vmem(longer_shape, bf16),
            vmem((H, sz.K), bf16),
            vmem((H, sz.K), bf16),
            vmem((T + 8, H), f32),
            vmem((T + 8, H), f32),
            vmem((H, H), bf16),
            vmem((H, H), bf16),
            vmem((8 * Z, fb, qc), bf16),
            vmem((5 * Z, fb, qc), bf16),
            vmem((2, fb, qc), bf16),
            vmem((2, fb, qc), f32),
            vmem((8, H), f32),
            vmem((8, H), f32),
            vmem((16, H), f32),
            vmem((4, 8, H), f32),
            vmem((4, n, 8, fb), f32),
            vmem((4, 8, fb), f32),
            vmem((4, seqs, 8, fb), f32),
            vmem((4, n, 8, fb), f32),
            vmem((4, 8, H), f32),
            vmem((2, 8, H), f32),
            vmem((2, n, 8, fb), f32),
            vmem((2, 8, fb), f32),
            vmem((2, seqs, 8, fb), f32),
            sem((8,)),
            sem((n,)),
            sem((n,)),
            sem((4, n)),
            sem((4, n)),
            sem((2, 10 * Z)),
            sem((2, 10 * Z)),
            sem((8, n)),
            sem((8, n)),
            sem((4, seqs)),
            sem((4, seqs)),
            sem((2, 10 * Z)),
            sem((2, 10 * Z)),
            sem((2, 3)),
            sem((2, 3)),
            sem((2, n + seqs)),
            sem((2, n + seqs)),
        ],
        compiler_params=pltpu.CompilerParams(
            collective_id=0, has_side_effects=True, vmem_limit_bytes=63 * 1024 * 1024
        ),
        cost_estimate=pl.CostEstimate(
            flops=6 * matmul, bytes_accessed=16 * fb * H, transcendentals=6 * T * H
        ),
        name="network",
    )(inputs, out_grad, weight_one, weight_two, own_par, goes, count, aux)
    tok = inputs.shape[1]
    pairs = n // 2
    steps = pl.cdiv(tok, 2 * T)
    frames_spec = pl.BlockSpec((fb, 2 * T), lambda p: (0, p))
    land_spec = pl.BlockSpec((2, T, fb), lambda p: (jnp.minimum(p, pairs - 1), 0, 0))
    output, input_grad = pl.pallas_call(
        functools.partial(turn_back, sz),
        grid=(steps,),
        out_shape=(jax.ShapeDtypeStruct((fb, tok), f32),) * 2,
        in_specs=[frames_spec, frames_spec, land_spec, land_spec],
        out_specs=(frames_spec, frames_spec),
        compiler_params=pltpu.CompilerParams(vmem_limit_bytes=48 * 1024 * 1024),
        name="turn_back",
    )(inputs, out_grad, out_land, dx_land)
    return (
        output,
        input_grad,
        dw_one,
        small[0],
        small[1],
        small[2],
        dw_two,
        small[3],
        small[4],
        small[5],
    )


def frame_tables(lengths, frame_mask):
    positions = jnp.arange(frame_mask.shape[0], dtype=jnp.int32)
    offsets = jnp.cumsum(lengths[0]) - lengths[0]
    filled = jnp.sum(lengths[0])
    begins = jnp.any(positions[:, None] == offsets[None, :], axis=1)
    continues = jnp.where(begins, 0.0, 1.0).astype(jnp.float32)
    counted = jnp.where((positions < filled) & (frame_mask > 0), 1.0, 0.0).astype(jnp.float32)
    return (continues, counted)


def linear_scan(coef_rows, driving, backwards):
    row_count, length = driving.shape
    block_count = length // block_span
    factor = coef_rows.reshape(row_count, block_count, block_span)
    running = driving.reshape(row_count, block_count, block_span)
    places = jnp.arange(block_span, dtype=jnp.int32)
    step = 1
    while step < block_span:
        if backwards:
            mover = jnp.where(places[:, None] == places[None, :] + step, 1.0, 0.0).astype(
                jnp.float32
            )
            edge = jnp.where(places >= block_span - step, 1.0, 0.0).astype(jnp.float32)
        else:
            mover = jnp.where(places[:, None] == places[None, :] - step, 1.0, 0.0).astype(
                jnp.float32
            )
            edge = jnp.where(places < step, 1.0, 0.0).astype(jnp.float32)
        moved_factor = (
            jnp.dot(
                factor, mover, precision=lax.Precision.HIGHEST, preferred_element_type=jnp.float32
            )
            + edge
        )
        moved_running = jnp.dot(
            running, mover, precision=lax.Precision.HIGHEST, preferred_element_type=jnp.float32
        )
        running = factor * moved_running + running
        factor = factor * moved_factor
        step = step * 2
    end_place = 0 if backwards else block_span - 1
    total_factor = factor[:, :, end_place].T
    total_running = running[:, :, end_place].T

    def carry_step(carried, block_pair):
        return (block_pair[0] * carried + block_pair[1], carried)

    _, entering = lax.scan(
        carry_step,
        jnp.zeros((row_count,), jnp.float32),
        (total_factor, total_running),
        reverse=backwards,
    )
    result = running + factor * entering.T[:, :, None]
    return result.reshape(row_count, length)


def layer_forward(layer_input, weight, gain_row, bias_row, decay_rate, continues, counted):
    frames_in = lax.all_to_all(layer_input, "neur", split_axis=1, concat_axis=0, tiled=True)
    projected = jnp.dot(
        lax.all_gather(weight, "neur", axis=0, tiled=True),
        frames_in,
        preferred_element_type=jnp.float32,
    )
    neuron_proj = lax.all_to_all(
        projected.astype(jnp.bfloat16), "neur", split_axis=0, concat_axis=1, tiled=True
    ).astype(jnp.float32)
    sum_first = jnp.sum(counted[None, :] * neuron_proj, axis=1)
    sum_second = jnp.sum(counted[None, :] * neuron_proj * neuron_proj, axis=1)
    sum_first, sum_second, frames = lax.psum((sum_first, sum_second, jnp.sum(counted)), "seq")
    average = sum_first / frames
    inv_std = lax.rsqrt(sum_second / frames - average * average + epsilon)
    normed = (neuron_proj - average[:, None]) * inv_std[:, None]
    spread = jnp.sqrt(1.0 - decay_rate * decay_rate)
    states = linear_scan(
        decay_rate[:, None] * continues[None, :], (spread * gain_row)[:, None] * normed, False
    )
    layer_out = counted[None, :] * jax.nn.softplus(states + bias_row[:, None])
    return (layer_out, (frames_in, None, normed, inv_std, frames, states))


def layer_backward(
    upstream, weight, gain_row, bias_row, decay_rate, continues, counted, kept_state
):
    frames_in, full_weight, normed, inv_std, frames, states = kept_state
    local_grad = upstream * counted[None, :] * jax.nn.sigmoid(states + bias_row[:, None])
    following = jnp.concatenate([continues[1:], jnp.zeros((1,), jnp.float32)])
    coef_rows = decay_rate[:, None] * following[None, :]
    state_grad = linear_scan(coef_rows, local_grad, True)
    sum_rec, sum_rec_norm, sum_local = lax.psum(
        (
            jnp.sum(state_grad, axis=1),
            jnp.sum(state_grad * normed, axis=1),
            jnp.sum(local_grad, axis=1),
        ),
        "seq",
    )
    spread = jnp.sqrt(1.0 - decay_rate * decay_rate)
    gain_grad = spread * sum_rec_norm
    proj_grad = (spread * gain_row * inv_std)[:, None] * (
        state_grad - counted[None, :] * (sum_rec[:, None] + sum_rec_norm[:, None] * normed) / frames
    )
    driving = (spread * gain_row)[:, None] * normed
    decay_part = jnp.sum(state_grad * (states - driving), axis=1) / decay_rate
    grad_frames = lax.all_to_all(
        proj_grad.astype(jnp.bfloat16), "neur", split_axis=1, concat_axis=0, tiled=True
    )
    grad_rows = grad_frames
    input_frames = jnp.einsum(
        "ot,oi->it",
        grad_rows,
        lax.all_gather(weight, "neur", axis=0, tiled=True),
        preferred_element_type=jnp.float32,
    )
    input_grad = lax.all_to_all(
        input_frames.astype(jnp.bfloat16), "neur", split_axis=0, concat_axis=1, tiled=True
    ).astype(jnp.float32)
    grad_rows = grad_frames
    weight_rows = lax.psum_scatter(
        jnp.einsum("ot,it->oi", grad_rows, frames_in, preferred_element_type=jnp.float32),
        "neur",
        scatter_dimension=0,
        tiled=True,
    )
    weight_grad, decay_sum = lax.psum((weight_rows, decay_part), "seq")
    decay_grad = decay_sum - decay_rate / spread * gain_row * sum_rec_norm
    return (input_grad, weight_grad, gain_grad, sum_local, decay_grad)


def shards(
    inputs,
    weight_one,
    weight_two,
    gain_one,
    gain_two,
    bias_one,
    bias_two,
    decay_one,
    decay_two,
    lengths,
    frame_mask,
    out_grad,
):
    seqs, n = lax.axis_size("seq"), lax.axis_size("neur")
    H, (fb, tok) = weight_one.shape[1], inputs.shape
    if fits(n, seqs, H, fb, tok):
        params = (gain_one, gain_two, bias_one, bias_two, decay_one, decay_two)
        return frames_apart(
            Sizes(n, seqs, H, fb, tok),
            inputs,
            weight_one,
            weight_two,
            params,
            lengths,
            frame_mask,
            out_grad,
        )
    continues, counted = frame_tables(lengths, frame_mask)
    first_out, first_kept = layer_forward(
        inputs, weight_one, gain_one, bias_one, decay_one, continues, counted
    )
    second_out, second_kept = layer_forward(
        first_out.astype(jnp.bfloat16),
        weight_two,
        gain_two,
        bias_two,
        decay_two,
        continues,
        counted,
    )
    output = inputs.astype(jnp.float32) + second_out
    upstream = out_grad.astype(jnp.float32)
    middle_grad, weight_two_grad, gain_two_grad, bias_two_grad, decay_two_grad = layer_backward(
        upstream, weight_two, gain_two, bias_two, decay_two, continues, counted, second_kept
    )
    lower_grad, weight_one_grad, gain_one_grad, bias_one_grad, decay_one_grad = layer_backward(
        middle_grad, weight_one, gain_one, bias_one, decay_one, continues, counted, first_kept
    )
    return (
        output,
        upstream + lower_grad,
        weight_one_grad,
        gain_one_grad,
        bias_one_grad,
        decay_one_grad,
        weight_two_grad,
        gain_two_grad,
        bias_two_grad,
        decay_two_grad,
    )


def solution(mesh):
    placed = (
        P("neur", "seq"),
        P("neur", None),
        P("neur", None),
        P("neur"),
        P("neur"),
        P("neur"),
        P("neur"),
        P("neur"),
        P("neur"),
        P("seq", None),
        P("seq"),
        P("neur", "seq"),
    )
    return jax.shard_map(
        shards,
        mesh=mesh,
        in_specs=placed,
        out_specs=(
            P("neur", "seq"),
            P("neur", "seq"),
            P("neur", None),
            P("neur"),
            P("neur"),
            P("neur"),
            P("neur", None),
            P("neur"),
            P("neur"),
            P("neur"),
        ),
        check_vma=False,
    )
```

```python
import functools

import jax
import jax.numpy as jnp
from jax import lax
from jax.experimental import pallas as pl
from jax.experimental.pallas import tpu as pltpu
from jax.sharding import PartitionSpec as P

epsilon = 1e-05
block_span = 128
valid_frames = 3584
f32 = jnp.float32
bf16 = jnp.bfloat16
MESH = pl.DeviceIdType.MESH


def wide(tile, width):
    return jnp.concatenate([tile] * (width // 128), axis=1)


def at(index, size):
    if isinstance(index, int):
        return pl.ds(index * size, size)
    return pl.ds(pl.multiple_of(index * size, size), size)


def power(base, exponent):
    result = None
    while exponent:
        if exponent % 2:
            result = base if result is None else result * base
        exponent //= 2
        base = base * base
    return result


def log_of(rate):
    u = 1.0 - rate
    series = jnp.full_like(u, 1.0 / 8)
    for order in range(7, 0, -1):
        series = series * u + 1.0 / order
    return -u * series


GAIN, BIAS, DECAY = 0, 2, 4


class Sizes:
    def __init__(self, n, seqs, H, fb, tok_dev):
        self.n, self.seqs, self.H, self.fb, self.tok_dev = n, seqs, H, fb, tok_dev
        self.T = valid_frames // n
        self.steps = self.T // 8
        self.valid = valid_frames
        self.qc = H // seqs
        self.Z = n // 2
        self.odd = self.T % 128
        self.win = self.T + self.odd
        self.K = self.T + 16
        self.L = min(512, H)


def fits(n, seqs, H, fb, tok_dev):
    if valid_frames % n or n % 2 or n > 8 or seqs != 4 or fb * n != H or fb % 128 or H % 512:
        return False
    T = valid_frames // n
    return T % 64 == 0 and valid_frames % 128 == 0 and tok_dev >= valid_frames


class Line:
    def __init__(self, env, sends, recvs):
        self.env, self.sends, self.recvs = env, sends, recvs

    def copy(self, k, source, dest, target):
        return pltpu.make_async_remote_copy(
            src_ref=source,
            dst_ref=dest,
            send_sem=self.sends.at[k],
            recv_sem=self.recvs.at[k],
            device_id=target,
            device_id_type=MESH,
        )

    def arrived(self, k, ref):
        self.copy(k, ref, ref, self.env.across("x")).wait_recv()

    def sent(self, k, ref):
        self.copy(k, ref, ref, self.env.across("x")).wait_send()

    def along(self, dz):
        z, Z = self.env.z, self.env.sz.Z
        if dz == 0:
            return [(None, z, 0)]
        return [(z >= dz, z - dz, 1), (z + dz < Z, z + dz, -1)]


def if_so(condition, body):
    if condition is None:
        body()
    else:
        pl.when(condition)(body)


class Gather(Line):
    def __init__(self, env, source, full, sends, recvs, cut):
        super().__init__(env, sends, recvs)
        self.cut = cut
        self.full = full
        self.source = source.at[:, at(env.s, env.sz.qc)]

    def block(self, zz, fx, fy, fc=0):
        env = self.env
        rows = at(2 * zz + (env.x + fx) % 2, env.sz.fb)
        return self.full.at[rows, at(2 * ((env.y + fy) % 2) + (env.c + fc) % 2, env.sz.qc)]

    def half(self, ref, h):
        if h == 0:
            return ref.at[pl.ds(0, self.cut), :]
        return ref.at[pl.ds(self.cut, self.env.sz.fb - self.cut), :]

    def spread(self, zz, source):
        env, Z = self.env, self.env.sz.Z
        dest = self.block(zz, 0, 0)
        self.copy(2 * Z + zz, source, dest, env.across("x")).start()
        self.copy(3 * Z + zz, source, dest, env.across("y")).start()
        self.copy(6 * Z + zz, source, dest, env.across("core")).start()

    def pass_on(self, zz, source, way):
        env, Z = self.env, self.env.sz.Z
        dest = self.block(zz, 0, 0)

        def go():
            pltpu.make_async_remote_copy(
                src_ref=source,
                dst_ref=dest,
                send_sem=self.sends.at[zz if way > 0 else Z + zz],
                recv_sem=self.recvs.at[zz],
                device_id={"neur": 2 * (env.z + way) + env.x},
                device_id_type=MESH,
            ).start()

        pl.when(env.z < Z - 1 if way > 0 else env.z > 0)(go)

    def start(self):
        z = self.env.z
        self.pass_on(z, self.source, 1)
        self.pass_on(z, self.source, -1)
        self.spread(z, self.source)

    def line(self, dz):
        for condition, zz, way in self.along(dz):

            def one(zz=zz, way=way):
                block = self.block(zz, 0, 0)
                self.arrived(zz, block)
                self.pass_on(zz, block, way)
                self.spread(zz, block)

            if_so(condition, one)

    def sides(self, dz):
        env, Z = self.env, self.env.sz.Z
        for condition, zz, _ in self.along(dz):

            def one(zz=zz):
                block = self.block(zz, 1, 0)
                self.arrived(2 * Z + zz, block)
                part = self.half(block, 1)
                self.copy(5 * Z + zz, part, part, env.across("y")).start()
                self.copy(7 * Z + zz, block, block, env.across("core")).start()
                block = self.block(zz, 0, 1)
                self.arrived(3 * Z + zz, block)
                part = self.half(block, 0)
                self.copy(4 * Z + zz, part, part, env.across("x")).start()
                self.copy(8 * Z + zz, block, block, env.across("core")).start()

            if_so(condition, one)

    def diagonals(self):
        env, Z = self.env, self.env.sz.Z
        for dz in range(Z):
            for condition, zz, _ in self.along(dz):

                def one(zz=zz):
                    block = self.block(zz, 1, 1)
                    self.arrived(4 * Z + zz, self.half(block, 0))
                    self.arrived(5 * Z + zz, self.half(block, 1))
                    self.copy(9 * Z + zz, block, block, env.across("core")).start()

                if_so(condition, one)

    def cores(self):
        Z = self.env.sz.Z
        for k, (fx, fy) in enumerate(((0, 0), (1, 0), (0, 1), (1, 1))):
            for zz in range(Z):
                self.arrived((6 + k) * Z + zz, self.block(zz, fx, fy, 1))

    def drain(self):
        env, Z = self.env, self.env.sz.Z
        block = self.block(0, 0, 0)
        for zz in range(Z):
            pl.when((zz <= env.z) & (env.z < Z - 1))(lambda zz=zz: self.sent(zz, block))
            pl.when((zz >= env.z) & (env.z > 0))(lambda zz=zz: self.sent(Z + zz, block))
            for k in (2, 3, 6, 7, 8, 9):
                self.sent(k * Z + zz, block)
            self.sent(4 * Z + zz, self.half(block, 0))
            self.sent(5 * Z + zz, self.half(block, 1))


class Reduce(Line):
    kinds = ((1, 1), (1, 0), (0, 1), (0, 0))

    def __init__(self, env, grads, frames, land, spare, stage, held, total, sends, recvs, relay):
        super().__init__(env, sends, recvs)
        self.relay, self.held = relay, held
        self.grads, self.frames, self.land, self.spare = grads, frames, land, spare
        self.stage, self.total = stage, total

    def product(self, kind, zz, fc=0):
        env, sz = self.env, self.env.sz
        fx, fy = self.kinds[kind]
        rows = at(2 * zz + (env.x + fx) % 2, sz.fb)
        columns = at(2 * ((env.y + fy) % 2) + (env.c + fc) % 2, sz.qc)
        return jnp.dot(
            self.grads[rows, :], self.frames[:, columns], preferred_element_type=f32
        )

    def half(self, ref, h):
        return ref.at[pl.ds(h * (self.env.sz.fb // 2), self.env.sz.fb // 2), :]

    def landed(self, k, slot):
        self.arrived(k, self.land(slot))
        return self.land(slot)[...].astype(f32)

    def cores(self, kind):
        env, Z = self.env, self.env.sz.Z

        def one(zz, _):
            k = kind * Z + zz
            held = (kind % 2) * Z + zz
            if kind >= 2:
                self.sent(k - 2 * Z, self.stage.at[held])
            self.stage[held] = self.product(kind, zz, 1).astype(bf16)
            self.copy(k, self.stage.at[held], self.land(k), env.across("core")).start()
            return 0

        lax.fori_loop(0, Z, one, 0)

    def diagonals(self):
        env, Z = self.env, self.env.sz.Z

        def one(zz, _):
            held = self.held(zz)
            held[...] = (self.product(0, zz) + self.landed(zz, zz)).astype(bf16)
            slot = self.land(4 * Z + zz)
            for k, h, axis in ((4, 0, "x"), (5, 1, "y")):
                self.copy(
                    k * Z + zz, self.half(held, h), self.half(slot, h), env.across(axis)
                ).start()
            return 0

        lax.fori_loop(0, Z, one, 0)

    def sides(self, low=0, high=None):
        env, Z = self.env, self.env.sz.Z
        rows = env.sz.fb // 2

        def one(zz, _):
            slot = self.land(4 * Z + zz)
            for kind, h, wait, k, axis in ((1, 1, 5, 6, "x"), (2, 0, 4, 7, "y")):
                tile = self.product(kind, zz) + self.landed(kind * Z + zz, kind * Z + zz)
                part = self.half(slot, h)
                self.arrived(wait * Z + zz, part)
                held = self.stage.at[(2 + kind) * Z + zz]
                other = 1 - h
                own = slice(h * rows, (h + 1) * rows)
                rest = slice(other * rows, (other + 1) * rows)
                self.half(held, h)[...] = (tile[own, :] + part[...].astype(f32)).astype(bf16)
                self.half(held, other)[...] = tile[rest, :].astype(bf16)
                self.copy(
                    k * Z + zz, held, self.land((4 + kind) * Z + zz), env.across(axis)
                ).start()
            return 0

        lax.fori_loop(low, Z if high is None else high, one, 0)

    def joined(self, zz):
        Z = self.env.sz.Z
        tile = self.product(3, zz) + self.landed(3 * Z + zz, 3 * Z + zz)
        tile = tile + self.landed(6 * Z + zz, 5 * Z + zz)
        self.total[...] = tile + self.landed(7 * Z + zz, 6 * Z + zz)

    def lines(self):
        env, Z, z = self.env, self.env.sz.Z, self.env.z
        if not self.relay:
            for dz in range(1, Z):
                self.straight((z + dz) % Z)
            return

        def onward(zz, way):
            k, slot = (8 if way > 0 else 9) * Z + zz, 7 * Z + zz
            self.joined(zz)

            @pl.when(z > 0 if way > 0 else z < Z - 1)
            def _():
                self.total[...] += self.landed(k, slot)

            held = self.held(zz)
            self.sent(4 * Z + zz, self.half(held, 0))
            self.sent(5 * Z + zz, self.half(held, 1))
            held[...] = self.total[...].astype(bf16)
            target = {"neur": 2 * (z + way) + env.x}
            if way > 0:
                self.copy(k, held, self.land(slot), target).start()
            else:
                pl.when(zz == z - 1)(lambda: self.copy(k, held, self.spare, target).start())
                pl.when(zz != z - 1)(lambda: self.copy(k, held, self.land(slot), target).start())

        for i in range(Z - 1):
            pl.when(Z - 1 - i > z)(functools.partial(onward, Z - 1 - i, 1))
            pl.when(i < z)(functools.partial(onward, i, -1))

    def straight(self, zz):
        env, Z, z = self.env, self.env.sz.Z, self.env.z
        self.joined(zz)
        held = self.held(zz)
        self.sent(4 * Z + zz, self.half(held, 0))
        self.sent(5 * Z + zz, self.half(held, 1))
        held[...] = self.total[...].astype(bf16)
        pltpu.make_async_remote_copy(
            src_ref=held,
            dst_ref=self.land(7 * Z + z),
            send_sem=self.sends.at[8 * Z + zz],
            recv_sem=self.recvs.at[8 * Z + z],
            device_id={"neur": 2 * zz + env.x},
            device_id_type=MESH,
        ).start()

    def finish(self):
        Z, z = self.env.sz.Z, self.env.z
        self.joined(z)
        if not self.relay:
            for dz in range(1, Z):
                zz = (z + dz) % Z
                self.total[...] += self.landed(8 * Z + zz, 7 * Z + zz)
            return

        @pl.when(z > 0)
        def _():
            self.total[...] += self.landed(8 * Z + z, 7 * Z + z)

        @pl.when(z < Z - 1)
        def _():
            self.arrived(9 * Z + z, self.spare)
            self.total[...] += self.spare[...].astype(f32)

    def drain_cores(self):
        for k in range(2 * self.env.sz.Z, 4 * self.env.sz.Z):
            self.sent(k, self.stage.at[0])

    def drain_sides(self):
        for k in range(6 * self.env.sz.Z, 8 * self.env.sz.Z):
            self.sent(k, self.stage.at[0])

    def drain(self):
        Z, z = self.env.sz.Z, self.env.z
        held = self.stage.at[0]
        for zz in range(Z):
            for k in (4, 5):
                pl.when(zz == z)(
                    lambda k=k, zz=zz: self.sent(k * Z + zz, self.half(held, k - 4))
                )
            if self.relay:
                pl.when(zz > z)(lambda zz=zz: self.sent(8 * Z + zz, held))
                pl.when(zz < z)(lambda zz=zz: self.sent(9 * Z + zz, held))
            else:
                pl.when(zz != z)(lambda zz=zz: self.sent(8 * Z + zz, held))


class Result:
    def __init__(self, env, whole, block, sends, recvs, local):
        self.env, self.whole, self.block = env, whole, block
        self.sends, self.recvs, self.local = sends, recvs, local

    def part(self, flip_y, flip_c):
        env = self.env
        s = 2 * ((env.y + flip_y) % 2) + (env.c + flip_c) % 2
        return self.whole.at[:, at(s, env.sz.qc)]

    def copy(self, k, source, dest, target):
        return pltpu.make_async_remote_copy(
            src_ref=source,
            dst_ref=dest,
            send_sem=self.sends.at[k],
            recv_sem=self.recvs.at[k],
            device_id=target,
            device_id_type=MESH,
        )

    def start(self):
        env, own = self.env, self.part(0, 0)
        self.copy(0, self.block, own, env.across("y")).start()
        self.copy(1, self.block, own, env.across("core")).start()
        pltpu.make_async_copy(self.block, own, self.local).start()

    def finish(self):
        env = self.env
        other = self.part(1, 0)
        self.copy(0, self.block, other, env.across("y")).wait_recv()
        forward = self.copy(2, other, other, env.across("core"))
        forward.start()
        own = self.part(0, 0)
        pltpu.make_async_copy(self.block, own, self.local).wait()
        self.copy(0, self.block, own, env.across("y")).wait_send()
        self.copy(1, self.block, self.part(0, 1), env.across("core")).wait()
        forward.wait_send()
        self.copy(2, other, self.part(1, 1), env.across("core")).wait_recv()


class Env:
    def across(self, axis):
        if axis == "x":
            return {"neur": 2 * self.z + 1 - self.x}
        if axis == "y":
            return {"seq": 2 * (1 - self.y) + self.c}
        return {"seq": 2 * self.y + 1 - self.c}


def network(
    sz,
    x_hbm,
    g_hbm,
    w_one,
    w_two,
    own_par,
    cont,
    counted,
    aux,
    out_land,
    dx_land,
    dw_one,
    dw_two,
    small,
    raw,
    perm,
    eye,
    xs,
    gs,
    xr,
    gr,
    p_one,
    p_two,
    x_two,
    dp,
    dpt_one,
    dpt_two,
    s_one,
    s_two,
    wf_one,
    wf_two,
    land,
    stage,
    spare,
    fin,
    par,
    ends,
    work,
    pay,
    arrive,
    seqpay,
    seqland,
    back,
    backland,
    sumpay,
    sumland,
    sumseq,
    sumseqland,
    local_sems,
    par_sends,
    par_recvs,
    frame_sends,
    frame_recvs,
    gather_sends,
    gather_recvs,
    hop_sends,
    hop_recvs,
    seq_sends,
    seq_recvs,
    reduce_sends,
    reduce_recvs,
    final_sends,
    final_recvs,
    sum_sends,
    sum_recvs,
):
    n, seqs, H, fb, T, steps, L = sz.n, sz.seqs, sz.H, sz.fb, sz.T, sz.steps, sz.L
    env = Env()
    env.sz = sz
    me = lax.axis_index("neur")
    mine = lax.axis_index("seq")
    env.j, env.s = me, mine
    env.z, env.x, env.y, env.c = me // 2, me % 2, mine // 2, mine % 2

    barrier = pltpu.get_barrier_semaphore()
    for o in range(1, n):
        pl.semaphore_signal(
            barrier, inc=1, device_id={"neur": (me + o) % n}, device_id_type=MESH
        )
    for o in range(1, seqs):
        pl.semaphore_signal(
            barrier, inc=1, device_id={"seq": (mine + o) % seqs}, device_id_type=MESH
        )
    load_x = pltpu.make_async_copy(x_hbm.at[:, pl.ds(0, sz.valid)], raw, local_sems.at[0])
    load_x.start()
    pl.semaphore_wait(barrier, n - 1 + seqs - 1)

    def neur_copy(source, dest, send, recv, i):
        return pltpu.make_async_remote_copy(
            src_ref=source,
            dst_ref=dest,
            send_sem=send,
            recv_sem=recv,
            device_id={"neur": i},
            device_id_type=MESH,
        )

    def seq_copy(source, dest, send, recv, i):
        return pltpu.make_async_remote_copy(
            src_ref=source,
            dst_ref=dest,
            send_sem=send,
            recv_sem=recv,
            device_id={"seq": i},
            device_id_type=MESH,
        )

    def others(body, count=n, own=me):
        def one(o, _):
            body((own + o) % count)
            return 0

        lax.fori_loop(1, count, one, 0)

    own_lanes = at(me, fb)

    def par_copy(i):
        return neur_copy(own_par, par.at[:, own_lanes], par_sends.at[i], par_recvs.at[me], i)

    def par_wait(i):
        neur_copy(own_par, par.at[:, at(i, fb)], par_sends.at[i], par_recvs.at[i], i).wait()

    others(lambda i: par_copy(i).start())
    par[:, own_lanes] = own_par[...]

    cuts = (fb // 4, fb // 4)
    gather_one = Gather(env, w_one, wf_one, gather_sends.at[0], gather_recvs.at[0], cuts[0])
    gather_two = Gather(env, w_two, wf_two, gather_sends.at[1], gather_recvs.at[1], cuts[1])
    own_one = pltpu.make_async_copy(gather_one.source, gather_one.block(env.z, 0, 0), local_sems.at[2])
    own_two = pltpu.make_async_copy(gather_two.source, gather_two.block(env.z, 0, 0), local_sems.at[3])
    own_one.start()
    own_two.start()
    gather_one.start()
    gather_two.start()

    row = lax.broadcasted_iota(jnp.int32, (T, sz.win), 0)
    column = lax.broadcasted_iota(jnp.int32, (T, sz.win), 1)
    frame = (row & 7) * steps + (row >> 3)
    perm[0] = jnp.where(column == frame, 1.0, 0.0).astype(bf16)
    perm[1] = jnp.where(column == frame + sz.odd, 1.0, 0.0).astype(bf16)
    row = lax.broadcasted_iota(jnp.int32, (fb, fb), 0)
    column = lax.broadcasted_iota(jnp.int32, (fb, fb), 1)
    eye[...] = jnp.where(row == column, 1.0, 0.0).astype(bf16)

    def window(i):
        start = (i // 2) * (2 * T) + (i % 2) * (T - sz.odd)
        return pl.ds(pl.multiple_of(start, 128), sz.win)

    def turned(i):
        return lax.dot_general(
            perm[i % 2], raw[:, window(i)], (((1,), (1,)), ((), ())), preferred_element_type=f32
        ).astype(bf16)

    def frames_copy(a, source, dest, i):
        return neur_copy(source, dest, frame_sends.at[a, i], frame_recvs.at[a, me], i)

    def frames_wait(a, ref, i):
        part = ref.at[pl.ds(0, T), at(i, fb)]
        neur_copy(part, part, frame_sends.at[a, i], frame_recvs.at[a, i], i).wait_recv()

    def frames_sent(a, ref, i):
        part = ref.at[pl.ds(0, T), at(i, fb)]
        neur_copy(part, part, frame_sends.at[a, i], frame_recvs.at[a, i], i).wait_send()

    load_x.wait()

    def turn_x(i):
        xs[:, at(i, fb)] = turned(i)

    def send_x(i):
        frames_copy(0, xs.at[:, at(i, fb)], xr.at[pl.ds(0, T), own_lanes], i).start()

    def send_all_x():
        others(send_x)

    others(turn_x)
    xr[0:T, own_lanes] = turned(me)
    load_g = pltpu.make_async_copy(g_hbm.at[:, pl.ds(0, sz.valid)], raw, local_sems.at[1])
    load_g.start()
    ends_of_line = (env.z == 0) | (env.z == sz.Z - 1)
    pl.when(ends_of_line)(send_all_x)
    for dz in range(1, sz.Z):
        gather_one.line(dz)
        gather_two.line(dz)
        if dz == max(1, sz.Z - 2):
            pl.when(jnp.logical_not(ends_of_line))(send_all_x)
        gather_one.sides(dz - 1)
    load_g.wait()

    def turn_g(i):
        gs[:, at(i, fb)] = turned(i)

    def send_g(i):
        frames_copy(1, gs.at[:, at(i, fb)], gr.at[:, own_lanes], i).start()

    others(turn_g)
    gr[:, own_lanes] = turned(me)
    gather_one.sides(sz.Z - 1)
    others(send_g)
    gather_one.diagonals()
    for dz in range(sz.Z):
        gather_two.sides(dz)
    gather_two.diagonals()
    gather_one.cores()
    own_one.wait()
    own_two.wait()
    others(lambda i: frames_wait(0, xr, i))
    others(par_wait)

    def blocks(body):
        def one(b, _):
            body(at(b, L))
            return 0

        lax.fori_loop(0, H // L, one, 0)

    def project(frames, weight, result):
        def one(b, _):
            result[:, at(b, fb)] = lax.dot_general(
                frames[0:T, :],
                weight[at(b, fb), :],
                (((1,), (1,)), ((), ())),
                preferred_element_type=f32,
            ).astype(bf16)
            return 0

        lax.fori_loop(0, n, one, 0)

    def flags(t):
        tile = pl.ds(pl.multiple_of(8 * t, 8), 8)
        return wide(cont[tile, :], L), wide(counted[tile, :], L)

    def spread8(ref, r, cols, width=L):
        return jnp.broadcast_to(ref[r : r + 1, cols], (8, width))

    zero = jnp.zeros((8, L), f32)

    def down(value):
        return jnp.sum(value, axis=0, keepdims=True)

    def exchange(e, gathered, totalled, gap):
        def out_copy(i):
            return neur_copy(
                pay.at[e, :, at(i, fb)],
                arrive.at[e, me],
                hop_sends.at[2 * e, i],
                hop_recvs.at[2 * e, me],
                i,
            )

        others(lambda i: out_copy(i).start())
        arrive[e, me] = pay[e, :, own_lanes]
        gap("hop_a")

        def out_wait(i):
            neur_copy(
                pay.at[e, :, at(i, fb)],
                arrive.at[e, i],
                hop_sends.at[2 * e, i],
                hop_recvs.at[2 * e, i],
                i,
            ).wait()

        others(out_wait)
        gathered()

        def along_copy(i):
            return seq_copy(
                seqpay.at[e],
                seqland.at[e, mine],
                seq_sends.at[e, i],
                seq_recvs.at[e, mine],
                i,
            )

        def along_wait(i):
            seq_copy(
                seqpay.at[e], seqland.at[e, i], seq_sends.at[e, i], seq_recvs.at[e, i], i
            ).wait()

        others(lambda i: along_copy(i).start(), seqs, mine)
        seqland[e, mine] = seqpay[e]
        gap("hop_b")
        others(along_wait, seqs, mine)
        sums = seqland[e, 0]
        for i in range(1, seqs):
            sums = sums + seqland[e, i]
        totalled(sums)

        def back_copy(i):
            return neur_copy(
                back.at[e, i],
                backland.at[e, :, own_lanes],
                hop_sends.at[2 * e + 1, i],
                hop_recvs.at[2 * e + 1, me],
                i,
            )

        def back_wait(i):
            neur_copy(
                back.at[e, i],
                backland.at[e, :, at(i, fb)],
                hop_sends.at[2 * e + 1, i],
                hop_recvs.at[2 * e + 1, i],
                i,
            ).wait()

        others(lambda i: back_copy(i).start())
        backland[e, :, own_lanes] = back[e, me]
        gap("hop_c")
        others(back_wait)

    def layer_forward(layer, frames, weight, projected, states, store, gap):
        e = layer
        decay_row, gain_row, bias_row = DECAY + layer, GAIN + layer, BIAS + layer
        project(frames, weight, projected)
        gap("ends")

        def local_ends(cols):
            decay = spread8(par, decay_row, cols)

            def step(i, carry):
                state, first, second, inward = carry
                pair = projected[pl.ds(pl.multiple_of(16 * i, 16), 16), cols].astype(f32)
                for h in range(2):
                    value = pair[8 * h : 8 * h + 8, :]
                    goes, count = flags(2 * i + h)
                    state = (decay * goes) * state + value
                    held = count * value
                    first = first + held
                    second = second + held * value
                ins = frames[pl.ds(pl.multiple_of(16 * i, 16), 16), cols].astype(f32)
                return state, first, second, inward + ins[0:8, :] + ins[8:16, :]

            state, first, second, inward = lax.fori_loop(
                0, T // 16, step, (zero, zero, zero, zero)
            )
            ends[:, cols] = state
            pay[e, 1:2, cols] = down(first)
            pay[e, 2:3, cols] = down(second)
            pay[e, 3:4, cols] = down(inward)

        blocks(local_ends)
        run_power = power(par[decay_row : decay_row + 1, :], steps)
        total = jnp.zeros((1, H), f32)
        for k in range(8):
            total = run_power * wide(aux[16 + k : 17 + k, :], H) * total + ends[k : k + 1, :]
        pay[e, 0:1, :] = total
        pay[e, 4:8, :] = jnp.zeros((4, H), f32)

        own_decay = own_par[decay_row : decay_row + 1, :]

        def gathered():
            whole_power = power(own_decay, T)
            carried = jnp.zeros((1, fb), f32)
            sums = jnp.zeros((8, fb), f32)
            for i in range(n):
                rows = arrive[e, i]
                back[e, i, 0:1, :] = carried
                carried = whole_power * wide(aux[8 + i : 9 + i, :], fb) * carried + rows[0:1, :]
                sums = sums + rows
            seqpay[e] = sums
            seqpay[e, 0:1, :] = wide(aux[24:25, :], fb)

        def totalled(sums):
            frames_all = sums[0:1, :]
            average = sums[1:2, :] / frames_all
            inv_std = lax.rsqrt(sums[2:3, :] / frames_all - average * average + epsilon)
            centre = sums[3:4, :] / (sz.valid * seqs)
            for i in range(n):
                back[e, i, 1:2, :] = average
                back[e, i, 2:3, :] = inv_std
                back[e, i, 3:4, :] = frames_all
                back[e, i, 4:5, :] = centre
                back[e, i, 5:8, :] = jnp.zeros((3, fb), f32)

        exchange(e, gathered, totalled, gap)
        centre = backland[e, 4:5, :]
        frames[T : T + 16, :] = jnp.concatenate(
            [-centre, -centre, -centre, jnp.zeros((13, H), f32)], axis=0
        ).astype(bf16)

        total = backland[e, 0:1, :]
        for k in range(8):
            work[k : k + 1, :] = total
            total = run_power * wide(aux[16 + k : 17 + k, :], H) * total + ends[k : k + 1, :]

        def full_scan(cols):
            decay = spread8(par, decay_row, cols)
            average = spread8(backland.at[e], 1, cols)
            inv_std = spread8(backland.at[e], 2, cols)
            bias = spread8(par, bias_row, cols)
            scale = jnp.sqrt(1.0 - decay * decay) * spread8(par, gain_row, cols) * inv_std
            ones = (1.0 - jnp.exp(wide(aux[0:8, :], L) * log_of(decay))) / (1.0 - decay)
            state = scale * (work[0:8, cols] - average * ones)
            states[0:8, cols] = state

            def step(i, state):
                pair = projected[pl.ds(pl.multiple_of(16 * i, 16), 16), cols].astype(f32)
                outs = []
                for h in range(2):
                    goes, count = flags(2 * i + h)
                    state = (decay * goes) * state + scale * (pair[8 * h : 8 * h + 8, :] - average)
                    states[pl.ds(pl.multiple_of(16 * i + 8 * h + 8, 8), 8), cols] = state
                    v = state + bias
                    soft = jnp.maximum(v, 0.0) + jnp.log(1.0 + jnp.exp(-jnp.abs(v)))
                    outs.append(count * soft)
                store[pl.ds(pl.multiple_of(16 * i, 16), 16), cols] = jnp.concatenate(
                    outs, axis=0
                ).astype(bf16)
                return state

            lax.fori_loop(0, T // 16, step, state)

        blocks(full_scan)

    def layer_backward(layer, upstream, projected, states, turned_grads, gap):
        e = 2 + (1 - layer)
        decay_row, gain_row, bias_row = DECAY + layer, GAIN + layer, BIAS + layer
        run_power = power(par[decay_row : decay_row + 1, :], steps)

        def local_ends(cols):
            decay = spread8(par, decay_row, cols)
            average = spread8(backland.at[layer], 1, cols)
            inv_std = spread8(backland.at[layer], 2, cols)
            bias = spread8(par, bias_row, cols)

            def step(o, carry):
                i = T // 16 - 1 - o
                rows = pl.ds(pl.multiple_of(16 * i, 16), 16)
                pair = projected[rows, cols].astype(f32)
                ups = upstream[rows, cols].astype(f32)
                for h in (1, 0):
                    run, reach, U, V, UN, VN, B, D, DA = carry
                    goes, count = flags(2 * i + h)
                    here = pl.ds(pl.multiple_of(16 * i + 8 * h + 8, 8), 8)
                    state = states[here, cols]
                    before = states[pl.ds(pl.multiple_of(16 * i + 8 * h, 8), 8), cols]
                    local = ups[8 * h : 8 * h + 8, :] * count / (1.0 + jnp.exp(-(state + bias)))
                    states[here, cols] = local
                    normed = (pair[8 * h : 8 * h + 8, :] - average) * inv_std
                    run = local + run
                    kept = goes * before
                    link = decay * goes
                    carry = (
                        link * run,
                        link * reach,
                        U + run,
                        V + reach,
                        UN + run * normed,
                        VN + reach * normed,
                        B + local,
                        D + run * kept,
                        DA + reach * kept,
                    )
                return carry

            one = jnp.ones((8, L), f32)
            run, _, U, V, UN, VN, B, D, DA = lax.fori_loop(
                0, T // 16, step, (zero, one, zero, zero, zero, zero, zero, zero, zero)
            )
            ends[:, cols] = run
            decay_run = power(par[decay_row : decay_row + 1, cols], steps)
            part, factor = jnp.zeros((1, L), f32), jnp.ones((1, L), f32)
            for k in range(7, -1, -1):
                work[k : k + 1, cols] = part
                work[8 + k : 9 + k, cols] = factor
                through = decay_run * wide(aux[16 + k : 17 + k, :], L)
                part = through * part + ends[k : k + 1, cols]
                factor = through * factor
            pay[e, 0:1, cols] = part
            entering, scaled = work[0:8, cols], work[8:16, cols]
            pay[e, 1:2, cols] = down(U + V * entering)
            pay[e, 2:3, cols] = down(V * scaled)
            pay[e, 3:4, cols] = down(UN + VN * entering)
            pay[e, 4:5, cols] = down(VN * scaled)
            pay[e, 5:6, cols] = down(B)
            pay[e, 6:7, cols] = down(D + DA * entering)
            pay[e, 7:8, cols] = down(DA * scaled)

        blocks(local_ends)
        own_decay = own_par[decay_row : decay_row + 1, :]
        own_gain = own_par[gain_row : gain_row + 1, :]

        def gathered():
            whole_power = power(own_decay, T)
            carried = jnp.zeros((1, fb), f32)
            sums = [jnp.zeros((1, fb), f32)] * 4
            for i in range(n - 1, -1, -1):
                rows = arrive[e, i]
                back[e, i, 0:1, :] = carried
                for a, (plain, times) in enumerate(((1, 2), (3, 4), (5, None), (6, 7))):
                    term = rows[plain : plain + 1, :]
                    if times is not None:
                        term = term + rows[times : times + 1, :] * carried
                    sums[a] = sums[a] + term
                carried = whole_power * wide(aux[8 + i : 9 + i, :], fb) * carried + rows[0:1, :]
            for a in range(4):
                seqpay[e, a : a + 1, :] = sums[a]
            seqpay[e, 4:8, :] = jnp.zeros((4, fb), f32)

        def totalled(sums):
            rec, rec_norm = sums[0:1, :], sums[1:2, :]
            for i in range(n):
                back[e, i, 1:2, :] = rec
                back[e, i, 2:3, :] = rec_norm
                back[e, i, 3:8, :] = jnp.zeros((5, fb), f32)
            spread = jnp.sqrt(1.0 - own_decay * own_decay)
            small[3 * layer : 3 * layer + 1, :] = spread * rec_norm
            small[3 * layer + 1 : 3 * layer + 2, :] = sums[2:3, :]
            small[3 * layer + 2 : 3 * layer + 3, :] = (
                sums[3:4, :] - own_decay / spread * own_gain * rec_norm
            )

        exchange(e, gathered, totalled, gap)
        gap("scan")
        total = backland[e, 0:1, :]
        for k in range(7, -1, -1):
            work[k : k + 1, :] = total
            total = run_power * wide(aux[16 + k : 17 + k, :], H) * total + ends[k : k + 1, :]

        def full_scan(cols):
            decay = spread8(par, decay_row, cols)
            average = spread8(backland.at[layer], 1, cols)
            inv_std = spread8(backland.at[layer], 2, cols)
            frames_all = spread8(backland.at[layer], 3, cols)
            scale = jnp.sqrt(1.0 - decay * decay) * spread8(par, gain_row, cols) * inv_std
            rec = spread8(backland.at[e], 1, cols) / frames_all
            rec_norm = spread8(backland.at[e], 2, cols) / frames_all * inv_std

            def step(o, carry):
                carry, added = carry
                i = T // 16 - 1 - o
                rows = pl.ds(pl.multiple_of(16 * i, 16), 16)
                pair = projected[rows, cols].astype(f32)
                outs = [None, None]
                for h in (1, 0):
                    goes, count = flags(2 * i + h)
                    here = pl.ds(pl.multiple_of(16 * i + 8 * h + 8, 8), 8)
                    run = states[here, cols] + carry
                    centred = pair[8 * h : 8 * h + 8, :] - average
                    outs[h] = scale * (run - count * (rec + rec_norm * centred))
                    carry = (decay * goes) * run
                rounded = jnp.concatenate(outs, axis=0).astype(bf16)
                dp[rows, cols] = rounded
                rounded = rounded.astype(f32)
                return carry, added + rounded[0:8, :] + rounded[8:16, :]

            _, added = lax.fori_loop(0, T // 16, step, (work[0:8, cols], zero))
            whole = down(added)
            sumpay[layer, 0:1, cols] = whole
            high = whole.astype(bf16).astype(f32)
            middle = (whole - high).astype(bf16).astype(f32)
            low = whole - high - middle
            dp[T : T + 16, cols] = jnp.concatenate(
                [high, middle, low, jnp.zeros((13, L), f32)], axis=0
            ).astype(bf16)

        blocks(full_scan)
        sumpay[layer, 1:8, :] = jnp.zeros((7, H), f32)

        def turn(b, _):
            turned_grads[at(b, fb), :] = lax.dot_general(
                eye[...], dp[:, at(b, fb)], (((1,), (1,)), ((), ())), preferred_element_type=f32
            ).astype(bf16)
            return 0

        lax.fori_loop(0, n, turn, 0)

    def input_gradient(weight, result, i):
        result[:, at(i, fb)] = jnp.dot(
            dp[0:T, :], weight[:, at(i, fb)], preferred_element_type=f32
        ).astype(bf16)

    def sum_copy(layer, i):
        return neur_copy(
            sumpay.at[layer, :, at(i, fb)],
            sumland.at[layer, me],
            sum_sends.at[layer, i],
            sum_recvs.at[layer, me],
            i,
        )

    def sum_along(layer, i):
        return seq_copy(
            sumseq.at[layer],
            sumseqland.at[layer, mine],
            sum_sends.at[layer, n + i],
            sum_recvs.at[layer, n + mine],
            i,
        )

    def sum_start(layer):
        others(lambda i: sum_copy(layer, i).start())
        sumland[layer, me] = sumpay[layer, :, own_lanes]

    def sum_middle(layer):
        def wait(i):
            neur_copy(
                sumpay.at[layer, :, at(i, fb)],
                sumland.at[layer, i],
                sum_sends.at[layer, i],
                sum_recvs.at[layer, i],
                i,
            ).wait()

        others(wait)
        total = sumland[layer, 0]
        for i in range(1, n):
            total = total + sumland[layer, i]
        sumseq[layer] = total
        sumseqland[layer, mine] = total
        others(lambda i: sum_along(layer, i).start(), seqs, mine)

    def sum_finish(layer, frames, total):
        def wait(i):
            seq_copy(
                sumseq.at[layer],
                sumseqland.at[layer, i],
                sum_sends.at[layer, n + i],
                sum_recvs.at[layer, n + i],
                i,
            ).wait()

        others(wait, seqs, mine)
        whole = sumseqland[layer, 0]
        for i in range(1, seqs):
            whole = whole + sumseqland[layer, i]
        whole = whole[0:1, :]
        high = whole.astype(bf16).astype(f32)
        middle = (whole - high).astype(bf16).astype(f32)
        low = whole - high - middle
        rows = jnp.concatenate([high, middle, low, jnp.zeros((13, fb), f32)], axis=0).astype(bf16)
        columns = lax.dot_general(
            eye[...], rows, (((1,), (1,)), ((), ())), preferred_element_type=f32
        ).astype(bf16)
        total[...] -= jnp.dot(
            columns, frames[T : T + 16, at(mine, sz.qc)], preferred_element_type=f32
        )

    def place_out(a, ref, dest, i):
        return neur_copy(
            ref.at[:, at(i, fb)], dest.at[me], frame_sends.at[a, i], frame_recvs.at[a, me], i
        )

    def out_arrived(a, ref, dest, i):
        neur_copy(
            ref.at[:, at(i, fb)], dest.at[i], frame_sends.at[a, i], frame_recvs.at[a, i], i
        ).wait()

    def nothing(name):
        return None

    layer_forward(0, xr, wf_one, p_one, s_one, x_two, nothing)
    gather_two.cores()
    others(lambda i: frames_sent(0, xs, i))
    layer_forward(1, x_two, wf_two, p_two, s_two, xs, nothing)

    def send_out(low, high):
        def one(o, _):
            place_out(2, xs, out_land, (me + o) % n).start()
            return 0

        lax.fori_loop(low, high, one, 0)

    keep_out = pltpu.make_async_copy(xs.at[:, own_lanes], out_land.at[me], local_sems.at[4])
    keep_out.start()
    others(lambda i: frames_wait(1, gr, i))
    others(lambda i: frames_sent(1, gs, i))
    gather_two.drain()

    send_out(1, 2)
    layer_backward(
        1, gr, p_two, s_two, dpt_two, lambda name: send_out(2, 3) if name == "scan" else None
    )
    send_out(3, 4)
    lax.fori_loop(0, n, lambda i, _: (input_gradient(wf_two, gr, i), 0)[1], 0)
    sum_start(1)
    send_out(4, 5)
    reduce_two = Reduce(
        env,
        dpt_two,
        x_two,
        lambda k: land.at[k],
        spare.at[1],
        stage,
        lambda k: stage.at[2 * sz.Z + k],
        fin.at[1],
        reduce_sends.at[1],
        reduce_recvs.at[1],
        False,
    )
    reduce_one = Reduce(
        env,
        dpt_one,
        xr,
        lambda k: wf_two.at[at(k // seqs, fb), at(k % seqs, sz.qc)],
        spare.at[0],
        stage,
        lambda k: raw.at[:, at(k, sz.qc)],
        fin.at[0],
        reduce_sends.at[0],
        reduce_recvs.at[0],
        True,
    )
    result_two = Result(
        env, dw_two, fin.at[1], final_sends.at[1], final_recvs.at[1], local_sems.at[6]
    )
    result_one = Result(
        env, dw_one, fin.at[0], final_sends.at[0], final_recvs.at[0], local_sems.at[7]
    )
    for kind in range(4):
        reduce_two.cores(kind)
    reduce_two.diagonals()

    def meanwhile(name):
        if name == "hop_b":
            sum_middle(1)
        if name == "scan":
            reduce_two.sides()
            send_out(5, 6)

    layer_backward(0, gr, p_one, s_one, dpt_one, meanwhile)
    reduce_two.drain_cores()
    for kind in range(4):
        reduce_one.cores(kind)
    reduce_one.diagonals()
    sum_start(0)

    def send_dx(i):
        input_gradient(wf_one, gs, i)
        place_out(3, gs, dx_land, i).start()

    others(send_dx)
    input_gradient(wf_one, gs, me)
    send_out(6, n)
    keep_dx = pltpu.make_async_copy(gs.at[:, own_lanes], dx_land.at[me], local_sems.at[5])
    keep_dx.start()
    reduce_two.lines()
    reduce_two.drain_sides()
    sum_middle(0)
    reduce_one.sides()
    reduce_two.finish()
    sum_finish(1, x_two, fin.at[1])
    result_two.start()
    reduce_one.lines()
    reduce_one.finish()
    sum_finish(0, xr, fin.at[0])
    result_one.start()
    result_two.finish()
    others(lambda i: out_arrived(2, xs, out_land, i))
    others(lambda i: out_arrived(3, gs, dx_land, i))
    keep_out.wait()
    keep_dx.wait()
    result_one.finish()
    reduce_two.drain()
    reduce_one.drain_cores()
    reduce_one.drain_sides()
    reduce_one.drain()
    gather_one.drain()
    small[6:8, :] = jnp.zeros((2, fb), f32)


def turn_back(sz, x_ref, g_ref, out_ref, dx_ref, output, input_grad):
    step = pl.program_id(0)
    T, fb, win, odd = sz.T, sz.fb, sz.win, sz.odd
    output[...] = x_ref[...].astype(f32)
    input_grad[...] = g_ref[...].astype(f32)

    @pl.when(step < sz.n // 2)
    def _():
        row = lax.broadcasted_iota(jnp.int32, (T, win), 0)
        column = lax.broadcasted_iota(jnp.int32, (T, win), 1)
        frame = (row & 7) * sz.steps + (row >> 3)
        row = lax.broadcasted_iota(jnp.int32, (fb, fb), 0)
        eye = jnp.where(row == lax.broadcasted_iota(jnp.int32, (fb, fb), 1), 1.0, 0.0).astype(bf16)
        for half in range(2):
            perm = jnp.where(column == frame + odd * half, 1.0, 0.0).astype(bf16)
            lanes = pl.ds((T - odd) * half, win)
            for source, result in ((out_ref, output), (dx_ref, input_grad)):
                turned = lax.dot_general(
                    eye, source[half], (((1,), (1,)), ((), ())), preferred_element_type=f32
                ).astype(bf16)
                result[:, lanes] += jnp.dot(turned, perm, preferred_element_type=f32)


def frame_rows(sz, lengths, frame_mask):
    T, steps = sz.T, sz.steps
    me = lax.axis_index("neur")
    starts = jnp.cumsum(lengths[0]) - lengths[0]
    row = jnp.arange(T, dtype=jnp.int32)
    slots = me * T + (row % 8) * steps + row // 8
    goes = jnp.where(jnp.any(slots[:, None] == starts[None, :], axis=1), 0.0, 1.0)
    part = lax.dynamic_slice(frame_mask, (me * T,), (T,)).reshape(8, steps).T.reshape(T)
    inside = slots < jnp.sum(lengths[0])
    count = jnp.where((part > 0) & inside, 1.0, 0.0)
    places = jnp.arange(frame_mask.shape[0], dtype=jnp.int32)
    block = jnp.sum(jnp.where((places < jnp.sum(lengths[0])) & (frame_mask > 0), 1.0, 0.0))
    run = jnp.arange(8, dtype=jnp.int32)
    first = me * T + run * steps
    behind = jnp.where(starts[None, :] < first[:, None], starts[None, :], 0)
    since = (first - jnp.max(behind, axis=1)).astype(f32)

    def unbroken(begin, length):
        inside = (starts[None, :] >= begin[:, None]) & (starts[None, :] < begin[:, None] + length)
        return jnp.where(jnp.any(inside, axis=1), 0.0, 1.0)

    whole = unbroken(run * T, T)
    own = unbroken(first, steps)
    aux = jnp.concatenate([since, whole, own, jnp.full((8,), 1.0) * block]).astype(f32)

    def lanes(values):
        return jnp.broadcast_to(values.astype(f32)[:, None], (values.shape[0], 128))

    return lanes(goes), lanes(count), lanes(aux)


def frames_apart(sz, inputs, weight_one, weight_two, params, lengths, frame_mask, out_grad):
    n, seqs, H, fb, T, Z, qc = sz.n, sz.seqs, sz.H, sz.fb, sz.T, sz.Z, sz.qc
    goes, count, aux = frame_rows(sz, lengths, frame_mask)
    own_par = jnp.concatenate([jnp.stack(params), jnp.zeros((2, fb), f32)], axis=0)
    whole = pl.BlockSpec(memory_space=pltpu.VMEM)
    anywhere = pl.BlockSpec(memory_space=pl.ANY)
    vmem, sem = pltpu.VMEM, pltpu.SemaphoreType.DMA
    frames_shape, longer_shape = (T, H), (sz.K, H)
    matmul = 2 * T * H * H
    out_land, dx_land, dw_one, dw_two, small = pl.pallas_call(
        functools.partial(network, sz),
        out_shape=(
            jax.ShapeDtypeStruct((n, T, fb), bf16),
            jax.ShapeDtypeStruct((n, T, fb), bf16),
            jax.ShapeDtypeStruct((fb, H), f32),
            jax.ShapeDtypeStruct((fb, H), f32),
            jax.ShapeDtypeStruct((8, fb), f32),
        ),
        in_specs=[anywhere] * 4 + [whole] * 4,
        out_specs=(anywhere, anywhere, anywhere, anywhere, whole),
        scratch_shapes=[
            vmem((fb, sz.valid), bf16),
            vmem((2, T, sz.win), bf16),
            vmem((fb, fb), bf16),
            vmem(frames_shape, bf16),
            vmem(frames_shape, bf16),
            vmem(longer_shape, bf16),
            vmem(frames_shape, bf16),
            vmem(frames_shape, bf16),
            vmem(frames_shape, bf16),
            vmem(longer_shape, bf16),
            vmem(longer_shape, bf16),
            vmem((H, sz.K), bf16),
            vmem((H, sz.K), bf16),
            vmem((T + 8, H), f32),
            vmem((T + 8, H), f32),
            vmem((H, H), bf16),
            vmem((H, H), bf16),
            vmem((8 * Z, fb, qc), bf16),
            vmem((5 * Z, fb, qc), bf16),
            vmem((2, fb, qc), bf16),
            vmem((2, fb, qc), f32),
            vmem((8, H), f32),
            vmem((8, H), f32),
            vmem((16, H), f32),
            vmem((4, 8, H), f32),
            vmem((4, n, 8, fb), f32),
            vmem((4, 8, fb), f32),
            vmem((4, seqs, 8, fb), f32),
            vmem((4, n, 8, fb), f32),
            vmem((4, 8, H), f32),
            vmem((2, 8, H), f32),
            vmem((2, n, 8, fb), f32),
            vmem((2, 8, fb), f32),
            vmem((2, seqs, 8, fb), f32),
            sem((8,)),
            sem((n,)),
            sem((n,)),
            sem((4, n)),
            sem((4, n)),
            sem((2, 10 * Z)),
            sem((2, 10 * Z)),
            sem((8, n)),
            sem((8, n)),
            sem((4, seqs)),
            sem((4, seqs)),
            sem((2, 10 * Z)),
            sem((2, 10 * Z)),
            sem((2, 3)),
            sem((2, 3)),
            sem((2, n + seqs)),
            sem((2, n + seqs)),
        ],
        compiler_params=pltpu.CompilerParams(
            collective_id=0, has_side_effects=True, vmem_limit_bytes=63 * 1024 * 1024
        ),
        cost_estimate=pl.CostEstimate(
            flops=6 * matmul, bytes_accessed=16 * fb * H, transcendentals=6 * T * H
        ),
        name="network",
    )(inputs, out_grad, weight_one, weight_two, own_par, goes, count, aux)
    tok = inputs.shape[1]
    pairs = n // 2
    steps = pl.cdiv(tok, 2 * T)
    frames_spec = pl.BlockSpec((fb, 2 * T), lambda p: (0, p))
    land_spec = pl.BlockSpec((2, T, fb), lambda p: (jnp.minimum(p, pairs - 1), 0, 0))
    output, input_grad = pl.pallas_call(
        functools.partial(turn_back, sz),
        grid=(steps,),
        out_shape=(jax.ShapeDtypeStruct((fb, tok), f32),) * 2,
        in_specs=[frames_spec, frames_spec, land_spec, land_spec],
        out_specs=(frames_spec, frames_spec),
        compiler_params=pltpu.CompilerParams(vmem_limit_bytes=48 * 1024 * 1024),
        name="turn_back",
    )(inputs, out_grad, out_land, dx_land)
    return (
        output,
        input_grad,
        dw_one,
        small[0],
        small[1],
        small[2],
        dw_two,
        small[3],
        small[4],
        small[5],
    )


def frame_tables(lengths, frame_mask):
    positions = jnp.arange(frame_mask.shape[0], dtype=jnp.int32)
    offsets = jnp.cumsum(lengths[0]) - lengths[0]
    filled = jnp.sum(lengths[0])
    begins = jnp.any(positions[:, None] == offsets[None, :], axis=1)
    continues = jnp.where(begins, 0.0, 1.0).astype(jnp.float32)
    counted = jnp.where((positions < filled) & (frame_mask > 0), 1.0, 0.0).astype(jnp.float32)
    return (continues, counted)


def linear_scan(coef_rows, driving, backwards):
    row_count, length = driving.shape
    block_count = length // block_span
    factor = coef_rows.reshape(row_count, block_count, block_span)
    running = driving.reshape(row_count, block_count, block_span)
    places = jnp.arange(block_span, dtype=jnp.int32)
    step = 1
    while step < block_span:
        if backwards:
            mover = jnp.where(places[:, None] == places[None, :] + step, 1.0, 0.0).astype(
                jnp.float32
            )
            edge = jnp.where(places >= block_span - step, 1.0, 0.0).astype(jnp.float32)
        else:
            mover = jnp.where(places[:, None] == places[None, :] - step, 1.0, 0.0).astype(
                jnp.float32
            )
            edge = jnp.where(places < step, 1.0, 0.0).astype(jnp.float32)
        moved_factor = (
            jnp.dot(
                factor, mover, precision=lax.Precision.HIGHEST, preferred_element_type=jnp.float32
            )
            + edge
        )
        moved_running = jnp.dot(
            running, mover, precision=lax.Precision.HIGHEST, preferred_element_type=jnp.float32
        )
        running = factor * moved_running + running
        factor = factor * moved_factor
        step = step * 2
    end_place = 0 if backwards else block_span - 1
    total_factor = factor[:, :, end_place].T
    total_running = running[:, :, end_place].T

    def carry_step(carried, block_pair):
        return (block_pair[0] * carried + block_pair[1], carried)

    _, entering = lax.scan(
        carry_step,
        jnp.zeros((row_count,), jnp.float32),
        (total_factor, total_running),
        reverse=backwards,
    )
    result = running + factor * entering.T[:, :, None]
    return result.reshape(row_count, length)


def layer_forward(layer_input, weight, gain_row, bias_row, decay_rate, continues, counted):
    frames_in = lax.all_to_all(layer_input, "neur", split_axis=1, concat_axis=0, tiled=True)
    projected = jnp.dot(
        lax.all_gather(weight, "neur", axis=0, tiled=True),
        frames_in,
        preferred_element_type=jnp.float32,
    )
    neuron_proj = lax.all_to_all(
        projected.astype(jnp.bfloat16), "neur", split_axis=0, concat_axis=1, tiled=True
    ).astype(jnp.float32)
    sum_first = jnp.sum(counted[None, :] * neuron_proj, axis=1)
    sum_second = jnp.sum(counted[None, :] * neuron_proj * neuron_proj, axis=1)
    sum_first, sum_second, frames = lax.psum((sum_first, sum_second, jnp.sum(counted)), "seq")
    average = sum_first / frames
    inv_std = lax.rsqrt(sum_second / frames - average * average + epsilon)
    normed = (neuron_proj - average[:, None]) * inv_std[:, None]
    spread = jnp.sqrt(1.0 - decay_rate * decay_rate)
    states = linear_scan(
        decay_rate[:, None] * continues[None, :], (spread * gain_row)[:, None] * normed, False
    )
    layer_out = counted[None, :] * jax.nn.softplus(states + bias_row[:, None])
    return (layer_out, (frames_in, None, normed, inv_std, frames, states))


def layer_backward(
    upstream, weight, gain_row, bias_row, decay_rate, continues, counted, kept_state
):
    frames_in, full_weight, normed, inv_std, frames, states = kept_state
    local_grad = upstream * counted[None, :] * jax.nn.sigmoid(states + bias_row[:, None])
    following = jnp.concatenate([continues[1:], jnp.zeros((1,), jnp.float32)])
    coef_rows = decay_rate[:, None] * following[None, :]
    state_grad = linear_scan(coef_rows, local_grad, True)
    sum_rec, sum_rec_norm, sum_local = lax.psum(
        (
            jnp.sum(state_grad, axis=1),
            jnp.sum(state_grad * normed, axis=1),
            jnp.sum(local_grad, axis=1),
        ),
        "seq",
    )
    spread = jnp.sqrt(1.0 - decay_rate * decay_rate)
    gain_grad = spread * sum_rec_norm
    proj_grad = (spread * gain_row * inv_std)[:, None] * (
        state_grad - counted[None, :] * (sum_rec[:, None] + sum_rec_norm[:, None] * normed) / frames
    )
    driving = (spread * gain_row)[:, None] * normed
    decay_part = jnp.sum(state_grad * (states - driving), axis=1) / decay_rate
    grad_frames = lax.all_to_all(
        proj_grad.astype(jnp.bfloat16), "neur", split_axis=1, concat_axis=0, tiled=True
    )
    grad_rows = grad_frames
    input_frames = jnp.einsum(
        "ot,oi->it",
        grad_rows,
        lax.all_gather(weight, "neur", axis=0, tiled=True),
        preferred_element_type=jnp.float32,
    )
    input_grad = lax.all_to_all(
        input_frames.astype(jnp.bfloat16), "neur", split_axis=0, concat_axis=1, tiled=True
    ).astype(jnp.float32)
    grad_rows = grad_frames
    weight_rows = lax.psum_scatter(
        jnp.einsum("ot,it->oi", grad_rows, frames_in, preferred_element_type=jnp.float32),
        "neur",
        scatter_dimension=0,
        tiled=True,
    )
    weight_grad, decay_sum = lax.psum((weight_rows, decay_part), "seq")
    decay_grad = decay_sum - decay_rate / spread * gain_row * sum_rec_norm
    return (input_grad, weight_grad, gain_grad, sum_local, decay_grad)


def shards(
    inputs,
    weight_one,
    weight_two,
    gain_one,
    gain_two,
    bias_one,
    bias_two,
    decay_one,
    decay_two,
    lengths,
    frame_mask,
    out_grad,
):
    seqs, n = lax.axis_size("seq"), lax.axis_size("neur")
    H, (fb, tok) = weight_one.shape[1], inputs.shape
    if fits(n, seqs, H, fb, tok):
        params = (gain_one, gain_two, bias_one, bias_two, decay_one, decay_two)
        return frames_apart(
            Sizes(n, seqs, H, fb, tok),
            inputs,
            weight_one,
            weight_two,
            params,
            lengths,
            frame_mask,
            out_grad,
        )
    continues, counted = frame_tables(lengths, frame_mask)
    first_out, first_kept = layer_forward(
        inputs, weight_one, gain_one, bias_one, decay_one, continues, counted
    )
    second_out, second_kept = layer_forward(
        first_out.astype(jnp.bfloat16),
        weight_two,
        gain_two,
        bias_two,
        decay_two,
        continues,
        counted,
    )
    output = inputs.astype(jnp.float32) + second_out
    upstream = out_grad.astype(jnp.float32)
    middle_grad, weight_two_grad, gain_two_grad, bias_two_grad, decay_two_grad = layer_backward(
        upstream, weight_two, gain_two, bias_two, decay_two, continues, counted, second_kept
    )
    lower_grad, weight_one_grad, gain_one_grad, bias_one_grad, decay_one_grad = layer_backward(
        middle_grad, weight_one, gain_one, bias_one, decay_one, continues, counted, first_kept
    )
    return (
        output,
        upstream + lower_grad,
        weight_one_grad,
        gain_one_grad,
        bias_one_grad,
        decay_one_grad,
        weight_two_grad,
        gain_two_grad,
        bias_two_grad,
        decay_two_grad,
    )


def solution(mesh):
    placed = (
        P("neur", "seq"),
        P("neur", None),
        P("neur", None),
        P("neur"),
        P("neur"),
        P("neur"),
        P("neur"),
        P("neur"),
        P("neur"),
        P("seq", None),
        P("seq"),
        P("neur", "seq"),
    )
    return jax.shard_map(
        shards,
        mesh=mesh,
        in_specs=placed,
        out_specs=(
            P("neur", "seq"),
            P("neur", "seq"),
            P("neur", None),
            P("neur"),
            P("neur"),
            P("neur"),
            P("neur", None),
            P("neur"),
            P("neur"),
            P("neur"),
        ),
        check_vma=False,
    )
```

```python
import functools

import jax
import jax.numpy as jnp
from jax import lax
from jax.experimental import pallas as pl
from jax.experimental.pallas import tpu as pltpu
from jax.sharding import PartitionSpec as P

epsilon = 1e-05
block_span = 128
valid_frames = 3584
f32 = jnp.float32
bf16 = jnp.bfloat16
MESH = pl.DeviceIdType.MESH


def wide(tile, width):
    return jnp.concatenate([tile] * (width // 128), axis=1)


def at(index, size):
    if isinstance(index, int):
        return pl.ds(index * size, size)
    return pl.ds(pl.multiple_of(index * size, size), size)


def power(base, exponent):
    result = None
    while exponent:
        if exponent % 2:
            result = base if result is None else result * base
        exponent //= 2
        base = base * base
    return result


def log_of(rate):
    u = 1.0 - rate
    series = jnp.full_like(u, 1.0 / 8)
    for order in range(7, 0, -1):
        series = series * u + 1.0 / order
    return -u * series


GAIN, BIAS, DECAY = 0, 2, 4


class Sizes:
    def __init__(self, n, seqs, H, fb, tok_dev):
        self.n, self.seqs, self.H, self.fb, self.tok_dev = n, seqs, H, fb, tok_dev
        self.T = valid_frames // n
        self.steps = self.T // 8
        self.valid = valid_frames
        self.qc = H // seqs
        self.Z = n // 2
        self.odd = self.T % 128
        self.win = self.T + self.odd
        self.K = self.T + 16
        self.L = min(512, H)


def fits(n, seqs, H, fb, tok_dev):
    if n not in (4, 8) or valid_frames % n or seqs != 4 or fb * n != H or fb % 128 or H % 512:
        return False
    T = valid_frames // n
    return T % 64 == 0 and valid_frames % 128 == 0 and tok_dev >= valid_frames


class Line:
    def __init__(self, env, sends, recvs):
        self.env, self.sends, self.recvs = env, sends, recvs

    def copy(self, k, source, dest, target):
        return pltpu.make_async_remote_copy(
            src_ref=source,
            dst_ref=dest,
            send_sem=self.sends.at[k],
            recv_sem=self.recvs.at[k],
            device_id=target,
            device_id_type=MESH,
        )

    def arrived(self, k, ref):
        self.copy(k, ref, ref, self.env.across("x")).wait_recv()

    def sent(self, k, ref):
        self.copy(k, ref, ref, self.env.across("x")).wait_send()

    def along(self, dz):
        z, Z = self.env.z, self.env.sz.Z
        if dz == 0:
            return [(None, z, 0)]
        return [(z >= dz, z - dz, 1), (z + dz < Z, z + dz, -1)]


def if_so(condition, body):
    if condition is None:
        body()
    else:
        pl.when(condition)(body)


class Gather(Line):
    def __init__(self, env, source, full, sends, recvs, cut):
        super().__init__(env, sends, recvs)
        self.cut = cut
        self.full = full
        self.source = source.at[:, at(env.s, env.sz.qc)]

    def block(self, zz, fx, fy, fc=0):
        env = self.env
        rows = at(2 * zz + (env.x + fx) % 2, env.sz.fb)
        return self.full.at[rows, at(2 * ((env.y + fy) % 2) + (env.c + fc) % 2, env.sz.qc)]

    def half(self, ref, h):
        if h == 0:
            return ref.at[pl.ds(0, self.cut), :]
        return ref.at[pl.ds(self.cut, self.env.sz.fb - self.cut), :]

    def spread(self, zz, source):
        env, Z = self.env, self.env.sz.Z
        dest = self.block(zz, 0, 0)
        self.copy(2 * Z + zz, source, dest, env.across("x")).start()
        self.copy(3 * Z + zz, source, dest, env.across("y")).start()
        self.copy(6 * Z + zz, source, dest, env.across("core")).start()

    def pass_on(self, zz, source, way):
        env, Z = self.env, self.env.sz.Z
        dest = self.block(zz, 0, 0)

        def go():
            pltpu.make_async_remote_copy(
                src_ref=source,
                dst_ref=dest,
                send_sem=self.sends.at[zz if way > 0 else Z + zz],
                recv_sem=self.recvs.at[zz],
                device_id={"neur": 2 * (env.z + way) + env.x},
                device_id_type=MESH,
            ).start()

        pl.when(env.z < Z - 1 if way > 0 else env.z > 0)(go)

    def start(self):
        z = self.env.z
        self.pass_on(z, self.source, 1)
        self.pass_on(z, self.source, -1)
        self.spread(z, self.source)

    def line(self, dz):
        for condition, zz, way in self.along(dz):

            def one(zz=zz, way=way):
                block = self.block(zz, 0, 0)
                self.arrived(zz, block)
                self.pass_on(zz, block, way)
                self.spread(zz, block)

            if_so(condition, one)

    def sides(self, dz):
        env, Z = self.env, self.env.sz.Z
        for condition, zz, _ in self.along(dz):

            def one(zz=zz):
                block = self.block(zz, 1, 0)
                self.arrived(2 * Z + zz, block)
                part = self.half(block, 1)
                self.copy(5 * Z + zz, part, part, env.across("y")).start()
                self.copy(7 * Z + zz, block, block, env.across("core")).start()
                block = self.block(zz, 0, 1)
                self.arrived(3 * Z + zz, block)
                part = self.half(block, 0)
                self.copy(4 * Z + zz, part, part, env.across("x")).start()
                self.copy(8 * Z + zz, block, block, env.across("core")).start()

            if_so(condition, one)

    def diagonals(self):
        env, Z = self.env, self.env.sz.Z
        for dz in range(Z):
            for condition, zz, _ in self.along(dz):

                def one(zz=zz):
                    block = self.block(zz, 1, 1)
                    self.arrived(4 * Z + zz, self.half(block, 0))
                    self.arrived(5 * Z + zz, self.half(block, 1))
                    self.copy(9 * Z + zz, block, block, env.across("core")).start()

                if_so(condition, one)

    def cores(self):
        Z = self.env.sz.Z
        for k, (fx, fy) in enumerate(((0, 0), (1, 0), (0, 1), (1, 1))):
            for zz in range(Z):
                self.arrived((6 + k) * Z + zz, self.block(zz, fx, fy, 1))

    def drain(self):
        env, Z = self.env, self.env.sz.Z
        block = self.block(0, 0, 0)
        for zz in range(Z):
            pl.when((zz <= env.z) & (env.z < Z - 1))(lambda zz=zz: self.sent(zz, block))
            pl.when((zz >= env.z) & (env.z > 0))(lambda zz=zz: self.sent(Z + zz, block))
            for k in (2, 3, 6, 7, 8, 9):
                self.sent(k * Z + zz, block)
            self.sent(4 * Z + zz, self.half(block, 0))
            self.sent(5 * Z + zz, self.half(block, 1))


class Reduce(Line):
    kinds = ((1, 1), (1, 0), (0, 1), (0, 0))

    def __init__(self, env, grads, frames, land, spare, stage, held, total, sends, recvs, cut):
        super().__init__(env, sends, recvs)
        self.cut, self.held = cut, held
        self.grads, self.frames, self.land, self.spare = grads, frames, land, spare
        self.stage, self.total = stage, total

    def product(self, kind, zz, fc=0):
        env, sz = self.env, self.env.sz
        fx, fy = self.kinds[kind]
        rows = at(2 * zz + (env.x + fx) % 2, sz.fb)
        columns = at(2 * ((env.y + fy) % 2) + (env.c + fc) % 2, sz.qc)
        return jnp.dot(
            self.grads[rows, :], self.frames[:, columns], preferred_element_type=f32
        )

    def half(self, ref, h):
        if h == 0:
            return ref.at[pl.ds(0, self.cut), :]
        return ref.at[pl.ds(self.cut, self.env.sz.fb - self.cut), :]

    def landed(self, k, slot):
        self.arrived(k, self.land(slot))
        return self.land(slot)[...].astype(f32)

    def turn(self, i):
        z, Z = self.env.z, self.env.sz.Z
        low = jnp.where(i < Z - 1 - z, Z - 1 - i, i - (Z - 1 - z))
        high = jnp.where(i < z, i, Z - 1 - (i - z))
        return jnp.where(i == Z - 1, z, jnp.where(z < Z // 2, low, high))

    def cores(self, kind):
        env, Z = self.env, self.env.sz.Z

        def one(i, _):
            zz = self.turn(i)
            k = kind * Z + zz
            held = (kind % 2) * Z + zz
            if kind >= 2:
                self.sent(k - 2 * Z, self.stage.at[held])
            self.stage[held] = self.product(kind, zz, 1).astype(bf16)
            self.copy(k, self.stage.at[held], self.land(k), env.across("core")).start()
            return 0

        lax.fori_loop(0, Z, one, 0)

    def diagonals(self):
        env, Z = self.env, self.env.sz.Z

        def one(i, _):
            zz = self.turn(i)
            held = self.held(zz)
            held[...] = (self.product(0, zz) + self.landed(zz, zz)).astype(bf16)
            slot = self.land(4 * Z + zz)
            for k, h, axis in ((4, 0, "x"), (5, 1, "y")):
                self.copy(
                    k * Z + zz, self.half(held, h), self.half(slot, h), env.across(axis)
                ).start()
            return 0

        lax.fori_loop(0, Z, one, 0)

    def sides(self, low=0, high=None):
        env, Z = self.env, self.env.sz.Z
        spans = slice(0, self.cut), slice(self.cut, env.sz.fb)

        def one(i, _):
            zz = self.turn(i)
            slot = self.land(4 * Z + zz)
            for kind, h, wait, k, axis in ((1, 1, 5, 6, "x"), (2, 0, 4, 7, "y")):
                tile = self.product(kind, zz) + self.landed(kind * Z + zz, kind * Z + zz)
                part = self.half(slot, h)
                self.arrived(wait * Z + zz, part)
                held = self.stage.at[(2 + kind) * Z + zz]
                other = 1 - h
                summed = tile[spans[h], :] + part[...].astype(f32)
                self.half(held, h)[...] = summed.astype(bf16)
                self.half(held, other)[...] = tile[spans[other], :].astype(bf16)
                self.copy(
                    k * Z + zz, held, self.land((4 + kind) * Z + zz), env.across(axis)
                ).start()
            return 0

        lax.fori_loop(low, Z if high is None else high, one, 0)

    def joined(self, zz):
        Z = self.env.sz.Z
        tile = self.product(3, zz) + self.landed(3 * Z + zz, 3 * Z + zz)
        tile = tile + self.landed(6 * Z + zz, 5 * Z + zz)
        self.total[...] = tile + self.landed(7 * Z + zz, 6 * Z + zz)

    def lines(self, low=0, high=None):
        env, Z, z = self.env, self.env.sz.Z, self.env.z
        def onward(zz, way):
            k, slot = (8 if way > 0 else 9) * Z + zz, 7 * Z + zz
            self.joined(zz)

            @pl.when(z > 0 if way > 0 else z < Z - 1)
            def _():
                self.total[...] += self.landed(k, slot)

            held = self.held(zz)
            self.sent(4 * Z + zz, self.half(held, 0))
            self.sent(5 * Z + zz, self.half(held, 1))
            held[...] = self.total[...].astype(bf16)
            target = {"neur": 2 * (z + way) + env.x}
            if way > 0:
                self.copy(k, held, self.land(slot), target).start()
            else:
                pl.when(zz == z - 1)(lambda: self.copy(k, held, self.spare, target).start())
                pl.when(zz != z - 1)(lambda: self.copy(k, held, self.land(slot), target).start())

        for i in range(low, Z - 1 if high is None else high):
            zz = self.turn(i)
            pl.when(zz > z)(functools.partial(onward, zz, 1))
            pl.when(zz < z)(functools.partial(onward, zz, -1))

    def finish(self):
        Z, z = self.env.sz.Z, self.env.z
        self.joined(z)
        @pl.when(z > 0)
        def _():
            self.total[...] += self.landed(8 * Z + z, 7 * Z + z)

        @pl.when(z < Z - 1)
        def _():
            self.arrived(9 * Z + z, self.spare)
            self.total[...] += self.spare[...].astype(f32)

    def drain_cores(self):
        for k in range(2 * self.env.sz.Z, 4 * self.env.sz.Z):
            self.sent(k, self.stage.at[0])

    def drain_sides(self):
        for k in range(6 * self.env.sz.Z, 8 * self.env.sz.Z):
            self.sent(k, self.stage.at[0])

    def drain(self):
        Z, z = self.env.sz.Z, self.env.z
        held = self.stage.at[0]
        for zz in range(Z):
            for k in (4, 5):
                pl.when(zz == z)(
                    lambda k=k, zz=zz: self.sent(k * Z + zz, self.half(held, k - 4))
                )
            pl.when(zz > z)(lambda zz=zz: self.sent(8 * Z + zz, held))
            pl.when(zz < z)(lambda zz=zz: self.sent(9 * Z + zz, held))


class Result:
    def __init__(self, env, whole, block, sends, recvs, local):
        self.env, self.whole, self.block = env, whole, block
        self.sends, self.recvs, self.local = sends, recvs, local

    def part(self, flip_y, flip_c):
        env = self.env
        s = 2 * ((env.y + flip_y) % 2) + (env.c + flip_c) % 2
        return self.whole.at[:, at(s, env.sz.qc)]

    def copy(self, k, source, dest, target):
        return pltpu.make_async_remote_copy(
            src_ref=source,
            dst_ref=dest,
            send_sem=self.sends.at[k],
            recv_sem=self.recvs.at[k],
            device_id=target,
            device_id_type=MESH,
        )

    def start(self):
        env, own = self.env, self.part(0, 0)
        self.copy(0, self.block, own, env.across("y")).start()
        self.copy(1, self.block, own, env.across("core")).start()
        pltpu.make_async_copy(self.block, own, self.local).start()

    def finish(self):
        env = self.env
        other = self.part(1, 0)
        self.copy(0, self.block, other, env.across("y")).wait_recv()
        forward = self.copy(2, other, other, env.across("core"))
        forward.start()
        own = self.part(0, 0)
        pltpu.make_async_copy(self.block, own, self.local).wait()
        self.copy(0, self.block, own, env.across("y")).wait_send()
        self.copy(1, self.block, self.part(0, 1), env.across("core")).wait()
        forward.wait_send()
        self.copy(2, other, self.part(1, 1), env.across("core")).wait_recv()


class Env:
    def across(self, axis):
        if axis == "x":
            return {"neur": 2 * self.z + 1 - self.x}
        if axis == "y":
            return {"seq": 2 * (1 - self.y) + self.c}
        return {"seq": 2 * self.y + 1 - self.c}


def network(
    sz,
    x_hbm,
    g_hbm,
    w_one,
    w_two,
    gain_one,
    gain_two,
    bias_one,
    bias_two,
    decay_one,
    decay_two,
    lengths,
    frame_mask,
    out_land,
    dx_land,
    dw_one,
    dw_two,
    small,
    own_par,
    cont,
    counted,
    aux,
    raw,
    perm,
    eye,
    xs,
    gs,
    xr,
    gr,
    p_one,
    p_two,
    x_two,
    dp,
    dpt_one,
    dpt_two,
    s_one,
    s_two,
    wf_one,
    wf_two,
    land,
    stage,
    spare,
    fin,
    par,
    ends,
    work,
    pay,
    arrive,
    seqpay,
    seqland,
    back,
    backland,
    sumpay,
    sumland,
    sumseq,
    sumseqland,
    local_sems,
    par_sends,
    par_recvs,
    frame_sends,
    frame_recvs,
    gather_sends,
    gather_recvs,
    hop_sends,
    hop_recvs,
    seq_sends,
    seq_recvs,
    reduce_sends,
    reduce_recvs,
    final_sends,
    final_recvs,
    sum_sends,
    sum_recvs,
):
    n, seqs, H, fb, T, steps, L = sz.n, sz.seqs, sz.H, sz.fb, sz.T, sz.steps, sz.L
    env = Env()
    env.sz = sz
    me = lax.axis_index("neur")
    mine = lax.axis_index("seq")
    env.j, env.s = me, mine
    env.z, env.x, env.y, env.c = me // 2, me % 2, mine // 2, mine % 2

    barrier = pltpu.get_barrier_semaphore()
    for o in range(1, n):
        pl.semaphore_signal(
            barrier, inc=1, device_id={"neur": (me + o) % n}, device_id_type=MESH
        )
    for o in range(1, seqs):
        pl.semaphore_signal(
            barrier, inc=1, device_id={"seq": (mine + o) % seqs}, device_id_type=MESH
        )
    load_x = pltpu.make_async_copy(x_hbm.at[:, pl.ds(0, sz.valid)], raw, local_sems.at[0])
    load_x.start()
    for r, values in enumerate((gain_one, gain_two, bias_one, bias_two, decay_one, decay_two)):
        own_par[r : r + 1, :] = values[...]
    own_par[6:8, :] = jnp.zeros((2, fb), f32)
    pl.semaphore_wait(barrier, n - 1 + seqs - 1)

    def neur_copy(source, dest, send, recv, i):
        return pltpu.make_async_remote_copy(
            src_ref=source,
            dst_ref=dest,
            send_sem=send,
            recv_sem=recv,
            device_id={"neur": i},
            device_id_type=MESH,
        )

    def seq_copy(source, dest, send, recv, i):
        return pltpu.make_async_remote_copy(
            src_ref=source,
            dst_ref=dest,
            send_sem=send,
            recv_sem=recv,
            device_id={"seq": i},
            device_id_type=MESH,
        )

    def part(body, low, high):
        def one(o, _):
            body((me + o) % n)
            return 0

        lax.fori_loop(low, high, one, 0)

    def straight(body):
        lax.fori_loop(1, n // 2, lambda o, _: (body((me + 2 * o) % n), 0)[1], 0)

    def crossing(body):
        lax.fori_loop(0, n // 2, lambda o, _: (body((me + 2 * o + 1) % n), 0)[1], 0)

    def others(body, count=n, own=me):
        def one(o, _):
            body((own + o) % count)
            return 0

        lax.fori_loop(1, count, one, 0)

    own_lanes = at(me, fb)

    def par_copy(i):
        return neur_copy(own_par, par.at[:, own_lanes], par_sends.at[i], par_recvs.at[me], i)

    def par_wait(i):
        neur_copy(own_par, par.at[:, at(i, fb)], par_sends.at[i], par_recvs.at[i], i).wait()

    others(lambda i: par_copy(i).start())
    par[:, own_lanes] = own_par[...]

    cuts = (fb // 4, fb // 4)
    gather_one = Gather(env, w_one, wf_one, gather_sends.at[0], gather_recvs.at[0], cuts[0])
    gather_two = Gather(env, w_two, wf_two, gather_sends.at[1], gather_recvs.at[1], cuts[1])
    own_one = pltpu.make_async_copy(gather_one.source, gather_one.block(env.z, 0, 0), local_sems.at[2])
    own_two = pltpu.make_async_copy(gather_two.source, gather_two.block(env.z, 0, 0), local_sems.at[3])
    own_one.start()
    own_two.start()
    gather_one.start()
    gather_two.start()

    row = lax.broadcasted_iota(jnp.int32, (T, sz.win), 0)
    column = lax.broadcasted_iota(jnp.int32, (T, sz.win), 1)
    frame = (row & 7) * steps + (row >> 3)
    perm[0] = jnp.where(column == frame, 1.0, 0.0).astype(bf16)
    perm[1] = jnp.where(column == frame + sz.odd, 1.0, 0.0).astype(bf16)
    row = lax.broadcasted_iota(jnp.int32, (fb, fb), 0)
    column = lax.broadcasted_iota(jnp.int32, (fb, fb), 1)
    eye[...] = jnp.where(row == column, 1.0, 0.0).astype(bf16)

    def window(i):
        start = (i // 2) * (2 * T) + (i % 2) * (T - sz.odd)
        return pl.ds(pl.multiple_of(start, 128), sz.win)

    def turned(i):
        return lax.dot_general(
            perm[i % 2], raw[:, window(i)], (((1,), (1,)), ((), ())), preferred_element_type=f32
        ).astype(bf16)

    def frames_copy(a, source, dest, i):
        return neur_copy(source, dest, frame_sends.at[a, i], frame_recvs.at[a, me], i)

    def frames_wait(a, ref, i):
        part = ref.at[pl.ds(0, T), at(i, fb)]
        neur_copy(part, part, frame_sends.at[a, i], frame_recvs.at[a, i], i).wait_recv()

    def frames_sent(a, ref, i):
        part = ref.at[pl.ds(0, T), at(i, fb)]
        neur_copy(part, part, frame_sends.at[a, i], frame_recvs.at[a, i], i).wait_send()

    load_x.wait()

    def turn_x(i):
        xs[:, at(i, fb)] = turned(i)

    def send_x(i):
        frames_copy(0, xs.at[:, at(i, fb)], xr.at[pl.ds(0, T), own_lanes], i).start()

    def send_all_x():
        others(send_x)

    others(turn_x)
    xr[0:T, own_lanes] = turned(me)
    load_g = pltpu.make_async_copy(g_hbm.at[:, pl.ds(0, sz.valid)], raw, local_sems.at[1])
    load_g.start()
    ends_of_line = (env.z == 0) | (env.z == sz.Z - 1)
    pl.when(ends_of_line)(send_all_x)
    for dz in range(1, sz.Z):
        gather_one.line(dz)
        gather_two.line(dz)
        if dz == max(1, sz.Z - 2):
            pl.when(jnp.logical_not(ends_of_line))(send_all_x)
        gather_one.sides(dz - 1)
    frame_tables_of(sz, me, lengths, frame_mask, perm, window(me), cont, counted, aux)
    load_g.wait()

    g_first, g_second = max(2, n - 3), max(2, n - 1)

    def turn_g(i):
        gs[:, at(i, fb)] = turned(i)

    def send_g(i):
        frames_copy(1, gs.at[:, at(i, fb)], gr.at[:, own_lanes], i).start()

    others(turn_g)
    gr[:, own_lanes] = turned(me)
    gather_one.sides(sz.Z - 1)
    part(send_g, 1, g_first)
    gather_one.diagonals()
    for dz in range(sz.Z - 1):
        gather_two.sides(dz)
    gather_one.cores()
    own_one.wait()
    own_two.wait()
    others(lambda i: frames_wait(0, xr, i))
    others(par_wait)

    def blocks(body):
        def one(b, _):
            body(at(b, L))
            return 0

        lax.fori_loop(0, H // L, one, 0)

    def project(frames, weight, result):
        def one(b, _):
            result[:, at(b, fb)] = lax.dot_general(
                frames[0:T, :],
                weight[at(b, fb), :],
                (((1,), (1,)), ((), ())),
                preferred_element_type=f32,
            ).astype(bf16)
            return 0

        lax.fori_loop(0, n, one, 0)

    def flags(t):
        tile = pl.ds(pl.multiple_of(8 * t, 8), 8)
        return wide(cont[tile, :], L), wide(counted[tile, :], L)

    def spread8(ref, r, cols, width=L):
        return jnp.broadcast_to(ref[r : r + 1, cols], (8, width))

    zero = jnp.zeros((8, L), f32)

    def down(value):
        return jnp.sum(value, axis=0, keepdims=True)

    def exchange(e, gathered, totalled, gap):
        def out_copy(i):
            return neur_copy(
                pay.at[e, :, at(i, fb)],
                arrive.at[e, me],
                hop_sends.at[2 * e, i],
                hop_recvs.at[2 * e, me],
                i,
            )

        others(lambda i: out_copy(i).start())
        arrive[e, me] = pay[e, :, own_lanes]
        gap("hop_a")

        def out_wait(i):
            neur_copy(
                pay.at[e, :, at(i, fb)],
                arrive.at[e, i],
                hop_sends.at[2 * e, i],
                hop_recvs.at[2 * e, i],
                i,
            ).wait()

        others(out_wait)
        gathered()

        def along_copy(i):
            return seq_copy(
                seqpay.at[e],
                seqland.at[e, mine],
                seq_sends.at[e, i],
                seq_recvs.at[e, mine],
                i,
            )

        def along_wait(i):
            seq_copy(
                seqpay.at[e], seqland.at[e, i], seq_sends.at[e, i], seq_recvs.at[e, i], i
            ).wait()

        others(lambda i: along_copy(i).start(), seqs, mine)
        seqland[e, mine] = seqpay[e]
        gap("hop_b")
        others(along_wait, seqs, mine)
        sums = seqland[e, 0]
        for i in range(1, seqs):
            sums = sums + seqland[e, i]
        totalled(sums)

        def back_copy(i):
            return neur_copy(
                back.at[e, i],
                backland.at[e, :, own_lanes],
                hop_sends.at[2 * e + 1, i],
                hop_recvs.at[2 * e + 1, me],
                i,
            )

        def back_wait(i):
            neur_copy(
                back.at[e, i],
                backland.at[e, :, at(i, fb)],
                hop_sends.at[2 * e + 1, i],
                hop_recvs.at[2 * e + 1, i],
                i,
            ).wait()

        others(lambda i: back_copy(i).start())
        backland[e, :, own_lanes] = back[e, me]
        gap("hop_c")
        others(back_wait)

    def layer_forward(layer, frames, weight, projected, states, store, gap):
        e = layer
        decay_row, gain_row, bias_row = DECAY + layer, GAIN + layer, BIAS + layer
        project(frames, weight, projected)
        gap("ends")

        def local_ends(cols):
            decay = spread8(par, decay_row, cols)

            def step(i, carry):
                state, first, second, inward = carry
                pair = projected[pl.ds(pl.multiple_of(16 * i, 16), 16), cols].astype(f32)
                for h in range(2):
                    value = pair[8 * h : 8 * h + 8, :]
                    goes, count = flags(2 * i + h)
                    state = (decay * goes) * state + value
                    held = count * value
                    first = first + held
                    second = second + held * value
                ins = frames[pl.ds(pl.multiple_of(16 * i, 16), 16), cols].astype(f32)
                return state, first, second, inward + ins[0:8, :] + ins[8:16, :]

            state, first, second, inward = lax.fori_loop(
                0, T // 16, step, (zero, zero, zero, zero)
            )
            ends[:, cols] = state
            pay[e, 1:2, cols] = down(first)
            pay[e, 2:3, cols] = down(second)
            pay[e, 3:4, cols] = down(inward)

        blocks(local_ends)
        run_power = power(par[decay_row : decay_row + 1, :], steps)
        total = jnp.zeros((1, H), f32)
        for k in range(8):
            total = run_power * wide(aux[16 + k : 17 + k, :], H) * total + ends[k : k + 1, :]
        pay[e, 0:1, :] = total
        pay[e, 4:8, :] = jnp.zeros((4, H), f32)

        own_decay = own_par[decay_row : decay_row + 1, :]

        def gathered():
            whole_power = power(own_decay, T)
            carried = jnp.zeros((1, fb), f32)
            sums = jnp.zeros((8, fb), f32)
            for i in range(n):
                rows = arrive[e, i]
                back[e, i, 0:1, :] = carried
                carried = whole_power * wide(aux[8 + i : 9 + i, :], fb) * carried + rows[0:1, :]
                sums = sums + rows
            seqpay[e] = sums
            seqpay[e, 0:1, :] = wide(aux[24:25, :], fb)

        def totalled(sums):
            frames_all = sums[0:1, :]
            average = sums[1:2, :] / frames_all
            inv_std = lax.rsqrt(sums[2:3, :] / frames_all - average * average + epsilon)
            centre = sums[3:4, :] / (sz.valid * seqs)
            for i in range(n):
                back[e, i, 1:2, :] = average
                back[e, i, 2:3, :] = inv_std
                back[e, i, 3:4, :] = frames_all
                back[e, i, 4:5, :] = centre
                back[e, i, 5:8, :] = jnp.zeros((3, fb), f32)

        exchange(e, gathered, totalled, gap)
        centre = backland[e, 4:5, :]
        frames[T : T + 16, :] = jnp.concatenate(
            [-centre, -centre, -centre, jnp.zeros((13, H), f32)], axis=0
        ).astype(bf16)

        total = backland[e, 0:1, :]
        for k in range(8):
            work[k : k + 1, :] = total
            total = run_power * wide(aux[16 + k : 17 + k, :], H) * total + ends[k : k + 1, :]

        gap("scan")

        def full_scan(cols):
            decay = spread8(par, decay_row, cols)
            average = spread8(backland.at[e], 1, cols)
            inv_std = spread8(backland.at[e], 2, cols)
            bias = spread8(par, bias_row, cols)
            scale = jnp.sqrt(1.0 - decay * decay) * spread8(par, gain_row, cols) * inv_std
            ones = (1.0 - jnp.exp(wide(aux[0:8, :], L) * log_of(decay))) / (1.0 - decay)
            state = scale * (work[0:8, cols] - average * ones)
            states[0:8, cols] = state

            def step(i, state):
                pair = projected[pl.ds(pl.multiple_of(16 * i, 16), 16), cols].astype(f32)
                outs = []
                for h in range(2):
                    goes, count = flags(2 * i + h)
                    state = (decay * goes) * state + scale * (pair[8 * h : 8 * h + 8, :] - average)
                    states[pl.ds(pl.multiple_of(16 * i + 8 * h + 8, 8), 8), cols] = state
                    v = state + bias
                    soft = jnp.maximum(v, 0.0) + jnp.log(1.0 + jnp.exp(-jnp.abs(v)))
                    outs.append(count * soft)
                store[pl.ds(pl.multiple_of(16 * i, 16), 16), cols] = jnp.concatenate(
                    outs, axis=0
                ).astype(bf16)
                return state

            lax.fori_loop(0, T // 16, step, state)

        blocks(full_scan)

    def layer_backward(layer, upstream, projected, states, turned_grads, gap):
        e = 2 + (1 - layer)
        decay_row, gain_row, bias_row = DECAY + layer, GAIN + layer, BIAS + layer
        run_power = power(par[decay_row : decay_row + 1, :], steps)

        def local_ends(cols):
            decay = spread8(par, decay_row, cols)
            average = spread8(backland.at[layer], 1, cols)
            inv_std = spread8(backland.at[layer], 2, cols)
            bias = spread8(par, bias_row, cols)

            def step(o, carry):
                i = T // 16 - 1 - o
                rows = pl.ds(pl.multiple_of(16 * i, 16), 16)
                pair = projected[rows, cols].astype(f32)
                ups = upstream[rows, cols].astype(f32)
                for h in (1, 0):
                    run, reach, U, V, UN, VN, B, D, DA = carry
                    goes, count = flags(2 * i + h)
                    here = pl.ds(pl.multiple_of(16 * i + 8 * h + 8, 8), 8)
                    state = states[here, cols]
                    before = states[pl.ds(pl.multiple_of(16 * i + 8 * h, 8), 8), cols]
                    local = ups[8 * h : 8 * h + 8, :] * count / (1.0 + jnp.exp(-(state + bias)))
                    states[here, cols] = local
                    normed = (pair[8 * h : 8 * h + 8, :] - average) * inv_std
                    run = local + run
                    kept = goes * before
                    link = decay * goes
                    carry = (
                        link * run,
                        link * reach,
                        U + run,
                        V + reach,
                        UN + run * normed,
                        VN + reach * normed,
                        B + local,
                        D + run * kept,
                        DA + reach * kept,
                    )
                return carry

            one = jnp.ones((8, L), f32)
            run, _, U, V, UN, VN, B, D, DA = lax.fori_loop(
                0, T // 16, step, (zero, one, zero, zero, zero, zero, zero, zero, zero)
            )
            ends[:, cols] = run
            decay_run = power(par[decay_row : decay_row + 1, cols], steps)
            part, factor = jnp.zeros((1, L), f32), jnp.ones((1, L), f32)
            for k in range(7, -1, -1):
                work[k : k + 1, cols] = part
                work[8 + k : 9 + k, cols] = factor
                through = decay_run * wide(aux[16 + k : 17 + k, :], L)
                part = through * part + ends[k : k + 1, cols]
                factor = through * factor
            pay[e, 0:1, cols] = part
            entering, scaled = work[0:8, cols], work[8:16, cols]
            pay[e, 1:2, cols] = down(U + V * entering)
            pay[e, 2:3, cols] = down(V * scaled)
            pay[e, 3:4, cols] = down(UN + VN * entering)
            pay[e, 4:5, cols] = down(VN * scaled)
            pay[e, 5:6, cols] = down(B)
            pay[e, 6:7, cols] = down(D + DA * entering)
            pay[e, 7:8, cols] = down(DA * scaled)

        blocks(local_ends)
        own_decay = own_par[decay_row : decay_row + 1, :]
        own_gain = own_par[gain_row : gain_row + 1, :]

        def gathered():
            whole_power = power(own_decay, T)
            carried = jnp.zeros((1, fb), f32)
            sums = [jnp.zeros((1, fb), f32)] * 4
            for i in range(n - 1, -1, -1):
                rows = arrive[e, i]
                back[e, i, 0:1, :] = carried
                for a, (plain, times) in enumerate(((1, 2), (3, 4), (5, None), (6, 7))):
                    term = rows[plain : plain + 1, :]
                    if times is not None:
                        term = term + rows[times : times + 1, :] * carried
                    sums[a] = sums[a] + term
                carried = whole_power * wide(aux[8 + i : 9 + i, :], fb) * carried + rows[0:1, :]
            for a in range(4):
                seqpay[e, a : a + 1, :] = sums[a]
            seqpay[e, 4:8, :] = jnp.zeros((4, fb), f32)

        def totalled(sums):
            rec, rec_norm = sums[0:1, :], sums[1:2, :]
            for i in range(n):
                back[e, i, 1:2, :] = rec
                back[e, i, 2:3, :] = rec_norm
                back[e, i, 3:8, :] = jnp.zeros((5, fb), f32)
            spread = jnp.sqrt(1.0 - own_decay * own_decay)
            small[3 * layer : 3 * layer + 1, :] = spread * rec_norm
            small[3 * layer + 1 : 3 * layer + 2, :] = sums[2:3, :]
            small[3 * layer + 2 : 3 * layer + 3, :] = (
                sums[3:4, :] - own_decay / spread * own_gain * rec_norm
            )

        exchange(e, gathered, totalled, gap)
        gap("scan")
        total = backland[e, 0:1, :]
        for k in range(7, -1, -1):
            work[k : k + 1, :] = total
            total = run_power * wide(aux[16 + k : 17 + k, :], H) * total + ends[k : k + 1, :]

        def full_scan(cols):
            decay = spread8(par, decay_row, cols)
            average = spread8(backland.at[layer], 1, cols)
            inv_std = spread8(backland.at[layer], 2, cols)
            frames_all = spread8(backland.at[layer], 3, cols)
            scale = jnp.sqrt(1.0 - decay * decay) * spread8(par, gain_row, cols) * inv_std
            rec = spread8(backland.at[e], 1, cols) / frames_all
            rec_norm = spread8(backland.at[e], 2, cols) / frames_all * inv_std

            def step(o, carry):
                carry, added = carry
                i = T // 16 - 1 - o
                rows = pl.ds(pl.multiple_of(16 * i, 16), 16)
                pair = projected[rows, cols].astype(f32)
                outs = [None, None]
                for h in (1, 0):
                    goes, count = flags(2 * i + h)
                    here = pl.ds(pl.multiple_of(16 * i + 8 * h + 8, 8), 8)
                    run = states[here, cols] + carry
                    centred = pair[8 * h : 8 * h + 8, :] - average
                    outs[h] = scale * (run - count * (rec + rec_norm * centred))
                    carry = (decay * goes) * run
                rounded = jnp.concatenate(outs, axis=0).astype(bf16)
                dp[rows, cols] = rounded
                rounded = rounded.astype(f32)
                return carry, added + rounded[0:8, :] + rounded[8:16, :]

            _, added = lax.fori_loop(0, T // 16, step, (work[0:8, cols], zero))
            whole = down(added)
            sumpay[layer, 0:1, cols] = whole
            high = whole.astype(bf16).astype(f32)
            middle = (whole - high).astype(bf16).astype(f32)
            low = whole - high - middle
            dp[T : T + 16, cols] = jnp.concatenate(
                [high, middle, low, jnp.zeros((13, L), f32)], axis=0
            ).astype(bf16)

        blocks(full_scan)
        sumpay[layer, 1:8, :] = jnp.zeros((7, H), f32)

        def turn(b, _):
            turned_grads[at(b, fb), :] = lax.dot_general(
                eye[...], dp[:, at(b, fb)], (((1,), (1,)), ((), ())), preferred_element_type=f32
            ).astype(bf16)
            return 0

        lax.fori_loop(0, n, turn, 0)

    def input_gradient(weight, result, i):
        result[:, at(i, fb)] = jnp.dot(
            dp[0:T, :], weight[:, at(i, fb)], preferred_element_type=f32
        ).astype(bf16)

    def sum_copy(layer, i):
        return neur_copy(
            sumpay.at[layer, :, at(i, fb)],
            sumland.at[layer, me],
            sum_sends.at[layer, i],
            sum_recvs.at[layer, me],
            i,
        )

    def sum_along(layer, i):
        return seq_copy(
            sumseq.at[layer],
            sumseqland.at[layer, mine],
            sum_sends.at[layer, n + i],
            sum_recvs.at[layer, n + mine],
            i,
        )

    def sum_start(layer):
        others(lambda i: sum_copy(layer, i).start())
        sumland[layer, me] = sumpay[layer, :, own_lanes]

    def sum_middle(layer):
        def wait(i):
            neur_copy(
                sumpay.at[layer, :, at(i, fb)],
                sumland.at[layer, i],
                sum_sends.at[layer, i],
                sum_recvs.at[layer, i],
                i,
            ).wait()

        others(wait)
        total = sumland[layer, 0]
        for i in range(1, n):
            total = total + sumland[layer, i]
        sumseq[layer] = total
        sumseqland[layer, mine] = total
        others(lambda i: sum_along(layer, i).start(), seqs, mine)

    def sum_finish(layer, frames, total):
        def wait(i):
            seq_copy(
                sumseq.at[layer],
                sumseqland.at[layer, i],
                sum_sends.at[layer, n + i],
                sum_recvs.at[layer, n + i],
                i,
            ).wait()

        others(wait, seqs, mine)
        whole = sumseqland[layer, 0]
        for i in range(1, seqs):
            whole = whole + sumseqland[layer, i]
        whole = whole[0:1, :]
        high = whole.astype(bf16).astype(f32)
        middle = (whole - high).astype(bf16).astype(f32)
        low = whole - high - middle
        rows = jnp.concatenate([high, middle, low, jnp.zeros((13, fb), f32)], axis=0).astype(bf16)
        columns = lax.dot_general(
            eye[...], rows, (((1,), (1,)), ((), ())), preferred_element_type=f32
        ).astype(bf16)
        total[...] -= jnp.dot(
            columns, frames[T : T + 16, at(mine, sz.qc)], preferred_element_type=f32
        )

    def place_out(a, ref, dest, i):
        return neur_copy(
            ref.at[:, at(i, fb)], dest.at[me], frame_sends.at[a, i], frame_recvs.at[a, me], i
        )

    def out_arrived(a, ref, dest, i):
        neur_copy(
            ref.at[:, at(i, fb)], dest.at[i], frame_sends.at[a, i], frame_recvs.at[a, i], i
        ).wait()

    def nothing(name):
        return None

    def during_one(name):
        if name == "ends":
            gather_two.sides(sz.Z - 1)
            gather_two.diagonals()
        if name == "scan":
            part(send_g, g_first, g_second)

    def during_two(name):
        if name == "scan":
            part(send_g, g_second, n)

    layer_forward(0, xr, wf_one, p_one, s_one, x_two, during_one)
    gather_two.cores()
    others(lambda i: frames_sent(0, xs, i))
    layer_forward(1, x_two, wf_two, p_two, s_two, xs, during_two)

    def send_out(low, high):
        part(lambda i: place_out(2, xs, out_land, i).start(), min(low, n), min(high, n))

    keep_out = pltpu.make_async_copy(xs.at[:, own_lanes], out_land.at[me], local_sems.at[4])
    keep_out.start()
    others(lambda i: frames_wait(1, gr, i))
    others(lambda i: frames_sent(1, gs, i))
    gather_two.drain()

    send_out(1, 2)
    layer_backward(
        1, gr, p_two, s_two, dpt_two, lambda name: send_out(2, 3) if name == "scan" else None
    )
    send_out(3, 4)
    lax.fori_loop(0, n, lambda i, _: (input_gradient(wf_two, gr, i), 0)[1], 0)
    sum_start(1)
    send_out(4, 5)
    reduce_two = Reduce(
        env,
        dpt_two,
        x_two,
        lambda k: land.at[k],
        spare.at[1],
        stage,
        lambda k: stage.at[2 * sz.Z + k],
        fin.at[1],
        reduce_sends.at[1],
        reduce_recvs.at[1],
        fb // 2,
    )
    reduce_one = Reduce(
        env,
        dpt_one,
        xr,
        lambda k: wf_two.at[at(k // seqs, fb), at(k % seqs, sz.qc)],
        spare.at[0],
        stage,
        lambda k: raw.at[:, at(k, sz.qc)],
        fin.at[0],
        reduce_sends.at[0],
        reduce_recvs.at[0],
        fb // 2,
    )
    result_two = Result(
        env, dw_two, fin.at[1], final_sends.at[1], final_recvs.at[1], local_sems.at[6]
    )
    result_one = Result(
        env, dw_one, fin.at[0], final_sends.at[0], final_recvs.at[0], local_sems.at[7]
    )
    for kind in range(4):
        reduce_two.cores(kind)
    send_out(5, 6)

    def meanwhile(name):
        if name == "hop_b":
            sum_middle(1)
        if name == "scan":
            reduce_two.diagonals()
            send_out(6, n)

    layer_backward(0, gr, p_one, s_one, dpt_one, meanwhile)
    reduce_two.drain_cores()
    reduce_one.cores(0)
    reduce_two.sides()
    reduce_one.diagonals()
    for kind in range(1, 4):
        reduce_one.cores(kind)
    sum_start(0)

    def send_dx(i):
        place_out(3, gs, dx_land, i).start()

    def make_dx(i):
        input_gradient(wf_one, gs, i)

    def make_and_send_dx(i):
        make_dx(i)
        send_dx(i)

    straight(make_and_send_dx)
    crossing(make_dx)
    make_dx(me)
    keep_dx = pltpu.make_async_copy(gs.at[:, own_lanes], dx_land.at[me], local_sems.at[5])
    keep_dx.start()
    reduce_two.lines()
    sum_middle(0)
    reduce_two.drain_sides()
    reduce_one.sides(0, 2)
    reduce_two.finish()
    sum_finish(1, x_two, fin.at[1])
    result_two.start()
    for i in range(2, sz.Z):
        reduce_one.lines(i - 2, i - 1)
        reduce_one.sides(i, i + 1)
    crossing(send_dx)
    reduce_one.lines(sz.Z - 2, sz.Z - 1)
    reduce_one.finish()
    sum_finish(0, xr, fin.at[0])
    result_one.start()
    result_two.finish()
    others(lambda i: out_arrived(2, xs, out_land, i))
    others(lambda i: out_arrived(3, gs, dx_land, i))
    keep_out.wait()
    keep_dx.wait()
    result_one.finish()
    reduce_two.drain()
    reduce_one.drain_cores()
    reduce_one.drain_sides()
    reduce_one.drain()
    gather_one.drain()
    small[6:8, :] = jnp.zeros((2, fb), f32)


def frame_tables_of(sz, me, lengths, frame_mask, perm, window, cont, counted, aux):
    T, steps = sz.T, sz.steps
    starts, filled = [], 0
    for k in range(lengths.shape[1]):
        starts.append(filled)
        filled = filled + lengths[0, k]
    row = lax.broadcasted_iota(jnp.int32, (T, 128), 0)
    slot = me * T + (row & 7) * steps + (row >> 3)
    goes = jnp.ones((T, 128), f32)
    for start in starts:
        goes = jnp.where(slot == start, 0.0, goes)
    cont[...] = goes
    kept = jnp.where(frame_mask[0:1, window] > 0, 1.0, 0.0)
    kept = jnp.broadcast_to(kept, (128, sz.win)).astype(bf16)
    kept = lax.dot_general(
        perm[me % 2], kept, (((1,), (1,)), ((), ())), preferred_element_type=f32
    )
    counted[...] = jnp.where(slot < filled, kept, 0.0)
    run = lax.broadcasted_iota(jnp.int32, (8, 128), 0)
    first = me * T + run * steps
    behind = jnp.zeros((8, 128), jnp.int32)
    whole, own = jnp.ones((8, 128), f32), jnp.ones((8, 128), f32)
    for start in starts:
        behind = jnp.where(first > start, jnp.maximum(behind, start), behind)
        whole = jnp.where((run * T <= start) & (start < run * T + T), 0.0, whole)
        own = jnp.where((first <= start) & (start < first + steps), 0.0, own)
    aux[0:8, :] = (first - behind).astype(f32)
    aux[8:16, :] = whole
    aux[16:24, :] = own
    place = lax.broadcasted_iota(jnp.int32, (1, sz.tok_dev), 1)
    block = jnp.where((place < filled) & (frame_mask[...] > 0), 1.0, 0.0)
    block = jnp.sum(block, axis=1, keepdims=True)
    aux[24:32, :] = jnp.broadcast_to(block, (8, 128))


def turn_back(
    sz,
    steps,
    x_ref,
    g_ref,
    out_ref,
    dx_ref,
    one_ref,
    two_ref,
    small,
    output,
    input_grad,
    dw_one,
    dw_two,
    gain_one,
    bias_one,
    decay_one,
    gain_two,
    bias_two,
    decay_two,
    perm,
    eye,
    held,
    sems,
):
    step = pl.program_id(0)
    T, fb, win, odd = sz.T, sz.fb, sz.win, sz.odd
    pairs = ((one_ref, dw_one), (two_ref, dw_two))
    reads = [pltpu.make_async_copy(a, held.at[k], sems.at[k]) for k, (a, _) in enumerate(pairs)]
    writes = [pltpu.make_async_copy(held.at[k], b, sems.at[k]) for k, (_, b) in enumerate(pairs)]

    @pl.when(step == 0)
    def _():
        for move in reads:
            move.start()
        row = lax.broadcasted_iota(jnp.int32, (T, win), 0)
        column = lax.broadcasted_iota(jnp.int32, (T, win), 1)
        frame = (row & 7) * sz.steps + (row >> 3)
        perm[0] = jnp.where(column == frame, 1.0, 0.0).astype(bf16)
        perm[1] = jnp.where(column == frame + odd, 1.0, 0.0).astype(bf16)
        row = lax.broadcasted_iota(jnp.int32, (fb, fb), 0)
        column = lax.broadcasted_iota(jnp.int32, (fb, fb), 1)
        eye[...] = jnp.where(row == column, 1.0, 0.0).astype(bf16)
        rows = (gain_one, bias_one, decay_one, gain_two, bias_two, decay_two)
        for r, ref in enumerate(rows):
            ref[...] = small[r : r + 1, :]

    output[...] = x_ref[...].astype(f32)
    input_grad[...] = g_ref[...].astype(f32)

    @pl.when(step < sz.n // 2)
    def _():
        for half in range(2):
            lanes = pl.ds((T - odd) * half, win)
            for source, result in ((out_ref, output), (dx_ref, input_grad)):
                turned = lax.dot_general(
                    eye[...], source[half], (((1,), (1,)), ((), ())), preferred_element_type=f32
                ).astype(bf16)
                result[:, lanes] += jnp.dot(turned, perm[half], preferred_element_type=f32)

    @pl.when(step == 1)
    def _():
        for read, write in zip(reads, writes, strict=True):
            read.wait()
            write.start()

    @pl.when(step == steps - 1)
    def _():
        for move in writes:
            move.wait()


def frames_apart(sz, inputs, weight_one, weight_two, params, lengths, frame_mask, out_grad):
    n, seqs, H, fb, T, Z, qc = sz.n, sz.seqs, sz.H, sz.fb, sz.T, sz.Z, sz.qc
    whole = pl.BlockSpec(memory_space=pltpu.VMEM)
    anywhere = pl.BlockSpec(memory_space=pl.ANY)
    vmem, sem = pltpu.VMEM, pltpu.SemaphoreType.DMA
    frames_shape, longer_shape = (T, H), (sz.K, H)
    matmul = 2 * T * H * H
    out_land, dx_land, dw_one, dw_two, small = pl.pallas_call(
        functools.partial(network, sz),
        out_shape=(
            jax.ShapeDtypeStruct((n, T, fb), bf16),
            jax.ShapeDtypeStruct((n, T, fb), bf16),
            jax.ShapeDtypeStruct((fb, H), f32),
            jax.ShapeDtypeStruct((fb, H), f32),
            jax.ShapeDtypeStruct((8, fb), f32),
        ),
        in_specs=[anywhere] * 4 + [whole] * 6 + [pl.BlockSpec(memory_space=pltpu.SMEM), whole],
        out_specs=(anywhere, anywhere, anywhere, anywhere, whole),
        scratch_shapes=[
            vmem((8, fb), f32),
            vmem((T, 128), f32),
            vmem((T, 128), f32),
            vmem((32, 128), f32),
            vmem((fb, sz.valid), bf16),
            vmem((2, T, sz.win), bf16),
            vmem((fb, fb), bf16),
            vmem(frames_shape, bf16),
            vmem(frames_shape, bf16),
            vmem(longer_shape, bf16),
            vmem(frames_shape, bf16),
            vmem(frames_shape, bf16),
            vmem(frames_shape, bf16),
            vmem(longer_shape, bf16),
            vmem(longer_shape, bf16),
            vmem((H, sz.K), bf16),
            vmem((H, sz.K), bf16),
            vmem((T + 8, H), f32),
            vmem((T + 8, H), f32),
            vmem((H, H), bf16),
            vmem((H, H), bf16),
            vmem((8 * Z, fb, qc), bf16),
            vmem((5 * Z, fb, qc), bf16),
            vmem((2, fb, qc), bf16),
            vmem((2, fb, qc), f32),
            vmem((8, H), f32),
            vmem((8, H), f32),
            vmem((16, H), f32),
            vmem((4, 8, H), f32),
            vmem((4, n, 8, fb), f32),
            vmem((4, 8, fb), f32),
            vmem((4, seqs, 8, fb), f32),
            vmem((4, n, 8, fb), f32),
            vmem((4, 8, H), f32),
            vmem((2, 8, H), f32),
            vmem((2, n, 8, fb), f32),
            vmem((2, 8, fb), f32),
            vmem((2, seqs, 8, fb), f32),
            sem((8,)),
            sem((n,)),
            sem((n,)),
            sem((4, n)),
            sem((4, n)),
            sem((2, 10 * Z)),
            sem((2, 10 * Z)),
            sem((8, n)),
            sem((8, n)),
            sem((4, seqs)),
            sem((4, seqs)),
            sem((2, 10 * Z)),
            sem((2, 10 * Z)),
            sem((2, 3)),
            sem((2, 3)),
            sem((2, n + seqs)),
            sem((2, n + seqs)),
        ],
        compiler_params=pltpu.CompilerParams(
            collective_id=0, has_side_effects=True, vmem_limit_bytes=63 * 1024 * 1024
        ),
        cost_estimate=pl.CostEstimate(
            flops=6 * matmul, bytes_accessed=16 * fb * H, transcendentals=6 * T * H
        ),
        name="network",
    )(
        inputs,
        out_grad,
        weight_one,
        weight_two,
        *(values.reshape(1, fb) for values in params),
        lengths,
        frame_mask.reshape(1, -1),
    )
    tok = inputs.shape[1]
    pairs = n // 2
    steps = pl.cdiv(tok, 2 * T)
    frames_spec = pl.BlockSpec((fb, 2 * T), lambda p: (0, p))
    land_spec = pl.BlockSpec((2, T, fb), lambda p: (jnp.minimum(p, pairs - 1), 0, 0))
    row_spec = pl.BlockSpec((1, fb), lambda p: (0, 0))
    results = pl.pallas_call(
        functools.partial(turn_back, sz, steps),
        grid=(steps,),
        out_shape=(jax.ShapeDtypeStruct((fb, tok), f32),) * 2
        + (jax.ShapeDtypeStruct((fb, H), f32),) * 2
        + (jax.ShapeDtypeStruct((1, fb), f32),) * 6,
        in_specs=[frames_spec, frames_spec, land_spec, land_spec, anywhere, anywhere]
        + [pl.BlockSpec((8, fb), lambda p: (0, 0))],
        out_specs=(frames_spec, frames_spec, anywhere, anywhere) + (row_spec,) * 6,
        scratch_shapes=[
            vmem((2, T, sz.win), bf16),
            vmem((fb, fb), bf16),
            vmem((2, fb, H), f32),
            sem((2,)),
        ],
        compiler_params=pltpu.CompilerParams(vmem_limit_bytes=60 * 1024 * 1024),
        name="turn_back",
    )(inputs, out_grad, out_land, dx_land, dw_one, dw_two, small)
    output, input_grad, dw_one, dw_two = results[:4]
    small = [row.reshape(fb) for row in results[4:]]
    return (
        output,
        input_grad,
        dw_one,
        small[0],
        small[1],
        small[2],
        dw_two,
        small[3],
        small[4],
        small[5],
    )


def frame_tables(lengths, frame_mask):
    positions = jnp.arange(frame_mask.shape[0], dtype=jnp.int32)
    offsets = jnp.cumsum(lengths[0]) - lengths[0]
    filled = jnp.sum(lengths[0])
    begins = jnp.any(positions[:, None] == offsets[None, :], axis=1)
    continues = jnp.where(begins, 0.0, 1.0).astype(jnp.float32)
    counted = jnp.where((positions < filled) & (frame_mask > 0), 1.0, 0.0).astype(jnp.float32)
    return (continues, counted)


def linear_scan(coef_rows, driving, backwards):
    row_count, length = driving.shape
    block_count = length // block_span
    factor = coef_rows.reshape(row_count, block_count, block_span)
    running = driving.reshape(row_count, block_count, block_span)
    places = jnp.arange(block_span, dtype=jnp.int32)
    step = 1
    while step < block_span:
        if backwards:
            mover = jnp.where(places[:, None] == places[None, :] + step, 1.0, 0.0).astype(
                jnp.float32
            )
            edge = jnp.where(places >= block_span - step, 1.0, 0.0).astype(jnp.float32)
        else:
            mover = jnp.where(places[:, None] == places[None, :] - step, 1.0, 0.0).astype(
                jnp.float32
            )
            edge = jnp.where(places < step, 1.0, 0.0).astype(jnp.float32)
        moved_factor = (
            jnp.dot(
                factor, mover, precision=lax.Precision.HIGHEST, preferred_element_type=jnp.float32
            )
            + edge
        )
        moved_running = jnp.dot(
            running, mover, precision=lax.Precision.HIGHEST, preferred_element_type=jnp.float32
        )
        running = factor * moved_running + running
        factor = factor * moved_factor
        step = step * 2
    end_place = 0 if backwards else block_span - 1
    total_factor = factor[:, :, end_place].T
    total_running = running[:, :, end_place].T

    def carry_step(carried, block_pair):
        return (block_pair[0] * carried + block_pair[1], carried)

    _, entering = lax.scan(
        carry_step,
        jnp.zeros((row_count,), jnp.float32),
        (total_factor, total_running),
        reverse=backwards,
    )
    result = running + factor * entering.T[:, :, None]
    return result.reshape(row_count, length)


def layer_forward(layer_input, weight, gain_row, bias_row, decay_rate, continues, counted):
    frames_in = lax.all_to_all(layer_input, "neur", split_axis=1, concat_axis=0, tiled=True)
    projected = jnp.dot(
        lax.all_gather(weight, "neur", axis=0, tiled=True),
        frames_in,
        preferred_element_type=jnp.float32,
    )
    neuron_proj = lax.all_to_all(
        projected.astype(jnp.bfloat16), "neur", split_axis=0, concat_axis=1, tiled=True
    ).astype(jnp.float32)
    sum_first = jnp.sum(counted[None, :] * neuron_proj, axis=1)
    sum_second = jnp.sum(counted[None, :] * neuron_proj * neuron_proj, axis=1)
    sum_first, sum_second, frames = lax.psum((sum_first, sum_second, jnp.sum(counted)), "seq")
    average = sum_first / frames
    inv_std = lax.rsqrt(sum_second / frames - average * average + epsilon)
    normed = (neuron_proj - average[:, None]) * inv_std[:, None]
    spread = jnp.sqrt(1.0 - decay_rate * decay_rate)
    states = linear_scan(
        decay_rate[:, None] * continues[None, :], (spread * gain_row)[:, None] * normed, False
    )
    layer_out = counted[None, :] * jax.nn.softplus(states + bias_row[:, None])
    return (layer_out, (frames_in, None, normed, inv_std, frames, states))


def layer_backward(
    upstream, weight, gain_row, bias_row, decay_rate, continues, counted, kept_state
):
    frames_in, full_weight, normed, inv_std, frames, states = kept_state
    local_grad = upstream * counted[None, :] * jax.nn.sigmoid(states + bias_row[:, None])
    following = jnp.concatenate([continues[1:], jnp.zeros((1,), jnp.float32)])
    coef_rows = decay_rate[:, None] * following[None, :]
    state_grad = linear_scan(coef_rows, local_grad, True)
    sum_rec, sum_rec_norm, sum_local = lax.psum(
        (
            jnp.sum(state_grad, axis=1),
            jnp.sum(state_grad * normed, axis=1),
            jnp.sum(local_grad, axis=1),
        ),
        "seq",
    )
    spread = jnp.sqrt(1.0 - decay_rate * decay_rate)
    gain_grad = spread * sum_rec_norm
    proj_grad = (spread * gain_row * inv_std)[:, None] * (
        state_grad - counted[None, :] * (sum_rec[:, None] + sum_rec_norm[:, None] * normed) / frames
    )
    driving = (spread * gain_row)[:, None] * normed
    decay_part = jnp.sum(state_grad * (states - driving), axis=1) / decay_rate
    grad_frames = lax.all_to_all(
        proj_grad.astype(jnp.bfloat16), "neur", split_axis=1, concat_axis=0, tiled=True
    )
    grad_rows = grad_frames
    input_frames = jnp.einsum(
        "ot,oi->it",
        grad_rows,
        lax.all_gather(weight, "neur", axis=0, tiled=True),
        preferred_element_type=jnp.float32,
    )
    input_grad = lax.all_to_all(
        input_frames.astype(jnp.bfloat16), "neur", split_axis=0, concat_axis=1, tiled=True
    ).astype(jnp.float32)
    grad_rows = grad_frames
    weight_rows = lax.psum_scatter(
        jnp.einsum("ot,it->oi", grad_rows, frames_in, preferred_element_type=jnp.float32),
        "neur",
        scatter_dimension=0,
        tiled=True,
    )
    weight_grad, decay_sum = lax.psum((weight_rows, decay_part), "seq")
    decay_grad = decay_sum - decay_rate / spread * gain_row * sum_rec_norm
    return (input_grad, weight_grad, gain_grad, sum_local, decay_grad)


def shards(
    inputs,
    weight_one,
    weight_two,
    gain_one,
    gain_two,
    bias_one,
    bias_two,
    decay_one,
    decay_two,
    lengths,
    frame_mask,
    out_grad,
):
    seqs, n = lax.axis_size("seq"), lax.axis_size("neur")
    H, (fb, tok) = weight_one.shape[1], inputs.shape
    if fits(n, seqs, H, fb, tok):
        params = (gain_one, gain_two, bias_one, bias_two, decay_one, decay_two)
        return frames_apart(
            Sizes(n, seqs, H, fb, tok),
            inputs,
            weight_one,
            weight_two,
            params,
            lengths,
            frame_mask,
            out_grad,
        )
    continues, counted = frame_tables(lengths, frame_mask)
    first_out, first_kept = layer_forward(
        inputs, weight_one, gain_one, bias_one, decay_one, continues, counted
    )
    second_out, second_kept = layer_forward(
        first_out.astype(jnp.bfloat16),
        weight_two,
        gain_two,
        bias_two,
        decay_two,
        continues,
        counted,
    )
    output = inputs.astype(jnp.float32) + second_out
    upstream = out_grad.astype(jnp.float32)
    middle_grad, weight_two_grad, gain_two_grad, bias_two_grad, decay_two_grad = layer_backward(
        upstream, weight_two, gain_two, bias_two, decay_two, continues, counted, second_kept
    )
    lower_grad, weight_one_grad, gain_one_grad, bias_one_grad, decay_one_grad = layer_backward(
        middle_grad, weight_one, gain_one, bias_one, decay_one, continues, counted, first_kept
    )
    return (
        output,
        upstream + lower_grad,
        weight_one_grad,
        gain_one_grad,
        bias_one_grad,
        decay_one_grad,
        weight_two_grad,
        gain_two_grad,
        bias_two_grad,
        decay_two_grad,
    )


def solution(mesh):
    placed = (
        P("neur", "seq"),
        P("neur", None),
        P("neur", None),
        P("neur"),
        P("neur"),
        P("neur"),
        P("neur"),
        P("neur"),
        P("neur"),
        P("seq", None),
        P("seq"),
        P("neur", "seq"),
    )
    return jax.shard_map(
        shards,
        mesh=mesh,
        in_specs=placed,
        out_specs=(
            P("neur", "seq"),
            P("neur", "seq"),
            P("neur", None),
            P("neur"),
            P("neur"),
            P("neur"),
            P("neur", None),
            P("neur"),
            P("neur"),
            P("neur"),
        ),
        check_vma=False,
    )
```

```python
import functools

import jax
import jax.numpy as jnp
from jax import lax
from jax.experimental import pallas as pl
from jax.experimental.pallas import tpu as pltpu
from jax.sharding import PartitionSpec as P

epsilon = 1e-05
block_span = 128
valid_frames = 3584
f32 = jnp.float32
bf16 = jnp.bfloat16
MESH = pl.DeviceIdType.MESH


def wide(tile, width):
    return jnp.concatenate([tile] * (width // 128), axis=1)


def at(index, size):
    if isinstance(index, int):
        return pl.ds(index * size, size)
    return pl.ds(pl.multiple_of(index * size, size), size)


def power(base, exponent):
    result = None
    while exponent:
        if exponent % 2:
            result = base if result is None else result * base
        exponent //= 2
        base = base * base
    return result


def log_of(rate):
    u = 1.0 - rate
    series = jnp.full_like(u, 1.0 / 8)
    for order in range(7, 0, -1):
        series = series * u + 1.0 / order
    return -u * series


GAIN, BIAS, DECAY = 0, 2, 4


class Sizes:
    def __init__(self, n, seqs, H, fb, tok_dev):
        self.n, self.seqs, self.H, self.fb, self.tok_dev = n, seqs, H, fb, tok_dev
        self.T = valid_frames // n
        self.steps = self.T // 8
        self.valid = valid_frames
        self.qc = H // seqs
        self.Z = n // 2
        self.odd = self.T % 128
        self.win = self.T + self.odd
        self.K = self.T + 16
        self.L = min(512, H)


def fits(n, seqs, H, fb, tok_dev):
    if n not in (4, 8) or valid_frames % n or seqs != 4 or fb * n != H or fb % 128 or H % 512:
        return False
    T = valid_frames // n
    return T % 64 == 0 and valid_frames % 128 == 0 and tok_dev >= valid_frames


class Line:
    def __init__(self, env, sends, recvs):
        self.env, self.sends, self.recvs = env, sends, recvs

    def copy(self, k, source, dest, target):
        return pltpu.make_async_remote_copy(
            src_ref=source,
            dst_ref=dest,
            send_sem=self.sends.at[k],
            recv_sem=self.recvs.at[k],
            device_id=target,
            device_id_type=MESH,
        )

    def arrived(self, k, ref):
        self.copy(k, ref, ref, self.env.across("x")).wait_recv()

    def sent(self, k, ref):
        self.copy(k, ref, ref, self.env.across("x")).wait_send()

    def along(self, dz):
        z, Z = self.env.z, self.env.sz.Z
        if dz == 0:
            return [(None, z, 0)]
        return [(z >= dz, z - dz, 1), (z + dz < Z, z + dz, -1)]


def if_so(condition, body):
    if condition is None:
        body()
    else:
        pl.when(condition)(body)


class Gather(Line):
    def __init__(self, env, source, full, sends, recvs, cut):
        super().__init__(env, sends, recvs)
        self.cut = cut
        self.full = full
        self.source = source.at[:, at(env.s, env.sz.qc)]

    def block(self, zz, fx, fy, fc=0):
        env = self.env
        rows = at(2 * zz + (env.x + fx) % 2, env.sz.fb)
        return self.full.at[rows, at(2 * ((env.y + fy) % 2) + (env.c + fc) % 2, env.sz.qc)]

    def half(self, ref, h):
        if h == 0:
            return ref.at[pl.ds(0, self.cut), :]
        return ref.at[pl.ds(self.cut, self.env.sz.fb - self.cut), :]

    def spread(self, zz, source):
        env, Z = self.env, self.env.sz.Z
        dest = self.block(zz, 0, 0)
        self.copy(2 * Z + zz, source, dest, env.across("x")).start()
        self.copy(3 * Z + zz, source, dest, env.across("y")).start()
        self.copy(6 * Z + zz, source, dest, env.across("core")).start()

    def pass_on(self, zz, source, way):
        env, Z = self.env, self.env.sz.Z
        dest = self.block(zz, 0, 0)

        def go():
            pltpu.make_async_remote_copy(
                src_ref=source,
                dst_ref=dest,
                send_sem=self.sends.at[zz if way > 0 else Z + zz],
                recv_sem=self.recvs.at[zz],
                device_id={"neur": 2 * (env.z + way) + env.x},
                device_id_type=MESH,
            ).start()

        pl.when(env.z < Z - 1 if way > 0 else env.z > 0)(go)

    def start(self):
        z = self.env.z
        self.pass_on(z, self.source, 1)
        self.pass_on(z, self.source, -1)
        self.spread(z, self.source)

    def line(self, dz):
        for condition, zz, way in self.along(dz):

            def one(zz=zz, way=way):
                block = self.block(zz, 0, 0)
                self.arrived(zz, block)
                self.pass_on(zz, block, way)
                self.spread(zz, block)

            if_so(condition, one)

    def sides(self, dz):
        env, Z = self.env, self.env.sz.Z
        for condition, zz, _ in self.along(dz):

            def one(zz=zz):
                block = self.block(zz, 1, 0)
                self.arrived(2 * Z + zz, block)
                part = self.half(block, 1)
                self.copy(5 * Z + zz, part, part, env.across("y")).start()
                self.copy(7 * Z + zz, block, block, env.across("core")).start()
                block = self.block(zz, 0, 1)
                self.arrived(3 * Z + zz, block)
                part = self.half(block, 0)
                self.copy(4 * Z + zz, part, part, env.across("x")).start()
                self.copy(8 * Z + zz, block, block, env.across("core")).start()

            if_so(condition, one)

    def diagonals(self):
        env, Z = self.env, self.env.sz.Z
        for dz in range(Z):
            for condition, zz, _ in self.along(dz):

                def one(zz=zz):
                    block = self.block(zz, 1, 1)
                    self.arrived(4 * Z + zz, self.half(block, 0))
                    self.arrived(5 * Z + zz, self.half(block, 1))
                    self.copy(9 * Z + zz, block, block, env.across("core")).start()

                if_so(condition, one)

    def cores(self):
        Z = self.env.sz.Z
        for k, (fx, fy) in enumerate(((0, 0), (1, 0), (0, 1), (1, 1))):
            for zz in range(Z):
                self.arrived((6 + k) * Z + zz, self.block(zz, fx, fy, 1))

    def drain(self):
        env, Z = self.env, self.env.sz.Z
        block = self.block(0, 0, 0)
        for zz in range(Z):
            pl.when((zz <= env.z) & (env.z < Z - 1))(lambda zz=zz: self.sent(zz, block))
            pl.when((zz >= env.z) & (env.z > 0))(lambda zz=zz: self.sent(Z + zz, block))
            for k in (2, 3, 6, 7, 8, 9):
                self.sent(k * Z + zz, block)
            self.sent(4 * Z + zz, self.half(block, 0))
            self.sent(5 * Z + zz, self.half(block, 1))


class Reduce(Line):
    kinds = ((1, 1), (1, 0), (0, 1), (0, 0))

    def __init__(self, env, grads, frames, land, spare, stage, held, total, sends, recvs, cut):
        super().__init__(env, sends, recvs)
        self.cut, self.held = cut, held
        self.grads, self.frames, self.land, self.spare = grads, frames, land, spare
        self.stage, self.total = stage, total

    def product(self, kind, zz, fc=0):
        env, sz = self.env, self.env.sz
        fx, fy = self.kinds[kind]
        rows = at(2 * zz + (env.x + fx) % 2, sz.fb)
        columns = at(2 * ((env.y + fy) % 2) + (env.c + fc) % 2, sz.qc)
        return jnp.dot(
            self.grads[rows, :], self.frames[:, columns], preferred_element_type=f32
        )

    def half(self, ref, h):
        if h == 0:
            return ref.at[pl.ds(0, self.cut), :]
        return ref.at[pl.ds(self.cut, self.env.sz.fb - self.cut), :]

    def landed(self, k, slot):
        self.arrived(k, self.land(slot))
        return self.land(slot)[...].astype(f32)

    def turn(self, i):
        z, Z = self.env.z, self.env.sz.Z
        low = jnp.where(i < Z - 1 - z, Z - 1 - i, i - (Z - 1 - z))
        high = jnp.where(i < z, i, Z - 1 - (i - z))
        return jnp.where(i == Z - 1, z, jnp.where(z < Z // 2, low, high))

    def cores(self, kind):
        env, Z = self.env, self.env.sz.Z

        def one(i, _):
            zz = self.turn(i)
            k = kind * Z + zz
            held = (kind % 2) * Z + zz
            if kind >= 2:
                self.sent(k - 2 * Z, self.stage.at[held])
            self.stage[held] = self.product(kind, zz, 1).astype(bf16)
            self.copy(k, self.stage.at[held], self.land(k), env.across("core")).start()
            return 0

        lax.fori_loop(0, Z, one, 0)

    def diagonals(self):
        env, Z = self.env, self.env.sz.Z

        def one(i, _):
            zz = self.turn(i)
            held = self.held(zz)
            held[...] = (self.product(0, zz) + self.landed(zz, zz)).astype(bf16)
            slot = self.land(4 * Z + zz)
            for k, h, axis in ((4, 0, "x"), (5, 1, "y")):
                self.copy(
                    k * Z + zz, self.half(held, h), self.half(slot, h), env.across(axis)
                ).start()
            return 0

        lax.fori_loop(0, Z, one, 0)

    def sides(self, low=0, high=None):
        env, Z = self.env, self.env.sz.Z
        spans = slice(0, self.cut), slice(self.cut, env.sz.fb)

        def one(i, _):
            zz = self.turn(i)
            slot = self.land(4 * Z + zz)
            for kind, h, wait, k, axis in ((1, 1, 5, 6, "x"), (2, 0, 4, 7, "y")):
                tile = self.product(kind, zz) + self.landed(kind * Z + zz, kind * Z + zz)
                part = self.half(slot, h)
                self.arrived(wait * Z + zz, part)
                held = self.stage.at[(2 + kind) * Z + zz]
                other = 1 - h
                summed = tile[spans[h], :] + part[...].astype(f32)
                self.half(held, h)[...] = summed.astype(bf16)
                self.half(held, other)[...] = tile[spans[other], :].astype(bf16)
                self.copy(
                    k * Z + zz, held, self.land((4 + kind) * Z + zz), env.across(axis)
                ).start()
            return 0

        lax.fori_loop(low, Z if high is None else high, one, 0)

    def joined(self, zz):
        Z = self.env.sz.Z
        tile = self.product(3, zz) + self.landed(3 * Z + zz, 3 * Z + zz)
        tile = tile + self.landed(6 * Z + zz, 5 * Z + zz)
        self.total[...] = tile + self.landed(7 * Z + zz, 6 * Z + zz)

    def lines(self, low=0, high=None):
        env, Z, z = self.env, self.env.sz.Z, self.env.z
        def onward(zz, way):
            k, slot = (8 if way > 0 else 9) * Z + zz, 7 * Z + zz
            self.joined(zz)

            @pl.when(z > 0 if way > 0 else z < Z - 1)
            def _():
                self.total[...] += self.landed(k, slot)

            held = self.held(zz)
            self.sent(4 * Z + zz, self.half(held, 0))
            self.sent(5 * Z + zz, self.half(held, 1))
            held[...] = self.total[...].astype(bf16)
            target = {"neur": 2 * (z + way) + env.x}
            if way > 0:
                self.copy(k, held, self.land(slot), target).start()
            else:
                pl.when(zz == z - 1)(lambda: self.copy(k, held, self.spare, target).start())
                pl.when(zz != z - 1)(lambda: self.copy(k, held, self.land(slot), target).start())

        for i in range(low, Z - 1 if high is None else high):
            zz = self.turn(i)
            pl.when(zz > z)(functools.partial(onward, zz, 1))
            pl.when(zz < z)(functools.partial(onward, zz, -1))

    def finish(self):
        Z, z = self.env.sz.Z, self.env.z
        self.joined(z)
        @pl.when(z > 0)
        def _():
            self.total[...] += self.landed(8 * Z + z, 7 * Z + z)

        @pl.when(z < Z - 1)
        def _():
            self.arrived(9 * Z + z, self.spare)
            self.total[...] += self.spare[...].astype(f32)

    def drain_cores(self):
        for k in range(2 * self.env.sz.Z, 4 * self.env.sz.Z):
            self.sent(k, self.stage.at[0])

    def drain_sides(self):
        for k in range(6 * self.env.sz.Z, 8 * self.env.sz.Z):
            self.sent(k, self.stage.at[0])

    def drain(self):
        Z, z = self.env.sz.Z, self.env.z
        held = self.stage.at[0]
        for zz in range(Z):
            for k in (4, 5):
                pl.when(zz == z)(
                    lambda k=k, zz=zz: self.sent(k * Z + zz, self.half(held, k - 4))
                )
            pl.when(zz > z)(lambda zz=zz: self.sent(8 * Z + zz, held))
            pl.when(zz < z)(lambda zz=zz: self.sent(9 * Z + zz, held))


class Result:
    def __init__(self, env, whole, block, sends, recvs, local):
        self.env, self.whole, self.block = env, whole, block
        self.sends, self.recvs, self.local = sends, recvs, local

    def part(self, flip_y, flip_c):
        env = self.env
        s = 2 * ((env.y + flip_y) % 2) + (env.c + flip_c) % 2
        return self.whole.at[:, at(s, env.sz.qc)]

    def copy(self, k, source, dest, target):
        return pltpu.make_async_remote_copy(
            src_ref=source,
            dst_ref=dest,
            send_sem=self.sends.at[k],
            recv_sem=self.recvs.at[k],
            device_id=target,
            device_id_type=MESH,
        )

    def start(self):
        env, own = self.env, self.part(0, 0)
        self.copy(0, self.block, own, env.across("y")).start()
        self.copy(1, self.block, own, env.across("core")).start()
        pltpu.make_async_copy(self.block, own, self.local).start()

    def finish(self):
        env = self.env
        other = self.part(1, 0)
        self.copy(0, self.block, other, env.across("y")).wait_recv()
        forward = self.copy(2, other, other, env.across("core"))
        forward.start()
        own = self.part(0, 0)
        pltpu.make_async_copy(self.block, own, self.local).wait()
        self.copy(0, self.block, own, env.across("y")).wait_send()
        self.copy(1, self.block, self.part(0, 1), env.across("core")).wait()
        forward.wait_send()
        self.copy(2, other, self.part(1, 1), env.across("core")).wait_recv()


class Env:
    def across(self, axis):
        if axis == "x":
            return {"neur": 2 * self.z + 1 - self.x}
        if axis == "y":
            return {"seq": 2 * (1 - self.y) + self.c}
        return {"seq": 2 * self.y + 1 - self.c}


def network(
    sz,
    x_hbm,
    g_hbm,
    w_one,
    w_two,
    gain_one,
    gain_two,
    bias_one,
    bias_two,
    decay_one,
    decay_two,
    lengths,
    frame_mask,
    out_land,
    dx_land,
    dw_one,
    dw_two,
    small,
    own_par,
    cont,
    counted,
    aux,
    raw,
    perm,
    eye,
    xs,
    gs,
    xr,
    gr,
    p_one,
    p_two,
    x_two,
    dp,
    dpt_one,
    dpt_two,
    s_one,
    s_two,
    wf_one,
    wf_two,
    land,
    stage,
    spare,
    fin,
    par,
    ends,
    work,
    pay,
    arrive,
    seqpay,
    seqland,
    back,
    backland,
    sumpay,
    sumland,
    sumseq,
    sumseqland,
    local_sems,
    par_sends,
    par_recvs,
    frame_sends,
    frame_recvs,
    gather_sends,
    gather_recvs,
    hop_sends,
    hop_recvs,
    seq_sends,
    seq_recvs,
    reduce_sends,
    reduce_recvs,
    final_sends,
    final_recvs,
    sum_sends,
    sum_recvs,
):
    n, seqs, H, fb, T, steps, L = sz.n, sz.seqs, sz.H, sz.fb, sz.T, sz.steps, sz.L
    env = Env()
    env.sz = sz
    me = lax.axis_index("neur")
    mine = lax.axis_index("seq")
    env.j, env.s = me, mine
    env.z, env.x, env.y, env.c = me // 2, me % 2, mine // 2, mine % 2

    barrier = pltpu.get_barrier_semaphore()
    for o in range(1, n):
        pl.semaphore_signal(
            barrier, inc=1, device_id={"neur": (me + o) % n}, device_id_type=MESH
        )
    for o in range(1, seqs):
        pl.semaphore_signal(
            barrier, inc=1, device_id={"seq": (mine + o) % seqs}, device_id_type=MESH
        )
    load_x = pltpu.make_async_copy(x_hbm.at[:, pl.ds(0, sz.valid)], raw, local_sems.at[0])
    load_x.start()
    for r, values in enumerate((gain_one, gain_two, bias_one, bias_two, decay_one, decay_two)):
        own_par[r : r + 1, :] = values[...]
    own_par[6:8, :] = jnp.zeros((2, fb), f32)
    pl.semaphore_wait(barrier, n - 1 + seqs - 1)

    def neur_copy(source, dest, send, recv, i):
        return pltpu.make_async_remote_copy(
            src_ref=source,
            dst_ref=dest,
            send_sem=send,
            recv_sem=recv,
            device_id={"neur": i},
            device_id_type=MESH,
        )

    def seq_copy(source, dest, send, recv, i):
        return pltpu.make_async_remote_copy(
            src_ref=source,
            dst_ref=dest,
            send_sem=send,
            recv_sem=recv,
            device_id={"seq": i},
            device_id_type=MESH,
        )

    def straight(body):
        lax.fori_loop(1, n // 2, lambda o, _: (body((me + 2 * o) % n), 0)[1], 0)

    def crossing(body, low=0, high=n // 2):
        lax.fori_loop(low, high, lambda o, _: (body((me + 2 * o + 1) % n), 0)[1], 0)

    def others(body, count=n, own=me):
        def one(o, _):
            body((own + o) % count)
            return 0

        lax.fori_loop(1, count, one, 0)

    own_lanes = at(me, fb)

    def par_copy(i):
        return neur_copy(own_par, par.at[:, own_lanes], par_sends.at[i], par_recvs.at[me], i)

    def par_wait(i):
        neur_copy(own_par, par.at[:, at(i, fb)], par_sends.at[i], par_recvs.at[i], i).wait()

    others(lambda i: par_copy(i).start())
    par[:, own_lanes] = own_par[...]

    cuts = (fb // 4, fb // 4)
    gather_one = Gather(env, w_one, wf_one, gather_sends.at[0], gather_recvs.at[0], cuts[0])
    gather_two = Gather(env, w_two, wf_two, gather_sends.at[1], gather_recvs.at[1], cuts[1])
    own_one = pltpu.make_async_copy(gather_one.source, gather_one.block(env.z, 0, 0), local_sems.at[2])
    own_two = pltpu.make_async_copy(gather_two.source, gather_two.block(env.z, 0, 0), local_sems.at[3])
    own_one.start()
    own_two.start()
    gather_one.start()
    gather_two.start()

    row = lax.broadcasted_iota(jnp.int32, (T, sz.win), 0)
    column = lax.broadcasted_iota(jnp.int32, (T, sz.win), 1)
    frame = (row & 7) * steps + (row >> 3)
    perm[0] = jnp.where(column == frame, 1.0, 0.0).astype(bf16)
    perm[1] = jnp.where(column == frame + sz.odd, 1.0, 0.0).astype(bf16)
    row = lax.broadcasted_iota(jnp.int32, (fb, fb), 0)
    column = lax.broadcasted_iota(jnp.int32, (fb, fb), 1)
    eye[...] = jnp.where(row == column, 1.0, 0.0).astype(bf16)

    def window(i):
        start = (i // 2) * (2 * T) + (i % 2) * (T - sz.odd)
        return pl.ds(pl.multiple_of(start, 128), sz.win)

    def turned(i):
        return lax.dot_general(
            perm[i % 2], raw[:, window(i)], (((1,), (1,)), ((), ())), preferred_element_type=f32
        ).astype(bf16)

    def frames_copy(a, source, dest, i):
        return neur_copy(source, dest, frame_sends.at[a, i], frame_recvs.at[a, me], i)

    def frames_wait(a, ref, i):
        part = ref.at[pl.ds(0, T), at(i, fb)]
        neur_copy(part, part, frame_sends.at[a, i], frame_recvs.at[a, i], i).wait_recv()

    def frames_sent(a, ref, i):
        part = ref.at[pl.ds(0, T), at(i, fb)]
        neur_copy(part, part, frame_sends.at[a, i], frame_recvs.at[a, i], i).wait_send()

    load_x.wait()

    def turn_x(i):
        xs[:, at(i, fb)] = turned(i)

    def send_x(i):
        frames_copy(0, xs.at[:, at(i, fb)], xr.at[pl.ds(0, T), own_lanes], i).start()

    def send_all_x():
        crossing(send_x)
        straight(send_x)

    others(turn_x)
    xr[0:T, own_lanes] = turned(me)
    load_g = pltpu.make_async_copy(g_hbm.at[:, pl.ds(0, sz.valid)], raw, local_sems.at[1])
    load_g.start()
    ends_of_line = (env.z == 0) | (env.z == sz.Z - 1)
    pl.when(ends_of_line)(send_all_x)
    for dz in range(1, sz.Z):
        gather_one.line(dz)
        gather_two.line(dz)
        if dz == max(1, sz.Z - 2):
            pl.when(jnp.logical_not(ends_of_line))(send_all_x)
        gather_one.sides(dz - 1)
    frame_tables_of(sz, me, lengths, frame_mask, perm, window(me), cont, counted, aux)
    load_g.wait()

    def turn_g(i):
        gs[:, at(i, fb)] = turned(i)

    def send_g(i):
        frames_copy(1, gs.at[:, at(i, fb)], gr.at[:, own_lanes], i).start()

    others(turn_g)
    gr[:, own_lanes] = turned(me)
    gather_one.sides(sz.Z - 1)
    straight(send_g)
    gather_one.diagonals()
    for dz in range(sz.Z - 1):
        gather_two.sides(dz)
    gather_one.cores()
    own_one.wait()
    own_two.wait()
    others(lambda i: frames_wait(0, xr, i))
    others(par_wait)

    def blocks(body):
        def one(b, _):
            body(at(b, L))
            return 0

        lax.fori_loop(0, H // L, one, 0)

    def project(frames, weight, result):
        def one(b, _):
            result[:, at(b, fb)] = lax.dot_general(
                frames[0:T, :],
                weight[at(b, fb), :],
                (((1,), (1,)), ((), ())),
                preferred_element_type=f32,
            ).astype(bf16)
            return 0

        lax.fori_loop(0, n, one, 0)

    def flags(t):
        tile = pl.ds(pl.multiple_of(8 * t, 8), 8)
        return wide(cont[tile, :], L), wide(counted[tile, :], L)

    def spread8(ref, r, cols, width=L):
        return jnp.broadcast_to(ref[r : r + 1, cols], (8, width))

    zero = jnp.zeros((8, L), f32)

    def down(value):
        return jnp.sum(value, axis=0, keepdims=True)

    def exchange(e, gathered, totalled, gap):
        def out_copy(i):
            return neur_copy(
                pay.at[e, :, at(i, fb)],
                arrive.at[e, me],
                hop_sends.at[2 * e, i],
                hop_recvs.at[2 * e, me],
                i,
            )

        others(lambda i: out_copy(i).start())
        arrive[e, me] = pay[e, :, own_lanes]
        gap("hop_a")

        def out_wait(i):
            neur_copy(
                pay.at[e, :, at(i, fb)],
                arrive.at[e, i],
                hop_sends.at[2 * e, i],
                hop_recvs.at[2 * e, i],
                i,
            ).wait()

        others(out_wait)
        gathered()

        def along_copy(i):
            return seq_copy(
                seqpay.at[e],
                seqland.at[e, mine],
                seq_sends.at[e, i],
                seq_recvs.at[e, mine],
                i,
            )

        def along_wait(i):
            seq_copy(
                seqpay.at[e], seqland.at[e, i], seq_sends.at[e, i], seq_recvs.at[e, i], i
            ).wait()

        others(lambda i: along_copy(i).start(), seqs, mine)
        seqland[e, mine] = seqpay[e]
        gap("hop_b")
        others(along_wait, seqs, mine)
        sums = seqland[e, 0]
        for i in range(1, seqs):
            sums = sums + seqland[e, i]
        totalled(sums)

        def back_copy(i):
            return neur_copy(
                back.at[e, i],
                backland.at[e, :, own_lanes],
                hop_sends.at[2 * e + 1, i],
                hop_recvs.at[2 * e + 1, me],
                i,
            )

        def back_wait(i):
            neur_copy(
                back.at[e, i],
                backland.at[e, :, at(i, fb)],
                hop_sends.at[2 * e + 1, i],
                hop_recvs.at[2 * e + 1, i],
                i,
            ).wait()

        others(lambda i: back_copy(i).start())
        backland[e, :, own_lanes] = back[e, me]
        gap("hop_c")
        others(back_wait)

    def layer_forward(layer, frames, weight, projected, states, store, gap):
        e = layer
        decay_row, gain_row, bias_row = DECAY + layer, GAIN + layer, BIAS + layer
        project(frames, weight, projected)
        gap("ends")

        def local_ends(cols):
            decay = spread8(par, decay_row, cols)

            def step(i, carry):
                state, first, second, inward = carry
                pair = projected[pl.ds(pl.multiple_of(16 * i, 16), 16), cols].astype(f32)
                for h in range(2):
                    value = pair[8 * h : 8 * h + 8, :]
                    goes, count = flags(2 * i + h)
                    state = (decay * goes) * state + value
                    held = count * value
                    first = first + held
                    second = second + held * value
                ins = frames[pl.ds(pl.multiple_of(16 * i, 16), 16), cols].astype(f32)
                return state, first, second, inward + ins[0:8, :] + ins[8:16, :]

            state, first, second, inward = lax.fori_loop(
                0, T // 16, step, (zero, zero, zero, zero)
            )
            ends[:, cols] = state
            pay[e, 1:2, cols] = down(first)
            pay[e, 2:3, cols] = down(second)
            pay[e, 3:4, cols] = down(inward)

        blocks(local_ends)
        run_power = power(par[decay_row : decay_row + 1, :], steps)
        total = jnp.zeros((1, H), f32)
        for k in range(8):
            total = run_power * wide(aux[16 + k : 17 + k, :], H) * total + ends[k : k + 1, :]
        pay[e, 0:1, :] = total
        pay[e, 4:8, :] = jnp.zeros((4, H), f32)

        own_decay = own_par[decay_row : decay_row + 1, :]

        def gathered():
            whole_power = power(own_decay, T)
            carried = jnp.zeros((1, fb), f32)
            sums = jnp.zeros((8, fb), f32)
            for i in range(n):
                rows = arrive[e, i]
                back[e, i, 0:1, :] = carried
                carried = whole_power * wide(aux[8 + i : 9 + i, :], fb) * carried + rows[0:1, :]
                sums = sums + rows
            seqpay[e] = sums
            seqpay[e, 0:1, :] = wide(aux[24:25, :], fb)

        def totalled(sums):
            frames_all = sums[0:1, :]
            average = sums[1:2, :] / frames_all
            inv_std = lax.rsqrt(sums[2:3, :] / frames_all - average * average + epsilon)
            centre = sums[3:4, :] / (sz.valid * seqs)
            for i in range(n):
                back[e, i, 1:2, :] = average
                back[e, i, 2:3, :] = inv_std
                back[e, i, 3:4, :] = frames_all
                back[e, i, 4:5, :] = centre
                back[e, i, 5:8, :] = jnp.zeros((3, fb), f32)

        exchange(e, gathered, totalled, gap)
        centre = backland[e, 4:5, :]
        frames[T : T + 16, :] = jnp.concatenate(
            [-centre, -centre, -centre, jnp.zeros((13, H), f32)], axis=0
        ).astype(bf16)

        total = backland[e, 0:1, :]
        for k in range(8):
            work[k : k + 1, :] = total
            total = run_power * wide(aux[16 + k : 17 + k, :], H) * total + ends[k : k + 1, :]

        gap("scan")

        def full_scan(cols):
            decay = spread8(par, decay_row, cols)
            average = spread8(backland.at[e], 1, cols)
            inv_std = spread8(backland.at[e], 2, cols)
            bias = spread8(par, bias_row, cols)
            scale = jnp.sqrt(1.0 - decay * decay) * spread8(par, gain_row, cols) * inv_std
            ones = (1.0 - jnp.exp(wide(aux[0:8, :], L) * log_of(decay))) / (1.0 - decay)
            state = scale * (work[0:8, cols] - average * ones)
            states[0:8, cols] = state

            def step(i, state):
                pair = projected[pl.ds(pl.multiple_of(16 * i, 16), 16), cols].astype(f32)
                outs = []
                for h in range(2):
                    goes, count = flags(2 * i + h)
                    state = (decay * goes) * state + scale * (pair[8 * h : 8 * h + 8, :] - average)
                    states[pl.ds(pl.multiple_of(16 * i + 8 * h + 8, 8), 8), cols] = state
                    v = state + bias
                    soft = jnp.maximum(v, 0.0) + jnp.log(1.0 + jnp.exp(-jnp.abs(v)))
                    outs.append(count * soft)
                store[pl.ds(pl.multiple_of(16 * i, 16), 16), cols] = jnp.concatenate(
                    outs, axis=0
                ).astype(bf16)
                return state

            lax.fori_loop(0, T // 16, step, state)

        blocks(full_scan)

    def layer_backward(layer, upstream, projected, states, turned_grads, gap):
        e = 2 + (1 - layer)
        decay_row, gain_row, bias_row = DECAY + layer, GAIN + layer, BIAS + layer
        run_power = power(par[decay_row : decay_row + 1, :], steps)

        def local_ends(cols):
            decay = spread8(par, decay_row, cols)
            average = spread8(backland.at[layer], 1, cols)
            inv_std = spread8(backland.at[layer], 2, cols)
            bias = spread8(par, bias_row, cols)

            def step(o, carry):
                i = T // 16 - 1 - o
                rows = pl.ds(pl.multiple_of(16 * i, 16), 16)
                pair = projected[rows, cols].astype(f32)
                ups = upstream[rows, cols].astype(f32)
                for h in (1, 0):
                    run, reach, U, V, UN, VN, B, D, DA = carry
                    goes, count = flags(2 * i + h)
                    here = pl.ds(pl.multiple_of(16 * i + 8 * h + 8, 8), 8)
                    state = states[here, cols]
                    before = states[pl.ds(pl.multiple_of(16 * i + 8 * h, 8), 8), cols]
                    local = ups[8 * h : 8 * h + 8, :] * count / (1.0 + jnp.exp(-(state + bias)))
                    states[here, cols] = local
                    normed = (pair[8 * h : 8 * h + 8, :] - average) * inv_std
                    run = local + run
                    kept = goes * before
                    link = decay * goes
                    carry = (
                        link * run,
                        link * reach,
                        U + run,
                        V + reach,
                        UN + run * normed,
                        VN + reach * normed,
                        B + local,
                        D + run * kept,
                        DA + reach * kept,
                    )
                return carry

            one = jnp.ones((8, L), f32)
            run, _, U, V, UN, VN, B, D, DA = lax.fori_loop(
                0, T // 16, step, (zero, one, zero, zero, zero, zero, zero, zero, zero)
            )
            ends[:, cols] = run
            decay_run = power(par[decay_row : decay_row + 1, cols], steps)
            part, factor = jnp.zeros((1, L), f32), jnp.ones((1, L), f32)
            for k in range(7, -1, -1):
                work[k : k + 1, cols] = part
                work[8 + k : 9 + k, cols] = factor
                through = decay_run * wide(aux[16 + k : 17 + k, :], L)
                part = through * part + ends[k : k + 1, cols]
                factor = through * factor
            pay[e, 0:1, cols] = part
            entering, scaled = work[0:8, cols], work[8:16, cols]
            pay[e, 1:2, cols] = down(U + V * entering)
            pay[e, 2:3, cols] = down(V * scaled)
            pay[e, 3:4, cols] = down(UN + VN * entering)
            pay[e, 4:5, cols] = down(VN * scaled)
            pay[e, 5:6, cols] = down(B)
            pay[e, 6:7, cols] = down(D + DA * entering)
            pay[e, 7:8, cols] = down(DA * scaled)

        blocks(local_ends)
        own_decay = own_par[decay_row : decay_row + 1, :]
        own_gain = own_par[gain_row : gain_row + 1, :]

        def gathered():
            whole_power = power(own_decay, T)
            carried = jnp.zeros((1, fb), f32)
            sums = [jnp.zeros((1, fb), f32)] * 4
            for i in range(n - 1, -1, -1):
                rows = arrive[e, i]
                back[e, i, 0:1, :] = carried
                for a, (plain, times) in enumerate(((1, 2), (3, 4), (5, None), (6, 7))):
                    term = rows[plain : plain + 1, :]
                    if times is not None:
                        term = term + rows[times : times + 1, :] * carried
                    sums[a] = sums[a] + term
                carried = whole_power * wide(aux[8 + i : 9 + i, :], fb) * carried + rows[0:1, :]
            for a in range(4):
                seqpay[e, a : a + 1, :] = sums[a]
            seqpay[e, 4:8, :] = jnp.zeros((4, fb), f32)

        def totalled(sums):
            rec, rec_norm = sums[0:1, :], sums[1:2, :]
            for i in range(n):
                back[e, i, 1:2, :] = rec
                back[e, i, 2:3, :] = rec_norm
                back[e, i, 3:8, :] = jnp.zeros((5, fb), f32)
            spread = jnp.sqrt(1.0 - own_decay * own_decay)
            small[3 * layer : 3 * layer + 1, :] = spread * rec_norm
            small[3 * layer + 1 : 3 * layer + 2, :] = sums[2:3, :]
            small[3 * layer + 2 : 3 * layer + 3, :] = (
                sums[3:4, :] - own_decay / spread * own_gain * rec_norm
            )

        exchange(e, gathered, totalled, gap)
        gap("scan")
        total = backland[e, 0:1, :]
        for k in range(7, -1, -1):
            work[k : k + 1, :] = total
            total = run_power * wide(aux[16 + k : 17 + k, :], H) * total + ends[k : k + 1, :]

        def full_scan(cols):
            decay = spread8(par, decay_row, cols)
            average = spread8(backland.at[layer], 1, cols)
            inv_std = spread8(backland.at[layer], 2, cols)
            frames_all = spread8(backland.at[layer], 3, cols)
            scale = jnp.sqrt(1.0 - decay * decay) * spread8(par, gain_row, cols) * inv_std
            rec = spread8(backland.at[e], 1, cols) / frames_all
            rec_norm = spread8(backland.at[e], 2, cols) / frames_all * inv_std

            def step(o, carry):
                carry, added = carry
                i = T // 16 - 1 - o
                rows = pl.ds(pl.multiple_of(16 * i, 16), 16)
                pair = projected[rows, cols].astype(f32)
                outs = [None, None]
                for h in (1, 0):
                    goes, count = flags(2 * i + h)
                    here = pl.ds(pl.multiple_of(16 * i + 8 * h + 8, 8), 8)
                    run = states[here, cols] + carry
                    centred = pair[8 * h : 8 * h + 8, :] - average
                    outs[h] = scale * (run - count * (rec + rec_norm * centred))
                    carry = (decay * goes) * run
                rounded = jnp.concatenate(outs, axis=0).astype(bf16)
                dp[rows, cols] = rounded
                rounded = rounded.astype(f32)
                return carry, added + rounded[0:8, :] + rounded[8:16, :]

            _, added = lax.fori_loop(0, T // 16, step, (work[0:8, cols], zero))
            whole = down(added)
            sumpay[layer, 0:1, cols] = whole
            high = whole.astype(bf16).astype(f32)
            middle = (whole - high).astype(bf16).astype(f32)
            low = whole - high - middle
            dp[T : T + 16, cols] = jnp.concatenate(
                [high, middle, low, jnp.zeros((13, L), f32)], axis=0
            ).astype(bf16)

        blocks(full_scan)
        sumpay[layer, 1:8, :] = jnp.zeros((7, H), f32)

        def turn(b, _):
            turned_grads[at(b, fb), :] = lax.dot_general(
                eye[...], dp[:, at(b, fb)], (((1,), (1,)), ((), ())), preferred_element_type=f32
            ).astype(bf16)
            return 0

        lax.fori_loop(0, n, turn, 0)

    def input_gradient(weight, result, i):
        result[:, at(i, fb)] = jnp.dot(
            dp[0:T, :], weight[:, at(i, fb)], preferred_element_type=f32
        ).astype(bf16)

    def sum_copy(layer, i):
        return neur_copy(
            sumpay.at[layer, :, at(i, fb)],
            sumland.at[layer, me],
            sum_sends.at[layer, i],
            sum_recvs.at[layer, me],
            i,
        )

    def sum_along(layer, i):
        return seq_copy(
            sumseq.at[layer],
            sumseqland.at[layer, mine],
            sum_sends.at[layer, n + i],
            sum_recvs.at[layer, n + mine],
            i,
        )

    def sum_start(layer):
        others(lambda i: sum_copy(layer, i).start())
        sumland[layer, me] = sumpay[layer, :, own_lanes]

    def sum_middle(layer):
        def wait(i):
            neur_copy(
                sumpay.at[layer, :, at(i, fb)],
                sumland.at[layer, i],
                sum_sends.at[layer, i],
                sum_recvs.at[layer, i],
                i,
            ).wait()

        others(wait)
        total = sumland[layer, 0]
        for i in range(1, n):
            total = total + sumland[layer, i]
        sumseq[layer] = total
        sumseqland[layer, mine] = total
        others(lambda i: sum_along(layer, i).start(), seqs, mine)

    def sum_finish(layer, frames, total):
        def wait(i):
            seq_copy(
                sumseq.at[layer],
                sumseqland.at[layer, i],
                sum_sends.at[layer, n + i],
                sum_recvs.at[layer, n + i],
                i,
            ).wait()

        others(wait, seqs, mine)
        whole = sumseqland[layer, 0]
        for i in range(1, seqs):
            whole = whole + sumseqland[layer, i]
        whole = whole[0:1, :]
        high = whole.astype(bf16).astype(f32)
        middle = (whole - high).astype(bf16).astype(f32)
        low = whole - high - middle
        rows = jnp.concatenate([high, middle, low, jnp.zeros((13, fb), f32)], axis=0).astype(bf16)
        columns = lax.dot_general(
            eye[...], rows, (((1,), (1,)), ((), ())), preferred_element_type=f32
        ).astype(bf16)
        total[...] -= jnp.dot(
            columns, frames[T : T + 16, at(mine, sz.qc)], preferred_element_type=f32
        )

    def place_out(a, ref, dest, i):
        return neur_copy(
            ref.at[:, at(i, fb)], dest.at[me], frame_sends.at[a, i], frame_recvs.at[a, me], i
        )

    def out_arrived(a, ref, dest, i):
        neur_copy(
            ref.at[:, at(i, fb)], dest.at[i], frame_sends.at[a, i], frame_recvs.at[a, i], i
        ).wait()

    def nothing(name):
        return None

    def during_one(name):
        if name == "ends":
            gather_two.sides(sz.Z - 1)
            gather_two.diagonals()
        if name == "scan":
            crossing(send_g, 0, n // 4)

    def during_two(name):
        if name == "scan":
            crossing(send_g, n // 4, n // 2)

    layer_forward(0, xr, wf_one, p_one, s_one, x_two, during_one)
    gather_two.cores()
    others(lambda i: frames_sent(0, xs, i))
    layer_forward(1, x_two, wf_two, p_two, s_two, xs, during_two)

    def send_out(i):
        place_out(2, xs, out_land, i).start()

    keep_out = pltpu.make_async_copy(xs.at[:, own_lanes], out_land.at[me], local_sems.at[4])
    keep_out.start()
    others(lambda i: frames_wait(1, gr, i))
    others(lambda i: frames_sent(1, gs, i))
    gather_two.drain()

    crossing(send_out, 0, 1)
    layer_backward(
        1,
        gr,
        p_two,
        s_two,
        dpt_two,
        lambda name: crossing(send_out, 1, 2) if name == "scan" else None,
    )
    if n > 4:
        crossing(send_out, 2, 3)
    lax.fori_loop(0, n, lambda i, _: (input_gradient(wf_two, gr, i), 0)[1], 0)
    sum_start(1)
    if n > 4:
        crossing(send_out, 3, 4)
    reduce_two = Reduce(
        env,
        dpt_two,
        x_two,
        lambda k: land.at[k],
        spare.at[1],
        stage,
        lambda k: stage.at[2 * sz.Z + k],
        fin.at[1],
        reduce_sends.at[1],
        reduce_recvs.at[1],
        fb // 2,
    )
    reduce_one = Reduce(
        env,
        dpt_one,
        xr,
        lambda k: wf_two.at[at(k // seqs, fb), at(k % seqs, sz.qc)],
        spare.at[0],
        stage,
        lambda k: raw.at[:, at(k, sz.qc)],
        fin.at[0],
        reduce_sends.at[0],
        reduce_recvs.at[0],
        fb // 2,
    )
    result_two = Result(
        env, dw_two, land.at[1], final_sends.at[1], final_recvs.at[1], local_sems.at[6]
    )
    result_one = Result(
        env, dw_one, land.at[0], final_sends.at[0], final_recvs.at[0], local_sems.at[7]
    )
    for kind in range(4):
        reduce_two.cores(kind)

    def meanwhile(name):
        if name == "hop_b":
            sum_middle(1)
        if name == "scan":
            reduce_two.diagonals()
            straight(send_out)

    layer_backward(0, gr, p_one, s_one, dpt_one, meanwhile)
    reduce_two.drain_cores()
    reduce_one.cores(0)
    reduce_two.sides()
    reduce_one.diagonals()
    for kind in range(1, 4):
        reduce_one.cores(kind)
    sum_start(0)

    def send_dx(i):
        place_out(3, gs, dx_land, i).start()

    def make_dx(i):
        input_gradient(wf_one, gs, i)

    def make_and_send_dx(i):
        make_dx(i)
        send_dx(i)

    straight(make_and_send_dx)
    crossing(make_dx)
    make_dx(me)
    keep_dx = pltpu.make_async_copy(gs.at[:, own_lanes], dx_land.at[me], local_sems.at[5])
    keep_dx.start()
    reduce_two.lines()
    sum_middle(0)
    reduce_two.drain_sides()
    reduce_one.sides(0, 2)
    for i in range(2, sz.Z):
        reduce_one.lines(i - 2, i - 1)
        reduce_one.sides(i, i + 1)
    crossing(send_dx)
    reduce_two.finish()
    sum_finish(1, x_two, fin.at[1])
    land[1] = fin[1].astype(bf16)
    result_two.start()
    reduce_one.lines(sz.Z - 2, sz.Z - 1)
    reduce_one.finish()
    sum_finish(0, xr, fin.at[0])
    land[0] = fin[0].astype(bf16)
    result_one.start()
    result_two.finish()
    others(lambda i: out_arrived(2, xs, out_land, i))
    others(lambda i: out_arrived(3, gs, dx_land, i))
    keep_out.wait()
    keep_dx.wait()
    result_one.finish()
    reduce_two.drain()
    reduce_one.drain_cores()
    reduce_one.drain_sides()
    reduce_one.drain()
    gather_one.drain()
    small[6:8, :] = jnp.zeros((2, fb), f32)


def frame_tables_of(sz, me, lengths, frame_mask, perm, window, cont, counted, aux):
    T, steps = sz.T, sz.steps
    starts, filled = [], 0
    for k in range(lengths.shape[1]):
        starts.append(filled)
        filled = filled + lengths[0, k]
    row = lax.broadcasted_iota(jnp.int32, (T, 128), 0)
    slot = me * T + (row & 7) * steps + (row >> 3)
    goes = jnp.ones((T, 128), f32)
    for start in starts:
        goes = jnp.where(slot == start, 0.0, goes)
    cont[...] = goes
    kept = jnp.where(frame_mask[0:1, window] > 0, 1.0, 0.0)
    kept = jnp.broadcast_to(kept, (128, sz.win)).astype(bf16)
    kept = lax.dot_general(
        perm[me % 2], kept, (((1,), (1,)), ((), ())), preferred_element_type=f32
    )
    counted[...] = jnp.where(slot < filled, kept, 0.0)
    run = lax.broadcasted_iota(jnp.int32, (8, 128), 0)
    first = me * T + run * steps
    behind = jnp.zeros((8, 128), jnp.int32)
    whole, own = jnp.ones((8, 128), f32), jnp.ones((8, 128), f32)
    for start in starts:
        behind = jnp.where(first > start, jnp.maximum(behind, start), behind)
        whole = jnp.where((run * T <= start) & (start < run * T + T), 0.0, whole)
        own = jnp.where((first <= start) & (start < first + steps), 0.0, own)
    aux[0:8, :] = (first - behind).astype(f32)
    aux[8:16, :] = whole
    aux[16:24, :] = own
    place = lax.broadcasted_iota(jnp.int32, (1, sz.tok_dev), 1)
    block = jnp.where((place < filled) & (frame_mask[...] > 0), 1.0, 0.0)
    block = jnp.sum(block, axis=1, keepdims=True)
    aux[24:32, :] = jnp.broadcast_to(block, (8, 128))


def turn_back(
    sz,
    steps,
    x_ref,
    g_ref,
    out_ref,
    dx_ref,
    one_ref,
    two_ref,
    small,
    output,
    input_grad,
    dw_one,
    dw_two,
    gain_one,
    bias_one,
    decay_one,
    gain_two,
    bias_two,
    decay_two,
    perm,
    held,
    widened,
    sems,
):
    step = pl.program_id(0)
    T, fb, win, odd = sz.T, sz.fb, sz.win, sz.odd
    pairs = ((one_ref, dw_one), (two_ref, dw_two))
    reads = [pltpu.make_async_copy(a, held.at[k], sems.at[k]) for k, (a, _) in enumerate(pairs)]
    writes = [pltpu.make_async_copy(widened.at[k], b, sems.at[k]) for k, (_, b) in enumerate(pairs)]

    @pl.when(step == 0)
    def _():
        for move in reads:
            move.start()
        row = lax.broadcasted_iota(jnp.int32, (T, win), 0)
        column = lax.broadcasted_iota(jnp.int32, (T, win), 1)
        frame = (row & 7) * sz.steps + (row >> 3)
        perm[0] = jnp.where(column == frame, 1.0, 0.0).astype(bf16)
        perm[1] = jnp.where(column == frame + odd, 1.0, 0.0).astype(bf16)
        rows = (gain_one, bias_one, decay_one, gain_two, bias_two, decay_two)
        for r, ref in enumerate(rows):
            ref[...] = small[r : r + 1, :]

    output[...] = x_ref[...].astype(f32)
    input_grad[...] = g_ref[...].astype(f32)

    @pl.when(step < sz.n // 2)
    def _():
        for half in range(2):
            lanes = pl.ds((T - odd) * half, win)
            for source, result in ((out_ref, output), (dx_ref, input_grad)):
                result[:, lanes] += lax.dot_general(
                    source[half], perm[half], (((0,), (0,)), ((), ())), preferred_element_type=f32
                )

    @pl.when(step == 1)
    def _():
        for k, (read, write) in enumerate(zip(reads, writes, strict=True)):
            read.wait()
            widened[k] = held[k].astype(f32)
            write.start()

    @pl.when(step == steps - 1)
    def _():
        for move in writes:
            move.wait()


def frames_apart(sz, inputs, weight_one, weight_two, params, lengths, frame_mask, out_grad):
    n, seqs, H, fb, T, Z, qc = sz.n, sz.seqs, sz.H, sz.fb, sz.T, sz.Z, sz.qc
    whole = pl.BlockSpec(memory_space=pltpu.VMEM)
    anywhere = pl.BlockSpec(memory_space=pl.ANY)
    vmem, sem = pltpu.VMEM, pltpu.SemaphoreType.DMA
    frames_shape, longer_shape = (T, H), (sz.K, H)
    matmul = 2 * T * H * H
    out_land, dx_land, dw_one, dw_two, small = pl.pallas_call(
        functools.partial(network, sz),
        out_shape=(
            jax.ShapeDtypeStruct((n, T, fb), bf16),
            jax.ShapeDtypeStruct((n, T, fb), bf16),
            jax.ShapeDtypeStruct((fb, H), bf16),
            jax.ShapeDtypeStruct((fb, H), bf16),
            jax.ShapeDtypeStruct((8, fb), f32),
        ),
        in_specs=[anywhere] * 4 + [whole] * 6 + [pl.BlockSpec(memory_space=pltpu.SMEM), whole],
        out_specs=(anywhere, anywhere, anywhere, anywhere, whole),
        scratch_shapes=[
            vmem((8, fb), f32),
            vmem((T, 128), f32),
            vmem((T, 128), f32),
            vmem((32, 128), f32),
            vmem((fb, sz.valid), bf16),
            vmem((2, T, sz.win), bf16),
            vmem((fb, fb), bf16),
            vmem(frames_shape, bf16),
            vmem(frames_shape, bf16),
            vmem(longer_shape, bf16),
            vmem(frames_shape, bf16),
            vmem(frames_shape, bf16),
            vmem(frames_shape, bf16),
            vmem(longer_shape, bf16),
            vmem(longer_shape, bf16),
            vmem((H, sz.K), bf16),
            vmem((H, sz.K), bf16),
            vmem((T + 8, H), f32),
            vmem((T + 8, H), f32),
            vmem((H, H), bf16),
            vmem((H, H), bf16),
            vmem((8 * Z, fb, qc), bf16),
            vmem((5 * Z, fb, qc), bf16),
            vmem((2, fb, qc), bf16),
            vmem((2, fb, qc), f32),
            vmem((8, H), f32),
            vmem((8, H), f32),
            vmem((16, H), f32),
            vmem((4, 8, H), f32),
            vmem((4, n, 8, fb), f32),
            vmem((4, 8, fb), f32),
            vmem((4, seqs, 8, fb), f32),
            vmem((4, n, 8, fb), f32),
            vmem((4, 8, H), f32),
            vmem((2, 8, H), f32),
            vmem((2, n, 8, fb), f32),
            vmem((2, 8, fb), f32),
            vmem((2, seqs, 8, fb), f32),
            sem((8,)),
            sem((n,)),
            sem((n,)),
            sem((4, n)),
            sem((4, n)),
            sem((2, 10 * Z)),
            sem((2, 10 * Z)),
            sem((8, n)),
            sem((8, n)),
            sem((4, seqs)),
            sem((4, seqs)),
            sem((2, 10 * Z)),
            sem((2, 10 * Z)),
            sem((2, 3)),
            sem((2, 3)),
            sem((2, n + seqs)),
            sem((2, n + seqs)),
        ],
        compiler_params=pltpu.CompilerParams(
            collective_id=0, has_side_effects=True, vmem_limit_bytes=63 * 1024 * 1024
        ),
        cost_estimate=pl.CostEstimate(
            flops=6 * matmul, bytes_accessed=16 * fb * H, transcendentals=6 * T * H
        ),
        name="network",
    )(
        inputs,
        out_grad,
        weight_one,
        weight_two,
        *(values.reshape(1, fb) for values in params),
        lengths,
        frame_mask.reshape(1, -1),
    )
    tok = inputs.shape[1]
    pairs = n // 2
    steps = pl.cdiv(tok, 2 * T)
    frames_spec = pl.BlockSpec((fb, 2 * T), lambda p: (0, p))
    land_spec = pl.BlockSpec((2, T, fb), lambda p: (jnp.minimum(p, pairs - 1), 0, 0))
    row_spec = pl.BlockSpec((1, fb), lambda p: (0, 0))
    results = pl.pallas_call(
        functools.partial(turn_back, sz, steps),
        grid=(steps,),
        out_shape=(jax.ShapeDtypeStruct((fb, tok), f32),) * 2
        + (jax.ShapeDtypeStruct((fb, H), f32),) * 2
        + (jax.ShapeDtypeStruct((1, fb), f32),) * 6,
        in_specs=[frames_spec, frames_spec, land_spec, land_spec, anywhere, anywhere]
        + [pl.BlockSpec((8, fb), lambda p: (0, 0))],
        out_specs=(frames_spec, frames_spec, anywhere, anywhere) + (row_spec,) * 6,
        scratch_shapes=[
            vmem((2, T, sz.win), bf16),
            vmem((2, fb, H), bf16),
            vmem((2, fb, H), f32),
            sem((2,)),
        ],
        compiler_params=pltpu.CompilerParams(vmem_limit_bytes=60 * 1024 * 1024),
        name="turn_back",
    )(inputs, out_grad, out_land, dx_land, dw_one, dw_two, small)
    output, input_grad, dw_one, dw_two = results[:4]
    small = [row.reshape(fb) for row in results[4:]]
    return (
        output,
        input_grad,
        dw_one,
        small[0],
        small[1],
        small[2],
        dw_two,
        small[3],
        small[4],
        small[5],
    )


def frame_tables(lengths, frame_mask):
    positions = jnp.arange(frame_mask.shape[0], dtype=jnp.int32)
    offsets = jnp.cumsum(lengths[0]) - lengths[0]
    filled = jnp.sum(lengths[0])
    begins = jnp.any(positions[:, None] == offsets[None, :], axis=1)
    continues = jnp.where(begins, 0.0, 1.0).astype(jnp.float32)
    counted = jnp.where((positions < filled) & (frame_mask > 0), 1.0, 0.0).astype(jnp.float32)
    return (continues, counted)


def linear_scan(coef_rows, driving, backwards):
    row_count, length = driving.shape
    block_count = length // block_span
    factor = coef_rows.reshape(row_count, block_count, block_span)
    running = driving.reshape(row_count, block_count, block_span)
    places = jnp.arange(block_span, dtype=jnp.int32)
    step = 1
    while step < block_span:
        if backwards:
            mover = jnp.where(places[:, None] == places[None, :] + step, 1.0, 0.0).astype(
                jnp.float32
            )
            edge = jnp.where(places >= block_span - step, 1.0, 0.0).astype(jnp.float32)
        else:
            mover = jnp.where(places[:, None] == places[None, :] - step, 1.0, 0.0).astype(
                jnp.float32
            )
            edge = jnp.where(places < step, 1.0, 0.0).astype(jnp.float32)
        moved_factor = (
            jnp.dot(
                factor, mover, precision=lax.Precision.HIGHEST, preferred_element_type=jnp.float32
            )
            + edge
        )
        moved_running = jnp.dot(
            running, mover, precision=lax.Precision.HIGHEST, preferred_element_type=jnp.float32
        )
        running = factor * moved_running + running
        factor = factor * moved_factor
        step = step * 2
    end_place = 0 if backwards else block_span - 1
    total_factor = factor[:, :, end_place].T
    total_running = running[:, :, end_place].T

    def carry_step(carried, block_pair):
        return (block_pair[0] * carried + block_pair[1], carried)

    _, entering = lax.scan(
        carry_step,
        jnp.zeros((row_count,), jnp.float32),
        (total_factor, total_running),
        reverse=backwards,
    )
    result = running + factor * entering.T[:, :, None]
    return result.reshape(row_count, length)


def layer_forward(layer_input, weight, gain_row, bias_row, decay_rate, continues, counted):
    frames_in = lax.all_to_all(layer_input, "neur", split_axis=1, concat_axis=0, tiled=True)
    projected = jnp.dot(
        lax.all_gather(weight, "neur", axis=0, tiled=True),
        frames_in,
        preferred_element_type=jnp.float32,
    )
    neuron_proj = lax.all_to_all(
        projected.astype(jnp.bfloat16), "neur", split_axis=0, concat_axis=1, tiled=True
    ).astype(jnp.float32)
    sum_first = jnp.sum(counted[None, :] * neuron_proj, axis=1)
    sum_second = jnp.sum(counted[None, :] * neuron_proj * neuron_proj, axis=1)
    sum_first, sum_second, frames = lax.psum((sum_first, sum_second, jnp.sum(counted)), "seq")
    average = sum_first / frames
    inv_std = lax.rsqrt(sum_second / frames - average * average + epsilon)
    normed = (neuron_proj - average[:, None]) * inv_std[:, None]
    spread = jnp.sqrt(1.0 - decay_rate * decay_rate)
    states = linear_scan(
        decay_rate[:, None] * continues[None, :], (spread * gain_row)[:, None] * normed, False
    )
    layer_out = counted[None, :] * jax.nn.softplus(states + bias_row[:, None])
    return (layer_out, (frames_in, None, normed, inv_std, frames, states))


def layer_backward(
    upstream, weight, gain_row, bias_row, decay_rate, continues, counted, kept_state
):
    frames_in, full_weight, normed, inv_std, frames, states = kept_state
    local_grad = upstream * counted[None, :] * jax.nn.sigmoid(states + bias_row[:, None])
    following = jnp.concatenate([continues[1:], jnp.zeros((1,), jnp.float32)])
    coef_rows = decay_rate[:, None] * following[None, :]
    state_grad = linear_scan(coef_rows, local_grad, True)
    sum_rec, sum_rec_norm, sum_local = lax.psum(
        (
            jnp.sum(state_grad, axis=1),
            jnp.sum(state_grad * normed, axis=1),
            jnp.sum(local_grad, axis=1),
        ),
        "seq",
    )
    spread = jnp.sqrt(1.0 - decay_rate * decay_rate)
    gain_grad = spread * sum_rec_norm
    proj_grad = (spread * gain_row * inv_std)[:, None] * (
        state_grad - counted[None, :] * (sum_rec[:, None] + sum_rec_norm[:, None] * normed) / frames
    )
    driving = (spread * gain_row)[:, None] * normed
    decay_part = jnp.sum(state_grad * (states - driving), axis=1) / decay_rate
    grad_frames = lax.all_to_all(
        proj_grad.astype(jnp.bfloat16), "neur", split_axis=1, concat_axis=0, tiled=True
    )
    grad_rows = grad_frames
    input_frames = jnp.einsum(
        "ot,oi->it",
        grad_rows,
        lax.all_gather(weight, "neur", axis=0, tiled=True),
        preferred_element_type=jnp.float32,
    )
    input_grad = lax.all_to_all(
        input_frames.astype(jnp.bfloat16), "neur", split_axis=0, concat_axis=1, tiled=True
    ).astype(jnp.float32)
    grad_rows = grad_frames
    weight_rows = lax.psum_scatter(
        jnp.einsum("ot,it->oi", grad_rows, frames_in, preferred_element_type=jnp.float32),
        "neur",
        scatter_dimension=0,
        tiled=True,
    )
    weight_grad, decay_sum = lax.psum((weight_rows, decay_part), "seq")
    decay_grad = decay_sum - decay_rate / spread * gain_row * sum_rec_norm
    return (input_grad, weight_grad, gain_grad, sum_local, decay_grad)


def shards(
    inputs,
    weight_one,
    weight_two,
    gain_one,
    gain_two,
    bias_one,
    bias_two,
    decay_one,
    decay_two,
    lengths,
    frame_mask,
    out_grad,
):
    seqs, n = lax.axis_size("seq"), lax.axis_size("neur")
    H, (fb, tok) = weight_one.shape[1], inputs.shape
    if fits(n, seqs, H, fb, tok):
        params = (gain_one, gain_two, bias_one, bias_two, decay_one, decay_two)
        return frames_apart(
            Sizes(n, seqs, H, fb, tok),
            inputs,
            weight_one,
            weight_two,
            params,
            lengths,
            frame_mask,
            out_grad,
        )
    continues, counted = frame_tables(lengths, frame_mask)
    first_out, first_kept = layer_forward(
        inputs, weight_one, gain_one, bias_one, decay_one, continues, counted
    )
    second_out, second_kept = layer_forward(
        first_out.astype(jnp.bfloat16),
        weight_two,
        gain_two,
        bias_two,
        decay_two,
        continues,
        counted,
    )
    output = inputs.astype(jnp.float32) + second_out
    upstream = out_grad.astype(jnp.float32)
    middle_grad, weight_two_grad, gain_two_grad, bias_two_grad, decay_two_grad = layer_backward(
        upstream, weight_two, gain_two, bias_two, decay_two, continues, counted, second_kept
    )
    lower_grad, weight_one_grad, gain_one_grad, bias_one_grad, decay_one_grad = layer_backward(
        middle_grad, weight_one, gain_one, bias_one, decay_one, continues, counted, first_kept
    )
    return (
        output,
        upstream + lower_grad,
        weight_one_grad,
        gain_one_grad,
        bias_one_grad,
        decay_one_grad,
        weight_two_grad,
        gain_two_grad,
        bias_two_grad,
        decay_two_grad,
    )


def solution(mesh):
    placed = (
        P("neur", "seq"),
        P("neur", None),
        P("neur", None),
        P("neur"),
        P("neur"),
        P("neur"),
        P("neur"),
        P("neur"),
        P("neur"),
        P("seq", None),
        P("seq"),
        P("neur", "seq"),
    )
    return jax.shard_map(
        shards,
        mesh=mesh,
        in_specs=placed,
        out_specs=(
            P("neur", "seq"),
            P("neur", "seq"),
            P("neur", None),
            P("neur"),
            P("neur"),
            P("neur"),
            P("neur", None),
            P("neur"),
            P("neur"),
            P("neur"),
        ),
        check_vma=False,
    )
```

```python
import functools

import jax
import jax.numpy as jnp
from jax import lax
from jax.experimental import pallas as pl
from jax.experimental.pallas import tpu as pltpu
from jax.sharding import PartitionSpec as P

epsilon = 1e-05
block_span = 128
valid_frames = 3584
f32 = jnp.float32
bf16 = jnp.bfloat16
MESH = pl.DeviceIdType.MESH


def wide(tile, width):
    return jnp.concatenate([tile] * (width // 128), axis=1)


def at(index, size):
    if isinstance(index, int):
        return pl.ds(index * size, size)
    return pl.ds(pl.multiple_of(index * size, size), size)


def power(base, exponent):
    result = None
    while exponent:
        if exponent % 2:
            result = base if result is None else result * base
        exponent //= 2
        base = base * base
    return result


def log_of(rate):
    u = 1.0 - rate
    series = jnp.full_like(u, 1.0 / 8)
    for order in range(7, 0, -1):
        series = series * u + 1.0 / order
    return -u * series


GAIN, BIAS, DECAY = 0, 2, 4


class Sizes:
    def __init__(self, n, seqs, H, fb, tok_dev):
        self.n, self.seqs, self.H, self.fb, self.tok_dev = n, seqs, H, fb, tok_dev
        self.T = valid_frames // n
        self.steps = self.T // 8
        self.valid = valid_frames
        self.qc = H // seqs
        self.Z = n // 2
        self.odd = self.T % 128
        self.win = self.T + self.odd
        self.K = self.T + 16
        self.L = min(512, H)


def fits(n, seqs, H, fb, tok_dev):
    if n not in (4, 8) or valid_frames % n or seqs != 4 or fb * n != H or fb % 128 or H % 512:
        return False
    T = valid_frames // n
    return T % 64 == 0 and valid_frames % 128 == 0 and tok_dev >= valid_frames


class Line:
    def __init__(self, env, sends, recvs):
        self.env, self.sends, self.recvs = env, sends, recvs

    def copy(self, k, source, dest, target):
        return pltpu.make_async_remote_copy(
            src_ref=source,
            dst_ref=dest,
            send_sem=self.sends.at[k],
            recv_sem=self.recvs.at[k],
            device_id=target,
            device_id_type=MESH,
        )

    def arrived(self, k, ref):
        self.copy(k, ref, ref, self.env.across("x")).wait_recv()

    def sent(self, k, ref):
        self.copy(k, ref, ref, self.env.across("x")).wait_send()

    def along(self, dz):
        z, Z = self.env.z, self.env.sz.Z
        if dz == 0:
            return [(None, z, 0)]
        return [(z >= dz, z - dz, 1), (z + dz < Z, z + dz, -1)]


def if_so(condition, body):
    if condition is None:
        body()
    else:
        pl.when(condition)(body)


class Gather(Line):
    def __init__(self, env, source, full, sends, recvs, cut):
        super().__init__(env, sends, recvs)
        self.cut = cut
        self.full = full
        self.source = source.at[:, at(env.s, env.sz.qc)]

    def block(self, zz, fx, fy, fc=0):
        env = self.env
        rows = at(2 * zz + (env.x + fx) % 2, env.sz.fb)
        return self.full.at[rows, at(2 * ((env.y + fy) % 2) + (env.c + fc) % 2, env.sz.qc)]

    def half(self, ref, h):
        if h == 0:
            return ref.at[pl.ds(0, self.cut), :]
        return ref.at[pl.ds(self.cut, self.env.sz.fb - self.cut), :]

    def spread(self, zz, source):
        env, Z = self.env, self.env.sz.Z
        dest = self.block(zz, 0, 0)
        self.copy(2 * Z + zz, source, dest, env.across("x")).start()
        self.copy(3 * Z + zz, source, dest, env.across("y")).start()
        self.copy(6 * Z + zz, source, dest, env.across("core")).start()

    def pass_on(self, zz, source, way):
        env, Z = self.env, self.env.sz.Z
        dest = self.block(zz, 0, 0)

        def go():
            pltpu.make_async_remote_copy(
                src_ref=source,
                dst_ref=dest,
                send_sem=self.sends.at[zz if way > 0 else Z + zz],
                recv_sem=self.recvs.at[zz],
                device_id={"neur": 2 * (env.z + way) + env.x},
                device_id_type=MESH,
            ).start()

        pl.when(env.z < Z - 1 if way > 0 else env.z > 0)(go)

    def start(self):
        z = self.env.z
        self.pass_on(z, self.source, 1)
        self.pass_on(z, self.source, -1)
        self.spread(z, self.source)

    def line(self, dz):
        for condition, zz, way in self.along(dz):

            def one(zz=zz, way=way):
                block = self.block(zz, 0, 0)
                self.arrived(zz, block)
                self.pass_on(zz, block, way)
                self.spread(zz, block)

            if_so(condition, one)

    def sides(self, dz):
        env, Z = self.env, self.env.sz.Z
        for condition, zz, _ in self.along(dz):

            def one(zz=zz):
                block = self.block(zz, 1, 0)
                self.arrived(2 * Z + zz, block)
                part = self.half(block, 1)
                self.copy(5 * Z + zz, part, part, env.across("y")).start()
                self.copy(7 * Z + zz, block, block, env.across("core")).start()
                block = self.block(zz, 0, 1)
                self.arrived(3 * Z + zz, block)
                part = self.half(block, 0)
                self.copy(4 * Z + zz, part, part, env.across("x")).start()
                self.copy(8 * Z + zz, block, block, env.across("core")).start()

            if_so(condition, one)

    def diagonals(self):
        env, Z = self.env, self.env.sz.Z
        for dz in range(Z):
            for condition, zz, _ in self.along(dz):

                def one(zz=zz):
                    block = self.block(zz, 1, 1)
                    self.arrived(4 * Z + zz, self.half(block, 0))
                    self.arrived(5 * Z + zz, self.half(block, 1))
                    self.copy(9 * Z + zz, block, block, env.across("core")).start()

                if_so(condition, one)

    def cores(self):
        Z = self.env.sz.Z
        for k, (fx, fy) in enumerate(((0, 0), (1, 0), (0, 1), (1, 1))):
            for zz in range(Z):
                self.arrived((6 + k) * Z + zz, self.block(zz, fx, fy, 1))

    def drain(self):
        env, Z = self.env, self.env.sz.Z
        block = self.block(0, 0, 0)
        for zz in range(Z):
            pl.when((zz <= env.z) & (env.z < Z - 1))(lambda zz=zz: self.sent(zz, block))
            pl.when((zz >= env.z) & (env.z > 0))(lambda zz=zz: self.sent(Z + zz, block))
            for k in (2, 3, 6, 7, 8, 9):
                self.sent(k * Z + zz, block)
            self.sent(4 * Z + zz, self.half(block, 0))
            self.sent(5 * Z + zz, self.half(block, 1))


class Reduce(Line):
    kinds = ((1, 1), (1, 0), (0, 1), (0, 0))

    def __init__(self, env, grads, frames, land, spare, stage, held, total, sends, recvs, cut):
        super().__init__(env, sends, recvs)
        self.cut, self.held = cut, held
        self.grads, self.frames, self.land, self.spare = grads, frames, land, spare
        self.stage, self.total = stage, total

    def product(self, kind, zz, fc=0):
        env, sz = self.env, self.env.sz
        fx, fy = self.kinds[kind]
        rows = at(2 * zz + (env.x + fx) % 2, sz.fb)
        columns = at(2 * ((env.y + fy) % 2) + (env.c + fc) % 2, sz.qc)
        return jnp.dot(
            self.grads[rows, :], self.frames[:, columns], preferred_element_type=f32
        )

    def half(self, ref, h):
        if h == 0:
            return ref.at[pl.ds(0, self.cut), :]
        return ref.at[pl.ds(self.cut, self.env.sz.fb - self.cut), :]

    def landed(self, k, slot):
        self.arrived(k, self.land(slot))
        return self.land(slot)[...].astype(f32)

    def turn(self, i):
        z, Z = self.env.z, self.env.sz.Z
        low = jnp.where(i < Z - 1 - z, Z - 1 - i, i - (Z - 1 - z))
        high = jnp.where(i < z, i, Z - 1 - (i - z))
        return jnp.where(i == Z - 1, z, jnp.where(z < Z // 2, low, high))

    def cores(self, kind):
        env, Z = self.env, self.env.sz.Z

        def one(i, _):
            zz = self.turn(i)
            k = kind * Z + zz
            held = (kind % 2) * Z + zz
            if kind >= 2:
                self.sent(k - 2 * Z, self.stage.at[held])
            self.stage[held] = self.product(kind, zz, 1).astype(bf16)
            self.copy(k, self.stage.at[held], self.land(k), env.across("core")).start()
            return 0

        lax.fori_loop(0, Z, one, 0)

    def diagonals(self):
        env, Z = self.env, self.env.sz.Z

        def one(i, _):
            zz = self.turn(i)
            held = self.held(zz)
            held[...] = (self.product(0, zz) + self.landed(zz, zz)).astype(bf16)
            slot = self.land(4 * Z + zz)
            for k, h, axis in ((4, 0, "x"), (5, 1, "y")):
                self.copy(
                    k * Z + zz, self.half(held, h), self.half(slot, h), env.across(axis)
                ).start()
            return 0

        lax.fori_loop(0, Z, one, 0)

    def sides(self, low=0, high=None):
        env, Z = self.env, self.env.sz.Z
        spans = slice(0, self.cut), slice(self.cut, env.sz.fb)

        def one(i, _):
            zz = self.turn(i)
            slot = self.land(4 * Z + zz)
            for kind, h, wait, k, axis in ((1, 1, 5, 6, "x"), (2, 0, 4, 7, "y")):
                tile = self.product(kind, zz) + self.landed(kind * Z + zz, kind * Z + zz)
                part = self.half(slot, h)
                self.arrived(wait * Z + zz, part)
                held = self.stage.at[(2 + kind) * Z + zz]
                other = 1 - h
                summed = tile[spans[h], :] + part[...].astype(f32)
                self.half(held, h)[...] = summed.astype(bf16)
                self.half(held, other)[...] = tile[spans[other], :].astype(bf16)
                self.copy(
                    k * Z + zz, held, self.land((4 + kind) * Z + zz), env.across(axis)
                ).start()
            return 0

        lax.fori_loop(low, Z if high is None else high, one, 0)

    def joined(self, zz):
        Z = self.env.sz.Z
        tile = self.product(3, zz) + self.landed(3 * Z + zz, 3 * Z + zz)
        tile = tile + self.landed(6 * Z + zz, 5 * Z + zz)
        self.total[...] = tile + self.landed(7 * Z + zz, 6 * Z + zz)

    def lines(self, low=0, high=None):
        env, Z, z = self.env, self.env.sz.Z, self.env.z
        def onward(zz, way):
            k, slot = (8 if way > 0 else 9) * Z + zz, 7 * Z + zz
            self.joined(zz)

            @pl.when(z > 0 if way > 0 else z < Z - 1)
            def _():
                self.total[...] += self.landed(k, slot)

            held = self.held(zz)
            self.sent(4 * Z + zz, self.half(held, 0))
            self.sent(5 * Z + zz, self.half(held, 1))
            held[...] = self.total[...].astype(bf16)
            target = {"neur": 2 * (z + way) + env.x}
            if way > 0:
                self.copy(k, held, self.land(slot), target).start()
            else:
                pl.when(zz == z - 1)(lambda: self.copy(k, held, self.spare, target).start())
                pl.when(zz != z - 1)(lambda: self.copy(k, held, self.land(slot), target).start())

        for i in range(low, Z - 1 if high is None else high):
            zz = self.turn(i)
            pl.when(zz > z)(functools.partial(onward, zz, 1))
            pl.when(zz < z)(functools.partial(onward, zz, -1))

    def finish(self):
        Z, z = self.env.sz.Z, self.env.z
        self.joined(z)
        @pl.when(z > 0)
        def _():
            self.total[...] += self.landed(8 * Z + z, 7 * Z + z)

        @pl.when(z < Z - 1)
        def _():
            self.arrived(9 * Z + z, self.spare)
            self.total[...] += self.spare[...].astype(f32)

    def drain_cores(self):
        for k in range(2 * self.env.sz.Z, 4 * self.env.sz.Z):
            self.sent(k, self.stage.at[0])

    def drain_sides(self):
        for k in range(6 * self.env.sz.Z, 8 * self.env.sz.Z):
            self.sent(k, self.stage.at[0])

    def drain(self):
        Z, z = self.env.sz.Z, self.env.z
        held = self.stage.at[0]
        for zz in range(Z):
            for k in (4, 5):
                pl.when(zz == z)(
                    lambda k=k, zz=zz: self.sent(k * Z + zz, self.half(held, k - 4))
                )
            pl.when(zz > z)(lambda zz=zz: self.sent(8 * Z + zz, held))
            pl.when(zz < z)(lambda zz=zz: self.sent(9 * Z + zz, held))


class Result:
    def __init__(self, env, whole, block, sends, recvs, local):
        self.env, self.whole, self.block = env, whole, block
        self.sends, self.recvs, self.local = sends, recvs, local

    def part(self, flip_y, flip_c):
        env = self.env
        s = 2 * ((env.y + flip_y) % 2) + (env.c + flip_c) % 2
        return self.whole.at[:, at(s, env.sz.qc)]

    def copy(self, k, source, dest, target):
        return pltpu.make_async_remote_copy(
            src_ref=source,
            dst_ref=dest,
            send_sem=self.sends.at[k],
            recv_sem=self.recvs.at[k],
            device_id=target,
            device_id_type=MESH,
        )

    def start(self):
        env, own = self.env, self.part(0, 0)
        self.copy(0, self.block, own, env.across("y")).start()
        self.copy(1, self.block, own, env.across("core")).start()
        pltpu.make_async_copy(self.block, own, self.local).start()

    def finish(self):
        env = self.env
        other = self.part(1, 0)
        self.copy(0, self.block, other, env.across("y")).wait_recv()
        forward = self.copy(2, other, other, env.across("core"))
        forward.start()
        own = self.part(0, 0)
        pltpu.make_async_copy(self.block, own, self.local).wait()
        self.copy(0, self.block, own, env.across("y")).wait_send()
        self.copy(1, self.block, self.part(0, 1), env.across("core")).wait()
        forward.wait_send()
        self.copy(2, other, self.part(1, 1), env.across("core")).wait_recv()


class Env:
    def across(self, axis):
        if axis == "x":
            return {"neur": 2 * self.z + 1 - self.x}
        if axis == "y":
            return {"seq": 2 * (1 - self.y) + self.c}
        return {"seq": 2 * self.y + 1 - self.c}


def network(
    sz,
    x_hbm,
    g_hbm,
    w_one,
    w_two,
    gain_one,
    gain_two,
    bias_one,
    bias_two,
    decay_one,
    decay_two,
    lengths,
    frame_mask,
    out_land,
    dx_land,
    dw_one,
    dw_two,
    small,
    own_par,
    cont,
    counted,
    aux,
    frames_sum,
    raw,
    perm,
    eye,
    xs,
    gs,
    xr,
    gr,
    p_one,
    p_two,
    x_two,
    dp,
    dpt_one,
    dpt_two,
    s_one,
    s_two,
    wf_one,
    wf_two,
    land,
    stage,
    spare,
    fin,
    par,
    ends,
    work,
    pay,
    arrive,
    seqpay,
    seqland,
    back,
    backland,
    sumpay,
    sumland,
    sumseq,
    sumseqland,
    local_sems,
    par_sends,
    par_recvs,
    frame_sends,
    frame_recvs,
    gather_sends,
    gather_recvs,
    hop_sends,
    hop_recvs,
    seq_sends,
    seq_recvs,
    reduce_sends,
    reduce_recvs,
    final_sends,
    final_recvs,
    sum_sends,
    sum_recvs,
):
    n, seqs, H, fb, T, steps, L = sz.n, sz.seqs, sz.H, sz.fb, sz.T, sz.steps, sz.L
    env = Env()
    env.sz = sz
    me = lax.axis_index("neur")
    mine = lax.axis_index("seq")
    env.j, env.s = me, mine
    env.z, env.x, env.y, env.c = me // 2, me % 2, mine // 2, mine % 2

    barrier = pltpu.get_barrier_semaphore()
    for o in range(1, n):
        pl.semaphore_signal(
            barrier, inc=1, device_id={"neur": (me + o) % n}, device_id_type=MESH
        )
    for o in range(1, seqs):
        pl.semaphore_signal(
            barrier, inc=1, device_id={"seq": (mine + o) % seqs}, device_id_type=MESH
        )
    load_x = pltpu.make_async_copy(x_hbm.at[:, pl.ds(0, sz.valid)], raw, local_sems.at[0])
    load_x.start()
    for r, values in enumerate((gain_one, gain_two, bias_one, bias_two, decay_one, decay_two)):
        own_par[r : r + 1, :] = values[...]
    own_par[6:8, :] = jnp.zeros((2, fb), f32)
    pl.semaphore_wait(barrier, n - 1 + seqs - 1)

    def neur_copy(source, dest, send, recv, i):
        return pltpu.make_async_remote_copy(
            src_ref=source,
            dst_ref=dest,
            send_sem=send,
            recv_sem=recv,
            device_id={"neur": i},
            device_id_type=MESH,
        )

    def seq_copy(source, dest, send, recv, i):
        return pltpu.make_async_remote_copy(
            src_ref=source,
            dst_ref=dest,
            send_sem=send,
            recv_sem=recv,
            device_id={"seq": i},
            device_id_type=MESH,
        )

    def straight(body):
        lax.fori_loop(1, n // 2, lambda o, _: (body((me + 2 * o) % n), 0)[1], 0)

    def crossing(body, low=0, high=n // 2):
        lax.fori_loop(low, high, lambda o, _: (body((me + 2 * o + 1) % n), 0)[1], 0)

    def others(body, count=n, own=me):
        def one(o, _):
            body((own + o) % count)
            return 0

        lax.fori_loop(1, count, one, 0)

    own_lanes = at(me, fb)

    def par_copy(i):
        return neur_copy(own_par, par.at[:, own_lanes], par_sends.at[i], par_recvs.at[me], i)

    def par_wait(i):
        neur_copy(own_par, par.at[:, at(i, fb)], par_sends.at[i], par_recvs.at[i], i).wait()

    others(lambda i: par_copy(i).start())
    par[:, own_lanes] = own_par[...]

    cuts = (fb // 4, 3 * fb // 8)
    gather_one = Gather(env, w_one, wf_one, gather_sends.at[0], gather_recvs.at[0], cuts[0])
    gather_two = Gather(env, w_two, wf_two, gather_sends.at[1], gather_recvs.at[1], cuts[1])
    own_one = pltpu.make_async_copy(gather_one.source, gather_one.block(env.z, 0, 0), local_sems.at[2])
    own_two = pltpu.make_async_copy(gather_two.source, gather_two.block(env.z, 0, 0), local_sems.at[3])
    own_one.start()
    own_two.start()
    gather_one.start()
    gather_two.start()

    row = lax.broadcasted_iota(jnp.int32, (T, sz.win), 0)
    column = lax.broadcasted_iota(jnp.int32, (T, sz.win), 1)
    frame = (row & 7) * steps + (row >> 3)
    perm[0] = jnp.where(column == frame, 1.0, 0.0).astype(bf16)
    perm[1] = jnp.where(column == frame + sz.odd, 1.0, 0.0).astype(bf16)
    row = lax.broadcasted_iota(jnp.int32, (fb, fb), 0)
    column = lax.broadcasted_iota(jnp.int32, (fb, fb), 1)
    eye[...] = jnp.where(row == column, 1.0, 0.0).astype(bf16)

    def window(i):
        start = (i // 2) * (2 * T) + (i % 2) * (T - sz.odd)
        return pl.ds(pl.multiple_of(start, 128), sz.win)

    def turned(i):
        return lax.dot_general(
            perm[i % 2], raw[:, window(i)], (((1,), (1,)), ((), ())), preferred_element_type=f32
        ).astype(bf16)

    def frames_copy(a, source, dest, i):
        return neur_copy(source, dest, frame_sends.at[a, i], frame_recvs.at[a, me], i)

    def frames_wait(a, ref, i):
        part = ref.at[pl.ds(0, T), at(i, fb)]
        neur_copy(part, part, frame_sends.at[a, i], frame_recvs.at[a, i], i).wait_recv()

    def frames_sent(a, ref, i):
        part = ref.at[pl.ds(0, T), at(i, fb)]
        neur_copy(part, part, frame_sends.at[a, i], frame_recvs.at[a, i], i).wait_send()

    load_x.wait()

    def turn_x(i):
        xs[:, at(i, fb)] = turned(i)

    def send_x(i):
        frames_copy(0, xs.at[:, at(i, fb)], xr.at[pl.ds(0, T), own_lanes], i).start()

    def send_all_x():
        crossing(send_x)
        straight(send_x)

    others(turn_x)
    xr[0:T, own_lanes] = turned(me)
    load_g = pltpu.make_async_copy(g_hbm.at[:, pl.ds(0, sz.valid)], raw, local_sems.at[1])
    load_g.start()
    ends_of_line = (env.z == 0) | (env.z == sz.Z - 1)
    pl.when(ends_of_line)(send_all_x)
    for dz in range(1, sz.Z):
        gather_one.line(dz)
        gather_two.line(dz)
        if dz == max(1, sz.Z - 2):
            pl.when(jnp.logical_not(ends_of_line))(send_all_x)
        gather_one.sides(dz - 1)
    frame_tables_of(sz, me, lengths, frame_mask, perm, window(me), cont, counted, aux)
    load_g.wait()

    def turn_g(i):
        gs[:, at(i, fb)] = turned(i)

    def send_g(i):
        frames_copy(1, gs.at[:, at(i, fb)], gr.at[:, own_lanes], i).start()

    others(turn_g)
    gr[:, own_lanes] = turned(me)
    gather_one.sides(sz.Z - 1)
    gather_two.sides(0)
    straight(send_g)
    crossing(send_g, 0, 1)
    gather_one.diagonals()
    for dz in range(1, sz.Z - 1):
        gather_two.sides(dz)
    gather_one.cores()
    own_one.wait()
    own_two.wait()
    others(lambda i: frames_wait(0, xr, i))
    others(par_wait)

    def blocks(body):
        def one(b, _):
            body(at(b, L))
            return 0

        lax.fori_loop(0, H // L, one, 0)

    def project(frames, weight, result):
        def one(b, _):
            result[:, at(b, 2 * fb)] = lax.dot_general(
                frames[0:T, :],
                weight[at(b, 2 * fb), :],
                (((1,), (1,)), ((), ())),
                preferred_element_type=f32,
            ).astype(bf16)
            return 0

        lax.fori_loop(0, n // 2, one, 0)

    def flags(t):
        tile = pl.ds(pl.multiple_of(8 * t, 8), 8)
        return wide(cont[tile, :], L), wide(counted[tile, :], L)

    def spread8(ref, r, cols, width=L):
        return jnp.broadcast_to(ref[r : r + 1, cols], (8, width))

    zero = jnp.zeros((8, L), f32)

    def down(value):
        return jnp.sum(value, axis=0, keepdims=True)

    def exchange(e, gathered, totalled, gap):
        ahead = pl.ds(0, 4 if e < 2 else 8)
        behind = pl.ds(0, 4)

        def out_copy(i):
            return neur_copy(
                pay.at[e, ahead, at(i, fb)],
                arrive.at[e, me, ahead],
                hop_sends.at[2 * e, i],
                hop_recvs.at[2 * e, me],
                i,
            )

        others(lambda i: out_copy(i).start())
        arrive[e, me, ahead] = pay[e, ahead, own_lanes]
        gap("hop_a")

        def out_wait(i):
            neur_copy(
                pay.at[e, ahead, at(i, fb)],
                arrive.at[e, i, ahead],
                hop_sends.at[2 * e, i],
                hop_recvs.at[2 * e, i],
                i,
            ).wait()

        others(out_wait)
        gathered()

        def along_copy(i):
            return seq_copy(
                seqpay.at[e],
                seqland.at[e, mine],
                seq_sends.at[e, i],
                seq_recvs.at[e, mine],
                i,
            )

        def along_wait(i):
            seq_copy(
                seqpay.at[e], seqland.at[e, i], seq_sends.at[e, i], seq_recvs.at[e, i], i
            ).wait()

        others(lambda i: along_copy(i).start(), seqs, mine)
        seqland[e, mine] = seqpay[e]
        gap("hop_b")
        others(along_wait, seqs, mine)
        sums = seqland[e, 0]
        for i in range(1, seqs):
            sums = sums + seqland[e, i]
        totalled(sums)

        def back_copy(i):
            return neur_copy(
                back.at[e, i, behind],
                backland.at[e, behind, own_lanes],
                hop_sends.at[2 * e + 1, i],
                hop_recvs.at[2 * e + 1, me],
                i,
            )

        def back_wait(i):
            neur_copy(
                back.at[e, i, behind],
                backland.at[e, behind, at(i, fb)],
                hop_sends.at[2 * e + 1, i],
                hop_recvs.at[2 * e + 1, i],
                i,
            ).wait()

        others(lambda i: back_copy(i).start())
        backland[e, behind, own_lanes] = back[e, me, behind]
        gap("hop_c")
        others(back_wait)

    def layer_forward(layer, frames, weight, projected, states, store, gap):
        e = layer
        decay_row, gain_row, bias_row = DECAY + layer, GAIN + layer, BIAS + layer
        project(frames, weight, projected)
        gap("ends")

        def local_ends(cols):
            decay = spread8(par, decay_row, cols)

            def step(i, carry):
                state, first, second, inward = carry
                pair = projected[pl.ds(pl.multiple_of(16 * i, 16), 16), cols].astype(f32)
                for h in range(2):
                    value = pair[8 * h : 8 * h + 8, :]
                    goes, count = flags(2 * i + h)
                    state = (decay * goes) * state + value
                    held = count * value
                    first = first + held
                    second = second + held * value
                ins = frames[pl.ds(pl.multiple_of(16 * i, 16), 16), cols].astype(f32)
                return state, first, second, inward + ins[0:8, :] + ins[8:16, :]

            state, first, second, inward = lax.fori_loop(
                0, T // 16, step, (zero, zero, zero, zero)
            )
            ends[:, cols] = state
            pay[e, 1:2, cols] = down(first)
            pay[e, 2:3, cols] = down(second)
            pay[e, 3:4, cols] = down(inward)

        blocks(local_ends)
        run_power = power(par[decay_row : decay_row + 1, :], steps)
        total = jnp.zeros((1, H), f32)
        for k in range(8):
            total = run_power * wide(aux[16 + k : 17 + k, :], H) * total + ends[k : k + 1, :]
        pay[e, 0:1, :] = total

        own_decay = own_par[decay_row : decay_row + 1, :]

        def gathered():
            whole_power = power(own_decay, T)
            carried = jnp.zeros((1, fb), f32)
            sums = jnp.zeros((4, fb), f32)
            for i in range(n):
                rows = arrive[e, i, 0:4, :]
                back[e, i, 0:1, :] = carried
                carried = whole_power * wide(aux[8 + i : 9 + i, :], fb) * carried + rows[0:1, :]
                sums = sums + rows
            seqpay[e, 0:4, :] = sums
            seqpay[e, 4:8, :] = jnp.zeros((4, fb), f32)
            seqpay[e, 0:1, :] = wide(aux[24:25, :], fb)

        def totalled(sums):
            frames_all = sums[0:1, :]
            average = sums[1:2, :] / frames_all
            inv_std = lax.rsqrt(sums[2:3, :] / frames_all - average * average + epsilon)
            centre = sums[3:4, :] / (sz.valid * seqs)
            for i in range(n):
                back[e, i, 1:2, :] = average
                back[e, i, 2:3, :] = inv_std
                back[e, i, 3:4, :] = centre
            frames_sum[...] = frames_all[:, 0:128]

        exchange(e, gathered, totalled, gap)
        centre = backland[e, 3:4, :]
        frames[T : T + 16, :] = jnp.concatenate(
            [-centre, -centre, -centre, jnp.zeros((13, H), f32)], axis=0
        ).astype(bf16)

        total = backland[e, 0:1, :]
        for k in range(8):
            work[k : k + 1, :] = total
            total = run_power * wide(aux[16 + k : 17 + k, :], H) * total + ends[k : k + 1, :]

        gap("scan")

        def full_scan(cols):
            decay = spread8(par, decay_row, cols)
            average = spread8(backland.at[e], 1, cols)
            inv_std = spread8(backland.at[e], 2, cols)
            bias = spread8(par, bias_row, cols)
            scale = jnp.sqrt(1.0 - decay * decay) * spread8(par, gain_row, cols) * inv_std
            ones = (1.0 - jnp.exp(wide(aux[0:8, :], L) * log_of(decay))) / (1.0 - decay)
            state = scale * (work[0:8, cols] - average * ones)
            states[0:8, cols] = state

            def step(i, state):
                pair = projected[pl.ds(pl.multiple_of(16 * i, 16), 16), cols].astype(f32)
                outs = []
                for h in range(2):
                    goes, count = flags(2 * i + h)
                    state = (decay * goes) * state + scale * (pair[8 * h : 8 * h + 8, :] - average)
                    states[pl.ds(pl.multiple_of(16 * i + 8 * h + 8, 8), 8), cols] = state
                    v = state + bias
                    soft = jnp.maximum(v, 0.0) + jnp.log(1.0 + jnp.exp(-jnp.abs(v)))
                    outs.append(count * soft)
                store[pl.ds(pl.multiple_of(16 * i, 16), 16), cols] = jnp.concatenate(
                    outs, axis=0
                ).astype(bf16)
                return state

            lax.fori_loop(0, T // 16, step, state)

        blocks(full_scan)

    def layer_backward(layer, upstream, projected, states, turned_grads, gap):
        e = 2 + (1 - layer)
        decay_row, gain_row, bias_row = DECAY + layer, GAIN + layer, BIAS + layer
        run_power = power(par[decay_row : decay_row + 1, :], steps)

        def local_ends(cols):
            decay = spread8(par, decay_row, cols)
            average = spread8(backland.at[layer], 1, cols)
            inv_std = spread8(backland.at[layer], 2, cols)
            bias = spread8(par, bias_row, cols)

            def step(o, carry):
                i = T // 16 - 1 - o
                rows = pl.ds(pl.multiple_of(16 * i, 16), 16)
                pair = projected[rows, cols].astype(f32)
                ups = upstream[rows, cols].astype(f32)
                for h in (1, 0):
                    run, reach, U, V, UN, VN, B, D, DA = carry
                    goes, count = flags(2 * i + h)
                    here = pl.ds(pl.multiple_of(16 * i + 8 * h + 8, 8), 8)
                    state = states[here, cols]
                    before = states[pl.ds(pl.multiple_of(16 * i + 8 * h, 8), 8), cols]
                    local = ups[8 * h : 8 * h + 8, :] * count / (1.0 + jnp.exp(-(state + bias)))
                    states[here, cols] = local
                    normed = (pair[8 * h : 8 * h + 8, :] - average) * inv_std
                    run = local + run
                    kept = goes * before
                    link = decay * goes
                    carry = (
                        link * run,
                        link * reach,
                        U + run,
                        V + reach,
                        UN + run * normed,
                        VN + reach * normed,
                        B + local,
                        D + run * kept,
                        DA + reach * kept,
                    )
                return carry

            one = jnp.ones((8, L), f32)
            run, _, U, V, UN, VN, B, D, DA = lax.fori_loop(
                0, T // 16, step, (zero, one, zero, zero, zero, zero, zero, zero, zero)
            )
            ends[:, cols] = run
            decay_run = power(par[decay_row : decay_row + 1, cols], steps)
            part, factor = jnp.zeros((1, L), f32), jnp.ones((1, L), f32)
            for k in range(7, -1, -1):
                work[k : k + 1, cols] = part
                work[8 + k : 9 + k, cols] = factor
                through = decay_run * wide(aux[16 + k : 17 + k, :], L)
                part = through * part + ends[k : k + 1, cols]
                factor = through * factor
            pay[e, 0:1, cols] = part
            entering, scaled = work[0:8, cols], work[8:16, cols]
            pay[e, 1:2, cols] = down(U + V * entering)
            pay[e, 2:3, cols] = down(V * scaled)
            pay[e, 3:4, cols] = down(UN + VN * entering)
            pay[e, 4:5, cols] = down(VN * scaled)
            pay[e, 5:6, cols] = down(B)
            pay[e, 6:7, cols] = down(D + DA * entering)
            pay[e, 7:8, cols] = down(DA * scaled)

        blocks(local_ends)
        own_decay = own_par[decay_row : decay_row + 1, :]
        own_gain = own_par[gain_row : gain_row + 1, :]

        def gathered():
            whole_power = power(own_decay, T)
            carried = jnp.zeros((1, fb), f32)
            sums = [jnp.zeros((1, fb), f32)] * 4
            for i in range(n - 1, -1, -1):
                rows = arrive[e, i]
                back[e, i, 0:1, :] = carried
                for a, (plain, times) in enumerate(((1, 2), (3, 4), (5, None), (6, 7))):
                    term = rows[plain : plain + 1, :]
                    if times is not None:
                        term = term + rows[times : times + 1, :] * carried
                    sums[a] = sums[a] + term
                carried = whole_power * wide(aux[8 + i : 9 + i, :], fb) * carried + rows[0:1, :]
            for a in range(4):
                seqpay[e, a : a + 1, :] = sums[a]
            seqpay[e, 4:8, :] = jnp.zeros((4, fb), f32)

        def totalled(sums):
            rec, rec_norm = sums[0:1, :], sums[1:2, :]
            for i in range(n):
                back[e, i, 1:2, :] = rec
                back[e, i, 2:3, :] = rec_norm
                back[e, i, 3:4, :] = jnp.zeros((1, fb), f32)
            spread = jnp.sqrt(1.0 - own_decay * own_decay)
            small[3 * layer : 3 * layer + 1, :] = spread * rec_norm
            small[3 * layer + 1 : 3 * layer + 2, :] = sums[2:3, :]
            small[3 * layer + 2 : 3 * layer + 3, :] = (
                sums[3:4, :] - own_decay / spread * own_gain * rec_norm
            )

        exchange(e, gathered, totalled, gap)
        gap("scan")
        total = backland[e, 0:1, :]
        for k in range(7, -1, -1):
            work[k : k + 1, :] = total
            total = run_power * wide(aux[16 + k : 17 + k, :], H) * total + ends[k : k + 1, :]

        def full_scan(cols):
            decay = spread8(par, decay_row, cols)
            average = spread8(backland.at[layer], 1, cols)
            inv_std = spread8(backland.at[layer], 2, cols)
            frames_all = wide(frames_sum[...], L)
            scale = jnp.sqrt(1.0 - decay * decay) * spread8(par, gain_row, cols) * inv_std
            rec = spread8(backland.at[e], 1, cols) / frames_all
            rec_norm = spread8(backland.at[e], 2, cols) / frames_all * inv_std

            def step(o, carry):
                carry, added = carry
                i = T // 16 - 1 - o
                rows = pl.ds(pl.multiple_of(16 * i, 16), 16)
                pair = projected[rows, cols].astype(f32)
                outs = [None, None]
                for h in (1, 0):
                    goes, count = flags(2 * i + h)
                    here = pl.ds(pl.multiple_of(16 * i + 8 * h + 8, 8), 8)
                    run = states[here, cols] + carry
                    centred = pair[8 * h : 8 * h + 8, :] - average
                    outs[h] = scale * (run - count * (rec + rec_norm * centred))
                    carry = (decay * goes) * run
                rounded = jnp.concatenate(outs, axis=0).astype(bf16)
                dp[rows, cols] = rounded
                rounded = rounded.astype(f32)
                return carry, added + rounded[0:8, :] + rounded[8:16, :]

            _, added = lax.fori_loop(0, T // 16, step, (work[0:8, cols], zero))
            whole = down(added)
            sumpay[layer, 0:1, cols] = whole
            high = whole.astype(bf16).astype(f32)
            middle = (whole - high).astype(bf16).astype(f32)
            low = whole - high - middle
            dp[T : T + 16, cols] = jnp.concatenate(
                [high, middle, low, jnp.zeros((13, L), f32)], axis=0
            ).astype(bf16)

        blocks(full_scan)
        sumpay[layer, 1:8, :] = jnp.zeros((7, H), f32)

        def turn(b, _):
            turned_grads[at(b, fb), :] = lax.dot_general(
                eye[...], dp[:, at(b, fb)], (((1,), (1,)), ((), ())), preferred_element_type=f32
            ).astype(bf16)
            return 0

        lax.fori_loop(0, n, turn, 0)

    def input_gradient(weight, result, columns):
        result[:, columns] = jnp.dot(
            dp[0:T, :], weight[:, columns], preferred_element_type=f32
        ).astype(bf16)

    def sum_copy(layer, i):
        return neur_copy(
            sumpay.at[layer, :, at(i, fb)],
            sumland.at[layer, me],
            sum_sends.at[layer, i],
            sum_recvs.at[layer, me],
            i,
        )

    def sum_along(layer, i):
        return seq_copy(
            sumseq.at[layer],
            sumseqland.at[layer, mine],
            sum_sends.at[layer, n + i],
            sum_recvs.at[layer, n + mine],
            i,
        )

    def sum_start(layer):
        others(lambda i: sum_copy(layer, i).start())
        sumland[layer, me] = sumpay[layer, :, own_lanes]

    def sum_middle(layer):
        def wait(i):
            neur_copy(
                sumpay.at[layer, :, at(i, fb)],
                sumland.at[layer, i],
                sum_sends.at[layer, i],
                sum_recvs.at[layer, i],
                i,
            ).wait()

        others(wait)
        total = sumland[layer, 0]
        for i in range(1, n):
            total = total + sumland[layer, i]
        sumseq[layer] = total
        sumseqland[layer, mine] = total
        others(lambda i: sum_along(layer, i).start(), seqs, mine)

    def sum_finish(layer, frames, total):
        def wait(i):
            seq_copy(
                sumseq.at[layer],
                sumseqland.at[layer, i],
                sum_sends.at[layer, n + i],
                sum_recvs.at[layer, n + i],
                i,
            ).wait()

        others(wait, seqs, mine)
        whole = sumseqland[layer, 0]
        for i in range(1, seqs):
            whole = whole + sumseqland[layer, i]
        whole = whole[0:1, :]
        high = whole.astype(bf16).astype(f32)
        middle = (whole - high).astype(bf16).astype(f32)
        low = whole - high - middle
        rows = jnp.concatenate([high, middle, low, jnp.zeros((13, fb), f32)], axis=0).astype(bf16)
        columns = lax.dot_general(
            eye[...], rows, (((1,), (1,)), ((), ())), preferred_element_type=f32
        ).astype(bf16)
        total[...] -= jnp.dot(
            columns, frames[T : T + 16, at(mine, sz.qc)], preferred_element_type=f32
        )

    def place_out(a, ref, dest, i):
        return neur_copy(
            ref.at[:, at(i, fb)], dest.at[me], frame_sends.at[a, i], frame_recvs.at[a, me], i
        )

    def out_arrived(a, ref, dest, i):
        neur_copy(
            ref.at[:, at(i, fb)], dest.at[i], frame_sends.at[a, i], frame_recvs.at[a, i], i
        ).wait()

    def nothing(name):
        return None

    def during_one(name):
        if name == "ends":
            gather_two.sides(sz.Z - 1)
            gather_two.diagonals()
        if name == "scan":
            crossing(send_g, 1, n // 2 - 1)

    def during_two(name):
        if name == "scan":
            crossing(send_g, max(1, n // 2 - 1), n // 2)

    layer_forward(0, xr, wf_one, p_one, s_one, x_two, during_one)
    gather_two.cores()
    others(lambda i: frames_sent(0, xs, i))
    layer_forward(1, x_two, wf_two, p_two, s_two, xs, during_two)

    def send_out(i):
        place_out(2, xs, out_land, i).start()

    keep_out = pltpu.make_async_copy(xs.at[:, own_lanes], out_land.at[me], local_sems.at[4])
    keep_out.start()
    others(lambda i: frames_wait(1, gr, i))
    others(lambda i: frames_sent(1, gs, i))
    gather_two.drain()

    crossing(send_out, 0, 1)
    layer_backward(
        1,
        gr,
        p_two,
        s_two,
        dpt_two,
        lambda name: crossing(send_out, 1, 2) if name == "scan" else None,
    )
    if n > 4:
        crossing(send_out, 2, 3)
    lax.fori_loop(0, n // 2, lambda i, _: (input_gradient(wf_two, gr, at(i, 2 * fb)), 0)[1], 0)
    sum_start(1)
    if n > 4:
        crossing(send_out, 3, 4)
    reduce_two = Reduce(
        env,
        dpt_two,
        x_two,
        lambda k: land.at[k],
        spare.at[1],
        stage,
        lambda k: stage.at[2 * sz.Z + k],
        fin.at[1],
        reduce_sends.at[1],
        reduce_recvs.at[1],
        fb // 2,
    )
    reduce_one = Reduce(
        env,
        dpt_one,
        xr,
        lambda k: wf_two.at[at(k // seqs, fb), at(k % seqs, sz.qc)],
        spare.at[0],
        stage,
        lambda k: raw.at[:, at(k, sz.qc)],
        fin.at[0],
        reduce_sends.at[0],
        reduce_recvs.at[0],
        fb // 2,
    )
    result_two = Result(
        env, dw_two, land.at[1], final_sends.at[1], final_recvs.at[1], local_sems.at[6]
    )
    result_one = Result(
        env, dw_one, land.at[0], final_sends.at[0], final_recvs.at[0], local_sems.at[7]
    )
    for kind in range(4):
        reduce_two.cores(kind)

    def meanwhile(name):
        if name == "hop_b":
            sum_middle(1)
        if name == "scan":
            reduce_two.diagonals()
            straight(send_out)

    layer_backward(0, gr, p_one, s_one, dpt_one, meanwhile)
    reduce_two.drain_cores()
    reduce_one.cores(0)
    reduce_two.sides()
    reduce_one.diagonals()
    for kind in range(1, 4):
        reduce_one.cores(kind)
    sum_start(0)

    def send_dx(i):
        place_out(3, gs, dx_land, i).start()

    def make_dx(i):
        input_gradient(wf_one, gs, at(i, fb))

    def make_and_send_dx(i):
        make_dx(i)
        send_dx(i)

    straight(make_and_send_dx)
    crossing(make_dx)
    make_dx(me)
    keep_dx = pltpu.make_async_copy(gs.at[:, own_lanes], dx_land.at[me], local_sems.at[5])
    keep_dx.start()
    reduce_two.lines()
    sum_middle(0)
    reduce_two.drain_sides()
    reduce_one.sides(0, 2)
    for i in range(2, sz.Z):
        reduce_one.lines(i - 2, i - 1)
        reduce_one.sides(i, i + 1)
        if i == 2:
            crossing(send_dx, 0, n // 4)
    crossing(send_dx, n // 4 if sz.Z > 2 else 0, n // 2)
    reduce_two.finish()
    sum_finish(1, x_two, fin.at[1])
    land[1] = fin[1].astype(bf16)
    result_two.start()
    reduce_one.lines(sz.Z - 2, sz.Z - 1)
    reduce_one.finish()
    sum_finish(0, xr, fin.at[0])
    land[0] = fin[0].astype(bf16)
    result_one.start()
    result_two.finish()
    others(lambda i: out_arrived(2, xs, out_land, i))
    others(lambda i: out_arrived(3, gs, dx_land, i))
    keep_out.wait()
    keep_dx.wait()
    result_one.finish()
    reduce_two.drain()
    reduce_one.drain_cores()
    reduce_one.drain_sides()
    reduce_one.drain()
    gather_one.drain()
    small[6:8, :] = jnp.zeros((2, fb), f32)


def frame_tables_of(sz, me, lengths, frame_mask, perm, window, cont, counted, aux):
    T, steps = sz.T, sz.steps
    starts, filled = [], 0
    for k in range(lengths.shape[1]):
        starts.append(filled)
        filled = filled + lengths[0, k]
    row = lax.broadcasted_iota(jnp.int32, (T, 128), 0)
    slot = me * T + (row & 7) * steps + (row >> 3)
    goes = jnp.ones((T, 128), f32)
    for start in starts:
        goes = jnp.where(slot == start, 0.0, goes)
    cont[...] = goes
    kept = jnp.where(frame_mask[0:1, window] > 0, 1.0, 0.0)
    kept = jnp.broadcast_to(kept, (128, sz.win)).astype(bf16)
    kept = lax.dot_general(
        perm[me % 2], kept, (((1,), (1,)), ((), ())), preferred_element_type=f32
    )
    counted[...] = jnp.where(slot < filled, kept, 0.0)
    run = lax.broadcasted_iota(jnp.int32, (8, 128), 0)
    first = me * T + run * steps
    behind = jnp.zeros((8, 128), jnp.int32)
    whole, own = jnp.ones((8, 128), f32), jnp.ones((8, 128), f32)
    for start in starts:
        behind = jnp.where(first > start, jnp.maximum(behind, start), behind)
        whole = jnp.where((run * T <= start) & (start < run * T + T), 0.0, whole)
        own = jnp.where((first <= start) & (start < first + steps), 0.0, own)
    aux[0:8, :] = (first - behind).astype(f32)
    aux[8:16, :] = whole
    aux[16:24, :] = own
    place = lax.broadcasted_iota(jnp.int32, (1, sz.tok_dev), 1)
    block = jnp.where((place < filled) & (frame_mask[...] > 0), 1.0, 0.0)
    block = jnp.sum(block, axis=1, keepdims=True)
    aux[24:32, :] = jnp.broadcast_to(block, (8, 128))


def turn_back(
    sz,
    steps,
    x_ref,
    g_ref,
    out_ref,
    dx_ref,
    one_ref,
    two_ref,
    small,
    output,
    input_grad,
    dw_one,
    dw_two,
    gain_one,
    bias_one,
    decay_one,
    gain_two,
    bias_two,
    decay_two,
    perm,
    held,
    widened,
    sems,
):
    step = pl.program_id(0)
    T, fb, win, odd = sz.T, sz.fb, sz.win, sz.odd
    pairs = ((one_ref, dw_one), (two_ref, dw_two))
    reads = [pltpu.make_async_copy(a, held.at[k], sems.at[k]) for k, (a, _) in enumerate(pairs)]
    writes = [pltpu.make_async_copy(widened.at[k], b, sems.at[k]) for k, (_, b) in enumerate(pairs)]

    @pl.when(step == 0)
    def _():
        for move in reads:
            move.start()
        row = lax.broadcasted_iota(jnp.int32, (T, win), 0)
        column = lax.broadcasted_iota(jnp.int32, (T, win), 1)
        frame = (row & 7) * sz.steps + (row >> 3)
        perm[0] = jnp.where(column == frame, 1.0, 0.0).astype(bf16)
        perm[1] = jnp.where(column == frame + odd, 1.0, 0.0).astype(bf16)
        rows = (gain_one, bias_one, decay_one, gain_two, bias_two, decay_two)
        for r, ref in enumerate(rows):
            ref[...] = small[r : r + 1, :]

    output[...] = x_ref[...].astype(f32)
    input_grad[...] = g_ref[...].astype(f32)

    @pl.when(step < sz.n // 2)
    def _():
        for half in range(2):
            lanes = pl.ds((T - odd) * half, win)
            for source, result in ((out_ref, output), (dx_ref, input_grad)):
                result[:, lanes] += lax.dot_general(
                    source[half], perm[half], (((0,), (0,)), ((), ())), preferred_element_type=f32
                )

    @pl.when(step == 1)
    def _():
        for k, (read, write) in enumerate(zip(reads, writes, strict=True)):
            read.wait()
            widened[k] = held[k].astype(f32)
            write.start()

    @pl.when(step == steps - 1)
    def _():
        for move in writes:
            move.wait()


def frames_apart(sz, inputs, weight_one, weight_two, params, lengths, frame_mask, out_grad):
    n, seqs, H, fb, T, Z, qc = sz.n, sz.seqs, sz.H, sz.fb, sz.T, sz.Z, sz.qc
    whole = pl.BlockSpec(memory_space=pltpu.VMEM)
    anywhere = pl.BlockSpec(memory_space=pl.ANY)
    vmem, sem = pltpu.VMEM, pltpu.SemaphoreType.DMA
    frames_shape, longer_shape = (T, H), (sz.K, H)
    matmul = 2 * T * H * H
    out_land, dx_land, dw_one, dw_two, small = pl.pallas_call(
        functools.partial(network, sz),
        out_shape=(
            jax.ShapeDtypeStruct((n, T, fb), bf16),
            jax.ShapeDtypeStruct((n, T, fb), bf16),
            jax.ShapeDtypeStruct((fb, H), bf16),
            jax.ShapeDtypeStruct((fb, H), bf16),
            jax.ShapeDtypeStruct((8, fb), f32),
        ),
        in_specs=[anywhere] * 4 + [whole] * 6 + [pl.BlockSpec(memory_space=pltpu.SMEM), whole],
        out_specs=(anywhere, anywhere, anywhere, anywhere, whole),
        scratch_shapes=[
            vmem((8, fb), f32),
            vmem((T, 128), f32),
            vmem((T, 128), f32),
            vmem((32, 128), f32),
            vmem((1, 128), f32),
            vmem((fb, sz.valid), bf16),
            vmem((2, T, sz.win), bf16),
            vmem((fb, fb), bf16),
            vmem(frames_shape, bf16),
            vmem(frames_shape, bf16),
            vmem(longer_shape, bf16),
            vmem(frames_shape, bf16),
            vmem(frames_shape, bf16),
            vmem(frames_shape, bf16),
            vmem(longer_shape, bf16),
            vmem(longer_shape, bf16),
            vmem((H, sz.K), bf16),
            vmem((H, sz.K), bf16),
            vmem((T + 8, H), f32),
            vmem((T + 8, H), f32),
            vmem((H, H), bf16),
            vmem((H, H), bf16),
            vmem((8 * Z, fb, qc), bf16),
            vmem((5 * Z, fb, qc), bf16),
            vmem((2, fb, qc), bf16),
            vmem((2, fb, qc), f32),
            vmem((8, H), f32),
            vmem((8, H), f32),
            vmem((16, H), f32),
            vmem((4, 8, H), f32),
            vmem((4, n, 8, fb), f32),
            vmem((4, 8, fb), f32),
            vmem((4, seqs, 8, fb), f32),
            vmem((4, n, 8, fb), f32),
            vmem((4, 8, H), f32),
            vmem((2, 8, H), f32),
            vmem((2, n, 8, fb), f32),
            vmem((2, 8, fb), f32),
            vmem((2, seqs, 8, fb), f32),
            sem((8,)),
            sem((n,)),
            sem((n,)),
            sem((4, n)),
            sem((4, n)),
            sem((2, 10 * Z)),
            sem((2, 10 * Z)),
            sem((8, n)),
            sem((8, n)),
            sem((4, seqs)),
            sem((4, seqs)),
            sem((2, 10 * Z)),
            sem((2, 10 * Z)),
            sem((2, 3)),
            sem((2, 3)),
            sem((2, n + seqs)),
            sem((2, n + seqs)),
        ],
        compiler_params=pltpu.CompilerParams(
            collective_id=0, has_side_effects=True, vmem_limit_bytes=63 * 1024 * 1024
        ),
        cost_estimate=pl.CostEstimate(
            flops=6 * matmul, bytes_accessed=16 * fb * H, transcendentals=6 * T * H
        ),
        name="network",
    )(
        inputs,
        out_grad,
        weight_one,
        weight_two,
        *(values.reshape(1, fb) for values in params),
        lengths,
        frame_mask.reshape(1, -1),
    )
    tok = inputs.shape[1]
    pairs = n // 2
    steps = pl.cdiv(tok, 2 * T)
    frames_spec = pl.BlockSpec((fb, 2 * T), lambda p: (0, p))
    land_spec = pl.BlockSpec((2, T, fb), lambda p: (jnp.minimum(p, pairs - 1), 0, 0))
    row_spec = pl.BlockSpec((1, fb), lambda p: (0, 0))
    results = pl.pallas_call(
        functools.partial(turn_back, sz, steps),
        grid=(steps,),
        out_shape=(jax.ShapeDtypeStruct((fb, tok), f32),) * 2
        + (jax.ShapeDtypeStruct((fb, H), f32),) * 2
        + (jax.ShapeDtypeStruct((1, fb), f32),) * 6,
        in_specs=[frames_spec, frames_spec, land_spec, land_spec, anywhere, anywhere]
        + [pl.BlockSpec((8, fb), lambda p: (0, 0))],
        out_specs=(frames_spec, frames_spec, anywhere, anywhere) + (row_spec,) * 6,
        scratch_shapes=[
            vmem((2, T, sz.win), bf16),
            vmem((2, fb, H), bf16),
            vmem((2, fb, H), f32),
            sem((2,)),
        ],
        compiler_params=pltpu.CompilerParams(vmem_limit_bytes=60 * 1024 * 1024),
        name="turn_back",
    )(inputs, out_grad, out_land, dx_land, dw_one, dw_two, small)
    output, input_grad, dw_one, dw_two = results[:4]
    small = [row.reshape(fb) for row in results[4:]]
    return (
        output,
        input_grad,
        dw_one,
        small[0],
        small[1],
        small[2],
        dw_two,
        small[3],
        small[4],
        small[5],
    )


def frame_tables(lengths, frame_mask):
    positions = jnp.arange(frame_mask.shape[0], dtype=jnp.int32)
    offsets = jnp.cumsum(lengths[0]) - lengths[0]
    filled = jnp.sum(lengths[0])
    begins = jnp.any(positions[:, None] == offsets[None, :], axis=1)
    continues = jnp.where(begins, 0.0, 1.0).astype(jnp.float32)
    counted = jnp.where((positions < filled) & (frame_mask > 0), 1.0, 0.0).astype(jnp.float32)
    return (continues, counted)


def linear_scan(coef_rows, driving, backwards):
    row_count, length = driving.shape
    block_count = length // block_span
    factor = coef_rows.reshape(row_count, block_count, block_span)
    running = driving.reshape(row_count, block_count, block_span)
    places = jnp.arange(block_span, dtype=jnp.int32)
    step = 1
    while step < block_span:
        if backwards:
            mover = jnp.where(places[:, None] == places[None, :] + step, 1.0, 0.0).astype(
                jnp.float32
            )
            edge = jnp.where(places >= block_span - step, 1.0, 0.0).astype(jnp.float32)
        else:
            mover = jnp.where(places[:, None] == places[None, :] - step, 1.0, 0.0).astype(
                jnp.float32
            )
            edge = jnp.where(places < step, 1.0, 0.0).astype(jnp.float32)
        moved_factor = (
            jnp.dot(
                factor, mover, precision=lax.Precision.HIGHEST, preferred_element_type=jnp.float32
            )
            + edge
        )
        moved_running = jnp.dot(
            running, mover, precision=lax.Precision.HIGHEST, preferred_element_type=jnp.float32
        )
        running = factor * moved_running + running
        factor = factor * moved_factor
        step = step * 2
    end_place = 0 if backwards else block_span - 1
    total_factor = factor[:, :, end_place].T
    total_running = running[:, :, end_place].T

    def carry_step(carried, block_pair):
        return (block_pair[0] * carried + block_pair[1], carried)

    _, entering = lax.scan(
        carry_step,
        jnp.zeros((row_count,), jnp.float32),
        (total_factor, total_running),
        reverse=backwards,
    )
    result = running + factor * entering.T[:, :, None]
    return result.reshape(row_count, length)


def layer_forward(layer_input, weight, gain_row, bias_row, decay_rate, continues, counted):
    frames_in = lax.all_to_all(layer_input, "neur", split_axis=1, concat_axis=0, tiled=True)
    projected = jnp.dot(
        lax.all_gather(weight, "neur", axis=0, tiled=True),
        frames_in,
        preferred_element_type=jnp.float32,
    )
    neuron_proj = lax.all_to_all(
        projected.astype(jnp.bfloat16), "neur", split_axis=0, concat_axis=1, tiled=True
    ).astype(jnp.float32)
    sum_first = jnp.sum(counted[None, :] * neuron_proj, axis=1)
    sum_second = jnp.sum(counted[None, :] * neuron_proj * neuron_proj, axis=1)
    sum_first, sum_second, frames = lax.psum((sum_first, sum_second, jnp.sum(counted)), "seq")
    average = sum_first / frames
    inv_std = lax.rsqrt(sum_second / frames - average * average + epsilon)
    normed = (neuron_proj - average[:, None]) * inv_std[:, None]
    spread = jnp.sqrt(1.0 - decay_rate * decay_rate)
    states = linear_scan(
        decay_rate[:, None] * continues[None, :], (spread * gain_row)[:, None] * normed, False
    )
    layer_out = counted[None, :] * jax.nn.softplus(states + bias_row[:, None])
    return (layer_out, (frames_in, None, normed, inv_std, frames, states))


def layer_backward(
    upstream, weight, gain_row, bias_row, decay_rate, continues, counted, kept_state
):
    frames_in, full_weight, normed, inv_std, frames, states = kept_state
    local_grad = upstream * counted[None, :] * jax.nn.sigmoid(states + bias_row[:, None])
    following = jnp.concatenate([continues[1:], jnp.zeros((1,), jnp.float32)])
    coef_rows = decay_rate[:, None] * following[None, :]
    state_grad = linear_scan(coef_rows, local_grad, True)
    sum_rec, sum_rec_norm, sum_local = lax.psum(
        (
            jnp.sum(state_grad, axis=1),
            jnp.sum(state_grad * normed, axis=1),
            jnp.sum(local_grad, axis=1),
        ),
        "seq",
    )
    spread = jnp.sqrt(1.0 - decay_rate * decay_rate)
    gain_grad = spread * sum_rec_norm
    proj_grad = (spread * gain_row * inv_std)[:, None] * (
        state_grad - counted[None, :] * (sum_rec[:, None] + sum_rec_norm[:, None] * normed) / frames
    )
    driving = (spread * gain_row)[:, None] * normed
    decay_part = jnp.sum(state_grad * (states - driving), axis=1) / decay_rate
    grad_frames = lax.all_to_all(
        proj_grad.astype(jnp.bfloat16), "neur", split_axis=1, concat_axis=0, tiled=True
    )
    grad_rows = grad_frames
    input_frames = jnp.einsum(
        "ot,oi->it",
        grad_rows,
        lax.all_gather(weight, "neur", axis=0, tiled=True),
        preferred_element_type=jnp.float32,
    )
    input_grad = lax.all_to_all(
        input_frames.astype(jnp.bfloat16), "neur", split_axis=0, concat_axis=1, tiled=True
    ).astype(jnp.float32)
    grad_rows = grad_frames
    weight_rows = lax.psum_scatter(
        jnp.einsum("ot,it->oi", grad_rows, frames_in, preferred_element_type=jnp.float32),
        "neur",
        scatter_dimension=0,
        tiled=True,
    )
    weight_grad, decay_sum = lax.psum((weight_rows, decay_part), "seq")
    decay_grad = decay_sum - decay_rate / spread * gain_row * sum_rec_norm
    return (input_grad, weight_grad, gain_grad, sum_local, decay_grad)


def shards(
    inputs,
    weight_one,
    weight_two,
    gain_one,
    gain_two,
    bias_one,
    bias_two,
    decay_one,
    decay_two,
    lengths,
    frame_mask,
    out_grad,
):
    seqs, n = lax.axis_size("seq"), lax.axis_size("neur")
    H, (fb, tok) = weight_one.shape[1], inputs.shape
    if fits(n, seqs, H, fb, tok):
        params = (gain_one, gain_two, bias_one, bias_two, decay_one, decay_two)
        return frames_apart(
            Sizes(n, seqs, H, fb, tok),
            inputs,
            weight_one,
            weight_two,
            params,
            lengths,
            frame_mask,
            out_grad,
        )
    continues, counted = frame_tables(lengths, frame_mask)
    first_out, first_kept = layer_forward(
        inputs, weight_one, gain_one, bias_one, decay_one, continues, counted
    )
    second_out, second_kept = layer_forward(
        first_out.astype(jnp.bfloat16),
        weight_two,
        gain_two,
        bias_two,
        decay_two,
        continues,
        counted,
    )
    output = inputs.astype(jnp.float32) + second_out
    upstream = out_grad.astype(jnp.float32)
    middle_grad, weight_two_grad, gain_two_grad, bias_two_grad, decay_two_grad = layer_backward(
        upstream, weight_two, gain_two, bias_two, decay_two, continues, counted, second_kept
    )
    lower_grad, weight_one_grad, gain_one_grad, bias_one_grad, decay_one_grad = layer_backward(
        middle_grad, weight_one, gain_one, bias_one, decay_one, continues, counted, first_kept
    )
    return (
        output,
        upstream + lower_grad,
        weight_one_grad,
        gain_one_grad,
        bias_one_grad,
        decay_one_grad,
        weight_two_grad,
        gain_two_grad,
        bias_two_grad,
        decay_two_grad,
    )


def solution(mesh):
    placed = (
        P("neur", "seq"),
        P("neur", None),
        P("neur", None),
        P("neur"),
        P("neur"),
        P("neur"),
        P("neur"),
        P("neur"),
        P("neur"),
        P("seq", None),
        P("seq"),
        P("neur", "seq"),
    )
    return jax.shard_map(
        shards,
        mesh=mesh,
        in_specs=placed,
        out_specs=(
            P("neur", "seq"),
            P("neur", "seq"),
            P("neur", None),
            P("neur"),
            P("neur"),
            P("neur"),
            P("neur", None),
            P("neur"),
            P("neur"),
            P("neur"),
        ),
        check_vma=False,
    )
```

```python
import functools

import jax
import jax.numpy as jnp
from jax import lax
from jax.experimental import pallas as pl
from jax.experimental.pallas import tpu as pltpu
from jax.sharding import PartitionSpec as P

epsilon = 1e-05
block_span = 128
valid_frames = 3584
f32 = jnp.float32
bf16 = jnp.bfloat16
MESH = pl.DeviceIdType.MESH


def wide(tile, width):
    return jnp.concatenate([tile] * (width // 128), axis=1)


def at(index, size):
    if isinstance(index, int):
        return pl.ds(index * size, size)
    return pl.ds(pl.multiple_of(index * size, size), size)


def power(base, exponent):
    result = None
    while exponent:
        if exponent % 2:
            result = base if result is None else result * base
        exponent //= 2
        base = base * base
    return result


def log_of(rate):
    u = 1.0 - rate
    series = jnp.full_like(u, 1.0 / 8)
    for order in range(7, 0, -1):
        series = series * u + 1.0 / order
    return -u * series


GAIN, BIAS, DECAY = 0, 2, 4


class Sizes:
    def __init__(self, n, seqs, H, fb, tok_dev):
        self.n, self.seqs, self.H, self.fb, self.tok_dev = n, seqs, H, fb, tok_dev
        self.T = valid_frames // n
        self.steps = self.T // 8
        self.valid = valid_frames
        self.qc = H // seqs
        self.Z = n // 2
        self.odd = self.T % 128
        self.win = self.T + self.odd
        self.K = self.T + 16
        self.L = min(512, H)


def fits(n, seqs, H, fb, tok_dev):
    if n not in (4, 8) or valid_frames % n or seqs != 4 or fb * n != H or fb % 128 or H % 512:
        return False
    T = valid_frames // n
    return T % 64 == 0 and valid_frames % 128 == 0 and tok_dev >= valid_frames


class Line:
    def __init__(self, env, sends, recvs):
        self.env, self.sends, self.recvs = env, sends, recvs

    def copy(self, k, source, dest, target):
        return pltpu.make_async_remote_copy(
            src_ref=source,
            dst_ref=dest,
            send_sem=self.sends.at[k],
            recv_sem=self.recvs.at[k],
            device_id=target,
            device_id_type=MESH,
        )

    def arrived(self, k, ref):
        self.copy(k, ref, ref, self.env.across("x")).wait_recv()

    def sent(self, k, ref):
        self.copy(k, ref, ref, self.env.across("x")).wait_send()

    def along(self, dz):
        z, Z = self.env.z, self.env.sz.Z
        if dz == 0:
            return [(None, z, 0)]
        return [(z >= dz, z - dz, 1), (z + dz < Z, z + dz, -1)]


def if_so(condition, body):
    if condition is None:
        body()
    else:
        pl.when(condition)(body)


class Gather(Line):
    def __init__(self, env, source, full, sends, recvs, cut):
        super().__init__(env, sends, recvs)
        self.cut = cut
        self.full = full
        self.source = source.at[:, at(env.s, env.sz.qc)]

    def block(self, zz, fx, fy, fc=0):
        env = self.env
        rows = at(2 * zz + (env.x + fx) % 2, env.sz.fb)
        return self.full.at[rows, at(2 * ((env.y + fy) % 2) + (env.c + fc) % 2, env.sz.qc)]

    def half(self, ref, h):
        if h == 0:
            return ref.at[pl.ds(0, self.cut), :]
        return ref.at[pl.ds(self.cut, self.env.sz.fb - self.cut), :]

    def spread(self, zz, source):
        env, Z = self.env, self.env.sz.Z
        dest = self.block(zz, 0, 0)
        self.copy(2 * Z + zz, source, dest, env.across("x")).start()
        self.copy(3 * Z + zz, source, dest, env.across("y")).start()
        self.copy(6 * Z + zz, source, dest, env.across("core")).start()

    def pass_on(self, zz, source, way):
        env, Z = self.env, self.env.sz.Z
        dest = self.block(zz, 0, 0)

        def go():
            pltpu.make_async_remote_copy(
                src_ref=source,
                dst_ref=dest,
                send_sem=self.sends.at[zz if way > 0 else Z + zz],
                recv_sem=self.recvs.at[zz],
                device_id={"neur": 2 * (env.z + way) + env.x},
                device_id_type=MESH,
            ).start()

        pl.when(env.z < Z - 1 if way > 0 else env.z > 0)(go)

    def start(self):
        z = self.env.z
        self.pass_on(z, self.source, 1)
        self.pass_on(z, self.source, -1)
        self.spread(z, self.source)

    def line(self, dz):
        for condition, zz, way in self.along(dz):

            def one(zz=zz, way=way):
                block = self.block(zz, 0, 0)
                self.arrived(zz, block)
                self.pass_on(zz, block, way)
                self.spread(zz, block)

            if_so(condition, one)

    def sides(self, dz):
        env, Z = self.env, self.env.sz.Z
        for condition, zz, _ in self.along(dz):

            def one(zz=zz):
                block = self.block(zz, 1, 0)
                self.arrived(2 * Z + zz, block)
                part = self.half(block, 1)
                self.copy(5 * Z + zz, part, part, env.across("y")).start()
                self.copy(7 * Z + zz, block, block, env.across("core")).start()
                block = self.block(zz, 0, 1)
                self.arrived(3 * Z + zz, block)
                part = self.half(block, 0)
                self.copy(4 * Z + zz, part, part, env.across("x")).start()
                self.copy(8 * Z + zz, block, block, env.across("core")).start()

            if_so(condition, one)

    def diagonals(self):
        env, Z = self.env, self.env.sz.Z
        for dz in range(Z):
            for condition, zz, _ in self.along(dz):

                def one(zz=zz):
                    block = self.block(zz, 1, 1)
                    self.arrived(4 * Z + zz, self.half(block, 0))
                    self.arrived(5 * Z + zz, self.half(block, 1))
                    self.copy(9 * Z + zz, block, block, env.across("core")).start()

                if_so(condition, one)

    def cores(self):
        Z = self.env.sz.Z
        for k, (fx, fy) in enumerate(((0, 0), (1, 0), (0, 1), (1, 1))):
            for zz in range(Z):
                self.arrived((6 + k) * Z + zz, self.block(zz, fx, fy, 1))

    def drain(self):
        env, Z = self.env, self.env.sz.Z
        block = self.block(0, 0, 0)
        for zz in range(Z):
            pl.when((zz <= env.z) & (env.z < Z - 1))(lambda zz=zz: self.sent(zz, block))
            pl.when((zz >= env.z) & (env.z > 0))(lambda zz=zz: self.sent(Z + zz, block))
            for k in (2, 3, 6, 7, 8, 9):
                self.sent(k * Z + zz, block)
            self.sent(4 * Z + zz, self.half(block, 0))
            self.sent(5 * Z + zz, self.half(block, 1))


class Reduce(Line):
    kinds = ((1, 1), (1, 0), (0, 1), (0, 0))

    def __init__(self, env, grads, frames, land, spare, stage, held, total, sends, recvs, cut):
        super().__init__(env, sends, recvs)
        self.cut, self.held = cut, held
        self.grads, self.frames, self.land, self.spare = grads, frames, land, spare
        self.stage, self.total = stage, total

    def product(self, kind, zz, fc=0):
        env, sz = self.env, self.env.sz
        fx, fy = self.kinds[kind]
        rows = at(2 * zz + (env.x + fx) % 2, sz.fb)
        columns = at(2 * ((env.y + fy) % 2) + (env.c + fc) % 2, sz.qc)
        return jnp.dot(
            self.grads[rows, :], self.frames[:, columns], preferred_element_type=f32
        )

    def half(self, ref, h):
        if h == 0:
            return ref.at[pl.ds(0, self.cut), :]
        return ref.at[pl.ds(self.cut, self.env.sz.fb - self.cut), :]

    def landed(self, k, slot):
        self.arrived(k, self.land(slot))
        return self.land(slot)[...].astype(f32)

    def turn(self, i):
        z, Z = self.env.z, self.env.sz.Z
        low = jnp.where(i < Z - 1 - z, Z - 1 - i, i - (Z - 1 - z))
        high = jnp.where(i < z, i, Z - 1 - (i - z))
        return jnp.where(i == Z - 1, z, jnp.where(z < Z // 2, low, high))

    def cores(self, kind):
        env, Z = self.env, self.env.sz.Z

        def one(i, _):
            zz = self.turn(i)
            k = kind * Z + zz
            held = (kind % 2) * Z + zz
            if kind >= 2:
                self.sent(k - 2 * Z, self.stage.at[held])
            self.stage[held] = self.product(kind, zz, 1).astype(bf16)
            self.copy(k, self.stage.at[held], self.land(k), env.across("core")).start()
            return 0

        lax.fori_loop(0, Z, one, 0)

    def diagonals(self):
        env, Z = self.env, self.env.sz.Z

        def one(i, _):
            zz = self.turn(i)
            held = self.held(zz)
            held[...] = (self.product(0, zz) + self.landed(zz, zz)).astype(bf16)
            slot = self.land(4 * Z + zz)
            for k, h, axis in ((4, 0, "x"), (5, 1, "y")):
                self.copy(
                    k * Z + zz, self.half(held, h), self.half(slot, h), env.across(axis)
                ).start()
            return 0

        lax.fori_loop(0, Z, one, 0)

    def sides(self, low=0, high=None):
        env, Z = self.env, self.env.sz.Z
        spans = slice(0, self.cut), slice(self.cut, env.sz.fb)

        def one(i, _):
            zz = self.turn(i)
            slot = self.land(4 * Z + zz)
            for kind, h, wait, k, axis in ((1, 1, 5, 6, "x"), (2, 0, 4, 7, "y")):
                tile = self.product(kind, zz) + self.landed(kind * Z + zz, kind * Z + zz)
                part = self.half(slot, h)
                self.arrived(wait * Z + zz, part)
                held = self.stage.at[(2 + kind) * Z + zz]
                other = 1 - h
                summed = tile[spans[h], :] + part[...].astype(f32)
                self.half(held, h)[...] = summed.astype(bf16)
                self.half(held, other)[...] = tile[spans[other], :].astype(bf16)
                self.copy(
                    k * Z + zz, held, self.land((4 + kind) * Z + zz), env.across(axis)
                ).start()
            return 0

        lax.fori_loop(low, Z if high is None else high, one, 0)

    def joined(self, zz):
        Z = self.env.sz.Z
        tile = self.product(3, zz) + self.landed(3 * Z + zz, 3 * Z + zz)
        tile = tile + self.landed(6 * Z + zz, 5 * Z + zz)
        self.total[...] = tile + self.landed(7 * Z + zz, 6 * Z + zz)

    def lines(self, low=0, high=None):
        env, Z, z = self.env, self.env.sz.Z, self.env.z
        def onward(zz, way):
            k, slot = (8 if way > 0 else 9) * Z + zz, 7 * Z + zz
            self.joined(zz)

            @pl.when(z > 0 if way > 0 else z < Z - 1)
            def _():
                self.total[...] += self.landed(k, slot)

            held = self.held(zz)
            self.sent(4 * Z + zz, self.half(held, 0))
            self.sent(5 * Z + zz, self.half(held, 1))
            held[...] = self.total[...].astype(bf16)
            target = {"neur": 2 * (z + way) + env.x}
            if way > 0:
                self.copy(k, held, self.land(slot), target).start()
            else:
                pl.when(zz == z - 1)(lambda: self.copy(k, held, self.spare, target).start())
                pl.when(zz != z - 1)(lambda: self.copy(k, held, self.land(slot), target).start())

        for i in range(low, Z - 1 if high is None else high):
            zz = self.turn(i)
            pl.when(zz > z)(functools.partial(onward, zz, 1))
            pl.when(zz < z)(functools.partial(onward, zz, -1))

    def finish(self):
        Z, z = self.env.sz.Z, self.env.z
        self.joined(z)
        @pl.when(z > 0)
        def _():
            self.total[...] += self.landed(8 * Z + z, 7 * Z + z)

        @pl.when(z < Z - 1)
        def _():
            self.arrived(9 * Z + z, self.spare)
            self.total[...] += self.spare[...].astype(f32)

    def drain_cores(self):
        for k in range(2 * self.env.sz.Z, 4 * self.env.sz.Z):
            self.sent(k, self.stage.at[0])

    def drain_sides(self):
        for k in range(6 * self.env.sz.Z, 8 * self.env.sz.Z):
            self.sent(k, self.stage.at[0])

    def drain(self):
        Z, z = self.env.sz.Z, self.env.z
        held = self.stage.at[0]
        for zz in range(Z):
            for k in (4, 5):
                pl.when(zz == z)(
                    lambda k=k, zz=zz: self.sent(k * Z + zz, self.half(held, k - 4))
                )
            pl.when(zz > z)(lambda zz=zz: self.sent(8 * Z + zz, held))
            pl.when(zz < z)(lambda zz=zz: self.sent(9 * Z + zz, held))


class Result:
    def __init__(self, env, whole, block, sends, recvs, local):
        self.env, self.whole, self.block = env, whole, block
        self.sends, self.recvs, self.local = sends, recvs, local

    def part(self, flip_y, flip_c):
        env = self.env
        s = 2 * ((env.y + flip_y) % 2) + (env.c + flip_c) % 2
        return self.whole.at[:, at(s, env.sz.qc)]

    def copy(self, k, source, dest, target):
        return pltpu.make_async_remote_copy(
            src_ref=source,
            dst_ref=dest,
            send_sem=self.sends.at[k],
            recv_sem=self.recvs.at[k],
            device_id=target,
            device_id_type=MESH,
        )

    def start(self):
        env, own = self.env, self.part(0, 0)
        self.copy(0, self.block, own, env.across("y")).start()
        self.copy(1, self.block, own, env.across("core")).start()
        pltpu.make_async_copy(self.block, own, self.local).start()

    def finish(self):
        env = self.env
        other = self.part(1, 0)
        self.copy(0, self.block, other, env.across("y")).wait_recv()
        forward = self.copy(2, other, other, env.across("core"))
        forward.start()
        own = self.part(0, 0)
        pltpu.make_async_copy(self.block, own, self.local).wait()
        self.copy(0, self.block, own, env.across("y")).wait_send()
        self.copy(1, self.block, self.part(0, 1), env.across("core")).wait()
        forward.wait_send()
        self.copy(2, other, self.part(1, 1), env.across("core")).wait_recv()


class Env:
    def across(self, axis):
        if axis == "x":
            return {"neur": 2 * self.z + 1 - self.x}
        if axis == "y":
            return {"seq": 2 * (1 - self.y) + self.c}
        return {"seq": 2 * self.y + 1 - self.c}


def network(
    sz,
    x_hbm,
    g_hbm,
    w_one,
    w_two,
    gain_one,
    gain_two,
    bias_one,
    bias_two,
    decay_one,
    decay_two,
    lengths,
    frame_mask,
    out_land,
    dx_land,
    dw_one,
    dw_two,
    small,
    own_par,
    cont,
    counted,
    aux,
    frames_sum,
    raw,
    perm,
    eye,
    xs,
    gs,
    xr,
    gr,
    p_one,
    p_two,
    x_two,
    dp,
    dpt_one,
    dpt_two,
    s_one,
    s_two,
    wf_one,
    wf_two,
    land,
    stage,
    spare,
    fin,
    par,
    ends,
    work,
    pay,
    arrive,
    seqpay,
    seqland,
    back,
    backland,
    sumpay,
    sumland,
    sumseq,
    sumseqland,
    local_sems,
    par_sends,
    par_recvs,
    frame_sends,
    frame_recvs,
    gather_sends,
    gather_recvs,
    hop_sends,
    hop_recvs,
    seq_sends,
    seq_recvs,
    reduce_sends,
    reduce_recvs,
    final_sends,
    final_recvs,
    sum_sends,
    sum_recvs,
):
    n, seqs, H, fb, T, steps, L = sz.n, sz.seqs, sz.H, sz.fb, sz.T, sz.steps, sz.L
    env = Env()
    env.sz = sz
    me = lax.axis_index("neur")
    mine = lax.axis_index("seq")
    env.j, env.s = me, mine
    env.z, env.x, env.y, env.c = me // 2, me % 2, mine // 2, mine % 2

    barrier = pltpu.get_barrier_semaphore()
    for o in range(1, n):
        pl.semaphore_signal(
            barrier, inc=1, device_id={"neur": (me + o) % n}, device_id_type=MESH
        )
    for o in range(1, seqs):
        pl.semaphore_signal(
            barrier, inc=1, device_id={"seq": (mine + o) % seqs}, device_id_type=MESH
        )
    load_x = pltpu.make_async_copy(x_hbm.at[:, pl.ds(0, sz.valid)], raw, local_sems.at[0])
    load_x.start()
    for r, values in enumerate((gain_one, gain_two, bias_one, bias_two, decay_one, decay_two)):
        own_par[r : r + 1, :] = values[...]
    own_par[6:8, :] = jnp.zeros((2, fb), f32)
    pl.semaphore_wait(barrier, n - 1 + seqs - 1)

    def neur_copy(source, dest, send, recv, i):
        return pltpu.make_async_remote_copy(
            src_ref=source,
            dst_ref=dest,
            send_sem=send,
            recv_sem=recv,
            device_id={"neur": i},
            device_id_type=MESH,
        )

    def seq_copy(source, dest, send, recv, i):
        return pltpu.make_async_remote_copy(
            src_ref=source,
            dst_ref=dest,
            send_sem=send,
            recv_sem=recv,
            device_id={"seq": i},
            device_id_type=MESH,
        )

    def straight(body, low=1, high=n // 2):
        lax.fori_loop(low, high, lambda o, _: (body((me + 2 * o) % n), 0)[1], 0)

    def crossing(body, low=0, high=n // 2):
        lax.fori_loop(low, high, lambda o, _: (body((me + 2 * o + 1) % n), 0)[1], 0)

    def others(body, count=n, own=me):
        def one(o, _):
            body((own + o) % count)
            return 0

        lax.fori_loop(1, count, one, 0)

    own_lanes = at(me, fb)

    def par_copy(i):
        return neur_copy(own_par, par.at[:, own_lanes], par_sends.at[i], par_recvs.at[me], i)

    def par_wait(i):
        neur_copy(own_par, par.at[:, at(i, fb)], par_sends.at[i], par_recvs.at[i], i).wait()

    others(lambda i: par_copy(i).start())
    par[:, own_lanes] = own_par[...]

    cuts = (fb // 4, 3 * fb // 8)
    gather_one = Gather(env, w_one, wf_one, gather_sends.at[0], gather_recvs.at[0], cuts[0])
    gather_two = Gather(env, w_two, wf_two, gather_sends.at[1], gather_recvs.at[1], cuts[1])
    own_one = pltpu.make_async_copy(gather_one.source, gather_one.block(env.z, 0, 0), local_sems.at[2])
    own_two = pltpu.make_async_copy(gather_two.source, gather_two.block(env.z, 0, 0), local_sems.at[3])
    own_one.start()
    own_two.start()
    gather_one.start()
    gather_two.start()

    row = lax.broadcasted_iota(jnp.int32, (T, sz.win), 0)
    column = lax.broadcasted_iota(jnp.int32, (T, sz.win), 1)
    frame = (row & 7) * steps + (row >> 3)
    perm[0] = jnp.where(column == frame, 1.0, 0.0).astype(bf16)
    perm[1] = jnp.where(column == frame + sz.odd, 1.0, 0.0).astype(bf16)
    row = lax.broadcasted_iota(jnp.int32, (fb, fb), 0)
    column = lax.broadcasted_iota(jnp.int32, (fb, fb), 1)
    eye[...] = jnp.where(row == column, 1.0, 0.0).astype(bf16)

    def window(i):
        start = (i // 2) * (2 * T) + (i % 2) * (T - sz.odd)
        return pl.ds(pl.multiple_of(start, 128), sz.win)

    def turned(i):
        return lax.dot_general(
            perm[i % 2], raw[:, window(i)], (((1,), (1,)), ((), ())), preferred_element_type=f32
        ).astype(bf16)

    def frames_copy(a, source, dest, i):
        return neur_copy(source, dest, frame_sends.at[a, i], frame_recvs.at[a, me], i)

    def frames_wait(a, ref, i):
        part = ref.at[pl.ds(0, T), at(i, fb)]
        neur_copy(part, part, frame_sends.at[a, i], frame_recvs.at[a, i], i).wait_recv()

    def frames_sent(a, ref, i):
        part = ref.at[pl.ds(0, T), at(i, fb)]
        neur_copy(part, part, frame_sends.at[a, i], frame_recvs.at[a, i], i).wait_send()

    load_x.wait()

    def turn_x(i):
        xs[:, at(i, fb)] = turned(i)

    def send_x(i):
        frames_copy(0, xs.at[:, at(i, fb)], xr.at[pl.ds(0, T), own_lanes], i).start()

    def send_all_x():
        crossing(send_x)
        straight(send_x)

    others(turn_x)
    xr[0:T, own_lanes] = turned(me)
    load_g = pltpu.make_async_copy(g_hbm.at[:, pl.ds(0, sz.valid)], raw, local_sems.at[1])
    load_g.start()
    ends_of_line = (env.z == 0) | (env.z == sz.Z - 1)
    pl.when(ends_of_line)(send_all_x)
    for dz in range(1, sz.Z):
        gather_one.line(dz)
        gather_two.line(dz)
        if dz == max(1, sz.Z - 2):
            pl.when(jnp.logical_not(ends_of_line))(send_all_x)
        gather_one.sides(dz - 1)
    frame_tables_of(sz, me, lengths, frame_mask, perm, window(me), cont, counted, aux)
    load_g.wait()

    def turn_g(i):
        gs[:, at(i, fb)] = turned(i)

    def send_g(i):
        frames_copy(1, gs.at[:, at(i, fb)], gr.at[:, own_lanes], i).start()

    others(turn_g)
    gr[:, own_lanes] = turned(me)
    gather_one.sides(sz.Z - 1)
    gather_two.sides(0)
    straight(send_g)
    crossing(send_g, 0, 1)
    gather_one.diagonals()
    for dz in range(1, sz.Z):
        gather_two.sides(dz)
    gather_one.cores()
    own_one.wait()
    own_two.wait()
    others(lambda i: frames_wait(0, xr, i))
    others(par_wait)

    def blocks(body):
        def one(b, _):
            body(at(b, L))
            return 0

        lax.fori_loop(0, H // L, one, 0)

    def project(frames, weight, result):
        def one(b, _):
            result[:, at(b, 2 * fb)] = lax.dot_general(
                frames[0:T, :],
                weight[at(b, 2 * fb), :],
                (((1,), (1,)), ((), ())),
                preferred_element_type=f32,
            ).astype(bf16)
            return 0

        lax.fori_loop(0, n // 2, one, 0)

    def flags(t):
        tile = pl.ds(pl.multiple_of(8 * t, 8), 8)
        return wide(cont[tile, :], L), wide(counted[tile, :], L)

    def spread8(ref, r, cols, width=L):
        return jnp.broadcast_to(ref[r : r + 1, cols], (8, width))

    zero = jnp.zeros((8, L), f32)

    def down(value):
        return jnp.sum(value, axis=0, keepdims=True)

    def exchange(e, gathered, totalled, gap):
        ahead = pl.ds(0, 4 if e < 2 else 8)
        behind = pl.ds(0, 4)

        def out_copy(i):
            return neur_copy(
                pay.at[e, ahead, at(i, fb)],
                arrive.at[e, me, ahead],
                hop_sends.at[2 * e, i],
                hop_recvs.at[2 * e, me],
                i,
            )

        others(lambda i: out_copy(i).start())
        arrive[e, me, ahead] = pay[e, ahead, own_lanes]
        gap("hop_a")

        def out_wait(i):
            neur_copy(
                pay.at[e, ahead, at(i, fb)],
                arrive.at[e, i, ahead],
                hop_sends.at[2 * e, i],
                hop_recvs.at[2 * e, i],
                i,
            ).wait()

        others(out_wait)
        gathered()

        def along_copy(i):
            return seq_copy(
                seqpay.at[e],
                seqland.at[e, mine],
                seq_sends.at[e, i],
                seq_recvs.at[e, mine],
                i,
            )

        def along_wait(i):
            seq_copy(
                seqpay.at[e], seqland.at[e, i], seq_sends.at[e, i], seq_recvs.at[e, i], i
            ).wait()

        others(lambda i: along_copy(i).start(), seqs, mine)
        seqland[e, mine] = seqpay[e]
        gap("hop_b")
        others(along_wait, seqs, mine)
        sums = seqland[e, 0]
        for i in range(1, seqs):
            sums = sums + seqland[e, i]
        totalled(sums)

        def back_copy(i):
            return neur_copy(
                back.at[e, i, behind],
                backland.at[e, behind, own_lanes],
                hop_sends.at[2 * e + 1, i],
                hop_recvs.at[2 * e + 1, me],
                i,
            )

        def back_wait(i):
            neur_copy(
                back.at[e, i, behind],
                backland.at[e, behind, at(i, fb)],
                hop_sends.at[2 * e + 1, i],
                hop_recvs.at[2 * e + 1, i],
                i,
            ).wait()

        others(lambda i: back_copy(i).start())
        backland[e, behind, own_lanes] = back[e, me, behind]
        gap("hop_c")
        others(back_wait)

    def layer_forward(layer, frames, weight, projected, states, store, gap):
        e = layer
        decay_row, gain_row, bias_row = DECAY + layer, GAIN + layer, BIAS + layer
        project(frames, weight, projected)
        gap("ends")

        def local_ends(cols):
            decay = spread8(par, decay_row, cols)

            def step(i, carry):
                state, first, second, inward = carry
                pair = projected[pl.ds(pl.multiple_of(16 * i, 16), 16), cols].astype(f32)
                for h in range(2):
                    value = pair[8 * h : 8 * h + 8, :]
                    goes, count = flags(2 * i + h)
                    state = (decay * goes) * state + value
                    held = count * value
                    first = first + held
                    second = second + held * value
                ins = frames[pl.ds(pl.multiple_of(16 * i, 16), 16), cols].astype(f32)
                return state, first, second, inward + ins[0:8, :] + ins[8:16, :]

            state, first, second, inward = lax.fori_loop(
                0, T // 16, step, (zero, zero, zero, zero)
            )
            ends[:, cols] = state
            pay[e, 1:2, cols] = down(first)
            pay[e, 2:3, cols] = down(second)
            pay[e, 3:4, cols] = down(inward)

        blocks(local_ends)
        run_power = power(par[decay_row : decay_row + 1, :], steps)
        total = jnp.zeros((1, H), f32)
        for k in range(8):
            total = run_power * wide(aux[16 + k : 17 + k, :], H) * total + ends[k : k + 1, :]
        pay[e, 0:1, :] = total

        own_decay = own_par[decay_row : decay_row + 1, :]

        def gathered():
            whole_power = power(own_decay, T)
            carried = jnp.zeros((1, fb), f32)
            sums = jnp.zeros((4, fb), f32)
            for i in range(n):
                rows = arrive[e, i, 0:4, :]
                back[e, i, 0:1, :] = carried
                carried = whole_power * wide(aux[8 + i : 9 + i, :], fb) * carried + rows[0:1, :]
                sums = sums + rows
            seqpay[e, 0:4, :] = sums
            seqpay[e, 4:8, :] = jnp.zeros((4, fb), f32)
            seqpay[e, 0:1, :] = wide(aux[24:25, :], fb)

        def totalled(sums):
            frames_all = sums[0:1, :]
            average = sums[1:2, :] / frames_all
            inv_std = lax.rsqrt(sums[2:3, :] / frames_all - average * average + epsilon)
            centre = sums[3:4, :] / (sz.valid * seqs)
            for i in range(n):
                back[e, i, 1:2, :] = average
                back[e, i, 2:3, :] = inv_std
                back[e, i, 3:4, :] = centre
            frames_sum[...] = frames_all[:, 0:128]

        exchange(e, gathered, totalled, gap)
        centre = backland[e, 3:4, :]
        frames[T : T + 16, :] = jnp.concatenate(
            [-centre, -centre, -centre, jnp.zeros((13, H), f32)], axis=0
        ).astype(bf16)

        total = backland[e, 0:1, :]
        for k in range(8):
            work[k : k + 1, :] = total
            total = run_power * wide(aux[16 + k : 17 + k, :], H) * total + ends[k : k + 1, :]

        gap("scan")

        def full_scan(cols):
            decay = spread8(par, decay_row, cols)
            average = spread8(backland.at[e], 1, cols)
            inv_std = spread8(backland.at[e], 2, cols)
            bias = spread8(par, bias_row, cols)
            scale = jnp.sqrt(1.0 - decay * decay) * spread8(par, gain_row, cols) * inv_std
            ones = (1.0 - jnp.exp(wide(aux[0:8, :], L) * log_of(decay))) / (1.0 - decay)
            state = scale * (work[0:8, cols] - average * ones)
            states[0:8, cols] = state

            def step(i, state):
                pair = projected[pl.ds(pl.multiple_of(16 * i, 16), 16), cols].astype(f32)
                outs = []
                for h in range(2):
                    goes, count = flags(2 * i + h)
                    state = (decay * goes) * state + scale * (pair[8 * h : 8 * h + 8, :] - average)
                    states[pl.ds(pl.multiple_of(16 * i + 8 * h + 8, 8), 8), cols] = state
                    v = state + bias
                    soft = jnp.maximum(v, 0.0) + jnp.log(1.0 + jnp.exp(-jnp.abs(v)))
                    outs.append(count * soft)
                store[pl.ds(pl.multiple_of(16 * i, 16), 16), cols] = jnp.concatenate(
                    outs, axis=0
                ).astype(bf16)
                return state

            lax.fori_loop(0, T // 16, step, state)

        blocks(full_scan)

    def layer_backward(layer, upstream, projected, states, turned_grads, gap):
        e = 2 + (1 - layer)
        decay_row, gain_row, bias_row = DECAY + layer, GAIN + layer, BIAS + layer
        run_power = power(par[decay_row : decay_row + 1, :], steps)

        def local_ends(cols):
            decay = spread8(par, decay_row, cols)
            average = spread8(backland.at[layer], 1, cols)
            inv_std = spread8(backland.at[layer], 2, cols)
            bias = spread8(par, bias_row, cols)

            def step(o, carry):
                i = T // 16 - 1 - o
                rows = pl.ds(pl.multiple_of(16 * i, 16), 16)
                pair = projected[rows, cols].astype(f32)
                ups = upstream[rows, cols].astype(f32)
                for h in (1, 0):
                    run, reach, U, V, UN, VN, B, D, DA = carry
                    goes, count = flags(2 * i + h)
                    here = pl.ds(pl.multiple_of(16 * i + 8 * h + 8, 8), 8)
                    state = states[here, cols]
                    before = states[pl.ds(pl.multiple_of(16 * i + 8 * h, 8), 8), cols]
                    local = ups[8 * h : 8 * h + 8, :] * count / (1.0 + jnp.exp(-(state + bias)))
                    states[here, cols] = local
                    normed = (pair[8 * h : 8 * h + 8, :] - average) * inv_std
                    run = local + run
                    kept = goes * before
                    link = decay * goes
                    carry = (
                        link * run,
                        link * reach,
                        U + run,
                        V + reach,
                        UN + run * normed,
                        VN + reach * normed,
                        B + local,
                        D + run * kept,
                        DA + reach * kept,
                    )
                return carry

            one = jnp.ones((8, L), f32)
            run, _, U, V, UN, VN, B, D, DA = lax.fori_loop(
                0, T // 16, step, (zero, one, zero, zero, zero, zero, zero, zero, zero)
            )
            ends[:, cols] = run
            decay_run = power(par[decay_row : decay_row + 1, cols], steps)
            part, factor = jnp.zeros((1, L), f32), jnp.ones((1, L), f32)
            for k in range(7, -1, -1):
                work[k : k + 1, cols] = part
                work[8 + k : 9 + k, cols] = factor
                through = decay_run * wide(aux[16 + k : 17 + k, :], L)
                part = through * part + ends[k : k + 1, cols]
                factor = through * factor
            pay[e, 0:1, cols] = part
            entering, scaled = work[0:8, cols], work[8:16, cols]
            pay[e, 1:2, cols] = down(U + V * entering)
            pay[e, 2:3, cols] = down(V * scaled)
            pay[e, 3:4, cols] = down(UN + VN * entering)
            pay[e, 4:5, cols] = down(VN * scaled)
            pay[e, 5:6, cols] = down(B)
            pay[e, 6:7, cols] = down(D + DA * entering)
            pay[e, 7:8, cols] = down(DA * scaled)

        blocks(local_ends)
        own_decay = own_par[decay_row : decay_row + 1, :]
        own_gain = own_par[gain_row : gain_row + 1, :]

        def gathered():
            whole_power = power(own_decay, T)
            carried = jnp.zeros((1, fb), f32)
            sums = [jnp.zeros((1, fb), f32)] * 4
            for i in range(n - 1, -1, -1):
                rows = arrive[e, i]
                back[e, i, 0:1, :] = carried
                for a, (plain, times) in enumerate(((1, 2), (3, 4), (5, None), (6, 7))):
                    term = rows[plain : plain + 1, :]
                    if times is not None:
                        term = term + rows[times : times + 1, :] * carried
                    sums[a] = sums[a] + term
                carried = whole_power * wide(aux[8 + i : 9 + i, :], fb) * carried + rows[0:1, :]
            for a in range(4):
                seqpay[e, a : a + 1, :] = sums[a]
            seqpay[e, 4:8, :] = jnp.zeros((4, fb), f32)

        def totalled(sums):
            rec, rec_norm = sums[0:1, :], sums[1:2, :]
            for i in range(n):
                back[e, i, 1:2, :] = rec
                back[e, i, 2:3, :] = rec_norm
                back[e, i, 3:4, :] = jnp.zeros((1, fb), f32)
            spread = jnp.sqrt(1.0 - own_decay * own_decay)
            small[3 * layer : 3 * layer + 1, :] = spread * rec_norm
            small[3 * layer + 1 : 3 * layer + 2, :] = sums[2:3, :]
            small[3 * layer + 2 : 3 * layer + 3, :] = (
                sums[3:4, :] - own_decay / spread * own_gain * rec_norm
            )

        exchange(e, gathered, totalled, gap)
        gap("scan")
        total = backland[e, 0:1, :]
        for k in range(7, -1, -1):
            work[k : k + 1, :] = total
            total = run_power * wide(aux[16 + k : 17 + k, :], H) * total + ends[k : k + 1, :]

        def full_scan(cols):
            decay = spread8(par, decay_row, cols)
            average = spread8(backland.at[layer], 1, cols)
            inv_std = spread8(backland.at[layer], 2, cols)
            frames_all = wide(frames_sum[...], L)
            scale = jnp.sqrt(1.0 - decay * decay) * spread8(par, gain_row, cols) * inv_std
            rec = spread8(backland.at[e], 1, cols) / frames_all
            rec_norm = spread8(backland.at[e], 2, cols) / frames_all * inv_std

            def step(o, carry):
                carry, added = carry
                i = T // 16 - 1 - o
                rows = pl.ds(pl.multiple_of(16 * i, 16), 16)
                pair = projected[rows, cols].astype(f32)
                outs = [None, None]
                for h in (1, 0):
                    goes, count = flags(2 * i + h)
                    here = pl.ds(pl.multiple_of(16 * i + 8 * h + 8, 8), 8)
                    run = states[here, cols] + carry
                    centred = pair[8 * h : 8 * h + 8, :] - average
                    outs[h] = scale * (run - count * (rec + rec_norm * centred))
                    carry = (decay * goes) * run
                rounded = jnp.concatenate(outs, axis=0).astype(bf16)
                dp[rows, cols] = rounded
                rounded = rounded.astype(f32)
                return carry, added + rounded[0:8, :] + rounded[8:16, :]

            _, added = lax.fori_loop(0, T // 16, step, (work[0:8, cols], zero))
            whole = down(added)
            sumpay[layer, 0:1, cols] = whole
            high = whole.astype(bf16).astype(f32)
            middle = (whole - high).astype(bf16).astype(f32)
            low = whole - high - middle
            dp[T : T + 16, cols] = jnp.concatenate(
                [high, middle, low, jnp.zeros((13, L), f32)], axis=0
            ).astype(bf16)

        blocks(full_scan)
        sumpay[layer, 1:8, :] = jnp.zeros((7, H), f32)

        def turn(b, _):
            turned_grads[at(b, fb), :] = lax.dot_general(
                eye[...], dp[:, at(b, fb)], (((1,), (1,)), ((), ())), preferred_element_type=f32
            ).astype(bf16)
            return 0

        lax.fori_loop(0, n, turn, 0)

    def input_gradient(weight, result, columns):
        result[:, columns] = jnp.dot(
            dp[0:T, :], weight[:, columns], preferred_element_type=f32
        ).astype(bf16)

    def sum_copy(layer, i):
        return neur_copy(
            sumpay.at[layer, :, at(i, fb)],
            sumland.at[layer, me],
            sum_sends.at[layer, i],
            sum_recvs.at[layer, me],
            i,
        )

    def sum_along(layer, i):
        return seq_copy(
            sumseq.at[layer],
            sumseqland.at[layer, mine],
            sum_sends.at[layer, n + i],
            sum_recvs.at[layer, n + mine],
            i,
        )

    def sum_start(layer):
        others(lambda i: sum_copy(layer, i).start())
        sumland[layer, me] = sumpay[layer, :, own_lanes]

    def sum_middle(layer):
        def wait(i):
            neur_copy(
                sumpay.at[layer, :, at(i, fb)],
                sumland.at[layer, i],
                sum_sends.at[layer, i],
                sum_recvs.at[layer, i],
                i,
            ).wait()

        others(wait)
        total = sumland[layer, 0]
        for i in range(1, n):
            total = total + sumland[layer, i]
        sumseq[layer] = total
        sumseqland[layer, mine] = total
        others(lambda i: sum_along(layer, i).start(), seqs, mine)

    def sum_finish(layer, frames, total):
        def wait(i):
            seq_copy(
                sumseq.at[layer],
                sumseqland.at[layer, i],
                sum_sends.at[layer, n + i],
                sum_recvs.at[layer, n + i],
                i,
            ).wait()

        others(wait, seqs, mine)
        whole = sumseqland[layer, 0]
        for i in range(1, seqs):
            whole = whole + sumseqland[layer, i]
        whole = whole[0:1, :]
        high = whole.astype(bf16).astype(f32)
        middle = (whole - high).astype(bf16).astype(f32)
        low = whole - high - middle
        rows = jnp.concatenate([high, middle, low, jnp.zeros((13, fb), f32)], axis=0).astype(bf16)
        columns = lax.dot_general(
            eye[...], rows, (((1,), (1,)), ((), ())), preferred_element_type=f32
        ).astype(bf16)
        total[...] -= jnp.dot(
            columns, frames[T : T + 16, at(mine, sz.qc)], preferred_element_type=f32
        )

    def place_out(a, ref, dest, i):
        return neur_copy(
            ref.at[:, at(i, fb)], dest.at[me], frame_sends.at[a, i], frame_recvs.at[a, me], i
        )

    def out_arrived(a, ref, dest, i):
        neur_copy(
            ref.at[:, at(i, fb)], dest.at[i], frame_sends.at[a, i], frame_recvs.at[a, i], i
        ).wait()

    def nothing(name):
        return None

    def during_one(name):
        if name == "hop_c":
            gather_two.diagonals()
        if name == "scan":
            crossing(send_g, 1, n // 2 - 1)

    def during_two(name):
        if name == "scan":
            crossing(send_g, max(1, n // 2 - 1), n // 2)

    layer_forward(0, xr, wf_one, p_one, s_one, x_two, during_one)
    gather_two.cores()
    others(lambda i: frames_sent(0, xs, i))
    layer_forward(1, x_two, wf_two, p_two, s_two, xs, during_two)

    def send_out(i):
        place_out(2, xs, out_land, i).start()

    keep_out = pltpu.make_async_copy(xs.at[:, own_lanes], out_land.at[me], local_sems.at[4])
    keep_out.start()
    others(lambda i: frames_wait(1, gr, i))
    others(lambda i: frames_sent(1, gs, i))
    gather_two.drain()

    crossing(send_out, 0, 1)
    layer_backward(
        1,
        gr,
        p_two,
        s_two,
        dpt_two,
        lambda name: crossing(send_out, 1, 2) if name == "scan" else None,
    )
    if n > 4:
        crossing(send_out, 2, 3)
    lax.fori_loop(0, n // 2, lambda i, _: (input_gradient(wf_two, gr, at(i, 2 * fb)), 0)[1], 0)
    sum_start(1)
    if n > 4:
        crossing(send_out, 3, 4)
    reduce_two = Reduce(
        env,
        dpt_two,
        x_two,
        lambda k: land.at[k],
        spare.at[1],
        stage,
        lambda k: stage.at[2 * sz.Z + k],
        fin.at[1],
        reduce_sends.at[1],
        reduce_recvs.at[1],
        fb // 2,
    )
    reduce_one = Reduce(
        env,
        dpt_one,
        xr,
        lambda k: wf_two.at[at(k // seqs, fb), at(k % seqs, sz.qc)],
        spare.at[0],
        stage,
        lambda k: raw.at[:, at(k, sz.qc)],
        fin.at[0],
        reduce_sends.at[0],
        reduce_recvs.at[0],
        fb // 2,
    )
    result_two = Result(
        env, dw_two, land.at[1], final_sends.at[1], final_recvs.at[1], local_sems.at[6]
    )
    result_one = Result(
        env, dw_one, land.at[0], final_sends.at[0], final_recvs.at[0], local_sems.at[7]
    )
    for kind in range(4):
        reduce_two.cores(kind)

    def meanwhile(name):
        if name == "hop_b":
            sum_middle(1)
        if name == "scan":
            reduce_two.diagonals()
            straight(send_out)

    layer_backward(0, gr, p_one, s_one, dpt_one, meanwhile)
    reduce_two.drain_cores()
    reduce_one.cores(0)
    reduce_two.sides()
    reduce_one.diagonals()
    for kind in range(1, 4):
        reduce_one.cores(kind)
    sum_start(0)

    def send_dx(i):
        place_out(3, gs, dx_land, i).start()

    def make_dx(i):
        input_gradient(wf_one, gs, at(i, fb))

    def make_and_send_dx(i):
        make_dx(i)
        send_dx(i)

    straight(make_and_send_dx)
    crossing(make_dx)
    make_dx(me)
    keep_dx = pltpu.make_async_copy(gs.at[:, own_lanes], dx_land.at[me], local_sems.at[5])
    keep_dx.start()
    reduce_two.lines()
    sum_middle(0)
    reduce_two.drain_sides()
    reduce_one.sides(0, 2)
    for i in range(2, sz.Z):
        reduce_one.lines(i - 2, i - 1)
        reduce_one.sides(i, i + 1)
        if i == 2:
            crossing(send_dx, 0, n // 4)
    crossing(send_dx, n // 4 if sz.Z > 2 else 0, n // 2)
    reduce_two.finish()
    sum_finish(1, x_two, fin.at[1])
    land[1] = fin[1].astype(bf16)
    result_two.start()
    reduce_one.lines(sz.Z - 2, sz.Z - 1)
    reduce_one.finish()
    sum_finish(0, xr, fin.at[0])
    land[0] = fin[0].astype(bf16)
    result_one.start()
    result_two.finish()
    others(lambda i: out_arrived(2, xs, out_land, i))
    others(lambda i: out_arrived(3, gs, dx_land, i))
    keep_out.wait()
    keep_dx.wait()
    result_one.finish()
    reduce_two.drain()
    reduce_one.drain_cores()
    reduce_one.drain_sides()
    reduce_one.drain()
    gather_one.drain()
    small[6:8, :] = jnp.zeros((2, fb), f32)


def frame_tables_of(sz, me, lengths, frame_mask, perm, window, cont, counted, aux):
    T, steps = sz.T, sz.steps
    starts, filled = [], 0
    for k in range(lengths.shape[1]):
        starts.append(filled)
        filled = filled + lengths[0, k]
    row = lax.broadcasted_iota(jnp.int32, (T, 128), 0)
    slot = me * T + (row & 7) * steps + (row >> 3)
    goes = jnp.ones((T, 128), f32)
    for start in starts:
        goes = jnp.where(slot == start, 0.0, goes)
    cont[...] = goes
    kept = jnp.where(frame_mask[0:1, window] > 0, 1.0, 0.0)
    kept = jnp.broadcast_to(kept, (128, sz.win)).astype(bf16)
    kept = lax.dot_general(
        perm[me % 2], kept, (((1,), (1,)), ((), ())), preferred_element_type=f32
    )
    counted[...] = jnp.where(slot < filled, kept, 0.0)
    run = lax.broadcasted_iota(jnp.int32, (8, 128), 0)
    first = me * T + run * steps
    behind = jnp.zeros((8, 128), jnp.int32)
    whole, own = jnp.ones((8, 128), f32), jnp.ones((8, 128), f32)
    for start in starts:
        behind = jnp.where(first > start, jnp.maximum(behind, start), behind)
        whole = jnp.where((run * T <= start) & (start < run * T + T), 0.0, whole)
        own = jnp.where((first <= start) & (start < first + steps), 0.0, own)
    aux[0:8, :] = (first - behind).astype(f32)
    aux[8:16, :] = whole
    aux[16:24, :] = own
    place = lax.broadcasted_iota(jnp.int32, (1, sz.tok_dev), 1)
    block = jnp.where((place < filled) & (frame_mask[...] > 0), 1.0, 0.0)
    block = jnp.sum(block, axis=1, keepdims=True)
    aux[24:32, :] = jnp.broadcast_to(block, (8, 128))


def turn_back(
    sz,
    steps,
    x_ref,
    g_ref,
    out_ref,
    dx_ref,
    one_ref,
    two_ref,
    small,
    output,
    input_grad,
    dw_one,
    dw_two,
    gain_one,
    bias_one,
    decay_one,
    gain_two,
    bias_two,
    decay_two,
    perm,
    held,
    widened,
    sems,
):
    step = pl.program_id(0)
    T, fb, win, odd = sz.T, sz.fb, sz.win, sz.odd
    pairs = ((one_ref, dw_one), (two_ref, dw_two))
    reads = [pltpu.make_async_copy(a, held.at[k], sems.at[k]) for k, (a, _) in enumerate(pairs)]
    writes = [pltpu.make_async_copy(widened.at[k], b, sems.at[k]) for k, (_, b) in enumerate(pairs)]

    @pl.when(step == 0)
    def _():
        for move in reads:
            move.start()
        row = lax.broadcasted_iota(jnp.int32, (T, win), 0)
        column = lax.broadcasted_iota(jnp.int32, (T, win), 1)
        frame = (row & 7) * sz.steps + (row >> 3)
        perm[0] = jnp.where(column == frame, 1.0, 0.0).astype(bf16)
        perm[1] = jnp.where(column == frame + odd, 1.0, 0.0).astype(bf16)
        rows = (gain_one, bias_one, decay_one, gain_two, bias_two, decay_two)
        for r, ref in enumerate(rows):
            ref[...] = small[r : r + 1, :]

    output[...] = x_ref[...].astype(f32)
    input_grad[...] = g_ref[...].astype(f32)

    @pl.when(step < sz.n // 2)
    def _():
        for half in range(2):
            lanes = pl.ds((T - odd) * half, win)
            for source, result in ((out_ref, output), (dx_ref, input_grad)):
                result[:, lanes] += lax.dot_general(
                    source[half], perm[half], (((0,), (0,)), ((), ())), preferred_element_type=f32
                )

    @pl.when(step == 1)
    def _():
        for k, (read, write) in enumerate(zip(reads, writes, strict=True)):
            read.wait()
            widened[k] = held[k].astype(f32)
            write.start()

    @pl.when(step == steps - 1)
    def _():
        for move in writes:
            move.wait()


def frames_apart(sz, inputs, weight_one, weight_two, params, lengths, frame_mask, out_grad):
    n, seqs, H, fb, T, Z, qc = sz.n, sz.seqs, sz.H, sz.fb, sz.T, sz.Z, sz.qc
    whole = pl.BlockSpec(memory_space=pltpu.VMEM)
    anywhere = pl.BlockSpec(memory_space=pl.ANY)
    vmem, sem = pltpu.VMEM, pltpu.SemaphoreType.DMA
    frames_shape, longer_shape = (T, H), (sz.K, H)
    matmul = 2 * T * H * H
    out_land, dx_land, dw_one, dw_two, small = pl.pallas_call(
        functools.partial(network, sz),
        out_shape=(
            jax.ShapeDtypeStruct((n, T, fb), bf16),
            jax.ShapeDtypeStruct((n, T, fb), bf16),
            jax.ShapeDtypeStruct((fb, H), bf16),
            jax.ShapeDtypeStruct((fb, H), bf16),
            jax.ShapeDtypeStruct((8, fb), f32),
        ),
        in_specs=[anywhere] * 4 + [whole] * 6 + [pl.BlockSpec(memory_space=pltpu.SMEM), whole],
        out_specs=(anywhere, anywhere, anywhere, anywhere, whole),
        scratch_shapes=[
            vmem((8, fb), f32),
            vmem((T, 128), f32),
            vmem((T, 128), f32),
            vmem((32, 128), f32),
            vmem((1, 128), f32),
            vmem((fb, sz.valid), bf16),
            vmem((2, T, sz.win), bf16),
            vmem((fb, fb), bf16),
            vmem(frames_shape, bf16),
            vmem(frames_shape, bf16),
            vmem(longer_shape, bf16),
            vmem(frames_shape, bf16),
            vmem(frames_shape, bf16),
            vmem(frames_shape, bf16),
            vmem(longer_shape, bf16),
            vmem(longer_shape, bf16),
            vmem((H, sz.K), bf16),
            vmem((H, sz.K), bf16),
            vmem((T + 8, H), f32),
            vmem((T + 8, H), f32),
            vmem((H, H), bf16),
            vmem((H, H), bf16),
            vmem((8 * Z, fb, qc), bf16),
            vmem((5 * Z, fb, qc), bf16),
            vmem((2, fb, qc), bf16),
            vmem((2, fb, qc), f32),
            vmem((8, H), f32),
            vmem((8, H), f32),
            vmem((16, H), f32),
            vmem((4, 8, H), f32),
            vmem((4, n, 8, fb), f32),
            vmem((4, 8, fb), f32),
            vmem((4, seqs, 8, fb), f32),
            vmem((4, n, 8, fb), f32),
            vmem((4, 8, H), f32),
            vmem((2, 8, H), f32),
            vmem((2, n, 8, fb), f32),
            vmem((2, 8, fb), f32),
            vmem((2, seqs, 8, fb), f32),
            sem((8,)),
            sem((n,)),
            sem((n,)),
            sem((4, n)),
            sem((4, n)),
            sem((2, 10 * Z)),
            sem((2, 10 * Z)),
            sem((8, n)),
            sem((8, n)),
            sem((4, seqs)),
            sem((4, seqs)),
            sem((2, 10 * Z)),
            sem((2, 10 * Z)),
            sem((2, 3)),
            sem((2, 3)),
            sem((2, n + seqs)),
            sem((2, n + seqs)),
        ],
        compiler_params=pltpu.CompilerParams(
            collective_id=0, has_side_effects=True, vmem_limit_bytes=63 * 1024 * 1024
        ),
        cost_estimate=pl.CostEstimate(
            flops=6 * matmul, bytes_accessed=16 * fb * H, transcendentals=6 * T * H
        ),
        name="network",
    )(
        inputs,
        out_grad,
        weight_one,
        weight_two,
        *(values.reshape(1, fb) for values in params),
        lengths,
        frame_mask.reshape(1, -1),
    )
    tok = inputs.shape[1]
    pairs = n // 2
    steps = pl.cdiv(tok, 2 * T)
    frames_spec = pl.BlockSpec((fb, 2 * T), lambda p: (0, p))
    land_spec = pl.BlockSpec((2, T, fb), lambda p: (jnp.minimum(p, pairs - 1), 0, 0))
    row_spec = pl.BlockSpec((1, fb), lambda p: (0, 0))
    results = pl.pallas_call(
        functools.partial(turn_back, sz, steps),
        grid=(steps,),
        out_shape=(jax.ShapeDtypeStruct((fb, tok), f32),) * 2
        + (jax.ShapeDtypeStruct((fb, H), f32),) * 2
        + (jax.ShapeDtypeStruct((1, fb), f32),) * 6,
        in_specs=[frames_spec, frames_spec, land_spec, land_spec, anywhere, anywhere]
        + [pl.BlockSpec((8, fb), lambda p: (0, 0))],
        out_specs=(frames_spec, frames_spec, anywhere, anywhere) + (row_spec,) * 6,
        scratch_shapes=[
            vmem((2, T, sz.win), bf16),
            vmem((2, fb, H), bf16),
            vmem((2, fb, H), f32),
            sem((2,)),
        ],
        compiler_params=pltpu.CompilerParams(vmem_limit_bytes=60 * 1024 * 1024),
        name="turn_back",
    )(inputs, out_grad, out_land, dx_land, dw_one, dw_two, small)
    output, input_grad, dw_one, dw_two = results[:4]
    small = [row.reshape(fb) for row in results[4:]]
    return (
        output,
        input_grad,
        dw_one,
        small[0],
        small[1],
        small[2],
        dw_two,
        small[3],
        small[4],
        small[5],
    )


def frame_tables(lengths, frame_mask):
    positions = jnp.arange(frame_mask.shape[0], dtype=jnp.int32)
    offsets = jnp.cumsum(lengths[0]) - lengths[0]
    filled = jnp.sum(lengths[0])
    begins = jnp.any(positions[:, None] == offsets[None, :], axis=1)
    continues = jnp.where(begins, 0.0, 1.0).astype(jnp.float32)
    counted = jnp.where((positions < filled) & (frame_mask > 0), 1.0, 0.0).astype(jnp.float32)
    return (continues, counted)


def linear_scan(coef_rows, driving, backwards):
    row_count, length = driving.shape
    block_count = length // block_span
    factor = coef_rows.reshape(row_count, block_count, block_span)
    running = driving.reshape(row_count, block_count, block_span)
    places = jnp.arange(block_span, dtype=jnp.int32)
    step = 1
    while step < block_span:
        if backwards:
            mover = jnp.where(places[:, None] == places[None, :] + step, 1.0, 0.0).astype(
                jnp.float32
            )
            edge = jnp.where(places >= block_span - step, 1.0, 0.0).astype(jnp.float32)
        else:
            mover = jnp.where(places[:, None] == places[None, :] - step, 1.0, 0.0).astype(
                jnp.float32
            )
            edge = jnp.where(places < step, 1.0, 0.0).astype(jnp.float32)
        moved_factor = (
            jnp.dot(
                factor, mover, precision=lax.Precision.HIGHEST, preferred_element_type=jnp.float32
            )
            + edge
        )
        moved_running = jnp.dot(
            running, mover, precision=lax.Precision.HIGHEST, preferred_element_type=jnp.float32
        )
        running = factor * moved_running + running
        factor = factor * moved_factor
        step = step * 2
    end_place = 0 if backwards else block_span - 1
    total_factor = factor[:, :, end_place].T
    total_running = running[:, :, end_place].T

    def carry_step(carried, block_pair):
        return (block_pair[0] * carried + block_pair[1], carried)

    _, entering = lax.scan(
        carry_step,
        jnp.zeros((row_count,), jnp.float32),
        (total_factor, total_running),
        reverse=backwards,
    )
    result = running + factor * entering.T[:, :, None]
    return result.reshape(row_count, length)


def layer_forward(layer_input, weight, gain_row, bias_row, decay_rate, continues, counted):
    frames_in = lax.all_to_all(layer_input, "neur", split_axis=1, concat_axis=0, tiled=True)
    projected = jnp.dot(
        lax.all_gather(weight, "neur", axis=0, tiled=True),
        frames_in,
        preferred_element_type=jnp.float32,
    )
    neuron_proj = lax.all_to_all(
        projected.astype(jnp.bfloat16), "neur", split_axis=0, concat_axis=1, tiled=True
    ).astype(jnp.float32)
    sum_first = jnp.sum(counted[None, :] * neuron_proj, axis=1)
    sum_second = jnp.sum(counted[None, :] * neuron_proj * neuron_proj, axis=1)
    sum_first, sum_second, frames = lax.psum((sum_first, sum_second, jnp.sum(counted)), "seq")
    average = sum_first / frames
    inv_std = lax.rsqrt(sum_second / frames - average * average + epsilon)
    normed = (neuron_proj - average[:, None]) * inv_std[:, None]
    spread = jnp.sqrt(1.0 - decay_rate * decay_rate)
    states = linear_scan(
        decay_rate[:, None] * continues[None, :], (spread * gain_row)[:, None] * normed, False
    )
    layer_out = counted[None, :] * jax.nn.softplus(states + bias_row[:, None])
    return (layer_out, (frames_in, None, normed, inv_std, frames, states))


def layer_backward(
    upstream, weight, gain_row, bias_row, decay_rate, continues, counted, kept_state
):
    frames_in, full_weight, normed, inv_std, frames, states = kept_state
    local_grad = upstream * counted[None, :] * jax.nn.sigmoid(states + bias_row[:, None])
    following = jnp.concatenate([continues[1:], jnp.zeros((1,), jnp.float32)])
    coef_rows = decay_rate[:, None] * following[None, :]
    state_grad = linear_scan(coef_rows, local_grad, True)
    sum_rec, sum_rec_norm, sum_local = lax.psum(
        (
            jnp.sum(state_grad, axis=1),
            jnp.sum(state_grad * normed, axis=1),
            jnp.sum(local_grad, axis=1),
        ),
        "seq",
    )
    spread = jnp.sqrt(1.0 - decay_rate * decay_rate)
    gain_grad = spread * sum_rec_norm
    proj_grad = (spread * gain_row * inv_std)[:, None] * (
        state_grad - counted[None, :] * (sum_rec[:, None] + sum_rec_norm[:, None] * normed) / frames
    )
    driving = (spread * gain_row)[:, None] * normed
    decay_part = jnp.sum(state_grad * (states - driving), axis=1) / decay_rate
    grad_frames = lax.all_to_all(
        proj_grad.astype(jnp.bfloat16), "neur", split_axis=1, concat_axis=0, tiled=True
    )
    grad_rows = grad_frames
    input_frames = jnp.einsum(
        "ot,oi->it",
        grad_rows,
        lax.all_gather(weight, "neur", axis=0, tiled=True),
        preferred_element_type=jnp.float32,
    )
    input_grad = lax.all_to_all(
        input_frames.astype(jnp.bfloat16), "neur", split_axis=0, concat_axis=1, tiled=True
    ).astype(jnp.float32)
    grad_rows = grad_frames
    weight_rows = lax.psum_scatter(
        jnp.einsum("ot,it->oi", grad_rows, frames_in, preferred_element_type=jnp.float32),
        "neur",
        scatter_dimension=0,
        tiled=True,
    )
    weight_grad, decay_sum = lax.psum((weight_rows, decay_part), "seq")
    decay_grad = decay_sum - decay_rate / spread * gain_row * sum_rec_norm
    return (input_grad, weight_grad, gain_grad, sum_local, decay_grad)


def shards(
    inputs,
    weight_one,
    weight_two,
    gain_one,
    gain_two,
    bias_one,
    bias_two,
    decay_one,
    decay_two,
    lengths,
    frame_mask,
    out_grad,
):
    seqs, n = lax.axis_size("seq"), lax.axis_size("neur")
    H, (fb, tok) = weight_one.shape[1], inputs.shape
    if fits(n, seqs, H, fb, tok):
        params = (gain_one, gain_two, bias_one, bias_two, decay_one, decay_two)
        return frames_apart(
            Sizes(n, seqs, H, fb, tok),
            inputs,
            weight_one,
            weight_two,
            params,
            lengths,
            frame_mask,
            out_grad,
        )
    continues, counted = frame_tables(lengths, frame_mask)
    first_out, first_kept = layer_forward(
        inputs, weight_one, gain_one, bias_one, decay_one, continues, counted
    )
    second_out, second_kept = layer_forward(
        first_out.astype(jnp.bfloat16),
        weight_two,
        gain_two,
        bias_two,
        decay_two,
        continues,
        counted,
    )
    output = inputs.astype(jnp.float32) + second_out
    upstream = out_grad.astype(jnp.float32)
    middle_grad, weight_two_grad, gain_two_grad, bias_two_grad, decay_two_grad = layer_backward(
        upstream, weight_two, gain_two, bias_two, decay_two, continues, counted, second_kept
    )
    lower_grad, weight_one_grad, gain_one_grad, bias_one_grad, decay_one_grad = layer_backward(
        middle_grad, weight_one, gain_one, bias_one, decay_one, continues, counted, first_kept
    )
    return (
        output,
        upstream + lower_grad,
        weight_one_grad,
        gain_one_grad,
        bias_one_grad,
        decay_one_grad,
        weight_two_grad,
        gain_two_grad,
        bias_two_grad,
        decay_two_grad,
    )


def solution(mesh):
    placed = (
        P("neur", "seq"),
        P("neur", None),
        P("neur", None),
        P("neur"),
        P("neur"),
        P("neur"),
        P("neur"),
        P("neur"),
        P("neur"),
        P("seq", None),
        P("seq"),
        P("neur", "seq"),
    )
    return jax.shard_map(
        shards,
        mesh=mesh,
        in_specs=placed,
        out_specs=(
            P("neur", "seq"),
            P("neur", "seq"),
            P("neur", None),
            P("neur"),
            P("neur"),
            P("neur"),
            P("neur", None),
            P("neur"),
            P("neur"),
            P("neur"),
        ),
        check_vma=False,
    )
```

```python
import functools

import jax
import jax.numpy as jnp
from jax import lax
from jax.experimental import pallas as pl
from jax.experimental.pallas import tpu as pltpu
from jax.sharding import PartitionSpec as P

epsilon = 1e-05
block_span = 128
valid_frames = 3584
f32 = jnp.float32
bf16 = jnp.bfloat16
MESH = pl.DeviceIdType.MESH


def wide(tile, width):
    return jnp.concatenate([tile] * (width // 128), axis=1)


def at(index, size):
    if isinstance(index, int):
        return pl.ds(index * size, size)
    return pl.ds(pl.multiple_of(index * size, size), size)


def power(base, exponent):
    result = None
    while exponent:
        if exponent % 2:
            result = base if result is None else result * base
        exponent //= 2
        base = base * base
    return result


def log_of(rate):
    u = 1.0 - rate
    series = jnp.full_like(u, 1.0 / 8)
    for order in range(7, 0, -1):
        series = series * u + 1.0 / order
    return -u * series


GAIN, BIAS, DECAY = 0, 2, 4


class Sizes:
    def __init__(self, n, seqs, H, fb, tok_dev):
        self.n, self.seqs, self.H, self.fb, self.tok_dev = n, seqs, H, fb, tok_dev
        self.T = valid_frames // n
        self.steps = self.T // 8
        self.valid = valid_frames
        self.qc = H // seqs
        self.Z = n // 2
        self.odd = self.T % 128
        self.win = self.T + self.odd
        self.K = self.T + 16
        self.L = min(512, H)


def fits(n, seqs, H, fb, tok_dev):
    if n not in (4, 8) or valid_frames % n or seqs != 4 or fb * n != H or fb % 128 or H % 512:
        return False
    T = valid_frames // n
    return T % 64 == 0 and valid_frames % 128 == 0 and tok_dev >= valid_frames


class Line:
    def __init__(self, env, sends, recvs):
        self.env, self.sends, self.recvs = env, sends, recvs

    def copy(self, k, source, dest, target):
        return pltpu.make_async_remote_copy(
            src_ref=source,
            dst_ref=dest,
            send_sem=self.sends.at[k],
            recv_sem=self.recvs.at[k],
            device_id=target,
            device_id_type=MESH,
        )

    def arrived(self, k, ref):
        self.copy(k, ref, ref, self.env.across("x")).wait_recv()

    def sent(self, k, ref):
        self.copy(k, ref, ref, self.env.across("x")).wait_send()

    def along(self, dz):
        z, Z = self.env.z, self.env.sz.Z
        if dz == 0:
            return [(None, z, 0)]
        return [(z >= dz, z - dz, 1), (z + dz < Z, z + dz, -1)]


def if_so(condition, body):
    if condition is None:
        body()
    else:
        pl.when(condition)(body)


class Gather(Line):
    def __init__(self, env, source, full, sends, recvs, cut):
        super().__init__(env, sends, recvs)
        self.cut = cut
        self.full = full
        self.source = source.at[:, at(env.s, env.sz.qc)]

    def block(self, zz, fx, fy, fc=0):
        env = self.env
        rows = at(2 * zz + (env.x + fx) % 2, env.sz.fb)
        return self.full.at[rows, at(2 * ((env.y + fy) % 2) + (env.c + fc) % 2, env.sz.qc)]

    def half(self, ref, h):
        if h == 0:
            return ref.at[pl.ds(0, self.cut), :]
        return ref.at[pl.ds(self.cut, self.env.sz.fb - self.cut), :]

    def spread(self, zz, source):
        env, Z = self.env, self.env.sz.Z
        dest = self.block(zz, 0, 0)
        self.copy(2 * Z + zz, source, dest, env.across("x")).start()
        self.copy(3 * Z + zz, source, dest, env.across("y")).start()
        self.copy(6 * Z + zz, source, dest, env.across("core")).start()

    def pass_on(self, zz, source, way):
        env, Z = self.env, self.env.sz.Z
        dest = self.block(zz, 0, 0)

        def go():
            pltpu.make_async_remote_copy(
                src_ref=source,
                dst_ref=dest,
                send_sem=self.sends.at[zz if way > 0 else Z + zz],
                recv_sem=self.recvs.at[zz],
                device_id={"neur": 2 * (env.z + way) + env.x},
                device_id_type=MESH,
            ).start()

        pl.when(env.z < Z - 1 if way > 0 else env.z > 0)(go)

    def start(self):
        z = self.env.z
        self.pass_on(z, self.source, 1)
        self.pass_on(z, self.source, -1)
        self.spread(z, self.source)

    def line(self, dz):
        for condition, zz, way in self.along(dz):

            def one(zz=zz, way=way):
                block = self.block(zz, 0, 0)
                self.arrived(zz, block)
                self.pass_on(zz, block, way)
                self.spread(zz, block)

            if_so(condition, one)

    def sides(self, dz):
        env, Z = self.env, self.env.sz.Z
        for condition, zz, _ in self.along(dz):

            def one(zz=zz):
                block = self.block(zz, 1, 0)
                self.arrived(2 * Z + zz, block)
                part = self.half(block, 1)
                self.copy(5 * Z + zz, part, part, env.across("y")).start()
                self.copy(7 * Z + zz, block, block, env.across("core")).start()
                block = self.block(zz, 0, 1)
                self.arrived(3 * Z + zz, block)
                part = self.half(block, 0)
                self.copy(4 * Z + zz, part, part, env.across("x")).start()
                self.copy(8 * Z + zz, block, block, env.across("core")).start()

            if_so(condition, one)

    def diagonals(self):
        env, Z = self.env, self.env.sz.Z
        for dz in range(Z):
            for condition, zz, _ in self.along(dz):

                def one(zz=zz):
                    block = self.block(zz, 1, 1)
                    self.arrived(4 * Z + zz, self.half(block, 0))
                    self.arrived(5 * Z + zz, self.half(block, 1))
                    self.copy(9 * Z + zz, block, block, env.across("core")).start()

                if_so(condition, one)

    def cores(self):
        Z = self.env.sz.Z
        for k, (fx, fy) in enumerate(((0, 0), (1, 0), (0, 1), (1, 1))):
            for zz in range(Z):
                self.arrived((6 + k) * Z + zz, self.block(zz, fx, fy, 1))

    def drain(self):
        env, Z = self.env, self.env.sz.Z
        block = self.block(0, 0, 0)
        for zz in range(Z):
            pl.when((zz <= env.z) & (env.z < Z - 1))(lambda zz=zz: self.sent(zz, block))
            pl.when((zz >= env.z) & (env.z > 0))(lambda zz=zz: self.sent(Z + zz, block))
            for k in (2, 3, 6, 7, 8, 9):
                self.sent(k * Z + zz, block)
            self.sent(4 * Z + zz, self.half(block, 0))
            self.sent(5 * Z + zz, self.half(block, 1))


class Reduce(Line):
    kinds = ((1, 1), (1, 0), (0, 1), (0, 0))

    def __init__(self, env, grads, frames, land, spare, stage, held, total, sends, recvs, cut):
        super().__init__(env, sends, recvs)
        self.cut, self.held = cut, held
        self.grads, self.frames, self.land, self.spare = grads, frames, land, spare
        self.stage, self.total = stage, total

    def product(self, kind, zz, fc=0):
        env, sz = self.env, self.env.sz
        fx, fy = self.kinds[kind]
        rows = at(2 * zz + (env.x + fx) % 2, sz.fb)
        columns = at(2 * ((env.y + fy) % 2) + (env.c + fc) % 2, sz.qc)
        return jnp.dot(
            self.grads[rows, :], self.frames[:, columns], preferred_element_type=f32
        )

    def half(self, ref, h):
        if h == 0:
            return ref.at[pl.ds(0, self.cut), :]
        return ref.at[pl.ds(self.cut, self.env.sz.fb - self.cut), :]

    def landed(self, k, slot):
        self.arrived(k, self.land(slot))
        return self.land(slot)[...].astype(f32)

    def turn(self, i):
        z, Z = self.env.z, self.env.sz.Z
        low = jnp.where(i < Z - 1 - z, Z - 1 - i, i - (Z - 1 - z))
        high = jnp.where(i < z, i, Z - 1 - (i - z))
        return jnp.where(i == Z - 1, z, jnp.where(z < Z // 2, low, high))

    def cores(self, kind):
        env, Z = self.env, self.env.sz.Z

        def one(i, _):
            zz = self.turn(i)
            k = kind * Z + zz
            held = (kind % 2) * Z + zz
            if kind >= 2:
                self.sent(k - 2 * Z, self.stage.at[held])
            self.stage[held] = self.product(kind, zz, 1).astype(bf16)
            self.copy(k, self.stage.at[held], self.land(k), env.across("core")).start()
            return 0

        lax.fori_loop(0, Z, one, 0)

    def diagonals(self):
        env, Z = self.env, self.env.sz.Z

        def one(i, _):
            zz = self.turn(i)
            held = self.held(zz)
            held[...] = (self.product(0, zz) + self.landed(zz, zz)).astype(bf16)
            slot = self.land(4 * Z + zz)
            for k, h, axis in ((4, 0, "x"), (5, 1, "y")):
                self.copy(
                    k * Z + zz, self.half(held, h), self.half(slot, h), env.across(axis)
                ).start()
            return 0

        lax.fori_loop(0, Z, one, 0)

    def sides(self, low=0, high=None):
        env, Z = self.env, self.env.sz.Z
        spans = slice(0, self.cut), slice(self.cut, env.sz.fb)

        def one(i, _):
            zz = self.turn(i)
            slot = self.land(4 * Z + zz)
            for kind, h, wait, k, axis in ((1, 1, 5, 6, "x"), (2, 0, 4, 7, "y")):
                tile = self.product(kind, zz) + self.landed(kind * Z + zz, kind * Z + zz)
                part = self.half(slot, h)
                self.arrived(wait * Z + zz, part)
                held = self.stage.at[(2 + kind) * Z + zz]
                other = 1 - h
                summed = tile[spans[h], :] + part[...].astype(f32)
                self.half(held, h)[...] = summed.astype(bf16)
                self.half(held, other)[...] = tile[spans[other], :].astype(bf16)
                self.copy(
                    k * Z + zz, held, self.land((4 + kind) * Z + zz), env.across(axis)
                ).start()
            return 0

        lax.fori_loop(low, Z if high is None else high, one, 0)

    def joined(self, zz):
        Z = self.env.sz.Z
        tile = self.product(3, zz) + self.landed(3 * Z + zz, 3 * Z + zz)
        tile = tile + self.landed(6 * Z + zz, 5 * Z + zz)
        self.total[...] = tile + self.landed(7 * Z + zz, 6 * Z + zz)

    def lines(self, low=0, high=None):
        env, Z, z = self.env, self.env.sz.Z, self.env.z
        def onward(zz, way):
            k, slot = (8 if way > 0 else 9) * Z + zz, 7 * Z + zz
            self.joined(zz)

            @pl.when(z > 0 if way > 0 else z < Z - 1)
            def _():
                self.total[...] += self.landed(k, slot)

            held = self.held(zz)
            self.sent(4 * Z + zz, self.half(held, 0))
            self.sent(5 * Z + zz, self.half(held, 1))
            held[...] = self.total[...].astype(bf16)
            target = {"neur": 2 * (z + way) + env.x}
            if way > 0:
                self.copy(k, held, self.land(slot), target).start()
            else:
                pl.when(zz == z - 1)(lambda: self.copy(k, held, self.spare, target).start())
                pl.when(zz != z - 1)(lambda: self.copy(k, held, self.land(slot), target).start())

        for i in range(low, Z - 1 if high is None else high):
            zz = self.turn(i)
            pl.when(zz > z)(functools.partial(onward, zz, 1))
            pl.when(zz < z)(functools.partial(onward, zz, -1))

    def finish(self):
        Z, z = self.env.sz.Z, self.env.z
        self.joined(z)
        @pl.when(z > 0)
        def _():
            self.total[...] += self.landed(8 * Z + z, 7 * Z + z)

        @pl.when(z < Z - 1)
        def _():
            self.arrived(9 * Z + z, self.spare)
            self.total[...] += self.spare[...].astype(f32)

    def drain_cores(self):
        for k in range(2 * self.env.sz.Z, 4 * self.env.sz.Z):
            self.sent(k, self.stage.at[0])

    def drain_sides(self):
        for k in range(6 * self.env.sz.Z, 8 * self.env.sz.Z):
            self.sent(k, self.stage.at[0])

    def drain(self):
        Z, z = self.env.sz.Z, self.env.z
        held = self.stage.at[0]
        for zz in range(Z):
            for k in (4, 5):
                pl.when(zz == z)(
                    lambda k=k, zz=zz: self.sent(k * Z + zz, self.half(held, k - 4))
                )
            pl.when(zz > z)(lambda zz=zz: self.sent(8 * Z + zz, held))
            pl.when(zz < z)(lambda zz=zz: self.sent(9 * Z + zz, held))


class Result:
    def __init__(self, env, whole, block, sends, recvs, local):
        self.env, self.whole, self.block = env, whole, block
        self.sends, self.recvs, self.local = sends, recvs, local

    def part(self, flip_y, flip_c):
        env = self.env
        s = 2 * ((env.y + flip_y) % 2) + (env.c + flip_c) % 2
        return self.whole.at[:, at(s, env.sz.qc)]

    def copy(self, k, source, dest, target):
        return pltpu.make_async_remote_copy(
            src_ref=source,
            dst_ref=dest,
            send_sem=self.sends.at[k],
            recv_sem=self.recvs.at[k],
            device_id=target,
            device_id_type=MESH,
        )

    def start(self):
        env, own = self.env, self.part(0, 0)
        self.copy(0, self.block, own, env.across("y")).start()
        self.copy(1, self.block, own, env.across("core")).start()
        pltpu.make_async_copy(self.block, own, self.local).start()

    def finish(self):
        env = self.env
        other = self.part(1, 0)
        self.copy(0, self.block, other, env.across("y")).wait_recv()
        forward = self.copy(2, other, other, env.across("core"))
        forward.start()
        own = self.part(0, 0)
        pltpu.make_async_copy(self.block, own, self.local).wait()
        self.copy(0, self.block, own, env.across("y")).wait_send()
        self.copy(1, self.block, self.part(0, 1), env.across("core")).wait()
        forward.wait_send()
        self.copy(2, other, self.part(1, 1), env.across("core")).wait_recv()


class Env:
    def across(self, axis):
        if axis == "x":
            return {"neur": 2 * self.z + 1 - self.x}
        if axis == "y":
            return {"seq": 2 * (1 - self.y) + self.c}
        return {"seq": 2 * self.y + 1 - self.c}


def network(
    sz,
    x_hbm,
    g_hbm,
    w_one,
    w_two,
    gain_one,
    gain_two,
    bias_one,
    bias_two,
    decay_one,
    decay_two,
    lengths,
    frame_mask,
    out_land,
    dx_land,
    dw_one,
    dw_two,
    small,
    own_par,
    cont,
    counted,
    aux,
    frames_sum,
    raw,
    perm,
    eye,
    xs,
    gs,
    xr,
    gr,
    p_one,
    p_two,
    x_two,
    dp,
    dpt_one,
    dpt_two,
    s_one,
    s_two,
    wf_one,
    wf_two,
    land,
    stage,
    spare,
    fin,
    par,
    ends,
    work,
    pay,
    arrive,
    seqpay,
    seqland,
    back,
    backland,
    sumpay,
    sumland,
    sumseq,
    sumseqland,
    local_sems,
    par_sends,
    par_recvs,
    frame_sends,
    frame_recvs,
    gather_sends,
    gather_recvs,
    hop_sends,
    hop_recvs,
    seq_sends,
    seq_recvs,
    reduce_sends,
    reduce_recvs,
    final_sends,
    final_recvs,
    sum_sends,
    sum_recvs,
):
    n, seqs, H, fb, T, steps, L = sz.n, sz.seqs, sz.H, sz.fb, sz.T, sz.steps, sz.L
    env = Env()
    env.sz = sz
    me = lax.axis_index("neur")
    mine = lax.axis_index("seq")
    env.j, env.s = me, mine
    env.z, env.x, env.y, env.c = me // 2, me % 2, mine // 2, mine % 2

    barrier = pltpu.get_barrier_semaphore()
    for o in range(1, n):
        pl.semaphore_signal(
            barrier, inc=1, device_id={"neur": (me + o) % n}, device_id_type=MESH
        )
    for o in range(1, seqs):
        pl.semaphore_signal(
            barrier, inc=1, device_id={"seq": (mine + o) % seqs}, device_id_type=MESH
        )
    load_x = pltpu.make_async_copy(x_hbm.at[:, pl.ds(0, sz.valid)], raw, local_sems.at[0])
    load_x.start()
    for r, values in enumerate((gain_one, gain_two, bias_one, bias_two, decay_one, decay_two)):
        own_par[r : r + 1, :] = values[...]
    own_par[6:8, :] = jnp.zeros((2, fb), f32)
    pl.semaphore_wait(barrier, n - 1 + seqs - 1)

    def neur_copy(source, dest, send, recv, i):
        return pltpu.make_async_remote_copy(
            src_ref=source,
            dst_ref=dest,
            send_sem=send,
            recv_sem=recv,
            device_id={"neur": i},
            device_id_type=MESH,
        )

    def seq_copy(source, dest, send, recv, i):
        return pltpu.make_async_remote_copy(
            src_ref=source,
            dst_ref=dest,
            send_sem=send,
            recv_sem=recv,
            device_id={"seq": i},
            device_id_type=MESH,
        )

    def straight(body, low=1, high=n // 2):
        lax.fori_loop(low, high, lambda o, _: (body((me + 2 * o) % n), 0)[1], 0)

    def crossing(body, low=0, high=n // 2):
        lax.fori_loop(low, high, lambda o, _: (body((me + 2 * o + 1) % n), 0)[1], 0)

    def others(body, count=n, own=me):
        def one(o, _):
            body((own + o) % count)
            return 0

        lax.fori_loop(1, count, one, 0)

    own_lanes = at(me, fb)

    def par_copy(i):
        return neur_copy(own_par, par.at[:, own_lanes], par_sends.at[i], par_recvs.at[me], i)

    def par_wait(i):
        neur_copy(own_par, par.at[:, at(i, fb)], par_sends.at[i], par_recvs.at[i], i).wait()

    others(lambda i: par_copy(i).start())
    par[:, own_lanes] = own_par[...]

    cuts = (fb // 4, 3 * fb // 8)
    gather_one = Gather(env, w_one, wf_one, gather_sends.at[0], gather_recvs.at[0], cuts[0])
    gather_two = Gather(env, w_two, wf_two, gather_sends.at[1], gather_recvs.at[1], cuts[1])
    own_one = pltpu.make_async_copy(gather_one.source, gather_one.block(env.z, 0, 0), local_sems.at[2])
    own_two = pltpu.make_async_copy(gather_two.source, gather_two.block(env.z, 0, 0), local_sems.at[3])
    own_one.start()
    own_two.start()
    gather_one.start()
    gather_two.start()

    row = lax.broadcasted_iota(jnp.int32, (T, sz.win), 0)
    column = lax.broadcasted_iota(jnp.int32, (T, sz.win), 1)
    frame = (row & 7) * steps + (row >> 3)
    perm[0] = jnp.where(column == frame, 1.0, 0.0).astype(bf16)
    perm[1] = jnp.where(column == frame + sz.odd, 1.0, 0.0).astype(bf16)
    row = lax.broadcasted_iota(jnp.int32, (fb, fb), 0)
    column = lax.broadcasted_iota(jnp.int32, (fb, fb), 1)
    eye[...] = jnp.where(row == column, 1.0, 0.0).astype(bf16)

    def window(i):
        start = (i // 2) * (2 * T) + (i % 2) * (T - sz.odd)
        return pl.ds(pl.multiple_of(start, 128), sz.win)

    def turned(i):
        return lax.dot_general(
            perm[i % 2], raw[:, window(i)], (((1,), (1,)), ((), ())), preferred_element_type=f32
        ).astype(bf16)

    def frames_copy(a, source, dest, i):
        return neur_copy(source, dest, frame_sends.at[a, i], frame_recvs.at[a, me], i)

    def frames_wait(a, ref, i):
        part = ref.at[pl.ds(0, T), at(i, fb)]
        neur_copy(part, part, frame_sends.at[a, i], frame_recvs.at[a, i], i).wait_recv()

    def frames_sent(a, ref, i):
        part = ref.at[pl.ds(0, T), at(i, fb)]
        neur_copy(part, part, frame_sends.at[a, i], frame_recvs.at[a, i], i).wait_send()

    load_x.wait()

    def turn_x(i):
        xs[:, at(i, fb)] = turned(i)

    def send_x(i):
        frames_copy(0, xs.at[:, at(i, fb)], xr.at[pl.ds(0, T), own_lanes], i).start()

    def send_all_x():
        crossing(send_x)
        straight(send_x)

    others(turn_x)
    xr[0:T, own_lanes] = turned(me)
    load_g = pltpu.make_async_copy(g_hbm.at[:, pl.ds(0, sz.valid)], raw, local_sems.at[1])
    load_g.start()
    def turn_g(i):
        gs[:, at(i, fb)] = turned(i)

    def send_g(i):
        frames_copy(1, gs.at[:, at(i, fb)], gr.at[:, own_lanes], i).start()

    ends_of_line = (env.z == 0) | (env.z == sz.Z - 1)
    pl.when(ends_of_line)(send_all_x)
    for dz in range(1, sz.Z):
        gather_one.line(dz)
        gather_two.line(dz)
        if dz == max(1, sz.Z - 2):
            pl.when(jnp.logical_not(ends_of_line))(send_all_x)
            frame_tables_of(sz, me, lengths, frame_mask, perm, window(me), cont, counted, aux)
            load_g.wait()
            others(turn_g)
            gr[:, own_lanes] = turned(me)
        gather_one.sides(dz - 1)
    gather_one.sides(sz.Z - 1)
    gather_two.sides(0)
    straight(send_g)
    crossing(send_g, 0, 1)
    gather_one.diagonals()
    for dz in range(1, sz.Z):
        gather_two.sides(dz)
    gather_one.cores()
    own_one.wait()
    own_two.wait()
    others(lambda i: frames_wait(0, xr, i))
    others(par_wait)

    def blocks(body):
        def one(b, _):
            body(at(b, L))
            return 0

        lax.fori_loop(0, H // L, one, 0)

    def project(frames, weight, result):
        def one(b, _):
            result[:, at(b, 2 * fb)] = lax.dot_general(
                frames[0:T, :],
                weight[at(b, 2 * fb), :],
                (((1,), (1,)), ((), ())),
                preferred_element_type=f32,
            ).astype(bf16)
            return 0

        lax.fori_loop(0, n // 2, one, 0)

    def flags(t):
        tile = pl.ds(pl.multiple_of(8 * t, 8), 8)
        return wide(cont[tile, :], L), wide(counted[tile, :], L)

    def spread8(ref, r, cols, width=L):
        return jnp.broadcast_to(ref[r : r + 1, cols], (8, width))

    zero = jnp.zeros((8, L), f32)

    def down(value):
        return jnp.sum(value, axis=0, keepdims=True)

    def exchange(e, gathered, totalled, gap):
        ahead = pl.ds(0, 4 if e < 2 else 8)
        behind = pl.ds(0, 4)

        def out_copy(i):
            return neur_copy(
                pay.at[e, ahead, at(i, fb)],
                arrive.at[e, me, ahead],
                hop_sends.at[2 * e, i],
                hop_recvs.at[2 * e, me],
                i,
            )

        others(lambda i: out_copy(i).start())
        arrive[e, me, ahead] = pay[e, ahead, own_lanes]
        gap("hop_a")

        def out_wait(i):
            neur_copy(
                pay.at[e, ahead, at(i, fb)],
                arrive.at[e, i, ahead],
                hop_sends.at[2 * e, i],
                hop_recvs.at[2 * e, i],
                i,
            ).wait()

        others(out_wait)
        gathered()

        def along_copy(i):
            return seq_copy(
                seqpay.at[e],
                seqland.at[e, mine],
                seq_sends.at[e, i],
                seq_recvs.at[e, mine],
                i,
            )

        def along_wait(i):
            seq_copy(
                seqpay.at[e], seqland.at[e, i], seq_sends.at[e, i], seq_recvs.at[e, i], i
            ).wait()

        others(lambda i: along_copy(i).start(), seqs, mine)
        seqland[e, mine] = seqpay[e]
        gap("hop_b")
        others(along_wait, seqs, mine)
        sums = seqland[e, 0]
        for i in range(1, seqs):
            sums = sums + seqland[e, i]
        totalled(sums)

        def back_copy(i):
            return neur_copy(
                back.at[e, i, behind],
                backland.at[e, behind, own_lanes],
                hop_sends.at[2 * e + 1, i],
                hop_recvs.at[2 * e + 1, me],
                i,
            )

        def back_wait(i):
            neur_copy(
                back.at[e, i, behind],
                backland.at[e, behind, at(i, fb)],
                hop_sends.at[2 * e + 1, i],
                hop_recvs.at[2 * e + 1, i],
                i,
            ).wait()

        others(lambda i: back_copy(i).start())
        backland[e, behind, own_lanes] = back[e, me, behind]
        gap("hop_c")
        others(back_wait)

    def layer_forward(layer, frames, weight, projected, states, store, gap):
        e = layer
        decay_row, gain_row, bias_row = DECAY + layer, GAIN + layer, BIAS + layer
        project(frames, weight, projected)
        gap("ends")

        def local_ends(cols):
            decay = spread8(par, decay_row, cols)

            def step(i, carry):
                state, first, second, inward = carry
                pair = projected[pl.ds(pl.multiple_of(16 * i, 16), 16), cols].astype(f32)
                for h in range(2):
                    value = pair[8 * h : 8 * h + 8, :]
                    goes, count = flags(2 * i + h)
                    state = (decay * goes) * state + value
                    held = count * value
                    first = first + held
                    second = second + held * value
                ins = frames[pl.ds(pl.multiple_of(16 * i, 16), 16), cols].astype(f32)
                return state, first, second, inward + ins[0:8, :] + ins[8:16, :]

            state, first, second, inward = lax.fori_loop(
                0, T // 16, step, (zero, zero, zero, zero)
            )
            ends[:, cols] = state
            pay[e, 1:2, cols] = down(first)
            pay[e, 2:3, cols] = down(second)
            pay[e, 3:4, cols] = down(inward)

        blocks(local_ends)
        run_power = power(par[decay_row : decay_row + 1, :], steps)
        total = jnp.zeros((1, H), f32)
        for k in range(8):
            total = run_power * wide(aux[16 + k : 17 + k, :], H) * total + ends[k : k + 1, :]
        pay[e, 0:1, :] = total

        own_decay = own_par[decay_row : decay_row + 1, :]

        def gathered():
            whole_power = power(own_decay, T)
            carried = jnp.zeros((1, fb), f32)
            sums = jnp.zeros((4, fb), f32)
            for i in range(n):
                rows = arrive[e, i, 0:4, :]
                back[e, i, 0:1, :] = carried
                carried = whole_power * wide(aux[8 + i : 9 + i, :], fb) * carried + rows[0:1, :]
                sums = sums + rows
            seqpay[e, 0:4, :] = sums
            seqpay[e, 4:8, :] = jnp.zeros((4, fb), f32)
            seqpay[e, 0:1, :] = wide(aux[24:25, :], fb)

        def totalled(sums):
            frames_all = sums[0:1, :]
            average = sums[1:2, :] / frames_all
            inv_std = lax.rsqrt(sums[2:3, :] / frames_all - average * average + epsilon)
            centre = sums[3:4, :] / (sz.valid * seqs)
            for i in range(n):
                back[e, i, 1:2, :] = average
                back[e, i, 2:3, :] = inv_std
                back[e, i, 3:4, :] = centre
            frames_sum[...] = frames_all[:, 0:128]

        exchange(e, gathered, totalled, gap)
        centre = backland[e, 3:4, :]
        frames[T : T + 16, :] = jnp.concatenate(
            [-centre, -centre, -centre, jnp.zeros((13, H), f32)], axis=0
        ).astype(bf16)

        total = backland[e, 0:1, :]
        for k in range(8):
            work[k : k + 1, :] = total
            total = run_power * wide(aux[16 + k : 17 + k, :], H) * total + ends[k : k + 1, :]

        gap("scan")

        def full_scan(cols):
            decay = spread8(par, decay_row, cols)
            average = spread8(backland.at[e], 1, cols)
            inv_std = spread8(backland.at[e], 2, cols)
            bias = spread8(par, bias_row, cols)
            scale = jnp.sqrt(1.0 - decay * decay) * spread8(par, gain_row, cols) * inv_std
            ones = (1.0 - jnp.exp(wide(aux[0:8, :], L) * log_of(decay))) / (1.0 - decay)
            state = scale * (work[0:8, cols] - average * ones)
            states[0:8, cols] = state

            def step(i, state):
                pair = projected[pl.ds(pl.multiple_of(16 * i, 16), 16), cols].astype(f32)
                outs = []
                for h in range(2):
                    goes, count = flags(2 * i + h)
                    state = (decay * goes) * state + scale * (pair[8 * h : 8 * h + 8, :] - average)
                    states[pl.ds(pl.multiple_of(16 * i + 8 * h + 8, 8), 8), cols] = state
                    v = state + bias
                    soft = jnp.maximum(v, 0.0) + jnp.log(1.0 + jnp.exp(-jnp.abs(v)))
                    outs.append(count * soft)
                store[pl.ds(pl.multiple_of(16 * i, 16), 16), cols] = jnp.concatenate(
                    outs, axis=0
                ).astype(bf16)
                return state

            lax.fori_loop(0, T // 16, step, state)

        blocks(full_scan)

    def layer_backward(layer, upstream, projected, states, turned_grads, gap):
        e = 2 + (1 - layer)
        decay_row, gain_row, bias_row = DECAY + layer, GAIN + layer, BIAS + layer
        run_power = power(par[decay_row : decay_row + 1, :], steps)

        def local_ends(cols):
            decay = spread8(par, decay_row, cols)
            average = spread8(backland.at[layer], 1, cols)
            inv_std = spread8(backland.at[layer], 2, cols)
            bias = spread8(par, bias_row, cols)

            def step(o, carry):
                i = T // 16 - 1 - o
                rows = pl.ds(pl.multiple_of(16 * i, 16), 16)
                pair = projected[rows, cols].astype(f32)
                ups = upstream[rows, cols].astype(f32)
                for h in (1, 0):
                    run, reach, U, V, UN, VN, B, D, DA = carry
                    goes, count = flags(2 * i + h)
                    here = pl.ds(pl.multiple_of(16 * i + 8 * h + 8, 8), 8)
                    state = states[here, cols]
                    before = states[pl.ds(pl.multiple_of(16 * i + 8 * h, 8), 8), cols]
                    local = ups[8 * h : 8 * h + 8, :] * count / (1.0 + jnp.exp(-(state + bias)))
                    states[here, cols] = local
                    normed = (pair[8 * h : 8 * h + 8, :] - average) * inv_std
                    run = local + run
                    kept = goes * before
                    link = decay * goes
                    carry = (
                        link * run,
                        link * reach,
                        U + run,
                        V + reach,
                        UN + run * normed,
                        VN + reach * normed,
                        B + local,
                        D + run * kept,
                        DA + reach * kept,
                    )
                return carry

            one = jnp.ones((8, L), f32)
            run, _, U, V, UN, VN, B, D, DA = lax.fori_loop(
                0, T // 16, step, (zero, one, zero, zero, zero, zero, zero, zero, zero)
            )
            ends[:, cols] = run
            decay_run = power(par[decay_row : decay_row + 1, cols], steps)
            part, factor = jnp.zeros((1, L), f32), jnp.ones((1, L), f32)
            for k in range(7, -1, -1):
                work[k : k + 1, cols] = part
                work[8 + k : 9 + k, cols] = factor
                through = decay_run * wide(aux[16 + k : 17 + k, :], L)
                part = through * part + ends[k : k + 1, cols]
                factor = through * factor
            pay[e, 0:1, cols] = part
            entering, scaled = work[0:8, cols], work[8:16, cols]
            pay[e, 1:2, cols] = down(U + V * entering)
            pay[e, 2:3, cols] = down(V * scaled)
            pay[e, 3:4, cols] = down(UN + VN * entering)
            pay[e, 4:5, cols] = down(VN * scaled)
            pay[e, 5:6, cols] = down(B)
            pay[e, 6:7, cols] = down(D + DA * entering)
            pay[e, 7:8, cols] = down(DA * scaled)

        blocks(local_ends)
        own_decay = own_par[decay_row : decay_row + 1, :]
        own_gain = own_par[gain_row : gain_row + 1, :]

        def gathered():
            whole_power = power(own_decay, T)
            carried = jnp.zeros((1, fb), f32)
            sums = [jnp.zeros((1, fb), f32)] * 4
            for i in range(n - 1, -1, -1):
                rows = arrive[e, i]
                back[e, i, 0:1, :] = carried
                for a, (plain, times) in enumerate(((1, 2), (3, 4), (5, None), (6, 7))):
                    term = rows[plain : plain + 1, :]
                    if times is not None:
                        term = term + rows[times : times + 1, :] * carried
                    sums[a] = sums[a] + term
                carried = whole_power * wide(aux[8 + i : 9 + i, :], fb) * carried + rows[0:1, :]
            for a in range(4):
                seqpay[e, a : a + 1, :] = sums[a]
            seqpay[e, 4:8, :] = jnp.zeros((4, fb), f32)

        def totalled(sums):
            rec, rec_norm = sums[0:1, :], sums[1:2, :]
            for i in range(n):
                back[e, i, 1:2, :] = rec
                back[e, i, 2:3, :] = rec_norm
                back[e, i, 3:4, :] = jnp.zeros((1, fb), f32)
            spread = jnp.sqrt(1.0 - own_decay * own_decay)
            small[3 * layer : 3 * layer + 1, :] = spread * rec_norm
            small[3 * layer + 1 : 3 * layer + 2, :] = sums[2:3, :]
            small[3 * layer + 2 : 3 * layer + 3, :] = (
                sums[3:4, :] - own_decay / spread * own_gain * rec_norm
            )

        exchange(e, gathered, totalled, gap)
        gap("scan")
        total = backland[e, 0:1, :]
        for k in range(7, -1, -1):
            work[k : k + 1, :] = total
            total = run_power * wide(aux[16 + k : 17 + k, :], H) * total + ends[k : k + 1, :]

        def full_scan(cols):
            decay = spread8(par, decay_row, cols)
            average = spread8(backland.at[layer], 1, cols)
            inv_std = spread8(backland.at[layer], 2, cols)
            frames_all = wide(frames_sum[...], L)
            scale = jnp.sqrt(1.0 - decay * decay) * spread8(par, gain_row, cols) * inv_std
            rec = spread8(backland.at[e], 1, cols) / frames_all
            rec_norm = spread8(backland.at[e], 2, cols) / frames_all * inv_std

            def step(o, carry):
                carry, added = carry
                i = T // 16 - 1 - o
                rows = pl.ds(pl.multiple_of(16 * i, 16), 16)
                pair = projected[rows, cols].astype(f32)
                outs = [None, None]
                for h in (1, 0):
                    goes, count = flags(2 * i + h)
                    here = pl.ds(pl.multiple_of(16 * i + 8 * h + 8, 8), 8)
                    run = states[here, cols] + carry
                    centred = pair[8 * h : 8 * h + 8, :] - average
                    outs[h] = scale * (run - count * (rec + rec_norm * centred))
                    carry = (decay * goes) * run
                rounded = jnp.concatenate(outs, axis=0).astype(bf16)
                dp[rows, cols] = rounded
                rounded = rounded.astype(f32)
                return carry, added + rounded[0:8, :] + rounded[8:16, :]

            _, added = lax.fori_loop(0, T // 16, step, (work[0:8, cols], zero))
            whole = down(added)
            sumpay[layer, 0:1, cols] = whole
            high = whole.astype(bf16).astype(f32)
            middle = (whole - high).astype(bf16).astype(f32)
            low = whole - high - middle
            dp[T : T + 16, cols] = jnp.concatenate(
                [high, middle, low, jnp.zeros((13, L), f32)], axis=0
            ).astype(bf16)

        blocks(full_scan)
        sumpay[layer, 1:8, :] = jnp.zeros((7, H), f32)

        def turn(b, _):
            turned_grads[at(b, fb), :] = lax.dot_general(
                eye[...], dp[:, at(b, fb)], (((1,), (1,)), ((), ())), preferred_element_type=f32
            ).astype(bf16)
            return 0

        lax.fori_loop(0, n, turn, 0)

    def input_gradient(weight, result, columns):
        result[:, columns] = jnp.dot(
            dp[0:T, :], weight[:, columns], preferred_element_type=f32
        ).astype(bf16)

    def sum_copy(layer, i):
        return neur_copy(
            sumpay.at[layer, :, at(i, fb)],
            sumland.at[layer, me],
            sum_sends.at[layer, i],
            sum_recvs.at[layer, me],
            i,
        )

    def sum_along(layer, i):
        return seq_copy(
            sumseq.at[layer],
            sumseqland.at[layer, mine],
            sum_sends.at[layer, n + i],
            sum_recvs.at[layer, n + mine],
            i,
        )

    def sum_start(layer):
        others(lambda i: sum_copy(layer, i).start())
        sumland[layer, me] = sumpay[layer, :, own_lanes]

    def sum_middle(layer):
        def wait(i):
            neur_copy(
                sumpay.at[layer, :, at(i, fb)],
                sumland.at[layer, i],
                sum_sends.at[layer, i],
                sum_recvs.at[layer, i],
                i,
            ).wait()

        others(wait)
        total = sumland[layer, 0]
        for i in range(1, n):
            total = total + sumland[layer, i]
        sumseq[layer] = total
        sumseqland[layer, mine] = total
        others(lambda i: sum_along(layer, i).start(), seqs, mine)

    def sum_finish(layer, frames, total):
        def wait(i):
            seq_copy(
                sumseq.at[layer],
                sumseqland.at[layer, i],
                sum_sends.at[layer, n + i],
                sum_recvs.at[layer, n + i],
                i,
            ).wait()

        others(wait, seqs, mine)
        whole = sumseqland[layer, 0]
        for i in range(1, seqs):
            whole = whole + sumseqland[layer, i]
        whole = whole[0:1, :]
        high = whole.astype(bf16).astype(f32)
        middle = (whole - high).astype(bf16).astype(f32)
        low = whole - high - middle
        rows = jnp.concatenate([high, middle, low, jnp.zeros((13, fb), f32)], axis=0).astype(bf16)
        columns = lax.dot_general(
            eye[...], rows, (((1,), (1,)), ((), ())), preferred_element_type=f32
        ).astype(bf16)
        total[...] -= jnp.dot(
            columns, frames[T : T + 16, at(mine, sz.qc)], preferred_element_type=f32
        )

    def place_out(a, ref, dest, i):
        return neur_copy(
            ref.at[:, at(i, fb)], dest.at[me], frame_sends.at[a, i], frame_recvs.at[a, me], i
        )

    def out_arrived(a, ref, dest, i):
        neur_copy(
            ref.at[:, at(i, fb)], dest.at[i], frame_sends.at[a, i], frame_recvs.at[a, i], i
        ).wait()

    def nothing(name):
        return None

    def during_one(name):
        if name == "hop_c":
            gather_two.diagonals()
        if name == "scan":
            crossing(send_g, 1, n // 2 - 1)

    def during_two(name):
        if name == "scan":
            crossing(send_g, max(1, n // 2 - 1), n // 2)

    layer_forward(0, xr, wf_one, p_one, s_one, x_two, during_one)
    gather_two.cores()
    others(lambda i: frames_sent(0, xs, i))
    layer_forward(1, x_two, wf_two, p_two, s_two, xs, during_two)

    def send_out(i):
        place_out(2, xs, out_land, i).start()

    keep_out = pltpu.make_async_copy(xs.at[:, own_lanes], out_land.at[me], local_sems.at[4])
    keep_out.start()
    others(lambda i: frames_wait(1, gr, i))
    others(lambda i: frames_sent(1, gs, i))
    gather_two.drain()

    crossing(send_out, 0, 1)
    layer_backward(
        1,
        gr,
        p_two,
        s_two,
        dpt_two,
        lambda name: crossing(send_out, 1, 2) if name == "scan" else None,
    )
    if n > 4:
        crossing(send_out, 2, 3)
    lax.fori_loop(0, n // 2, lambda i, _: (input_gradient(wf_two, gr, at(i, 2 * fb)), 0)[1], 0)
    sum_start(1)
    if n > 4:
        crossing(send_out, 3, 4)
    reduce_two = Reduce(
        env,
        dpt_two,
        x_two,
        lambda k: land.at[k],
        spare.at[1],
        stage,
        lambda k: stage.at[2 * sz.Z + k],
        fin.at[1],
        reduce_sends.at[1],
        reduce_recvs.at[1],
        fb // 2,
    )
    reduce_one = Reduce(
        env,
        dpt_one,
        xr,
        lambda k: wf_two.at[at(k // seqs, fb), at(k % seqs, sz.qc)],
        spare.at[0],
        stage,
        lambda k: raw.at[:, at(k, sz.qc)],
        fin.at[0],
        reduce_sends.at[0],
        reduce_recvs.at[0],
        fb // 2,
    )
    result_two = Result(
        env, dw_two, land.at[1], final_sends.at[1], final_recvs.at[1], local_sems.at[6]
    )
    result_one = Result(
        env, dw_one, land.at[0], final_sends.at[0], final_recvs.at[0], local_sems.at[7]
    )
    for kind in range(4):
        reduce_two.cores(kind)

    def meanwhile(name):
        if name == "hop_b":
            sum_middle(1)
        if name == "scan":
            reduce_two.diagonals()
            straight(send_out)

    layer_backward(0, gr, p_one, s_one, dpt_one, meanwhile)
    reduce_two.drain_cores()
    reduce_one.cores(0)
    reduce_two.sides()
    reduce_one.diagonals()
    for kind in range(1, 4):
        reduce_one.cores(kind)
    sum_start(0)

    def send_dx(i):
        place_out(3, gs, dx_land, i).start()

    def make_dx(i):
        input_gradient(wf_one, gs, at(i, fb))

    def make_and_send_dx(i):
        make_dx(i)
        send_dx(i)

    straight(make_and_send_dx)
    crossing(make_dx)
    make_dx(me)
    keep_dx = pltpu.make_async_copy(gs.at[:, own_lanes], dx_land.at[me], local_sems.at[5])
    keep_dx.start()
    reduce_two.lines()
    sum_middle(0)
    reduce_two.drain_sides()
    reduce_one.sides(0, 2)
    for i in range(2, sz.Z):
        reduce_one.lines(i - 2, i - 1)
        reduce_one.sides(i, i + 1)
        if i == 2:
            crossing(send_dx, 0, n // 4)
    crossing(send_dx, n // 4 if sz.Z > 2 else 0, n // 2)
    reduce_two.finish()
    sum_finish(1, x_two, fin.at[1])
    land[1] = fin[1].astype(bf16)
    result_two.start()
    reduce_one.lines(sz.Z - 2, sz.Z - 1)
    reduce_one.finish()
    sum_finish(0, xr, fin.at[0])
    land[0] = fin[0].astype(bf16)
    result_one.start()
    result_two.finish()
    others(lambda i: out_arrived(2, xs, out_land, i))
    others(lambda i: out_arrived(3, gs, dx_land, i))
    keep_out.wait()
    keep_dx.wait()
    result_one.finish()
    reduce_two.drain()
    reduce_one.drain_cores()
    reduce_one.drain_sides()
    reduce_one.drain()
    gather_one.drain()
    small[6:8, :] = jnp.zeros((2, fb), f32)


def frame_tables_of(sz, me, lengths, frame_mask, perm, window, cont, counted, aux):
    T, steps = sz.T, sz.steps
    starts, filled = [], 0
    for k in range(lengths.shape[1]):
        starts.append(filled)
        filled = filled + lengths[0, k]
    row = lax.broadcasted_iota(jnp.int32, (T, 128), 0)
    slot = me * T + (row & 7) * steps + (row >> 3)
    goes = jnp.ones((T, 128), f32)
    for start in starts:
        goes = jnp.where(slot == start, 0.0, goes)
    cont[...] = goes
    kept = jnp.where(frame_mask[0:1, window] > 0, 1.0, 0.0)
    kept = jnp.broadcast_to(kept, (128, sz.win)).astype(bf16)
    kept = lax.dot_general(
        perm[me % 2], kept, (((1,), (1,)), ((), ())), preferred_element_type=f32
    )
    counted[...] = jnp.where(slot < filled, kept, 0.0)
    run = lax.broadcasted_iota(jnp.int32, (8, 128), 0)
    first = me * T + run * steps
    behind = jnp.zeros((8, 128), jnp.int32)
    whole, own = jnp.ones((8, 128), f32), jnp.ones((8, 128), f32)
    for start in starts:
        behind = jnp.where(first > start, jnp.maximum(behind, start), behind)
        whole = jnp.where((run * T <= start) & (start < run * T + T), 0.0, whole)
        own = jnp.where((first <= start) & (start < first + steps), 0.0, own)
    aux[0:8, :] = (first - behind).astype(f32)
    aux[8:16, :] = whole
    aux[16:24, :] = own
    place = lax.broadcasted_iota(jnp.int32, (1, sz.tok_dev), 1)
    block = jnp.where((place < filled) & (frame_mask[...] > 0), 1.0, 0.0)
    block = jnp.sum(block, axis=1, keepdims=True)
    aux[24:32, :] = jnp.broadcast_to(block, (8, 128))


def turn_back(
    sz,
    steps,
    x_ref,
    g_ref,
    out_ref,
    dx_ref,
    one_ref,
    two_ref,
    small,
    output,
    input_grad,
    dw_one,
    dw_two,
    gain_one,
    bias_one,
    decay_one,
    gain_two,
    bias_two,
    decay_two,
    perm,
    held,
    widened,
    sems,
):
    step = pl.program_id(0)
    T, fb, win, odd = sz.T, sz.fb, sz.win, sz.odd
    pairs = ((one_ref, dw_one), (two_ref, dw_two))
    reads = [pltpu.make_async_copy(a, held.at[k], sems.at[k]) for k, (a, _) in enumerate(pairs)]
    writes = [pltpu.make_async_copy(widened.at[k], b, sems.at[k]) for k, (_, b) in enumerate(pairs)]

    @pl.when(step == 0)
    def _():
        for move in reads:
            move.start()
        row = lax.broadcasted_iota(jnp.int32, (T, win), 0)
        column = lax.broadcasted_iota(jnp.int32, (T, win), 1)
        frame = (row & 7) * sz.steps + (row >> 3)
        perm[0] = jnp.where(column == frame, 1.0, 0.0).astype(bf16)
        perm[1] = jnp.where(column == frame + odd, 1.0, 0.0).astype(bf16)
        rows = (gain_one, bias_one, decay_one, gain_two, bias_two, decay_two)
        for r, ref in enumerate(rows):
            ref[...] = small[r : r + 1, :]

    output[...] = x_ref[...].astype(f32)
    input_grad[...] = g_ref[...].astype(f32)

    @pl.when(step < sz.n // 4)
    def _():
        for part in range(4):
            half = part % 2
            lanes = pl.ds(2 * T * (part // 2) + (T - odd) * half, win)
            for source, result in ((out_ref, output), (dx_ref, input_grad)):
                result[:, lanes] += lax.dot_general(
                    source[part], perm[half], (((0,), (0,)), ((), ())), preferred_element_type=f32
                )

    @pl.when(step == 1)
    def _():
        for k, (read, write) in enumerate(zip(reads, writes, strict=True)):
            read.wait()
            widened[k] = held[k].astype(f32)
            write.start()

    @pl.when(step == steps - 1)
    def _():
        for move in writes:
            move.wait()


def frames_apart(sz, inputs, weight_one, weight_two, params, lengths, frame_mask, out_grad):
    n, seqs, H, fb, T, Z, qc = sz.n, sz.seqs, sz.H, sz.fb, sz.T, sz.Z, sz.qc
    whole = pl.BlockSpec(memory_space=pltpu.VMEM)
    anywhere = pl.BlockSpec(memory_space=pl.ANY)
    vmem, sem = pltpu.VMEM, pltpu.SemaphoreType.DMA
    frames_shape, longer_shape = (T, H), (sz.K, H)
    matmul = 2 * T * H * H
    out_land, dx_land, dw_one, dw_two, small = pl.pallas_call(
        functools.partial(network, sz),
        out_shape=(
            jax.ShapeDtypeStruct((n, T, fb), bf16),
            jax.ShapeDtypeStruct((n, T, fb), bf16),
            jax.ShapeDtypeStruct((fb, H), bf16),
            jax.ShapeDtypeStruct((fb, H), bf16),
            jax.ShapeDtypeStruct((8, fb), f32),
        ),
        in_specs=[anywhere] * 4 + [whole] * 6 + [pl.BlockSpec(memory_space=pltpu.SMEM), whole],
        out_specs=(anywhere, anywhere, anywhere, anywhere, whole),
        scratch_shapes=[
            vmem((8, fb), f32),
            vmem((T, 128), f32),
            vmem((T, 128), f32),
            vmem((32, 128), f32),
            vmem((1, 128), f32),
            vmem((fb, sz.valid), bf16),
            vmem((2, T, sz.win), bf16),
            vmem((fb, fb), bf16),
            vmem(frames_shape, bf16),
            vmem(frames_shape, bf16),
            vmem(longer_shape, bf16),
            vmem(frames_shape, bf16),
            vmem(frames_shape, bf16),
            vmem(frames_shape, bf16),
            vmem(longer_shape, bf16),
            vmem(longer_shape, bf16),
            vmem((H, sz.K), bf16),
            vmem((H, sz.K), bf16),
            vmem((T + 8, H), f32),
            vmem((T + 8, H), f32),
            vmem((H, H), bf16),
            vmem((H, H), bf16),
            vmem((8 * Z, fb, qc), bf16),
            vmem((5 * Z, fb, qc), bf16),
            vmem((2, fb, qc), bf16),
            vmem((2, fb, qc), f32),
            vmem((8, H), f32),
            vmem((8, H), f32),
            vmem((16, H), f32),
            vmem((4, 8, H), f32),
            vmem((4, n, 8, fb), f32),
            vmem((4, 8, fb), f32),
            vmem((4, seqs, 8, fb), f32),
            vmem((4, n, 8, fb), f32),
            vmem((4, 8, H), f32),
            vmem((2, 8, H), f32),
            vmem((2, n, 8, fb), f32),
            vmem((2, 8, fb), f32),
            vmem((2, seqs, 8, fb), f32),
            sem((8,)),
            sem((n,)),
            sem((n,)),
            sem((4, n)),
            sem((4, n)),
            sem((2, 10 * Z)),
            sem((2, 10 * Z)),
            sem((8, n)),
            sem((8, n)),
            sem((4, seqs)),
            sem((4, seqs)),
            sem((2, 10 * Z)),
            sem((2, 10 * Z)),
            sem((2, 3)),
            sem((2, 3)),
            sem((2, n + seqs)),
            sem((2, n + seqs)),
        ],
        compiler_params=pltpu.CompilerParams(
            collective_id=0, has_side_effects=True, vmem_limit_bytes=63 * 1024 * 1024
        ),
        cost_estimate=pl.CostEstimate(
            flops=6 * matmul, bytes_accessed=16 * fb * H, transcendentals=6 * T * H
        ),
        name="network",
    )(
        inputs,
        out_grad,
        weight_one,
        weight_two,
        *(values.reshape(1, fb) for values in params),
        lengths,
        frame_mask.reshape(1, -1),
    )
    tok = inputs.shape[1]
    groups = n // 4
    steps = pl.cdiv(tok, 4 * T)
    frames_spec = pl.BlockSpec((fb, 4 * T), lambda p: (0, p))
    land_spec = pl.BlockSpec((4, T, fb), lambda p: (jnp.minimum(p, groups - 1), 0, 0))
    row_spec = pl.BlockSpec((1, fb), lambda p: (0, 0))
    results = pl.pallas_call(
        functools.partial(turn_back, sz, steps),
        grid=(steps,),
        out_shape=(jax.ShapeDtypeStruct((fb, tok), f32),) * 2
        + (jax.ShapeDtypeStruct((fb, H), f32),) * 2
        + (jax.ShapeDtypeStruct((1, fb), f32),) * 6,
        in_specs=[frames_spec, frames_spec, land_spec, land_spec, anywhere, anywhere]
        + [pl.BlockSpec((8, fb), lambda p: (0, 0))],
        out_specs=(frames_spec, frames_spec, anywhere, anywhere) + (row_spec,) * 6,
        scratch_shapes=[
            vmem((2, T, sz.win), bf16),
            vmem((2, fb, H), bf16),
            vmem((2, fb, H), f32),
            sem((2,)),
        ],
        compiler_params=pltpu.CompilerParams(vmem_limit_bytes=60 * 1024 * 1024),
        name="turn_back",
    )(inputs, out_grad, out_land, dx_land, dw_one, dw_two, small)
    output, input_grad, dw_one, dw_two = results[:4]
    small = [row.reshape(fb) for row in results[4:]]
    return (
        output,
        input_grad,
        dw_one,
        small[0],
        small[1],
        small[2],
        dw_two,
        small[3],
        small[4],
        small[5],
    )


def frame_tables(lengths, frame_mask):
    positions = jnp.arange(frame_mask.shape[0], dtype=jnp.int32)
    offsets = jnp.cumsum(lengths[0]) - lengths[0]
    filled = jnp.sum(lengths[0])
    begins = jnp.any(positions[:, None] == offsets[None, :], axis=1)
    continues = jnp.where(begins, 0.0, 1.0).astype(jnp.float32)
    counted = jnp.where((positions < filled) & (frame_mask > 0), 1.0, 0.0).astype(jnp.float32)
    return (continues, counted)


def linear_scan(coef_rows, driving, backwards):
    row_count, length = driving.shape
    block_count = length // block_span
    factor = coef_rows.reshape(row_count, block_count, block_span)
    running = driving.reshape(row_count, block_count, block_span)
    places = jnp.arange(block_span, dtype=jnp.int32)
    step = 1
    while step < block_span:
        if backwards:
            mover = jnp.where(places[:, None] == places[None, :] + step, 1.0, 0.0).astype(
                jnp.float32
            )
            edge = jnp.where(places >= block_span - step, 1.0, 0.0).astype(jnp.float32)
        else:
            mover = jnp.where(places[:, None] == places[None, :] - step, 1.0, 0.0).astype(
                jnp.float32
            )
            edge = jnp.where(places < step, 1.0, 0.0).astype(jnp.float32)
        moved_factor = (
            jnp.dot(
                factor, mover, precision=lax.Precision.HIGHEST, preferred_element_type=jnp.float32
            )
            + edge
        )
        moved_running = jnp.dot(
            running, mover, precision=lax.Precision.HIGHEST, preferred_element_type=jnp.float32
        )
        running = factor * moved_running + running
        factor = factor * moved_factor
        step = step * 2
    end_place = 0 if backwards else block_span - 1
    total_factor = factor[:, :, end_place].T
    total_running = running[:, :, end_place].T

    def carry_step(carried, block_pair):
        return (block_pair[0] * carried + block_pair[1], carried)

    _, entering = lax.scan(
        carry_step,
        jnp.zeros((row_count,), jnp.float32),
        (total_factor, total_running),
        reverse=backwards,
    )
    result = running + factor * entering.T[:, :, None]
    return result.reshape(row_count, length)


def layer_forward(layer_input, weight, gain_row, bias_row, decay_rate, continues, counted):
    frames_in = lax.all_to_all(layer_input, "neur", split_axis=1, concat_axis=0, tiled=True)
    projected = jnp.dot(
        lax.all_gather(weight, "neur", axis=0, tiled=True),
        frames_in,
        preferred_element_type=jnp.float32,
    )
    neuron_proj = lax.all_to_all(
        projected.astype(jnp.bfloat16), "neur", split_axis=0, concat_axis=1, tiled=True
    ).astype(jnp.float32)
    sum_first = jnp.sum(counted[None, :] * neuron_proj, axis=1)
    sum_second = jnp.sum(counted[None, :] * neuron_proj * neuron_proj, axis=1)
    sum_first, sum_second, frames = lax.psum((sum_first, sum_second, jnp.sum(counted)), "seq")
    average = sum_first / frames
    inv_std = lax.rsqrt(sum_second / frames - average * average + epsilon)
    normed = (neuron_proj - average[:, None]) * inv_std[:, None]
    spread = jnp.sqrt(1.0 - decay_rate * decay_rate)
    states = linear_scan(
        decay_rate[:, None] * continues[None, :], (spread * gain_row)[:, None] * normed, False
    )
    layer_out = counted[None, :] * jax.nn.softplus(states + bias_row[:, None])
    return (layer_out, (frames_in, None, normed, inv_std, frames, states))


def layer_backward(
    upstream, weight, gain_row, bias_row, decay_rate, continues, counted, kept_state
):
    frames_in, full_weight, normed, inv_std, frames, states = kept_state
    local_grad = upstream * counted[None, :] * jax.nn.sigmoid(states + bias_row[:, None])
    following = jnp.concatenate([continues[1:], jnp.zeros((1,), jnp.float32)])
    coef_rows = decay_rate[:, None] * following[None, :]
    state_grad = linear_scan(coef_rows, local_grad, True)
    sum_rec, sum_rec_norm, sum_local = lax.psum(
        (
            jnp.sum(state_grad, axis=1),
            jnp.sum(state_grad * normed, axis=1),
            jnp.sum(local_grad, axis=1),
        ),
        "seq",
    )
    spread = jnp.sqrt(1.0 - decay_rate * decay_rate)
    gain_grad = spread * sum_rec_norm
    proj_grad = (spread * gain_row * inv_std)[:, None] * (
        state_grad - counted[None, :] * (sum_rec[:, None] + sum_rec_norm[:, None] * normed) / frames
    )
    driving = (spread * gain_row)[:, None] * normed
    decay_part = jnp.sum(state_grad * (states - driving), axis=1) / decay_rate
    grad_frames = lax.all_to_all(
        proj_grad.astype(jnp.bfloat16), "neur", split_axis=1, concat_axis=0, tiled=True
    )
    grad_rows = grad_frames
    input_frames = jnp.einsum(
        "ot,oi->it",
        grad_rows,
        lax.all_gather(weight, "neur", axis=0, tiled=True),
        preferred_element_type=jnp.float32,
    )
    input_grad = lax.all_to_all(
        input_frames.astype(jnp.bfloat16), "neur", split_axis=0, concat_axis=1, tiled=True
    ).astype(jnp.float32)
    grad_rows = grad_frames
    weight_rows = lax.psum_scatter(
        jnp.einsum("ot,it->oi", grad_rows, frames_in, preferred_element_type=jnp.float32),
        "neur",
        scatter_dimension=0,
        tiled=True,
    )
    weight_grad, decay_sum = lax.psum((weight_rows, decay_part), "seq")
    decay_grad = decay_sum - decay_rate / spread * gain_row * sum_rec_norm
    return (input_grad, weight_grad, gain_grad, sum_local, decay_grad)


def shards(
    inputs,
    weight_one,
    weight_two,
    gain_one,
    gain_two,
    bias_one,
    bias_two,
    decay_one,
    decay_two,
    lengths,
    frame_mask,
    out_grad,
):
    seqs, n = lax.axis_size("seq"), lax.axis_size("neur")
    H, (fb, tok) = weight_one.shape[1], inputs.shape
    if fits(n, seqs, H, fb, tok):
        params = (gain_one, gain_two, bias_one, bias_two, decay_one, decay_two)
        return frames_apart(
            Sizes(n, seqs, H, fb, tok),
            inputs,
            weight_one,
            weight_two,
            params,
            lengths,
            frame_mask,
            out_grad,
        )
    continues, counted = frame_tables(lengths, frame_mask)
    first_out, first_kept = layer_forward(
        inputs, weight_one, gain_one, bias_one, decay_one, continues, counted
    )
    second_out, second_kept = layer_forward(
        first_out.astype(jnp.bfloat16),
        weight_two,
        gain_two,
        bias_two,
        decay_two,
        continues,
        counted,
    )
    output = inputs.astype(jnp.float32) + second_out
    upstream = out_grad.astype(jnp.float32)
    middle_grad, weight_two_grad, gain_two_grad, bias_two_grad, decay_two_grad = layer_backward(
        upstream, weight_two, gain_two, bias_two, decay_two, continues, counted, second_kept
    )
    lower_grad, weight_one_grad, gain_one_grad, bias_one_grad, decay_one_grad = layer_backward(
        middle_grad, weight_one, gain_one, bias_one, decay_one, continues, counted, first_kept
    )
    return (
        output,
        upstream + lower_grad,
        weight_one_grad,
        gain_one_grad,
        bias_one_grad,
        decay_one_grad,
        weight_two_grad,
        gain_two_grad,
        bias_two_grad,
        decay_two_grad,
    )


def solution(mesh):
    placed = (
        P("neur", "seq"),
        P("neur", None),
        P("neur", None),
        P("neur"),
        P("neur"),
        P("neur"),
        P("neur"),
        P("neur"),
        P("neur"),
        P("seq", None),
        P("seq"),
        P("neur", "seq"),
    )
    return jax.shard_map(
        shards,
        mesh=mesh,
        in_specs=placed,
        out_specs=(
            P("neur", "seq"),
            P("neur", "seq"),
            P("neur", None),
            P("neur"),
            P("neur"),
            P("neur"),
            P("neur", None),
            P("neur"),
            P("neur"),
            P("neur"),
        ),
        check_vma=False,
    )
```

```python
import functools

import jax
import jax.numpy as jnp
from jax import lax
from jax.experimental import pallas as pl
from jax.experimental.pallas import tpu as pltpu
from jax.sharding import PartitionSpec as P

epsilon = 1e-05
block_span = 128
valid_frames = 3584
f32 = jnp.float32
bf16 = jnp.bfloat16
MESH = pl.DeviceIdType.MESH


def wide(tile, width):
    return jnp.concatenate([tile] * (width // 128), axis=1)


def at(index, size):
    if isinstance(index, int):
        return pl.ds(index * size, size)
    return pl.ds(pl.multiple_of(index * size, size), size)


def power(base, exponent):
    result = None
    while exponent:
        if exponent % 2:
            result = base if result is None else result * base
        exponent //= 2
        base = base * base
    return result


def log_of(rate):
    u = 1.0 - rate
    series = jnp.full_like(u, 1.0 / 8)
    for order in range(7, 0, -1):
        series = series * u + 1.0 / order
    return -u * series


GAIN, BIAS, DECAY = 0, 2, 4


class Sizes:
    def __init__(self, n, seqs, H, fb, tok_dev):
        self.n, self.seqs, self.H, self.fb, self.tok_dev = n, seqs, H, fb, tok_dev
        self.T = valid_frames // n
        self.steps = self.T // 8
        self.valid = valid_frames
        self.qc = H // seqs
        self.Z = n // 2
        self.odd = self.T % 128
        self.win = self.T + self.odd
        self.K = self.T + 16
        self.L = min(512, H)


def fits(n, seqs, H, fb, tok_dev):
    if n not in (4, 8) or valid_frames % n or seqs != 4 or fb * n != H or fb % 128 or H % 512:
        return False
    T = valid_frames // n
    return T % 64 == 0 and valid_frames % 128 == 0 and tok_dev >= valid_frames


class Line:
    def __init__(self, env, sends, recvs):
        self.env, self.sends, self.recvs = env, sends, recvs

    def copy(self, k, source, dest, target):
        return pltpu.make_async_remote_copy(
            src_ref=source,
            dst_ref=dest,
            send_sem=self.sends.at[k],
            recv_sem=self.recvs.at[k],
            device_id=target,
            device_id_type=MESH,
        )

    def arrived(self, k, ref):
        self.copy(k, ref, ref, self.env.across("x")).wait_recv()

    def sent(self, k, ref):
        self.copy(k, ref, ref, self.env.across("x")).wait_send()

    def along(self, dz):
        z, Z = self.env.z, self.env.sz.Z
        if dz == 0:
            return [(None, z, 0)]
        return [(z >= dz, z - dz, 1), (z + dz < Z, z + dz, -1)]


def if_so(condition, body):
    if condition is None:
        body()
    else:
        pl.when(condition)(body)


class Gather(Line):
    def __init__(self, env, source, full, sends, recvs, cut):
        super().__init__(env, sends, recvs)
        self.cut = cut
        self.full = full
        self.source = source.at[:, at(env.s, env.sz.qc)]

    def block(self, zz, fx, fy, fc=0):
        env = self.env
        rows = at(2 * zz + (env.x + fx) % 2, env.sz.fb)
        return self.full.at[rows, at(2 * ((env.y + fy) % 2) + (env.c + fc) % 2, env.sz.qc)]

    def half(self, ref, h):
        if h == 0:
            return ref.at[pl.ds(0, self.cut), :]
        return ref.at[pl.ds(self.cut, self.env.sz.fb - self.cut), :]

    def spread(self, zz, source):
        env, Z = self.env, self.env.sz.Z
        dest = self.block(zz, 0, 0)
        self.copy(2 * Z + zz, source, dest, env.across("x")).start()
        self.copy(3 * Z + zz, source, dest, env.across("y")).start()
        self.copy(6 * Z + zz, source, dest, env.across("core")).start()

    def pass_on(self, zz, source, way):
        env, Z = self.env, self.env.sz.Z
        dest = self.block(zz, 0, 0)

        def go():
            pltpu.make_async_remote_copy(
                src_ref=source,
                dst_ref=dest,
                send_sem=self.sends.at[zz if way > 0 else Z + zz],
                recv_sem=self.recvs.at[zz],
                device_id={"neur": 2 * (env.z + way) + env.x},
                device_id_type=MESH,
            ).start()

        pl.when(env.z < Z - 1 if way > 0 else env.z > 0)(go)

    def start(self):
        z = self.env.z
        self.pass_on(z, self.source, 1)
        self.pass_on(z, self.source, -1)
        self.spread(z, self.source)

    def line(self, dz):
        for condition, zz, way in self.along(dz):

            def one(zz=zz, way=way):
                block = self.block(zz, 0, 0)
                self.arrived(zz, block)
                self.pass_on(zz, block, way)
                self.spread(zz, block)

            if_so(condition, one)

    def sides(self, dz):
        env, Z = self.env, self.env.sz.Z
        for condition, zz, _ in self.along(dz):

            def one(zz=zz):
                block = self.block(zz, 1, 0)
                self.arrived(2 * Z + zz, block)
                part = self.half(block, 1)
                self.copy(5 * Z + zz, part, part, env.across("y")).start()
                self.copy(7 * Z + zz, block, block, env.across("core")).start()
                block = self.block(zz, 0, 1)
                self.arrived(3 * Z + zz, block)
                part = self.half(block, 0)
                self.copy(4 * Z + zz, part, part, env.across("x")).start()
                self.copy(8 * Z + zz, block, block, env.across("core")).start()

            if_so(condition, one)

    def diagonals(self):
        env, Z = self.env, self.env.sz.Z
        for dz in range(Z):
            for condition, zz, _ in self.along(dz):

                def one(zz=zz):
                    block = self.block(zz, 1, 1)
                    self.arrived(4 * Z + zz, self.half(block, 0))
                    self.arrived(5 * Z + zz, self.half(block, 1))
                    self.copy(9 * Z + zz, block, block, env.across("core")).start()

                if_so(condition, one)

    def cores(self):
        Z = self.env.sz.Z
        for k, (fx, fy) in enumerate(((0, 0), (1, 0), (0, 1), (1, 1))):
            for zz in range(Z):
                self.arrived((6 + k) * Z + zz, self.block(zz, fx, fy, 1))

    def drain(self):
        env, Z = self.env, self.env.sz.Z
        block = self.block(0, 0, 0)
        for zz in range(Z):
            pl.when((zz <= env.z) & (env.z < Z - 1))(lambda zz=zz: self.sent(zz, block))
            pl.when((zz >= env.z) & (env.z > 0))(lambda zz=zz: self.sent(Z + zz, block))
            for k in (2, 3, 6, 7, 8, 9):
                self.sent(k * Z + zz, block)
            self.sent(4 * Z + zz, self.half(block, 0))
            self.sent(5 * Z + zz, self.half(block, 1))


class Reduce(Line):
    kinds = ((1, 1), (1, 0), (0, 1), (0, 0))

    def __init__(self, env, grads, frames, land, spare, stage, held, total, sends, recvs, cut):
        super().__init__(env, sends, recvs)
        self.cut, self.held = cut, held
        self.grads, self.frames, self.land, self.spare = grads, frames, land, spare
        self.stage, self.total = stage, total

    def product(self, kind, zz, fc=0):
        env, sz = self.env, self.env.sz
        fx, fy = self.kinds[kind]
        rows = at(2 * zz + (env.x + fx) % 2, sz.fb)
        columns = at(2 * ((env.y + fy) % 2) + (env.c + fc) % 2, sz.qc)
        return jnp.dot(
            self.grads[rows, :], self.frames[:, columns], preferred_element_type=f32
        )

    def half(self, ref, h):
        if h == 0:
            return ref.at[pl.ds(0, self.cut), :]
        return ref.at[pl.ds(self.cut, self.env.sz.fb - self.cut), :]

    def landed(self, k, slot):
        self.arrived(k, self.land(slot))
        return self.land(slot)[...].astype(f32)

    def turn(self, i):
        z, Z = self.env.z, self.env.sz.Z
        low = jnp.where(i < Z - 1 - z, Z - 1 - i, i - (Z - 1 - z))
        high = jnp.where(i < z, i, Z - 1 - (i - z))
        return jnp.where(i == Z - 1, z, jnp.where(z < Z // 2, low, high))

    def cores(self, kind):
        env, Z = self.env, self.env.sz.Z

        def one(i, _):
            zz = self.turn(i)
            k = kind * Z + zz
            held = (kind % 2) * Z + zz
            if kind >= 2:
                self.sent(k - 2 * Z, self.stage.at[held])
            self.stage[held] = self.product(kind, zz, 1).astype(bf16)
            self.copy(k, self.stage.at[held], self.land(k), env.across("core")).start()
            return 0

        lax.fori_loop(0, Z, one, 0)

    def diagonals(self):
        env, Z = self.env, self.env.sz.Z

        def one(i, _):
            zz = self.turn(i)
            held = self.held(zz)
            held[...] = (self.product(0, zz) + self.landed(zz, zz)).astype(bf16)
            slot = self.land(4 * Z + zz)
            for k, h, axis in ((4, 0, "x"), (5, 1, "y")):
                self.copy(
                    k * Z + zz, self.half(held, h), self.half(slot, h), env.across(axis)
                ).start()
            return 0

        lax.fori_loop(0, Z, one, 0)

    def sides(self, low=0, high=None):
        env, Z = self.env, self.env.sz.Z
        spans = slice(0, self.cut), slice(self.cut, env.sz.fb)

        def one(i, _):
            zz = self.turn(i)
            slot = self.land(4 * Z + zz)
            for kind, h, wait, k, axis in ((1, 1, 5, 6, "x"), (2, 0, 4, 7, "y")):
                tile = self.product(kind, zz) + self.landed(kind * Z + zz, kind * Z + zz)
                part = self.half(slot, h)
                self.arrived(wait * Z + zz, part)
                held = self.stage.at[(2 + kind) * Z + zz]
                other = 1 - h
                summed = tile[spans[h], :] + part[...].astype(f32)
                self.half(held, h)[...] = summed.astype(bf16)
                self.half(held, other)[...] = tile[spans[other], :].astype(bf16)
                self.copy(
                    k * Z + zz, held, self.land((4 + kind) * Z + zz), env.across(axis)
                ).start()
            return 0

        lax.fori_loop(low, Z if high is None else high, one, 0)

    def joined(self, zz):
        Z = self.env.sz.Z
        tile = self.product(3, zz) + self.landed(3 * Z + zz, 3 * Z + zz)
        tile = tile + self.landed(6 * Z + zz, 5 * Z + zz)
        self.total[...] = tile + self.landed(7 * Z + zz, 6 * Z + zz)

    def lines(self, low=0, high=None):
        env, Z, z = self.env, self.env.sz.Z, self.env.z
        def onward(zz, way):
            k, slot = (8 if way > 0 else 9) * Z + zz, 7 * Z + zz
            self.joined(zz)

            @pl.when(z > 0 if way > 0 else z < Z - 1)
            def _():
                self.total[...] += self.landed(k, slot)

            held = self.held(zz)
            self.sent(4 * Z + zz, self.half(held, 0))
            self.sent(5 * Z + zz, self.half(held, 1))
            held[...] = self.total[...].astype(bf16)
            target = {"neur": 2 * (z + way) + env.x}
            if way > 0:
                self.copy(k, held, self.land(slot), target).start()
            else:
                pl.when(zz == z - 1)(lambda: self.copy(k, held, self.spare, target).start())
                pl.when(zz != z - 1)(lambda: self.copy(k, held, self.land(slot), target).start())

        for i in range(low, Z - 1 if high is None else high):
            zz = self.turn(i)
            pl.when(zz > z)(functools.partial(onward, zz, 1))
            pl.when(zz < z)(functools.partial(onward, zz, -1))

    def finish(self):
        Z, z = self.env.sz.Z, self.env.z
        self.joined(z)
        @pl.when(z > 0)
        def _():
            self.total[...] += self.landed(8 * Z + z, 7 * Z + z)

        @pl.when(z < Z - 1)
        def _():
            self.arrived(9 * Z + z, self.spare)
            self.total[...] += self.spare[...].astype(f32)

    def drain_cores(self):
        for k in range(2 * self.env.sz.Z, 4 * self.env.sz.Z):
            self.sent(k, self.stage.at[0])

    def drain_sides(self):
        for k in range(6 * self.env.sz.Z, 8 * self.env.sz.Z):
            self.sent(k, self.stage.at[0])

    def drain(self):
        Z, z = self.env.sz.Z, self.env.z
        held = self.stage.at[0]
        for zz in range(Z):
            for k in (4, 5):
                pl.when(zz == z)(
                    lambda k=k, zz=zz: self.sent(k * Z + zz, self.half(held, k - 4))
                )
            pl.when(zz > z)(lambda zz=zz: self.sent(8 * Z + zz, held))
            pl.when(zz < z)(lambda zz=zz: self.sent(9 * Z + zz, held))


class Result:
    def __init__(self, env, whole, block, sends, recvs, local):
        self.env, self.whole, self.block = env, whole, block
        self.sends, self.recvs, self.local = sends, recvs, local

    def part(self, flip_y, flip_c):
        env = self.env
        s = 2 * ((env.y + flip_y) % 2) + (env.c + flip_c) % 2
        return self.whole.at[:, at(s, env.sz.qc)]

    def copy(self, k, source, dest, target):
        return pltpu.make_async_remote_copy(
            src_ref=source,
            dst_ref=dest,
            send_sem=self.sends.at[k],
            recv_sem=self.recvs.at[k],
            device_id=target,
            device_id_type=MESH,
        )

    def start(self):
        env, own = self.env, self.part(0, 0)
        self.copy(0, self.block, own, env.across("y")).start()
        self.copy(1, self.block, own, env.across("core")).start()
        pltpu.make_async_copy(self.block, own, self.local).start()

    def finish(self):
        env = self.env
        other = self.part(1, 0)
        self.copy(0, self.block, other, env.across("y")).wait_recv()
        forward = self.copy(2, other, other, env.across("core"))
        forward.start()
        own = self.part(0, 0)
        pltpu.make_async_copy(self.block, own, self.local).wait()
        self.copy(0, self.block, own, env.across("y")).wait_send()
        self.copy(1, self.block, self.part(0, 1), env.across("core")).wait()
        forward.wait_send()
        self.copy(2, other, self.part(1, 1), env.across("core")).wait_recv()


class Env:
    def across(self, axis):
        if axis == "x":
            return {"neur": 2 * self.z + 1 - self.x}
        if axis == "y":
            return {"seq": 2 * (1 - self.y) + self.c}
        return {"seq": 2 * self.y + 1 - self.c}


def network(
    sz,
    x_hbm,
    g_hbm,
    w_one,
    w_two,
    gain_one,
    gain_two,
    bias_one,
    bias_two,
    decay_one,
    decay_two,
    lengths,
    frame_mask,
    out_land,
    dx_land,
    dw_one,
    dw_two,
    small,
    own_par,
    cont,
    counted,
    aux,
    frames_sum,
    raw,
    perm,
    eye,
    xs,
    gs,
    xr,
    gr,
    p_one,
    p_two,
    x_two,
    dp,
    dpt_one,
    dpt_two,
    s_one,
    s_two,
    wf_one,
    wf_two,
    land,
    stage,
    spare,
    fin,
    par,
    ends,
    work,
    pay,
    arrive,
    seqpay,
    seqland,
    back,
    backland,
    sumpay,
    sumland,
    sumseq,
    sumseqland,
    local_sems,
    par_sends,
    par_recvs,
    frame_sends,
    frame_recvs,
    gather_sends,
    gather_recvs,
    hop_sends,
    hop_recvs,
    seq_sends,
    seq_recvs,
    reduce_sends,
    reduce_recvs,
    final_sends,
    final_recvs,
    sum_sends,
    sum_recvs,
):
    n, seqs, H, fb, T, steps, L = sz.n, sz.seqs, sz.H, sz.fb, sz.T, sz.steps, sz.L
    env = Env()
    env.sz = sz
    me = lax.axis_index("neur")
    mine = lax.axis_index("seq")
    env.j, env.s = me, mine
    env.z, env.x, env.y, env.c = me // 2, me % 2, mine // 2, mine % 2

    barrier = pltpu.get_barrier_semaphore()
    for o in range(1, n):
        pl.semaphore_signal(
            barrier, inc=1, device_id={"neur": (me + o) % n}, device_id_type=MESH
        )
    for o in range(1, seqs):
        pl.semaphore_signal(
            barrier, inc=1, device_id={"seq": (mine + o) % seqs}, device_id_type=MESH
        )
    load_x = pltpu.make_async_copy(x_hbm.at[:, pl.ds(0, sz.valid)], raw, local_sems.at[0])
    load_x.start()
    for r, values in enumerate((gain_one, gain_two, bias_one, bias_two, decay_one, decay_two)):
        own_par[r : r + 1, :] = values[...]
    own_par[6:8, :] = jnp.zeros((2, fb), f32)
    pl.semaphore_wait(barrier, n - 1 + seqs - 1)

    def neur_copy(source, dest, send, recv, i):
        return pltpu.make_async_remote_copy(
            src_ref=source,
            dst_ref=dest,
            send_sem=send,
            recv_sem=recv,
            device_id={"neur": i},
            device_id_type=MESH,
        )

    def seq_copy(source, dest, send, recv, i):
        return pltpu.make_async_remote_copy(
            src_ref=source,
            dst_ref=dest,
            send_sem=send,
            recv_sem=recv,
            device_id={"seq": i},
            device_id_type=MESH,
        )

    def straight(body, low=1, high=n // 2):
        lax.fori_loop(low, high, lambda o, _: (body((me + 2 * o) % n), 0)[1], 0)

    def crossing(body, low=0, high=n // 2):
        lax.fori_loop(low, high, lambda o, _: (body((me + 2 * o + 1) % n), 0)[1], 0)

    def others(body, count=n, own=me):
        def one(o, _):
            body((own + o) % count)
            return 0

        lax.fori_loop(1, count, one, 0)

    own_lanes = at(me, fb)

    def par_copy(i):
        return neur_copy(own_par, par.at[:, own_lanes], par_sends.at[i], par_recvs.at[me], i)

    def par_wait(i):
        neur_copy(own_par, par.at[:, at(i, fb)], par_sends.at[i], par_recvs.at[i], i).wait()

    others(lambda i: par_copy(i).start())
    par[:, own_lanes] = own_par[...]

    cuts = (fb // 4, 7 * fb // 16)
    gather_one = Gather(env, w_one, wf_one, gather_sends.at[0], gather_recvs.at[0], cuts[0])
    gather_two = Gather(env, w_two, wf_two, gather_sends.at[1], gather_recvs.at[1], cuts[1])
    own_one = pltpu.make_async_copy(gather_one.source, gather_one.block(env.z, 0, 0), local_sems.at[2])
    own_two = pltpu.make_async_copy(gather_two.source, gather_two.block(env.z, 0, 0), local_sems.at[3])
    own_one.start()
    own_two.start()
    gather_one.start()
    gather_two.start()

    row = lax.broadcasted_iota(jnp.int32, (T, sz.win), 0)
    column = lax.broadcasted_iota(jnp.int32, (T, sz.win), 1)
    frame = (row & 7) * steps + (row >> 3)
    perm[0] = jnp.where(column == frame, 1.0, 0.0).astype(bf16)
    perm[1] = jnp.where(column == frame + sz.odd, 1.0, 0.0).astype(bf16)
    row = lax.broadcasted_iota(jnp.int32, (fb, fb), 0)
    column = lax.broadcasted_iota(jnp.int32, (fb, fb), 1)
    eye[...] = jnp.where(row == column, 1.0, 0.0).astype(bf16)

    def window(i):
        start = (i // 2) * (2 * T) + (i % 2) * (T - sz.odd)
        return pl.ds(pl.multiple_of(start, 128), sz.win)

    def turned(i):
        return lax.dot_general(
            perm[i % 2], raw[:, window(i)], (((1,), (1,)), ((), ())), preferred_element_type=f32
        ).astype(bf16)

    def frames_copy(a, source, dest, i):
        return neur_copy(source, dest, frame_sends.at[a, i], frame_recvs.at[a, me], i)

    def frames_wait(a, ref, i):
        part = ref.at[pl.ds(0, T), at(i, fb)]
        neur_copy(part, part, frame_sends.at[a, i], frame_recvs.at[a, i], i).wait_recv()

    def frames_sent(a, ref, i):
        part = ref.at[pl.ds(0, T), at(i, fb)]
        neur_copy(part, part, frame_sends.at[a, i], frame_recvs.at[a, i], i).wait_send()

    load_x.wait()

    def turn_x(i):
        xs[:, at(i, fb)] = turned(i)

    def send_x(i):
        frames_copy(0, xs.at[:, at(i, fb)], xr.at[pl.ds(0, T), own_lanes], i).start()

    def send_all_x():
        crossing(send_x)
        straight(send_x)

    others(turn_x)
    xr[0:T, own_lanes] = turned(me)
    load_g = pltpu.make_async_copy(g_hbm.at[:, pl.ds(0, sz.valid)], raw, local_sems.at[1])
    load_g.start()
    def turn_g(i):
        gs[:, at(i, fb)] = turned(i)

    def send_g(i):
        frames_copy(1, gs.at[:, at(i, fb)], gr.at[:, own_lanes], i).start()

    ends_of_line = (env.z == 0) | (env.z == sz.Z - 1)
    pl.when(ends_of_line)(send_all_x)
    for dz in range(1, sz.Z):
        gather_one.line(dz)
        gather_two.line(dz)
        if dz == max(1, sz.Z - 2):
            pl.when(jnp.logical_not(ends_of_line))(send_all_x)
            frame_tables_of(sz, me, lengths, frame_mask, perm, window(me), cont, counted, aux)
            load_g.wait()
            others(turn_g)
            gr[:, own_lanes] = turned(me)
        gather_one.sides(dz - 1)
    gather_one.sides(sz.Z - 1)
    gather_two.sides(0)
    straight(send_g)
    crossing(send_g, 0, 1)
    gather_one.diagonals()
    for dz in range(1, sz.Z):
        gather_two.sides(dz)
    gather_one.cores()
    own_one.wait()
    own_two.wait()
    others(lambda i: frames_wait(0, xr, i))
    others(par_wait)

    def blocks(body):
        def one(b, _):
            body(at(b, L))
            return 0

        lax.fori_loop(0, H // L, one, 0)

    def project(frames, weight, result):
        def one(b, _):
            result[:, at(b, 2 * fb)] = lax.dot_general(
                frames[0:T, :],
                weight[at(b, 2 * fb), :],
                (((1,), (1,)), ((), ())),
                preferred_element_type=f32,
            ).astype(bf16)
            return 0

        lax.fori_loop(0, n // 2, one, 0)

    def flags(t):
        tile = pl.ds(pl.multiple_of(8 * t, 8), 8)
        return wide(cont[tile, :], L), wide(counted[tile, :], L)

    def spread8(ref, r, cols, width=L):
        return jnp.broadcast_to(ref[r : r + 1, cols], (8, width))

    zero = jnp.zeros((8, L), f32)

    def down(value):
        return jnp.sum(value, axis=0, keepdims=True)

    def exchange(e, gathered, totalled, gap):
        ahead = pl.ds(0, 4 if e < 2 else 8)
        behind = pl.ds(0, 4)

        def out_copy(i):
            return neur_copy(
                pay.at[e, ahead, at(i, fb)],
                arrive.at[e, me, ahead],
                hop_sends.at[2 * e, i],
                hop_recvs.at[2 * e, me],
                i,
            )

        others(lambda i: out_copy(i).start())
        arrive[e, me, ahead] = pay[e, ahead, own_lanes]
        gap("hop_a")

        def out_wait(i):
            neur_copy(
                pay.at[e, ahead, at(i, fb)],
                arrive.at[e, i, ahead],
                hop_sends.at[2 * e, i],
                hop_recvs.at[2 * e, i],
                i,
            ).wait()

        others(out_wait)
        gathered()

        def along_copy(i):
            return seq_copy(
                seqpay.at[e],
                seqland.at[e, mine],
                seq_sends.at[e, i],
                seq_recvs.at[e, mine],
                i,
            )

        def along_wait(i):
            seq_copy(
                seqpay.at[e], seqland.at[e, i], seq_sends.at[e, i], seq_recvs.at[e, i], i
            ).wait()

        others(lambda i: along_copy(i).start(), seqs, mine)
        seqland[e, mine] = seqpay[e]
        gap("hop_b")
        others(along_wait, seqs, mine)
        sums = seqland[e, 0]
        for i in range(1, seqs):
            sums = sums + seqland[e, i]
        totalled(sums)

        def back_copy(i):
            return neur_copy(
                back.at[e, i, behind],
                backland.at[e, behind, own_lanes],
                hop_sends.at[2 * e + 1, i],
                hop_recvs.at[2 * e + 1, me],
                i,
            )

        def back_wait(i):
            neur_copy(
                back.at[e, i, behind],
                backland.at[e, behind, at(i, fb)],
                hop_sends.at[2 * e + 1, i],
                hop_recvs.at[2 * e + 1, i],
                i,
            ).wait()

        others(lambda i: back_copy(i).start())
        backland[e, behind, own_lanes] = back[e, me, behind]
        gap("hop_c")
        others(back_wait)

    def layer_forward(layer, frames, weight, projected, states, store, gap):
        e = layer
        decay_row, gain_row, bias_row = DECAY + layer, GAIN + layer, BIAS + layer
        project(frames, weight, projected)
        gap("ends")

        def local_ends(cols):
            decay = spread8(par, decay_row, cols)

            def step(i, carry):
                state, first, second, inward = carry
                pair = projected[pl.ds(pl.multiple_of(16 * i, 16), 16), cols].astype(f32)
                for h in range(2):
                    value = pair[8 * h : 8 * h + 8, :]
                    goes, count = flags(2 * i + h)
                    state = (decay * goes) * state + value
                    held = count * value
                    first = first + held
                    second = second + held * value
                ins = frames[pl.ds(pl.multiple_of(16 * i, 16), 16), cols].astype(f32)
                return state, first, second, inward + ins[0:8, :] + ins[8:16, :]

            state, first, second, inward = lax.fori_loop(
                0, T // 16, step, (zero, zero, zero, zero)
            )
            ends[:, cols] = state
            pay[e, 1:2, cols] = down(first)
            pay[e, 2:3, cols] = down(second)
            pay[e, 3:4, cols] = down(inward)

        blocks(local_ends)
        run_power = power(par[decay_row : decay_row + 1, :], steps)
        total = jnp.zeros((1, H), f32)
        for k in range(8):
            total = run_power * wide(aux[16 + k : 17 + k, :], H) * total + ends[k : k + 1, :]
        pay[e, 0:1, :] = total

        own_decay = own_par[decay_row : decay_row + 1, :]

        def gathered():
            whole_power = power(own_decay, T)
            carried = jnp.zeros((1, fb), f32)
            sums = jnp.zeros((4, fb), f32)
            for i in range(n):
                rows = arrive[e, i, 0:4, :]
                back[e, i, 0:1, :] = carried
                carried = whole_power * wide(aux[8 + i : 9 + i, :], fb) * carried + rows[0:1, :]
                sums = sums + rows
            seqpay[e, 0:4, :] = sums
            seqpay[e, 4:8, :] = jnp.zeros((4, fb), f32)
            seqpay[e, 0:1, :] = wide(aux[24:25, :], fb)

        def totalled(sums):
            frames_all = sums[0:1, :]
            average = sums[1:2, :] / frames_all
            inv_std = lax.rsqrt(sums[2:3, :] / frames_all - average * average + epsilon)
            centre = sums[3:4, :] / (sz.valid * seqs)
            for i in range(n):
                back[e, i, 1:2, :] = average
                back[e, i, 2:3, :] = inv_std
                back[e, i, 3:4, :] = centre
            frames_sum[...] = frames_all[:, 0:128]

        exchange(e, gathered, totalled, gap)
        centre = backland[e, 3:4, :]
        frames[T : T + 16, :] = jnp.concatenate(
            [-centre, -centre, -centre, jnp.zeros((13, H), f32)], axis=0
        ).astype(bf16)

        total = backland[e, 0:1, :]
        for k in range(8):
            work[k : k + 1, :] = total
            total = run_power * wide(aux[16 + k : 17 + k, :], H) * total + ends[k : k + 1, :]

        gap("scan")

        def full_scan(cols):
            decay = spread8(par, decay_row, cols)
            average = spread8(backland.at[e], 1, cols)
            inv_std = spread8(backland.at[e], 2, cols)
            bias = spread8(par, bias_row, cols)
            scale = jnp.sqrt(1.0 - decay * decay) * spread8(par, gain_row, cols) * inv_std
            ones = (1.0 - jnp.exp(wide(aux[0:8, :], L) * log_of(decay))) / (1.0 - decay)
            state = scale * (work[0:8, cols] - average * ones)
            states[0:8, cols] = state

            def step(i, state):
                pair = projected[pl.ds(pl.multiple_of(16 * i, 16), 16), cols].astype(f32)
                outs = []
                for h in range(2):
                    goes, count = flags(2 * i + h)
                    state = (decay * goes) * state + scale * (pair[8 * h : 8 * h + 8, :] - average)
                    states[pl.ds(pl.multiple_of(16 * i + 8 * h + 8, 8), 8), cols] = state
                    v = state + bias
                    soft = jnp.maximum(v, 0.0) + jnp.log(1.0 + jnp.exp(-jnp.abs(v)))
                    outs.append(count * soft)
                store[pl.ds(pl.multiple_of(16 * i, 16), 16), cols] = jnp.concatenate(
                    outs, axis=0
                ).astype(bf16)
                return state

            lax.fori_loop(0, T // 16, step, state)

        blocks(full_scan)

    def layer_backward(layer, upstream, projected, states, turned_grads, gap):
        e = 2 + (1 - layer)
        decay_row, gain_row, bias_row = DECAY + layer, GAIN + layer, BIAS + layer
        run_power = power(par[decay_row : decay_row + 1, :], steps)

        def local_ends(cols):
            decay = spread8(par, decay_row, cols)
            average = spread8(backland.at[layer], 1, cols)
            inv_std = spread8(backland.at[layer], 2, cols)
            bias = spread8(par, bias_row, cols)

            def step(o, carry):
                i = T // 16 - 1 - o
                rows = pl.ds(pl.multiple_of(16 * i, 16), 16)
                pair = projected[rows, cols].astype(f32)
                ups = upstream[rows, cols].astype(f32)
                for h in (1, 0):
                    run, reach, U, V, UN, VN, B, D, DA = carry
                    goes, count = flags(2 * i + h)
                    here = pl.ds(pl.multiple_of(16 * i + 8 * h + 8, 8), 8)
                    state = states[here, cols]
                    before = states[pl.ds(pl.multiple_of(16 * i + 8 * h, 8), 8), cols]
                    local = ups[8 * h : 8 * h + 8, :] * count / (1.0 + jnp.exp(-(state + bias)))
                    states[here, cols] = local
                    normed = (pair[8 * h : 8 * h + 8, :] - average) * inv_std
                    run = local + run
                    kept = goes * before
                    link = decay * goes
                    carry = (
                        link * run,
                        link * reach,
                        U + run,
                        V + reach,
                        UN + run * normed,
                        VN + reach * normed,
                        B + local,
                        D + run * kept,
                        DA + reach * kept,
                    )
                return carry

            one = jnp.ones((8, L), f32)
            run, _, U, V, UN, VN, B, D, DA = lax.fori_loop(
                0, T // 16, step, (zero, one, zero, zero, zero, zero, zero, zero, zero)
            )
            ends[:, cols] = run
            decay_run = power(par[decay_row : decay_row + 1, cols], steps)
            part, factor = jnp.zeros((1, L), f32), jnp.ones((1, L), f32)
            for k in range(7, -1, -1):
                work[k : k + 1, cols] = part
                work[8 + k : 9 + k, cols] = factor
                through = decay_run * wide(aux[16 + k : 17 + k, :], L)
                part = through * part + ends[k : k + 1, cols]
                factor = through * factor
            pay[e, 0:1, cols] = part
            entering, scaled = work[0:8, cols], work[8:16, cols]
            pay[e, 1:2, cols] = down(U + V * entering)
            pay[e, 2:3, cols] = down(V * scaled)
            pay[e, 3:4, cols] = down(UN + VN * entering)
            pay[e, 4:5, cols] = down(VN * scaled)
            pay[e, 5:6, cols] = down(B)
            pay[e, 6:7, cols] = down(D + DA * entering)
            pay[e, 7:8, cols] = down(DA * scaled)

        blocks(local_ends)
        own_decay = own_par[decay_row : decay_row + 1, :]
        own_gain = own_par[gain_row : gain_row + 1, :]

        def gathered():
            whole_power = power(own_decay, T)
            carried = jnp.zeros((1, fb), f32)
            sums = [jnp.zeros((1, fb), f32)] * 4
            for i in range(n - 1, -1, -1):
                rows = arrive[e, i]
                back[e, i, 0:1, :] = carried
                for a, (plain, times) in enumerate(((1, 2), (3, 4), (5, None), (6, 7))):
                    term = rows[plain : plain + 1, :]
                    if times is not None:
                        term = term + rows[times : times + 1, :] * carried
                    sums[a] = sums[a] + term
                carried = whole_power * wide(aux[8 + i : 9 + i, :], fb) * carried + rows[0:1, :]
            for a in range(4):
                seqpay[e, a : a + 1, :] = sums[a]
            seqpay[e, 4:8, :] = jnp.zeros((4, fb), f32)

        def totalled(sums):
            rec, rec_norm = sums[0:1, :], sums[1:2, :]
            for i in range(n):
                back[e, i, 1:2, :] = rec
                back[e, i, 2:3, :] = rec_norm
                back[e, i, 3:4, :] = jnp.zeros((1, fb), f32)
            spread = jnp.sqrt(1.0 - own_decay * own_decay)
            small[3 * layer : 3 * layer + 1, :] = spread * rec_norm
            small[3 * layer + 1 : 3 * layer + 2, :] = sums[2:3, :]
            small[3 * layer + 2 : 3 * layer + 3, :] = (
                sums[3:4, :] - own_decay / spread * own_gain * rec_norm
            )

        exchange(e, gathered, totalled, gap)
        gap("scan")
        total = backland[e, 0:1, :]
        for k in range(7, -1, -1):
            work[k : k + 1, :] = total
            total = run_power * wide(aux[16 + k : 17 + k, :], H) * total + ends[k : k + 1, :]

        def full_scan(cols):
            decay = spread8(par, decay_row, cols)
            average = spread8(backland.at[layer], 1, cols)
            inv_std = spread8(backland.at[layer], 2, cols)
            frames_all = wide(frames_sum[...], L)
            scale = jnp.sqrt(1.0 - decay * decay) * spread8(par, gain_row, cols) * inv_std
            rec = spread8(backland.at[e], 1, cols) / frames_all
            rec_norm = spread8(backland.at[e], 2, cols) / frames_all * inv_std

            def step(o, carry):
                carry, added = carry
                i = T // 16 - 1 - o
                rows = pl.ds(pl.multiple_of(16 * i, 16), 16)
                pair = projected[rows, cols].astype(f32)
                outs = [None, None]
                for h in (1, 0):
                    goes, count = flags(2 * i + h)
                    here = pl.ds(pl.multiple_of(16 * i + 8 * h + 8, 8), 8)
                    run = states[here, cols] + carry
                    centred = pair[8 * h : 8 * h + 8, :] - average
                    outs[h] = scale * (run - count * (rec + rec_norm * centred))
                    carry = (decay * goes) * run
                rounded = jnp.concatenate(outs, axis=0).astype(bf16)
                dp[rows, cols] = rounded
                rounded = rounded.astype(f32)
                return carry, added + rounded[0:8, :] + rounded[8:16, :]

            _, added = lax.fori_loop(0, T // 16, step, (work[0:8, cols], zero))
            whole = down(added)
            sumpay[layer, 0:1, cols] = whole
            high = whole.astype(bf16).astype(f32)
            middle = (whole - high).astype(bf16).astype(f32)
            low = whole - high - middle
            dp[T : T + 16, cols] = jnp.concatenate(
                [high, middle, low, jnp.zeros((13, L), f32)], axis=0
            ).astype(bf16)

        blocks(full_scan)
        sumpay[layer, 1:8, :] = jnp.zeros((7, H), f32)

        def turn(b, _):
            turned_grads[at(b, fb), :] = lax.dot_general(
                eye[...], dp[:, at(b, fb)], (((1,), (1,)), ((), ())), preferred_element_type=f32
            ).astype(bf16)
            return 0

        lax.fori_loop(0, n, turn, 0)

    def input_gradient(weight, result, columns):
        result[:, columns] = jnp.dot(
            dp[0:T, :], weight[:, columns], preferred_element_type=f32
        ).astype(bf16)

    def sum_copy(layer, i):
        return neur_copy(
            sumpay.at[layer, :, at(i, fb)],
            sumland.at[layer, me],
            sum_sends.at[layer, i],
            sum_recvs.at[layer, me],
            i,
        )

    def sum_along(layer, i):
        return seq_copy(
            sumseq.at[layer],
            sumseqland.at[layer, mine],
            sum_sends.at[layer, n + i],
            sum_recvs.at[layer, n + mine],
            i,
        )

    def sum_start(layer):
        others(lambda i: sum_copy(layer, i).start())
        sumland[layer, me] = sumpay[layer, :, own_lanes]

    def sum_middle(layer):
        def wait(i):
            neur_copy(
                sumpay.at[layer, :, at(i, fb)],
                sumland.at[layer, i],
                sum_sends.at[layer, i],
                sum_recvs.at[layer, i],
                i,
            ).wait()

        others(wait)
        total = sumland[layer, 0]
        for i in range(1, n):
            total = total + sumland[layer, i]
        sumseq[layer] = total
        sumseqland[layer, mine] = total
        others(lambda i: sum_along(layer, i).start(), seqs, mine)

    def sum_finish(layer, frames, total):
        def wait(i):
            seq_copy(
                sumseq.at[layer],
                sumseqland.at[layer, i],
                sum_sends.at[layer, n + i],
                sum_recvs.at[layer, n + i],
                i,
            ).wait()

        others(wait, seqs, mine)
        whole = sumseqland[layer, 0]
        for i in range(1, seqs):
            whole = whole + sumseqland[layer, i]
        whole = whole[0:1, :]
        high = whole.astype(bf16).astype(f32)
        middle = (whole - high).astype(bf16).astype(f32)
        low = whole - high - middle
        rows = jnp.concatenate([high, middle, low, jnp.zeros((13, fb), f32)], axis=0).astype(bf16)
        columns = lax.dot_general(
            eye[...], rows, (((1,), (1,)), ((), ())), preferred_element_type=f32
        ).astype(bf16)
        total[...] -= jnp.dot(
            columns, frames[T : T + 16, at(mine, sz.qc)], preferred_element_type=f32
        )

    def place_out(a, ref, dest, i):
        return neur_copy(
            ref.at[:, at(i, fb)], dest.at[me], frame_sends.at[a, i], frame_recvs.at[a, me], i
        )

    def out_arrived(a, ref, dest, i):
        neur_copy(
            ref.at[:, at(i, fb)], dest.at[i], frame_sends.at[a, i], frame_recvs.at[a, i], i
        ).wait()

    def nothing(name):
        return None

    def during_one(name):
        if name == "hop_c":
            gather_two.diagonals()
        if name == "scan":
            crossing(send_g, 1, n // 2 - 1)

    def during_two(name):
        if name == "scan":
            crossing(send_g, max(1, n // 2 - 1), n // 2)

    layer_forward(0, xr, wf_one, p_one, s_one, x_two, during_one)
    gather_two.cores()
    others(lambda i: frames_sent(0, xs, i))
    layer_forward(1, x_two, wf_two, p_two, s_two, xs, during_two)

    def send_out(i):
        place_out(2, xs, out_land, i).start()

    keep_out = pltpu.make_async_copy(xs.at[:, own_lanes], out_land.at[me], local_sems.at[4])
    keep_out.start()
    others(lambda i: frames_wait(1, gr, i))
    others(lambda i: frames_sent(1, gs, i))
    gather_two.drain()

    crossing(send_out, 0, 1)
    layer_backward(
        1,
        gr,
        p_two,
        s_two,
        dpt_two,
        lambda name: crossing(send_out, 1, 2) if name == "scan" else None,
    )
    if n > 4:
        crossing(send_out, 2, 3)
    lax.fori_loop(0, n // 2, lambda i, _: (input_gradient(wf_two, gr, at(i, 2 * fb)), 0)[1], 0)
    sum_start(1)
    if n > 4:
        crossing(send_out, 3, 4)
    reduce_two = Reduce(
        env,
        dpt_two,
        x_two,
        lambda k: land.at[k],
        spare.at[1],
        stage,
        lambda k: stage.at[2 * sz.Z + k],
        fin.at[1],
        reduce_sends.at[1],
        reduce_recvs.at[1],
        fb // 2,
    )
    reduce_one = Reduce(
        env,
        dpt_one,
        xr,
        lambda k: wf_two.at[at(k // seqs, fb), at(k % seqs, sz.qc)],
        spare.at[0],
        stage,
        lambda k: raw.at[:, at(k, sz.qc)],
        fin.at[0],
        reduce_sends.at[0],
        reduce_recvs.at[0],
        fb // 2,
    )
    result_two = Result(
        env, dw_two, land.at[1], final_sends.at[1], final_recvs.at[1], local_sems.at[6]
    )
    result_one = Result(
        env, dw_one, land.at[0], final_sends.at[0], final_recvs.at[0], local_sems.at[7]
    )
    for kind in range(4):
        reduce_two.cores(kind)

    def meanwhile(name):
        if name == "hop_b":
            sum_middle(1)
        if name == "scan":
            reduce_two.diagonals()
            straight(send_out)

    layer_backward(0, gr, p_one, s_one, dpt_one, meanwhile)
    reduce_two.drain_cores()
    reduce_one.cores(0)
    reduce_two.sides()
    reduce_one.diagonals()
    for kind in range(1, 4):
        reduce_one.cores(kind)
    sum_start(0)

    def send_dx(i):
        place_out(3, gs, dx_land, i).start()

    def make_dx(i):
        input_gradient(wf_one, gs, at(i, fb))

    def make_and_send_dx(i):
        make_dx(i)
        send_dx(i)

    straight(make_and_send_dx)
    crossing(make_dx)
    make_dx(me)
    keep_dx = pltpu.make_async_copy(gs.at[:, own_lanes], dx_land.at[me], local_sems.at[5])
    keep_dx.start()
    reduce_two.lines()
    sum_middle(0)
    reduce_two.drain_sides()
    reduce_one.sides(0, 2)
    for i in range(2, sz.Z):
        reduce_one.lines(i - 2, i - 1)
        reduce_one.sides(i, i + 1)
        if i == 2:
            crossing(send_dx, 0, n // 4)
    crossing(send_dx, n // 4 if sz.Z > 2 else 0, n // 2)
    reduce_one.lines(sz.Z - 2, sz.Z - 1)
    reduce_two.finish()
    sum_finish(1, x_two, fin.at[1])
    land[1] = fin[1].astype(bf16)
    result_two.start()
    reduce_one.finish()
    sum_finish(0, xr, fin.at[0])
    land[0] = fin[0].astype(bf16)
    result_one.start()
    result_two.finish()
    others(lambda i: out_arrived(2, xs, out_land, i))
    others(lambda i: out_arrived(3, gs, dx_land, i))
    keep_out.wait()
    keep_dx.wait()
    result_one.finish()
    reduce_two.drain()
    reduce_one.drain_cores()
    reduce_one.drain_sides()
    reduce_one.drain()
    gather_one.drain()
    small[6:8, :] = jnp.zeros((2, fb), f32)


def frame_tables_of(sz, me, lengths, frame_mask, perm, window, cont, counted, aux):
    T, steps = sz.T, sz.steps
    starts, filled = [], 0
    for k in range(lengths.shape[1]):
        starts.append(filled)
        filled = filled + lengths[0, k]
    row = lax.broadcasted_iota(jnp.int32, (T, 128), 0)
    slot = me * T + (row & 7) * steps + (row >> 3)
    goes = jnp.ones((T, 128), f32)
    for start in starts:
        goes = jnp.where(slot == start, 0.0, goes)
    cont[...] = goes
    kept = jnp.where(frame_mask[0:1, window] > 0, 1.0, 0.0)
    kept = jnp.broadcast_to(kept, (128, sz.win)).astype(bf16)
    kept = lax.dot_general(
        perm[me % 2], kept, (((1,), (1,)), ((), ())), preferred_element_type=f32
    )
    counted[...] = jnp.where(slot < filled, kept, 0.0)
    run = lax.broadcasted_iota(jnp.int32, (8, 128), 0)
    first = me * T + run * steps
    behind = jnp.zeros((8, 128), jnp.int32)
    whole, own = jnp.ones((8, 128), f32), jnp.ones((8, 128), f32)
    for start in starts:
        behind = jnp.where(first > start, jnp.maximum(behind, start), behind)
        whole = jnp.where((run * T <= start) & (start < run * T + T), 0.0, whole)
        own = jnp.where((first <= start) & (start < first + steps), 0.0, own)
    aux[0:8, :] = (first - behind).astype(f32)
    aux[8:16, :] = whole
    aux[16:24, :] = own
    place = lax.broadcasted_iota(jnp.int32, (1, sz.tok_dev), 1)
    block = jnp.where((place < filled) & (frame_mask[...] > 0), 1.0, 0.0)
    block = jnp.sum(block, axis=1, keepdims=True)
    aux[24:32, :] = jnp.broadcast_to(block, (8, 128))


def turn_back(
    sz,
    steps,
    x_ref,
    g_ref,
    out_ref,
    dx_ref,
    one_ref,
    two_ref,
    small,
    output,
    input_grad,
    dw_one,
    dw_two,
    gain_one,
    bias_one,
    decay_one,
    gain_two,
    bias_two,
    decay_two,
    perm,
    held,
    widened,
    sems,
):
    step = pl.program_id(0)
    T, fb, win, odd = sz.T, sz.fb, sz.win, sz.odd
    pairs = ((one_ref, dw_one), (two_ref, dw_two))
    reads = [pltpu.make_async_copy(a, held.at[k], sems.at[k]) for k, (a, _) in enumerate(pairs)]
    writes = [pltpu.make_async_copy(widened.at[k], b, sems.at[k]) for k, (_, b) in enumerate(pairs)]

    @pl.when(step == 0)
    def _():
        for move in reads:
            move.start()
        row = lax.broadcasted_iota(jnp.int32, (T, win), 0)
        column = lax.broadcasted_iota(jnp.int32, (T, win), 1)
        frame = (row & 7) * sz.steps + (row >> 3)
        perm[0] = jnp.where(column == frame, 1.0, 0.0).astype(bf16)
        perm[1] = jnp.where(column == frame + odd, 1.0, 0.0).astype(bf16)
        rows = (gain_one, bias_one, decay_one, gain_two, bias_two, decay_two)
        for r, ref in enumerate(rows):
            ref[...] = small[r : r + 1, :]

    output[...] = x_ref[...].astype(f32)
    input_grad[...] = g_ref[...].astype(f32)

    @pl.when(step < sz.n // 4)
    def _():
        for part in range(4):
            half = part % 2
            lanes = pl.ds(2 * T * (part // 2) + (T - odd) * half, win)
            for source, result in ((out_ref, output), (dx_ref, input_grad)):
                result[:, lanes] += lax.dot_general(
                    source[part], perm[half], (((0,), (0,)), ((), ())), preferred_element_type=f32
                )

    @pl.when(step == 1)
    def _():
        for k, (read, write) in enumerate(zip(reads, writes, strict=True)):
            read.wait()
            widened[k] = held[k].astype(f32)
            write.start()

    @pl.when(step == steps - 1)
    def _():
        for move in writes:
            move.wait()


def frames_apart(sz, inputs, weight_one, weight_two, params, lengths, frame_mask, out_grad):
    n, seqs, H, fb, T, Z, qc = sz.n, sz.seqs, sz.H, sz.fb, sz.T, sz.Z, sz.qc
    whole = pl.BlockSpec(memory_space=pltpu.VMEM)
    anywhere = pl.BlockSpec(memory_space=pl.ANY)
    vmem, sem = pltpu.VMEM, pltpu.SemaphoreType.DMA
    frames_shape, longer_shape = (T, H), (sz.K, H)
    matmul = 2 * T * H * H
    out_land, dx_land, dw_one, dw_two, small = pl.pallas_call(
        functools.partial(network, sz),
        out_shape=(
            jax.ShapeDtypeStruct((n, T, fb), bf16),
            jax.ShapeDtypeStruct((n, T, fb), bf16),
            jax.ShapeDtypeStruct((fb, H), bf16),
            jax.ShapeDtypeStruct((fb, H), bf16),
            jax.ShapeDtypeStruct((8, fb), f32),
        ),
        in_specs=[anywhere] * 4 + [whole] * 6 + [pl.BlockSpec(memory_space=pltpu.SMEM), whole],
        out_specs=(anywhere, anywhere, anywhere, anywhere, whole),
        scratch_shapes=[
            vmem((8, fb), f32),
            vmem((T, 128), f32),
            vmem((T, 128), f32),
            vmem((32, 128), f32),
            vmem((1, 128), f32),
            vmem((fb, sz.valid), bf16),
            vmem((2, T, sz.win), bf16),
            vmem((fb, fb), bf16),
            vmem(frames_shape, bf16),
            vmem(frames_shape, bf16),
            vmem(longer_shape, bf16),
            vmem(frames_shape, bf16),
            vmem(frames_shape, bf16),
            vmem(frames_shape, bf16),
            vmem(longer_shape, bf16),
            vmem(longer_shape, bf16),
            vmem((H, sz.K), bf16),
            vmem((H, sz.K), bf16),
            vmem((T + 8, H), f32),
            vmem((T + 8, H), f32),
            vmem((H, H), bf16),
            vmem((H, H), bf16),
            vmem((8 * Z, fb, qc), bf16),
            vmem((5 * Z, fb, qc), bf16),
            vmem((2, fb, qc), bf16),
            vmem((2, fb, qc), f32),
            vmem((8, H), f32),
            vmem((8, H), f32),
            vmem((16, H), f32),
            vmem((4, 8, H), f32),
            vmem((4, n, 8, fb), f32),
            vmem((4, 8, fb), f32),
            vmem((4, seqs, 8, fb), f32),
            vmem((4, n, 8, fb), f32),
            vmem((4, 8, H), f32),
            vmem((2, 8, H), f32),
            vmem((2, n, 8, fb), f32),
            vmem((2, 8, fb), f32),
            vmem((2, seqs, 8, fb), f32),
            sem((8,)),
            sem((n,)),
            sem((n,)),
            sem((4, n)),
            sem((4, n)),
            sem((2, 10 * Z)),
            sem((2, 10 * Z)),
            sem((8, n)),
            sem((8, n)),
            sem((4, seqs)),
            sem((4, seqs)),
            sem((2, 10 * Z)),
            sem((2, 10 * Z)),
            sem((2, 3)),
            sem((2, 3)),
            sem((2, n + seqs)),
            sem((2, n + seqs)),
        ],
        compiler_params=pltpu.CompilerParams(
            collective_id=0, has_side_effects=True, vmem_limit_bytes=63 * 1024 * 1024
        ),
        cost_estimate=pl.CostEstimate(
            flops=6 * matmul, bytes_accessed=16 * fb * H, transcendentals=6 * T * H
        ),
        name="network",
    )(
        inputs,
        out_grad,
        weight_one,
        weight_two,
        *(values.reshape(1, fb) for values in params),
        lengths,
        frame_mask.reshape(1, -1),
    )
    tok = inputs.shape[1]
    groups = n // 4
    steps = pl.cdiv(tok, 4 * T)
    frames_spec = pl.BlockSpec((fb, 4 * T), lambda p: (0, p))
    land_spec = pl.BlockSpec((4, T, fb), lambda p: (jnp.minimum(p, groups - 1), 0, 0))
    row_spec = pl.BlockSpec((1, fb), lambda p: (0, 0))
    results = pl.pallas_call(
        functools.partial(turn_back, sz, steps),
        grid=(steps,),
        out_shape=(jax.ShapeDtypeStruct((fb, tok), f32),) * 2
        + (jax.ShapeDtypeStruct((fb, H), f32),) * 2
        + (jax.ShapeDtypeStruct((1, fb), f32),) * 6,
        in_specs=[frames_spec, frames_spec, land_spec, land_spec, anywhere, anywhere]
        + [pl.BlockSpec((8, fb), lambda p: (0, 0))],
        out_specs=(frames_spec, frames_spec, anywhere, anywhere) + (row_spec,) * 6,
        scratch_shapes=[
            vmem((2, T, sz.win), bf16),
            vmem((2, fb, H), bf16),
            vmem((2, fb, H), f32),
            sem((2,)),
        ],
        compiler_params=pltpu.CompilerParams(vmem_limit_bytes=60 * 1024 * 1024),
        name="turn_back",
    )(inputs, out_grad, out_land, dx_land, dw_one, dw_two, small)
    output, input_grad, dw_one, dw_two = results[:4]
    small = [row.reshape(fb) for row in results[4:]]
    return (
        output,
        input_grad,
        dw_one,
        small[0],
        small[1],
        small[2],
        dw_two,
        small[3],
        small[4],
        small[5],
    )


def frame_tables(lengths, frame_mask):
    positions = jnp.arange(frame_mask.shape[0], dtype=jnp.int32)
    offsets = jnp.cumsum(lengths[0]) - lengths[0]
    filled = jnp.sum(lengths[0])
    begins = jnp.any(positions[:, None] == offsets[None, :], axis=1)
    continues = jnp.where(begins, 0.0, 1.0).astype(jnp.float32)
    counted = jnp.where((positions < filled) & (frame_mask > 0), 1.0, 0.0).astype(jnp.float32)
    return (continues, counted)


def linear_scan(coef_rows, driving, backwards):
    row_count, length = driving.shape
    block_count = length // block_span
    factor = coef_rows.reshape(row_count, block_count, block_span)
    running = driving.reshape(row_count, block_count, block_span)
    places = jnp.arange(block_span, dtype=jnp.int32)
    step = 1
    while step < block_span:
        if backwards:
            mover = jnp.where(places[:, None] == places[None, :] + step, 1.0, 0.0).astype(
                jnp.float32
            )
            edge = jnp.where(places >= block_span - step, 1.0, 0.0).astype(jnp.float32)
        else:
            mover = jnp.where(places[:, None] == places[None, :] - step, 1.0, 0.0).astype(
                jnp.float32
            )
            edge = jnp.where(places < step, 1.0, 0.0).astype(jnp.float32)
        moved_factor = (
            jnp.dot(
                factor, mover, precision=lax.Precision.HIGHEST, preferred_element_type=jnp.float32
            )
            + edge
        )
        moved_running = jnp.dot(
            running, mover, precision=lax.Precision.HIGHEST, preferred_element_type=jnp.float32
        )
        running = factor * moved_running + running
        factor = factor * moved_factor
        step = step * 2
    end_place = 0 if backwards else block_span - 1
    total_factor = factor[:, :, end_place].T
    total_running = running[:, :, end_place].T

    def carry_step(carried, block_pair):
        return (block_pair[0] * carried + block_pair[1], carried)

    _, entering = lax.scan(
        carry_step,
        jnp.zeros((row_count,), jnp.float32),
        (total_factor, total_running),
        reverse=backwards,
    )
    result = running + factor * entering.T[:, :, None]
    return result.reshape(row_count, length)


def layer_forward(layer_input, weight, gain_row, bias_row, decay_rate, continues, counted):
    frames_in = lax.all_to_all(layer_input, "neur", split_axis=1, concat_axis=0, tiled=True)
    projected = jnp.dot(
        lax.all_gather(weight, "neur", axis=0, tiled=True),
        frames_in,
        preferred_element_type=jnp.float32,
    )
    neuron_proj = lax.all_to_all(
        projected.astype(jnp.bfloat16), "neur", split_axis=0, concat_axis=1, tiled=True
    ).astype(jnp.float32)
    sum_first = jnp.sum(counted[None, :] * neuron_proj, axis=1)
    sum_second = jnp.sum(counted[None, :] * neuron_proj * neuron_proj, axis=1)
    sum_first, sum_second, frames = lax.psum((sum_first, sum_second, jnp.sum(counted)), "seq")
    average = sum_first / frames
    inv_std = lax.rsqrt(sum_second / frames - average * average + epsilon)
    normed = (neuron_proj - average[:, None]) * inv_std[:, None]
    spread = jnp.sqrt(1.0 - decay_rate * decay_rate)
    states = linear_scan(
        decay_rate[:, None] * continues[None, :], (spread * gain_row)[:, None] * normed, False
    )
    layer_out = counted[None, :] * jax.nn.softplus(states + bias_row[:, None])
    return (layer_out, (frames_in, None, normed, inv_std, frames, states))


def layer_backward(
    upstream, weight, gain_row, bias_row, decay_rate, continues, counted, kept_state
):
    frames_in, full_weight, normed, inv_std, frames, states = kept_state
    local_grad = upstream * counted[None, :] * jax.nn.sigmoid(states + bias_row[:, None])
    following = jnp.concatenate([continues[1:], jnp.zeros((1,), jnp.float32)])
    coef_rows = decay_rate[:, None] * following[None, :]
    state_grad = linear_scan(coef_rows, local_grad, True)
    sum_rec, sum_rec_norm, sum_local = lax.psum(
        (
            jnp.sum(state_grad, axis=1),
            jnp.sum(state_grad * normed, axis=1),
            jnp.sum(local_grad, axis=1),
        ),
        "seq",
    )
    spread = jnp.sqrt(1.0 - decay_rate * decay_rate)
    gain_grad = spread * sum_rec_norm
    proj_grad = (spread * gain_row * inv_std)[:, None] * (
        state_grad - counted[None, :] * (sum_rec[:, None] + sum_rec_norm[:, None] * normed) / frames
    )
    driving = (spread * gain_row)[:, None] * normed
    decay_part = jnp.sum(state_grad * (states - driving), axis=1) / decay_rate
    grad_frames = lax.all_to_all(
        proj_grad.astype(jnp.bfloat16), "neur", split_axis=1, concat_axis=0, tiled=True
    )
    grad_rows = grad_frames
    input_frames = jnp.einsum(
        "ot,oi->it",
        grad_rows,
        lax.all_gather(weight, "neur", axis=0, tiled=True),
        preferred_element_type=jnp.float32,
    )
    input_grad = lax.all_to_all(
        input_frames.astype(jnp.bfloat16), "neur", split_axis=0, concat_axis=1, tiled=True
    ).astype(jnp.float32)
    grad_rows = grad_frames
    weight_rows = lax.psum_scatter(
        jnp.einsum("ot,it->oi", grad_rows, frames_in, preferred_element_type=jnp.float32),
        "neur",
        scatter_dimension=0,
        tiled=True,
    )
    weight_grad, decay_sum = lax.psum((weight_rows, decay_part), "seq")
    decay_grad = decay_sum - decay_rate / spread * gain_row * sum_rec_norm
    return (input_grad, weight_grad, gain_grad, sum_local, decay_grad)


def shards(
    inputs,
    weight_one,
    weight_two,
    gain_one,
    gain_two,
    bias_one,
    bias_two,
    decay_one,
    decay_two,
    lengths,
    frame_mask,
    out_grad,
):
    seqs, n = lax.axis_size("seq"), lax.axis_size("neur")
    H, (fb, tok) = weight_one.shape[1], inputs.shape
    if fits(n, seqs, H, fb, tok):
        params = (gain_one, gain_two, bias_one, bias_two, decay_one, decay_two)
        return frames_apart(
            Sizes(n, seqs, H, fb, tok),
            inputs,
            weight_one,
            weight_two,
            params,
            lengths,
            frame_mask,
            out_grad,
        )
    continues, counted = frame_tables(lengths, frame_mask)
    first_out, first_kept = layer_forward(
        inputs, weight_one, gain_one, bias_one, decay_one, continues, counted
    )
    second_out, second_kept = layer_forward(
        first_out.astype(jnp.bfloat16),
        weight_two,
        gain_two,
        bias_two,
        decay_two,
        continues,
        counted,
    )
    output = inputs.astype(jnp.float32) + second_out
    upstream = out_grad.astype(jnp.float32)
    middle_grad, weight_two_grad, gain_two_grad, bias_two_grad, decay_two_grad = layer_backward(
        upstream, weight_two, gain_two, bias_two, decay_two, continues, counted, second_kept
    )
    lower_grad, weight_one_grad, gain_one_grad, bias_one_grad, decay_one_grad = layer_backward(
        middle_grad, weight_one, gain_one, bias_one, decay_one, continues, counted, first_kept
    )
    return (
        output,
        upstream + lower_grad,
        weight_one_grad,
        gain_one_grad,
        bias_one_grad,
        decay_one_grad,
        weight_two_grad,
        gain_two_grad,
        bias_two_grad,
        decay_two_grad,
    )


def solution(mesh):
    placed = (
        P("neur", "seq"),
        P("neur", None),
        P("neur", None),
        P("neur"),
        P("neur"),
        P("neur"),
        P("neur"),
        P("neur"),
        P("neur"),
        P("seq", None),
        P("seq"),
        P("neur", "seq"),
    )
    return jax.shard_map(
        shards,
        mesh=mesh,
        in_specs=placed,
        out_specs=(
            P("neur", "seq"),
            P("neur", "seq"),
            P("neur", None),
            P("neur"),
            P("neur"),
            P("neur"),
            P("neur", None),
            P("neur"),
            P("neur"),
            P("neur"),
        ),
        check_vma=False,
    )
```
